32 devices in a mesh: fsdp: 2 (over x), context: 4 (over z), tensor: 4 (over y, core).
Axes of the slice: x: 2, y: 2, z: 4, core: 2. Of those that a mesh axis runs over, the one named last changes fastest.
Arguments:
- hidden_in: bfloat16 [4, 512, 2048], P('fsdp', 'context'), may hold values from -6 to 6
- segment_ids: int32 [4, 512], P('fsdp', 'context'), may hold values from 0 to 3, as said below
- norm_gains: bfloat16 [2, 2, 2048], P(None, None, ('fsdp', 'context')), may hold values from 0.25 to 1.75
- norm_shifts: bfloat16 [2, 2, 2048], P(None, None, ('fsdp', 'context')), may hold values from -3 to 3
- qkv_weight: bfloat16 [2, 2048, 3, 2048], P(None, ('fsdp', 'context'), None, 'tensor'), may hold values from -0.125 to 0.125
- qkv_bias: bfloat16 [2, 3, 2048], P(None, None, 'tensor'), may hold values from -4 to 4
- out_weight: bfloat16 [2, 2048, 2048], P(None, ('fsdp', 'context'), 'tensor'), may hold values from -1 to 1
- gate_up_weight: bfloat16 [2, 2048, 2, 5632], P(None, ('fsdp', 'context'), None, 'tensor'), may hold values from -0.125 to 0.125
- down_weight: bfloat16 [2, 2048, 5632], P(None, ('fsdp', 'context'), 'tensor'), may hold values from -0.078125 to 0.078125
- cotangent: bfloat16 [4, 512, 2048], P('fsdp', 'context'), may hold values from -6 to 6
Outputs:
- block_out: bfloat16 [4, 512, 2048], P('fsdp', 'context')
- input_grad: float32 [4, 512, 2048], P('fsdp', 'context')
- gains_grad: float32 [2, 2, 2048], P(None, None, ('fsdp', 'context'))
- shifts_grad: float32 [2, 2, 2048], P(None, None, ('fsdp', 'context'))
- qkv_weight_grad: float32 [2, 2048, 3, 2048], P(None, ('fsdp', 'context'), None, 'tensor')
- qkv_bias_grad: float32 [2, 3, 2048], P(None, None, 'tensor')
- out_weight_grad: float32 [2, 2048, 2048], P(None, ('fsdp', 'context'), 'tensor')
- gate_up_grad: float32 [2, 2048, 2, 5632], P(None, ('fsdp', 'context'), None, 'tensor')
- down_grad: float32 [2, 2048, 5632], P(None, ('fsdp', 'context'), 'tensor')
The draws below stay inside these ranges and needn't reach their ends.
Inputs may be any that keep to these rules, and one draw needn't show every extreme that they name: `segment_ids`: within each sequence of 512 tokens the ids never fall and the first is 0; a run of equal ids is one document.
All inputs are finite; a program needn't handle non-finite values.
Results may differ from the reference program's by a relative error of at most 0.017.
Values may be sent and summed in bfloat16 or wider, within the bound.
A program may use at most 256 MiB of HBM per device.

```python
import math
from functools import partial
import jax
import jax.numpy as jnp
from jax import lax

H = 32
HD = 64
FF = 5632
D = 2048
ROT = 16
LAYERS = 2
SEQ_LEN = 512
SHARD = 128
SEQUENCES = 4
TOKENS = 2048


def draw_segment_ids(key, part):
    key = jax.random.fold_in(key, 7)
    sequences = SEQUENCES
    key_start, key_end, key_third = jax.random.split(key, 3)
    opening = jax.random.randint(key_start, (sequences, 1), 1, SHARD)
    closing = jax.random.randint(key_end, (sequences, 1), SEQ_LEN - SHARD + 1, SEQ_LEN - 1)
    third_cut = jax.random.randint(key_third, (sequences, 1), closing + 1, SEQ_LEN)
    places = jnp.arange(SEQ_LEN, dtype=jnp.int32)[None, :]
    labels = (places >= opening).astype(jnp.int32) + (places >= closing).astype(jnp.int32) + (places >= third_cut).astype(jnp.int32)
    return labels


def block_scale(key, dims, pieces, smallest, top_value):
    level, own = 1.0, jax.random.fold_in(key, 6)
    for dim, shards_of in pieces:
        heights = jnp.exp(jax.random.uniform(jax.random.fold_in(own, dim), (shards_of,), jnp.float32, smallest / len(pieces), top_value / len(pieces)))
        level = level * jnp.repeat(heights, dims[dim] // shards_of).reshape([-1 if axis == dim else 1 for axis in range(len(dims))])
    return level


def normal_values(own_key, dims, scale, reach, shards=(), kind=jnp.bfloat16):
    entries = scale * jax.random.normal(own_key, dims, jnp.float32)
    if shards:
        entries = entries * block_scale(own_key, dims, shards, -0.22, 0.18)
    return jnp.clip(entries, -reach, reach).astype(kind)


def setup_inputs(seed: int = 0) -> dict:
    keys = jax.random.split(jax.random.key(seed), 11)
    hidden_in = normal_values(keys[0], (SEQUENCES, SEQ_LEN, D), 1.0, 6.0, ((0, 2), (1, 4)))
    segment_ids = draw_segment_ids(jax.random.fold_in(keys[10], 71), 0)
    norm_gains = jnp.clip(1.0 + 0.15 * jax.random.normal(keys[2], (LAYERS, 2, D), jnp.float32), 0.25, 1.75).astype(jnp.bfloat16)
    norm_shifts = normal_values(keys[3], (LAYERS, 2, D), 0.3, 3.0, ((2, 8),))
    qkv_weight = normal_values(keys[4], (LAYERS, D, 3, D), D ** -0.5, 0.125, ((1, 8), (3, 4)))
    qkv_bias = normal_values(keys[5], (LAYERS, 3, D), 0.5, 4.0, ((2, 4),))
    out_weight = normal_values(keys[6], (LAYERS, D, D), (D // 64) ** -0.5, 1.0, ((1, 8), (2, 4)))
    gate_up_weight = normal_values(keys[7], (LAYERS, D, 2, FF), D ** -0.5, 0.125, ((1, 8), (3, 4)))
    down_weight = normal_values(keys[8], (LAYERS, D, FF), FF ** -0.5, 0.078125, ((1, 8), (2, 4)))
    cotangent = normal_values(keys[9], (SEQUENCES, SEQ_LEN, D), 1.0, 6.0, ((0, 2), (1, 4)))
    return dict(hidden_in=hidden_in, segment_ids=segment_ids, norm_gains=norm_gains, norm_shifts=norm_shifts, qkv_weight=qkv_weight, qkv_bias=qkv_bias, out_weight=out_weight, gate_up_weight=gate_up_weight, down_weight=down_weight, cotangent=cotangent)


EPS = 1e-05
ROPE_BASE = 10000.0
NEGATIVE = -1e+30
PRECISE = lax.Precision.HIGHEST

@jax.custom_vjp
def low(v):
    return lax.optimization_barrier(v.astype(jnp.bfloat16)).astype(jnp.float32)

@jax.custom_vjp
def low_back(v):
    return v

def low_keep(v):
    return (low(v), None)

def low_pass(kept, grad):
    return (grad,)

def back_keep(v):
    return (v, None)

def back_low(kept, grad):
    return (low(grad),)
low.defvjp(low_keep, low_pass)
low_back.defvjp(back_keep, back_low)

def layer_norm(values, gain_row, shift_row):
    row_mean = lax.optimization_barrier(jnp.mean(values, -1, keepdims=True))
    centred = values - row_mean
    row_var = lax.optimization_barrier(jnp.mean(centred * centred, -1, keepdims=True))
    return centred * lax.rsqrt(row_var + EPS) * gain_row + shift_row

def rotate(values, cosine_rows, sine_rows):
    middle = ROT // 2
    leading = values[..., :middle]
    trailing = values[..., middle:ROT]
    return jnp.concatenate([leading * cosine_rows - trailing * sine_rows, trailing * cosine_rows + leading * sine_rows, values[..., ROT:]], -1)

def rotary_tables(labels):
    places = jnp.arange(labels.shape[-1], dtype=jnp.int32)
    fresh_start = jnp.concatenate([jnp.ones(labels.shape[:-1] + (1,), jnp.bool_), labels[..., 1:] != labels[..., :-1]], -1)
    starts = lax.cummax(jnp.where(fresh_start, places, 0).astype(jnp.int32), axis=labels.ndim - 1)
    offsets = (places - starts).astype(jnp.float32)
    frequency = jnp.exp(jnp.arange(ROT // 2, dtype=jnp.float32) * (-2.0 * math.log(ROPE_BASE) / ROT))
    angles = offsets[..., None] * frequency
    return (jnp.cos(angles), jnp.sin(angles))

def attend_head(head_items):
    queries, keys_in, values, labels, cosine_rows, sine_rows = head_items
    places = jnp.arange(labels.shape[0], dtype=jnp.int32)
    allowed = (labels[:, None] == labels[None, :]) & (places[:, None] >= places[None, :])
    q_rot = low(rotate(queries, cosine_rows, sine_rows))
    k_rot = low(rotate(keys_in, cosine_rows, sine_rows))
    scaling = HD ** (-0.5)
    scores = low_back(scaling * jnp.dot(q_rot, k_rot.T, precision=PRECISE))
    scores = jnp.where(allowed, scores, NEGATIVE)
    row_peak = lax.optimization_barrier(jnp.max(scores, -1, keepdims=True))
    exponent = jnp.exp(scores - row_peak)
    probabilities = exponent / lax.optimization_barrier(jnp.sum(exponent, -1, keepdims=True))
    return jnp.dot(low(probabilities), values, precision=PRECISE)

def forward(stream, gain_rows, shift_rows, w_qkv, b_qkv, w_out, w_gate_up, w_down, head_labels, head_cosine, head_sine):
    for layer_index in range(LAYERS):
        normed = low(layer_norm(stream, gain_rows[layer_index, 0], shift_rows[layer_index, 0]))
        projected = jnp.dot(normed, w_qkv[layer_index].reshape(D, 3 * D), precision=PRECISE) + b_qkv[layer_index].reshape(3 * D)
        projected = low_back(low(projected))
        head_rows = projected.reshape(SEQUENCES, SEQ_LEN, 3, H, HD).transpose(2, 0, 3, 1, 4).reshape(3, SEQUENCES * H, SEQ_LEN, HD)
        mixture = lax.map(jax.checkpoint(attend_head), (head_rows[0], head_rows[1], head_rows[2], head_labels, head_cosine, head_sine))
        mixture = mixture.reshape(SEQUENCES, H, SEQ_LEN, HD).transpose(0, 2, 1, 3).reshape(TOKENS, D)
        mixture = low_back(low(mixture))
        branch = low_back(jnp.dot(mixture, w_out[layer_index].T, precision=PRECISE))
        middle = stream + branch
        normed_two = low(layer_norm(middle, gain_rows[layer_index, 1], shift_rows[layer_index, 1]))
        gate_up = low_back(jnp.einsum('td,dcf->tcf', normed_two, w_gate_up[layer_index], precision=PRECISE))
        activated = low(jax.nn.silu(gate_up[:, 0]) * gate_up[:, 1])
        stream = middle + low_back(jnp.dot(activated, w_down[layer_index].T, precision=PRECISE))
    return stream

def reference(hidden_in, segment_ids, norm_gains, norm_shifts, qkv_weight, qkv_bias, out_weight, gate_up_weight, down_weight, cotangent):
    labels = segment_ids.reshape(SEQUENCES, SEQ_LEN)
    cosine_rows, sine_rows = rotary_tables(labels)
    head_labels = jnp.repeat(labels, H, axis=0)
    head_cosine = jnp.repeat(cosine_rows, H, axis=0)
    head_sine = jnp.repeat(sine_rows, H, axis=0)
    layered = partial(forward, head_labels=head_labels, head_cosine=head_cosine, head_sine=head_sine)
    flat_in = hidden_in.reshape(TOKENS, D).astype(jnp.float32)
    block_out, pullback = jax.vjp(layered, flat_in, norm_gains.astype(jnp.float32), norm_shifts.astype(jnp.float32), qkv_weight.astype(jnp.float32), qkv_bias.astype(jnp.float32), out_weight.astype(jnp.float32), gate_up_weight.astype(jnp.float32), down_weight.astype(jnp.float32))
    gradients = pullback(cotangent.reshape(TOKENS, D).astype(jnp.float32))
    return (block_out.reshape(SEQUENCES, SEQ_LEN, D).astype(jnp.bfloat16), gradients[0].reshape(SEQUENCES, SEQ_LEN, D), gradients[1], gradients[2], gradients[3], gradients[4], gradients[5], gradients[6], gradients[7])
```

```python
import functools
import math

import jax
import jax.numpy as jnp
from jax import lax
from jax.experimental import pallas as pl
from jax.experimental.pallas import tpu as pltpu
from jax.sharding import PartitionSpec as P

HD = 64
ROT = 16
EPS = 1e-05
ROPE_BASE = 10000.0
NEGATIVE = -1e30
MESH = pl.DeviceIdType.MESH
BF = jnp.bfloat16
F32 = jnp.float32
MIB = 2**20
TILE = 128


def dot_nn(a, b):
    return jnp.dot(a, b, preferred_element_type=F32)


def dot_nt(a, b):
    return lax.dot_general(a, b, (((1,), (1,)), ((), ())), preferred_element_type=F32)


def dot_tn(a, b):
    return lax.dot_general(a, b, (((0,), (0,)), ((), ())), preferred_element_type=F32)


class Place:
    def __init__(self, nc, nk):
        self.nc, self.nk = nc, nk
        self.c = lax.axis_index("context")
        self.t = lax.axis_index("tensor")
        self.k = lax.rem(self.t, nk)

    def mate(self):
        return {"tensor": self.t + 1 - 2 * self.k}

    def right(self):
        return {"context": self.c + 1}

    def left(self):
        return {"context": self.c - 1}


def greet(place):
    barrier = pltpu.get_barrier_semaphore()
    pl.semaphore_signal(barrier, inc=1, device_id=place.mate(), device_id_type=MESH)

    @pl.when(place.c > 0)
    def _():
        pl.semaphore_signal(barrier, inc=1, device_id=place.left(), device_id_type=MESH)

    @pl.when(place.c < place.nc - 1)
    def _():
        pl.semaphore_signal(barrier, inc=1, device_id=place.right(), device_id_type=MESH)

    has_left = jnp.minimum(place.c, 1)
    has_right = jnp.minimum(place.nc - 1 - place.c, 1)
    pl.semaphore_wait(barrier, 1 + has_left + has_right)


def gather_part(place, own_ref, out_ref, sems, rows):
    nc, nk, c, k = place.nc, place.nk, place.c, place.k
    local_sem, line_send, line_recv, mate_send, mate_recv = sems

    def slot(source, kk):
        return out_ref.at[pl.ds(pl.multiple_of((source * nk + kk) * rows, rows), rows)]

    def line_copy(source, device, first, way):
        return pltpu.make_async_remote_copy(
            src_ref=own_ref if first else slot(source, k),
            dst_ref=slot(source, k),
            send_sem=line_send.at[way, source],
            recv_sem=line_recv.at[source],
            device_id=device,
            device_id_type=MESH,
        )

    def mate_copy(source, first):
        return pltpu.make_async_remote_copy(
            src_ref=own_ref if first else slot(source, k),
            dst_ref=slot(source, k),
            send_sem=mate_send.at[source],
            recv_sem=mate_recv.at[source],
            device_id=place.mate(),
            device_id_type=MESH,
        )

    def mate_arrival(source):
        return pltpu.make_async_remote_copy(
            src_ref=own_ref,
            dst_ref=slot(source, 1 - k),
            send_sem=mate_send.at[source],
            recv_sem=mate_recv.at[source],
            device_id=place.mate(),
            device_id_type=MESH,
        )

    @pl.when(c < nc - 1)
    def _():
        line_copy(c, place.right(), True, 0).start()

    @pl.when(c > 0)
    def _():
        line_copy(c, place.left(), True, 1).start()

    mate_copy(c, True).start()
    keep = pltpu.make_async_copy(own_ref, slot(c, k), local_sem)
    keep.start()
    for step in range(1, nc):
        source = c - step

        @pl.when(source >= 0)
        def _():
            line_copy(source, place.left(), False, 0).wait_recv()

            @pl.when(c < nc - 1)
            def _():
                line_copy(source, place.right(), False, 0).start()

            mate_copy(source, False).start()

        other = c + step

        @pl.when(other <= nc - 1)
        def _():
            line_copy(other, place.right(), False, 1).wait_recv()

            @pl.when(c > 0)
            def _():
                line_copy(other, place.left(), False, 1).start()

            mate_copy(other, False).start()

    keep.wait()
    for source in range(nc):
        mate_arrival(source).wait_recv()
        mate_copy(source, False).wait_send()

        @pl.when((source <= c) & (c < nc - 1))
        def _():
            line_copy(source, place.right(), False, 0).wait_send()

        @pl.when((source >= c) & (c > 0))
        def _():
            line_copy(source, place.left(), False, 1).wait_send()


def gather_scratch(nc):
    dma = pltpu.SemaphoreType.DMA
    return [dma(()), dma((2, nc)), dma((nc,)), dma((nc,)), dma((nc,))]


def scatter_part(place, part_ref, bufs, rows):
    nc, nk, c, k = place.nc, place.nk, place.c, place.k
    mate_buf, to_right, to_left, from_left, from_right = bufs[:5]
    mate_send, mate_recv, right_send, right_recv, left_send, left_recv = bufs[5:]

    def block(dest, kk):
        return part_ref.at[pl.ds(pl.multiple_of((dest * nk + kk) * rows, rows), rows)]

    def mate_copy(dest):
        return pltpu.make_async_remote_copy(
            src_ref=block(dest, 1 - k),
            dst_ref=mate_buf.at[dest],
            send_sem=mate_send.at[dest],
            recv_sem=mate_recv.at[dest],
            device_id=place.mate(),
            device_id_type=MESH,
        )

    def right_copy(dest):
        return pltpu.make_async_remote_copy(
            src_ref=to_right.at[dest],
            dst_ref=from_left.at[dest],
            send_sem=right_send.at[dest],
            recv_sem=right_recv.at[dest],
            device_id=place.right(),
            device_id_type=MESH,
        )

    def left_copy(dest):
        return pltpu.make_async_remote_copy(
            src_ref=to_left.at[dest],
            dst_ref=from_right.at[dest],
            send_sem=left_send.at[dest],
            recv_sem=left_recv.at[dest],
            device_id=place.left(),
            device_id_type=MESH,
        )

    def each(visit_right, visit_left):
        for step in range(nc - 1):
            far = nc - 1 - step

            @pl.when(far > c)
            def _():
                visit_right(far)

            @pl.when(step < c)
            def _():
                visit_left(step)

    def send_mate(dest):
        mate_copy(dest).start()

    each(send_mate, send_mate)
    mate_copy(c).start()

    def chip_sum(dest):
        mate_copy(dest).wait_recv()
        return block(dest, k)[...].astype(F32) + mate_buf[dest].astype(F32)

    def pass_right(dest):
        total = chip_sum(dest)
        to_right[dest] = total.astype(BF)

        @pl.when(c > 0)
        def _():
            right_copy(dest).wait_recv()
            to_right[dest] = (total + from_left[dest].astype(F32)).astype(BF)

        right_copy(dest).start()

    def pass_left(dest):
        total = chip_sum(dest)
        to_left[dest] = total.astype(BF)

        @pl.when(c < nc - 1)
        def _():
            left_copy(dest).wait_recv()
            to_left[dest] = (total + from_right[dest].astype(F32)).astype(BF)

        left_copy(dest).start()

    each(pass_right, pass_left)
    total = chip_sum(c)

    @pl.when(c > 0)
    def _():
        right_copy(c).wait_recv()

    @pl.when(c < nc - 1)
    def _():
        left_copy(c).wait_recv()

    total = total + jnp.where(c > 0, from_left[c].astype(F32), 0.0)
    total = total + jnp.where(c < nc - 1, from_right[c].astype(F32), 0.0)
    for dest in range(nc):
        mate_copy(dest).wait_send()

        @pl.when(dest > c)
        def _():
            right_copy(dest).wait_send()

        @pl.when(dest < c)
        def _():
            left_copy(dest).wait_send()

    return total


def scatter_scratch(nc, rows, width):
    dma = pltpu.SemaphoreType.DMA
    return [pltpu.VMEM((nc, rows, width), BF) for _ in range(5)] + [dma((nc,)) for _ in range(6)]


N_SCATTER = 11
VMEM_SPEC = pl.BlockSpec(memory_space=pltpu.VMEM)
ANY_SPEC = pl.BlockSpec(memory_space=pl.ANY)


def unit_rows_of(values):
    row_mean = jnp.mean(values, -1, keepdims=True)
    centred = values - row_mean
    row_var = jnp.mean(centred * centred, -1, keepdims=True)
    inverse = lax.rsqrt(row_var + EPS)
    return centred * inverse, inverse


def norm_back(grad_rows, saved_rows, gain_row):
    unit_rows, inverse = unit_rows_of(saved_rows)
    scaled = grad_rows * gain_row
    inner = inverse * (
        scaled
        - jnp.mean(scaled, -1, keepdims=True)
        - unit_rows * jnp.mean(scaled * unit_rows, -1, keepdims=True)
    )
    return inner, jnp.sum(grad_rows * unit_rows, 0, keepdims=True), jnp.sum(grad_rows, 0, keepdims=True)


def gather_kernel(nc, nk, own_ref, out_ref, *sems):
    place = Place(nc, nk)
    greet(place)
    gather_part(place, own_ref, out_ref, sems, own_ref.shape[0])


def gather_rows(own, nc, nk):
    rows, width = own.shape
    return pl.pallas_call(
        functools.partial(gather_kernel, nc, nk),
        out_shape=jax.ShapeDtypeStruct((nc * nk * rows, width), BF),
        in_specs=[ANY_SPEC],
        out_specs=ANY_SPEC,
        scratch_shapes=gather_scratch(nc),
        compiler_params=pltpu.CompilerParams(collective_id=1, has_side_effects=True),
        cost_estimate=pl.CostEstimate(flops=0, bytes_accessed=64 * MIB, transcendentals=0),
    )(own)


def next_norm_kernel(nc, nk, part_ref, stream_ref, gain_ref, shift_ref, full_ref, new_ref, low_ref, *scratch):
    place = Place(nc, nk)
    greet(place)
    rows = stream_ref.shape[0]
    new_rows = stream_ref[...] + scatter_part(place, part_ref, scratch[:N_SCATTER], rows)
    new_ref[...] = new_rows
    unit_rows, _ = unit_rows_of(new_rows)
    low_ref[...] = (unit_rows * gain_ref[...] + shift_ref[...]).astype(BF)
    gather_part(place, low_ref, full_ref, scratch[N_SCATTER:], rows)


def next_norm(part, stream, gain_row, shift_row, nc, nk):
    rows, width = stream.shape
    return pl.pallas_call(
        functools.partial(next_norm_kernel, nc, nk),
        out_shape=[
            jax.ShapeDtypeStruct((nc * nk * rows, width), BF),
            jax.ShapeDtypeStruct((rows, width), F32),
            jax.ShapeDtypeStruct((rows, width), BF),
        ],
        in_specs=[VMEM_SPEC] * 4,
        out_specs=[ANY_SPEC, VMEM_SPEC, VMEM_SPEC],
        scratch_shapes=scatter_scratch(nc, rows, width) + gather_scratch(nc),
        compiler_params=pltpu.CompilerParams(
            collective_id=2, has_side_effects=True, vmem_limit_bytes=24 * MIB
        ),
        cost_estimate=pl.CostEstimate(flops=0, bytes_accessed=128 * MIB, transcendentals=0),
    )(part, stream, gain_row, shift_row)[:2]


def last_rows_kernel(nc, nk, part_ref, stream_ref, new_ref, *scratch):
    place = Place(nc, nk)
    greet(place)
    rows = stream_ref.shape[0]
    new_ref[...] = stream_ref[...] + scatter_part(place, part_ref, scratch, rows)


def last_rows(part, stream, nc, nk):
    rows, width = stream.shape
    return pl.pallas_call(
        functools.partial(last_rows_kernel, nc, nk),
        out_shape=jax.ShapeDtypeStruct((rows, width), F32),
        in_specs=[VMEM_SPEC] * 2,
        out_specs=VMEM_SPEC,
        scratch_shapes=scatter_scratch(nc, rows, width),
        compiler_params=pltpu.CompilerParams(
            collective_id=3, has_side_effects=True, vmem_limit_bytes=24 * MIB
        ),
        cost_estimate=pl.CostEstimate(flops=0, bytes_accessed=64 * MIB, transcendentals=0),
    )(part, stream)


def back_norm_kernel(
    nc, nk, part_ref, grad_ref, saved_ref, gain_ref, full_ref, new_ref, norm_ref, low_ref, *scratch
):
    place = Place(nc, nk)
    greet(place)
    rows = grad_ref.shape[0]
    total = scatter_part(place, part_ref, scratch[:N_SCATTER], rows)
    inner, gain_grad, shift_grad = norm_back(total, saved_ref[...], gain_ref[...])
    new_rows = grad_ref[...] + inner
    new_ref[...] = new_rows
    norm_ref[0:1] = gain_grad
    norm_ref[1:2] = shift_grad
    low_ref[...] = new_rows.astype(BF)
    gather_part(place, low_ref, full_ref, scratch[N_SCATTER:], rows)


def back_norm(part, grad, saved, gain_row, nc, nk):
    rows, width = grad.shape
    return pl.pallas_call(
        functools.partial(back_norm_kernel, nc, nk),
        out_shape=[
            jax.ShapeDtypeStruct((nc * nk * rows, width), BF),
            jax.ShapeDtypeStruct((rows, width), F32),
            jax.ShapeDtypeStruct((2, width), F32),
            jax.ShapeDtypeStruct((rows, width), BF),
        ],
        in_specs=[VMEM_SPEC] * 4,
        out_specs=[ANY_SPEC, VMEM_SPEC, VMEM_SPEC, VMEM_SPEC],
        scratch_shapes=scatter_scratch(nc, rows, width) + gather_scratch(nc),
        compiler_params=pltpu.CompilerParams(
            collective_id=4, has_side_effects=True, vmem_limit_bytes=24 * MIB
        ),
        cost_estimate=pl.CostEstimate(flops=0, bytes_accessed=128 * MIB, transcendentals=0),
    )(part, grad, saved, gain_row)[:3]


def last_back_kernel(nc, nk, part_ref, grad_ref, saved_ref, gain_ref, new_ref, norm_ref, *scratch):
    place = Place(nc, nk)
    greet(place)
    rows = grad_ref.shape[0]
    total = scatter_part(place, part_ref, scratch, rows)
    inner, gain_grad, shift_grad = norm_back(total, saved_ref[...], gain_ref[...])
    new_ref[...] = grad_ref[...] + inner
    norm_ref[0:1] = gain_grad
    norm_ref[1:2] = shift_grad


def last_back(part, grad, saved, gain_row, nc, nk):
    rows, width = grad.shape
    return pl.pallas_call(
        functools.partial(last_back_kernel, nc, nk),
        out_shape=[
            jax.ShapeDtypeStruct((rows, width), F32),
            jax.ShapeDtypeStruct((2, width), F32),
        ],
        in_specs=[VMEM_SPEC] * 4,
        out_specs=[VMEM_SPEC, VMEM_SPEC],
        scratch_shapes=scatter_scratch(nc, rows, width),
        compiler_params=pltpu.CompilerParams(
            collective_id=5, has_side_effects=True, vmem_limit_bytes=24 * MIB
        ),
        cost_estimate=pl.CostEstimate(flops=0, bytes_accessed=64 * MIB, transcendentals=0),
    )(part, grad, saved, gain_row)


def swap_lanes(values):
    lane = lax.broadcasted_iota(jnp.int32, values.shape, 1) % HD
    width = values.shape[1]
    up = pltpu.roll(values, width - ROT // 2, 1)
    down = pltpu.roll(values, ROT // 2, 1)
    return jnp.where(lane < ROT // 2, up, jnp.where(lane < ROT, down, 0.0))


def allowed_of(label_col, label_row):
    length = label_col.shape[0]
    row = lax.broadcasted_iota(jnp.int32, (length, length), 0)
    col = lax.broadcasted_iota(jnp.int32, (length, length), 1)
    return (label_col == label_row) & (row >= col)


def attend_kernel(proj_ref, col_ref, row_ref, cos_ref, sin_ref, mix_ref, q_ref, k_ref, lse_ref):
    blocks, length, triple = proj_ref.shape
    width = triple // 3
    heads = width // HD
    allowed = allowed_of(col_ref[...], row_ref[...])
    cosine, sine = cos_ref[...], sin_ref[...]
    scaling = HD ** (-0.5)
    for b in range(blocks):
        for ref, at in ((q_ref, 0), (k_ref, 1)):
            values = proj_ref[b, :, at * width : (at + 1) * width].astype(F32)
            ref[b] = (values * cosine + swap_lanes(values) * sine).astype(BF)
        for h in range(heads):
            span = slice(h * HD, (h + 1) * HD)
            scores = scaling * dot_nt(q_ref[b, :, span], k_ref[b, :, span])
            scores = jnp.where(allowed, scores, NEGATIVE)
            peak = jnp.max(scores, -1, keepdims=True)
            exponent = jnp.exp(scores - peak)
            total = jnp.sum(exponent, -1, keepdims=True)
            probs = (exponent * (1.0 / total)).astype(BF)
            values = proj_ref[b, :, 2 * width + h * HD : 2 * width + (h + 1) * HD]
            mix_ref[b, :, span] = dot_nn(probs, values).astype(BF)
            at = b * heads + h
            lse_ref[:, at : at + 1] = peak + jnp.log(total)


def attend(proj, label_col, label_row, cosine, sine):
    blocks, length, triple = proj.shape
    width = triple // 3
    heads = blocks * width // HD
    return pl.pallas_call(
        attend_kernel,
        out_shape=[
            jax.ShapeDtypeStruct((blocks, length, width), BF),
            jax.ShapeDtypeStruct((blocks, length, width), BF),
            jax.ShapeDtypeStruct((blocks, length, width), BF),
            jax.ShapeDtypeStruct((length, heads), F32),
        ],
        in_specs=[VMEM_SPEC] * 5,
        out_specs=[VMEM_SPEC] * 4,
        compiler_params=pltpu.CompilerParams(vmem_limit_bytes=32 * MIB),
        cost_estimate=pl.CostEstimate(flops=2**30, bytes_accessed=16 * MIB, transcendentals=2**20),
    )(proj, label_col, label_row, cosine, sine)


def attend_back_kernel(
    proj_ref, q_ref, k_ref, lse_ref, grad_ref, col_ref, row_ref, cos_ref, sin_ref, out_ref, bias_ref
):
    blocks, length, triple = proj_ref.shape
    width = triple // 3
    heads = width // HD
    allowed = allowed_of(col_ref[...], row_ref[...])
    cosine, sine = cos_ref[...], sin_ref[...]
    scaling = HD ** (-0.5)
    for b in range(blocks):
        parts = [[], [], []]
        for h in range(heads):
            span = slice(h * HD, (h + 1) * HD)
            at = b * heads + h
            q_rows, k_rows, out_grad = q_ref[b, :, span], k_ref[b, :, span], grad_ref[b, :, span]
            scores = jnp.where(allowed, scaling * dot_nt(q_rows, k_rows), NEGATIVE)
            probs = jnp.exp(scores - lse_ref[:, at : at + 1])
            values = proj_ref[b, :, 2 * width + h * HD : 2 * width + (h + 1) * HD]
            prob_grad = dot_nt(out_grad, values)
            inner = jnp.sum(probs * prob_grad, -1, keepdims=True)
            score_low = (probs * (prob_grad - inner)).astype(BF)
            parts[0].append(scaling * dot_nn(score_low, k_rows))
            parts[1].append(scaling * dot_tn(score_low, q_rows))
            parts[2].append(dot_tn(probs.astype(BF), out_grad))
        for at in range(3):
            rows = jnp.concatenate(parts[at], axis=1)
            if at < 2:
                rows = rows * cosine - swap_lanes(rows) * sine
            low = rows.astype(BF)
            out_ref[b, :, at * width : (at + 1) * width] = low
            bias_ref[b : b + 1, at * width : (at + 1) * width] = jnp.sum(
                low.astype(F32), 0, keepdims=True
            )


def attend_back(proj, q_rot, k_rot, lse, grad, label_col, label_row, cosine, sine):
    blocks, length, triple = proj.shape
    return pl.pallas_call(
        attend_back_kernel,
        out_shape=[
            jax.ShapeDtypeStruct((blocks, length, triple), BF),
            jax.ShapeDtypeStruct((blocks, triple), F32),
        ],
        in_specs=[VMEM_SPEC] * 9,
        out_specs=[VMEM_SPEC] * 2,
        compiler_params=pltpu.CompilerParams(vmem_limit_bytes=40 * MIB),
        cost_estimate=pl.CostEstimate(flops=2**31, bytes_accessed=24 * MIB, transcendentals=2**20),
    )(proj, q_rot, k_rot, lse, grad, label_col, label_row, cosine, sine)


class Plan:
    def __init__(self, mesh, hidden_in):
        self.nf, self.nc, self.nt = mesh.shape["fsdp"], mesh.shape["context"], mesh.shape["tensor"]
        self.ns = hidden_in.shape[0]
        self.nk = self.nt // self.ns
        self.f = lax.axis_index("fsdp")
        self.c = lax.axis_index("context")
        self.t = lax.axis_index("tensor")
        self.s, self.k = self.t // self.nk, self.t % self.nk

    def pair(self, df, ds):
        nf, nt, nk = self.nf, self.nt, self.nk
        moves = []
        for f in range(nf):
            for t in range(nt):
                s, k = t // nk, t % nk
                moves.append((((f + df) % nf) * nt + (s ^ ds) * nk + k, f * nt + t))
        return moves

    def take(self, value, df, ds):
        if df == 0 and ds == 0:
            return value
        return lax.ppermute(value, ("fsdp", "tensor"), self.pair(df, ds))

    def ranges(self):
        return [(df, ds) for df in range(self.nf) for ds in range(self.ns)]

    def gather_context(self, value):
        nc = self.nc
        out = jnp.zeros((nc,) + value.shape, value.dtype)
        out = lax.dynamic_update_index_in_dim(out, value, self.c, 0)
        for step in range(1, nc):
            moved = lax.ppermute(value, "context", [(i, (i + step) % nc) for i in range(nc)])
            out = lax.dynamic_update_index_in_dim(out, moved, (self.c + nc - step) % nc, 0)
        return out


def exchange_context(value):
    return lax.all_to_all(value, "context", split_axis=0, concat_axis=0, tiled=True)


def pack_columns(weights, nc, sub):
    out = []
    for weight in weights:
        rows, columns = weight.shape
        if columns < nc * sub:
            weight = jnp.pad(weight, ((0, 0), (0, nc * sub - columns)))
        out.append(weight.reshape(rows, nc, sub).transpose(1, 0, 2))
    return jnp.concatenate(out, axis=2)


def unpack_columns(blocks, position, columns, sub):
    cut = blocks[:, :, position * sub : (position + 1) * sub]
    return cut.transpose(1, 0, 2).reshape(cut.shape[1], -1)[:, :columns]


def fetch(plan, pack):
    nc, rows, width = pack.shape
    mine = exchange_context(pack).reshape(nc * rows, width)
    return {at: plan.take(mine, *at) for at in plan.ranges()}


def deliver(plan, grads):
    nc = plan.nc
    total = grads[(0, 0)].astype(F32)
    for df, ds in plan.ranges():
        if df or ds:
            moved = plan.take(grads[((plan.nf - df) % plan.nf, ds)], df, ds)
            total = total + moved.astype(F32)
    total = total.astype(BF)
    rows, width = total.shape
    return exchange_context(total.reshape(nc, rows // nc, width)).astype(F32)


def rotary_tables(labels, width):
    places = jnp.arange(labels.shape[-1], dtype=jnp.int32)
    fresh = jnp.concatenate([jnp.ones((1,), jnp.bool_), labels[1:] != labels[:-1]])
    starts = lax.cummax(jnp.where(fresh, places, 0))
    offsets = (places - starts).astype(F32)
    frequency = jnp.exp(jnp.arange(ROT // 2, dtype=F32) * (-2.0 * math.log(ROPE_BASE) / ROT))
    angles = offsets[:, None] * frequency
    cosine, sine = jnp.cos(angles), jnp.sin(angles)
    rest = jnp.ones((labels.shape[0], HD - ROT), F32)
    cosine = jnp.concatenate([cosine, cosine, rest], 1)
    sine = jnp.concatenate([-sine, sine, 0.0 * rest], 1)
    return jnp.tile(cosine, (1, width // HD)), jnp.tile(sine, (1, width // HD))


def body(
    mesh,
    hidden_in,
    segment_ids,
    norm_gains,
    norm_shifts,
    qkv_weight,
    qkv_bias,
    out_weight,
    gate_up_weight,
    down_weight,
    cotangent,
):
    plan = Plan(mesh, hidden_in)
    nf, nc, nk, ns = plan.nf, plan.nc, plan.nk, plan.ns
    layers = qkv_weight.shape[0]
    _, shard_rows, width = hidden_in.shape
    rows = shard_rows // nk
    part = width // nf
    q_sub = qkv_weight.shape[3] // nc
    hidden = gate_up_weight.shape[3]
    f_sub = -(-hidden // (nc * TILE)) * TILE

    def own_rows(value):
        mine = lax.dynamic_index_in_dim(value, plan.s, 0, keepdims=False)
        mine = lax.dynamic_slice_in_dim(mine, plan.k * rows, rows, 0)
        blocks = mine.reshape(rows, nf, part)
        return jnp.roll(blocks, -plan.f, axis=1).reshape(rows, width)

    labels = plan.gather_context(segment_ids)
    labels = lax.dynamic_index_in_dim(labels, plan.s, 1, keepdims=False).reshape(-1)
    norms = jnp.stack([norm_gains, norm_shifts])
    norms = plan.gather_context(norms)
    norms = jnp.moveaxis(norms, 0, 3).reshape(2, layers, 2, part)
    norms = jnp.concatenate([plan.take(norms, df, 0) for df in range(nf)], axis=-1).astype(F32)
    gains, shifts = norms[0], norms[1]
    cosine, sine = rotary_tables(labels, q_sub)
    label_col, label_row = labels[:, None], labels[None, :]
    own_bias = lax.dynamic_slice_in_dim(qkv_bias, plan.c * q_sub, q_sub, 2)
    biases = [plan.take(own_bias, 0, ds).reshape(layers, 1, 3 * q_sub).astype(F32) for ds in range(ns)]

    attn_packs, ffn_packs = [], []
    for layer in range(layers):
        attn_packs.append(
            pack_columns(
                [qkv_weight[layer, :, 0], qkv_weight[layer, :, 1], qkv_weight[layer, :, 2], out_weight[layer]],
                nc,
                q_sub,
            )
        )
        ffn_packs.append(
            pack_columns(
                [gate_up_weight[layer, :, 0], gate_up_weight[layer, :, 1], down_weight[layer]], nc, f_sub
            )
        )

    def cut(full, df):
        return full[:, df * part : (df + 1) * part]

    stream = own_rows(hidden_in).astype(F32)
    unit_rows, _ = unit_rows_of(stream)
    normed = (unit_rows * gains[0, 0] + shifts[0, 0]).astype(BF)
    full_one = gather_rows(normed, nc, nk)
    grad = own_rows(cotangent)
    grad_full = gather_rows(grad, nc, nk)
    grad = grad.astype(F32)
    kept = []
    for layer in range(layers):
        attn = fetch(plan, attn_packs[layer])
        proj = jnp.stack(
            [
                (
                    sum(dot_nn(cut(full_one, df), attn[(df, ds)][:, : 3 * q_sub]) for df in range(nf))
                    + biases[ds][layer]
                ).astype(BF)
                for ds in range(ns)
            ]
        )
        mixed, q_rot, k_rot, lse = attend(proj, label_col, label_row, cosine, sine)
        partial_sum = jnp.concatenate(
            [
                sum(dot_nt(mixed[ds], attn[(df, ds)][:, 3 * q_sub :]) for ds in range(ns)).astype(BF)
                for df in range(nf)
            ],
            axis=1,
        )
        full_two, middle = next_norm(partial_sum, stream, gains[layer, 1:2], shifts[layer, 1:2], nc, nk)
        ffn = fetch(plan, ffn_packs[layer])
        gates, ups, acts = [], [], []
        for ds in range(ns):
            both = sum(dot_nn(cut(full_two, df), ffn[(df, ds)][:, : 2 * f_sub]) for df in range(nf))
            gate, up = both[:, :f_sub], both[:, f_sub:]
            gates.append(gate)
            ups.append(up)
            acts.append((jax.nn.silu(gate) * up).astype(BF))
        partial_sum = jnp.concatenate(
            [
                sum(dot_nt(acts[ds], ffn[(df, ds)][:, 2 * f_sub :]) for ds in range(ns)).astype(BF)
                for df in range(nf)
            ],
            axis=1,
        )
        saved = (attn, ffn, stream, middle, full_one, full_two, proj, mixed, q_rot, k_rot, lse, gates, ups, acts)
        kept.append(saved)
        if layer + 1 < layers:
            full_one, stream = next_norm(
                partial_sum, middle, gains[layer + 1, 0:1], shifts[layer + 1, 0:1], nc, nk
            )
        else:
            stream = last_rows(partial_sum, middle, nc, nk)

    def whole_rows(value):
        blocks = value.reshape(rows, nf, part)
        value = jnp.roll(blocks, plan.f, axis=1).reshape(rows, width)
        nt = plan.nt
        out = jnp.zeros((nt, rows, width), value.dtype)
        out = lax.dynamic_update_index_in_dim(out, value, plan.t, 0)
        for step in range(1, nt):
            moved = lax.ppermute(value, "tensor", [(i, (i + step) % nt) for i in range(nt)])
            out = lax.dynamic_update_index_in_dim(out, moved, (plan.t + nt - step) % nt, 0)
        return out.reshape(ns, shard_rows, width)

    block_out = whole_rows(stream.astype(BF))

    qkv_grads, out_grads, gate_up_grads, down_grads, norm_grads, bias_grads = [], [], [], [], [], []
    for layer in range(layers - 1, -1, -1):
        attn, ffn, stream, middle, full_one, full_two, proj, mixed, q_rot, k_rot, lse, gates, ups, acts = kept[layer]
        low = []
        for ds in range(ns):
            act_grad = sum(dot_nn(cut(grad_full, df), ffn[(df, ds)][:, 2 * f_sub :]) for df in range(nf))
            gate, up = gates[ds], ups[ds]
            sg = jax.nn.sigmoid(gate)
            gate_grad = act_grad * up * sg * (1.0 + gate * (1.0 - sg))
            up_grad = act_grad * gate * sg
            low.append(jnp.concatenate([gate_grad, up_grad], 1).astype(BF))
        partial_sum = jnp.concatenate(
            [
                sum(dot_nt(low[ds], ffn[(df, ds)][:, : 2 * f_sub]) for ds in range(ns)).astype(BF)
                for df in range(nf)
            ],
            axis=1,
        )
        ffn_grads = {}
        for df, ds in plan.ranges():
            ffn_grads[(df, ds)] = jnp.concatenate(
                [dot_tn(cut(full_two, df), low[ds]), dot_tn(cut(grad_full, df), acts[ds])], 1
            ).astype(BF)
        middle_full, grad, norm_two = back_norm(partial_sum, grad, middle, gains[layer, 1:2], nc, nk)
        ffn_sum = deliver(plan, ffn_grads)
        gate_up_grads.append(
            jnp.stack([unpack_columns(ffn_sum, at, hidden, f_sub) for at in range(2)], axis=1)
        )
        down_grads.append(unpack_columns(ffn_sum, 2, hidden, f_sub))
        mixed_grad = jnp.stack(
            [
                sum(dot_nn(cut(middle_full, df), attn[(df, ds)][:, 3 * q_sub :]) for df in range(nf)).astype(BF)
                for ds in range(ns)
            ]
        )
        proj_grad, bias_grad = attend_back(
            proj, q_rot, k_rot, lse, mixed_grad, label_col, label_row, cosine, sine
        )
        bias_grads.append(bias_grad)
        partial_sum = jnp.concatenate(
            [
                sum(dot_nt(proj_grad[ds], attn[(df, ds)][:, : 3 * q_sub]) for ds in range(ns)).astype(BF)
                for df in range(nf)
            ],
            axis=1,
        )
        attn_grads = {}
        for df, ds in plan.ranges():
            attn_grads[(df, ds)] = jnp.concatenate(
                [dot_tn(cut(full_one, df), proj_grad[ds]), dot_tn(cut(middle_full, df), mixed[ds])], 1
            ).astype(BF)
        if layer > 0:
            grad_full, grad, norm_one = back_norm(partial_sum, grad, stream, gains[layer, 0:1], nc, nk)
        else:
            grad, norm_one = last_back(partial_sum, grad, stream, gains[layer, 0:1], nc, nk)
        norm_grads.append(jnp.stack([norm_one, norm_two], axis=1))
        attn_sum = deliver(plan, attn_grads)
        qkv_grads.append(
            jnp.stack([unpack_columns(attn_sum, at, nc * q_sub, q_sub) for at in range(3)], axis=1)
        )
        out_grads.append(unpack_columns(attn_sum, 3, nc * q_sub, q_sub))

    input_grad = whole_rows(grad.astype(BF)).astype(F32)

    norm_part = jnp.stack(norm_grads[::-1], axis=1).reshape(2, layers, 2, nf, part)
    norm_total = sum(
        plan.take(norm_part[:, :, :, (nf - df) % nf], df, 0) for df in range(nf)
    )
    norm_total = lax.psum(norm_total, ("context", "tensor"))
    piece = part // nc
    norm_total = lax.dynamic_slice_in_dim(norm_total, plan.c * piece, piece, 3)

    bias_part = jnp.stack(bias_grads[::-1])
    bias_total = sum(plan.take(bias_part[:, ds], 0, ds) for ds in range(ns))
    bias_total = sum(plan.take(bias_total, df, 0) for df in range(nf))
    bias_total = plan.gather_context(bias_total).reshape(nc, layers, 3, q_sub)
    bias_total = bias_total.transpose(1, 2, 0, 3).reshape(layers, 3, nc * q_sub)

    def in_order(values):
        return jnp.stack(values[::-1])

    return (
        block_out,
        input_grad,
        norm_total[0],
        norm_total[1],
        in_order(qkv_grads),
        bias_total,
        in_order(out_grads),
        in_order(gate_up_grads),
        in_order(down_grads),
    )


def solution(mesh):
    return jax.shard_map(
        functools.partial(body, mesh),
        mesh=mesh,
        in_specs=(
            P("fsdp", "context", None),
            P("fsdp", "context"),
            P(None, None, ("fsdp", "context")),
            P(None, None, ("fsdp", "context")),
            P(None, ("fsdp", "context"), None, "tensor"),
            P(None, None, "tensor"),
            P(None, ("fsdp", "context"), "tensor"),
            P(None, ("fsdp", "context"), None, "tensor"),
            P(None, ("fsdp", "context"), "tensor"),
            P("fsdp", "context", None),
        ),
        out_specs=(
            P("fsdp", "context", None),
            P("fsdp", "context", None),
            P(None, None, ("fsdp", "context")),
            P(None, None, ("fsdp", "context")),
            P(None, ("fsdp", "context"), None, "tensor"),
            P(None, None, "tensor"),
            P(None, ("fsdp", "context"), "tensor"),
            P(None, ("fsdp", "context"), None, "tensor"),
            P(None, ("fsdp", "context"), "tensor"),
        ),
        check_vma=False,
    )
```

```python
import functools
import math

import jax
import jax.numpy as jnp
from jax import lax
from jax.experimental import pallas as pl
from jax.experimental.pallas import tpu as pltpu
from jax.sharding import PartitionSpec as P

HD = 64
ROT = 16
EPS = 1e-05
ROPE_BASE = 10000.0
NEGATIVE = -1e30
MESH = pl.DeviceIdType.MESH
BF = jnp.bfloat16
F32 = jnp.float32
MIB = 2**20
TILE = 128


def dot_nn(a, b):
    return jnp.dot(a, b, preferred_element_type=F32)


def dot_nt(a, b):
    return lax.dot_general(a, b, (((1,), (1,)), ((), ())), preferred_element_type=F32)


def dot_tn(a, b):
    return lax.dot_general(a, b, (((0,), (0,)), ((), ())), preferred_element_type=F32)


class Sizes:
    def __init__(self, mesh, ns):
        self.nf, self.nc, self.nt = mesh.shape["fsdp"], mesh.shape["context"], mesh.shape["tensor"]
        self.ns = ns
        self.nk = self.nt // ns


class Place:
    def __init__(self, sizes):
        self.sizes = sizes
        self.f = lax.axis_index("fsdp")
        self.c = lax.axis_index("context")
        self.t = lax.axis_index("tensor")
        self.s, self.k = self.t // sizes.nk, lax.rem(self.t, sizes.nk)

    def mate(self):
        return {"tensor": self.t + 1 - 2 * self.k}

    def twin(self):
        return {"tensor": self.t + self.sizes.nk * (1 - 2 * self.s)}

    def right(self):
        return {"context": self.c + 1}

    def left(self):
        return {"context": self.c - 1}

    def ahead(self, step):
        return {"context": lax.rem(self.c + step, self.sizes.nc)}

    def across(self, step):
        return {"fsdp": lax.rem(self.f + step, self.sizes.nf)}


def greet(place, kinds):
    barrier = pltpu.get_barrier_semaphore()
    nc, nf = place.sizes.nc, place.sizes.nf

    def signal(device):
        pl.semaphore_signal(barrier, inc=1, device_id=device, device_id_type=MESH)

    count = 0
    if "mate" in kinds:
        signal(place.mate())
        count += 1
    if "ctx" in kinds:
        for step in range(1, nc):
            signal(place.ahead(step))
        count += nc - 1
    elif "line" in kinds:

        @pl.when(place.c > 0)
        def _():
            signal(place.left())

        @pl.when(place.c < nc - 1)
        def _():
            signal(place.right())

        count += jnp.minimum(place.c, 1) + jnp.minimum(nc - 1 - place.c, 1)
    if "fsdp" in kinds:
        for step in range(1, nf):
            signal(place.across(step))
        count += nf - 1
    if "twin" in kinds:
        signal(place.twin())
        count += 1
    pl.semaphore_wait(barrier, count)


def push(src, dst, send, recv, device):
    return pltpu.make_async_remote_copy(
        src_ref=src, dst_ref=dst, send_sem=send, recv_sem=recv, device_id=device, device_id_type=MESH
    )


DMA = pltpu.SemaphoreType.DMA
VMEM_SPEC = pl.BlockSpec(memory_space=pltpu.VMEM)
ANY_SPEC = pl.BlockSpec(memory_space=pl.ANY)


class Gather:
    def __init__(self, place, own, out, sems, rows):
        self.place, self.own, self.out, self.rows = place, own, out, rows
        self.local, self.line_send, self.line_recv, self.mate_send, self.mate_recv = sems

    @staticmethod
    def scratch(sizes):
        nc = sizes.nc
        return [DMA(()), DMA((2, nc)), DMA((nc,)), DMA((nc,)), DMA((nc,))]

    def slot(self, source, k):
        rows = self.rows
        at = (source * self.place.sizes.nk + k) * rows
        return self.out.at[pl.ds(pl.multiple_of(at, rows), rows)]

    def line(self, source, device, first, way):
        mine = self.slot(source, self.place.k)
        return push(
            self.own if first else mine, mine, self.line_send.at[way, source], self.line_recv.at[source], device
        )

    def pass_on(self, source, first):
        mine = self.slot(source, self.place.k)
        place = self.place
        return push(
            self.own if first else mine, mine, self.mate_send.at[source], self.mate_recv.at[source], place.mate()
        )

    def keep(self):
        return pltpu.make_async_copy(self.own, self.slot(self.place.c, self.place.k), self.local)

    def begin(self):
        place, c, nc = self.place, self.place.c, self.place.sizes.nc

        @pl.when(c < nc - 1)
        def _():
            self.line(c, place.right(), True, 0).start()

        @pl.when(c > 0)
        def _():
            self.line(c, place.left(), True, 1).start()

        self.pass_on(c, True).start()
        self.keep().start()

    def forward(self, step):
        place, c, nc = self.place, self.place.c, self.place.sizes.nc
        source = c - step

        @pl.when(source >= 0)
        def _():
            self.line(source, place.left(), False, 0).wait_recv()

            @pl.when(c < nc - 1)
            def _():
                self.line(source, place.right(), False, 0).start()

            self.pass_on(source, False).start()

        other = c + step

        @pl.when(other <= nc - 1)
        def _():
            self.line(other, place.right(), False, 1).wait_recv()

            @pl.when(c > 0)
            def _():
                self.line(other, place.left(), False, 1).start()

            self.pass_on(other, False).start()

    def end(self):
        place, c, nc = self.place, self.place.c, self.place.sizes.nc
        self.keep().wait()
        for source in range(nc):
            arrival = self.slot(source, 1 - place.k)
            push(arrival, arrival, self.mate_send.at[source], self.mate_recv.at[source], place.mate()).wait_recv()
            self.pass_on(source, False).wait_send()

            @pl.when((source <= c) & (c < nc - 1))
            def _():
                self.line(source, place.right(), False, 0).wait_send()

            @pl.when((source >= c) & (c > 0))
            def _():
                self.line(source, place.left(), False, 1).wait_send()


def scatter_part(place, part_ref, bufs, rows):
    nc, nk, c, k = place.sizes.nc, place.sizes.nk, place.c, place.k
    mate_buf, to_right, to_left, from_left, from_right = bufs[:5]
    mate_send, mate_recv, right_send, right_recv, left_send, left_recv = bufs[5:]

    def block(dest, kk):
        return part_ref.at[pl.ds(pl.multiple_of((dest * nk + kk) * rows, rows), rows)]

    def mate_copy(dest):
        return push(
            block(dest, 1 - k), mate_buf.at[dest], mate_send.at[dest], mate_recv.at[dest], place.mate()
        )

    def right_copy(dest):
        return push(
            to_right.at[dest], from_left.at[dest], right_send.at[dest], right_recv.at[dest], place.right()
        )

    def left_copy(dest):
        return push(
            to_left.at[dest], from_right.at[dest], left_send.at[dest], left_recv.at[dest], place.left()
        )

    def each(visit_right, visit_left):
        for step in range(nc - 1):
            far = nc - 1 - step

            @pl.when(far > c)
            def _():
                visit_right(far)

            @pl.when(step < c)
            def _():
                visit_left(step)

    def send_mate(dest):
        mate_copy(dest).start()

    each(send_mate, send_mate)
    mate_copy(c).start()

    def chip_sum(dest):
        mate_copy(dest).wait_recv()
        return block(dest, k)[...].astype(F32) + mate_buf[dest].astype(F32)

    def pass_right(dest):
        total = chip_sum(dest)
        to_right[dest] = total.astype(BF)

        @pl.when(c > 0)
        def _():
            right_copy(dest).wait_recv()
            to_right[dest] = (total + from_left[dest].astype(F32)).astype(BF)

        right_copy(dest).start()

    def pass_left(dest):
        total = chip_sum(dest)
        to_left[dest] = total.astype(BF)

        @pl.when(c < nc - 1)
        def _():
            left_copy(dest).wait_recv()
            to_left[dest] = (total + from_right[dest].astype(F32)).astype(BF)

        left_copy(dest).start()

    each(pass_right, pass_left)
    total = chip_sum(c)

    @pl.when(c > 0)
    def _():
        right_copy(c).wait_recv()

    @pl.when(c < nc - 1)
    def _():
        left_copy(c).wait_recv()

    total = total + jnp.where(c > 0, from_left[c].astype(F32), 0.0)
    total = total + jnp.where(c < nc - 1, from_right[c].astype(F32), 0.0)
    for dest in range(nc):
        mate_copy(dest).wait_send()

        @pl.when(dest > c)
        def _():
            right_copy(dest).wait_send()

        @pl.when(dest < c)
        def _():
            left_copy(dest).wait_send()

    return total


def scatter_scratch(sizes, rows, width):
    nc = sizes.nc
    return [pltpu.VMEM((nc, rows, width), BF) for _ in range(5)] + [DMA((nc,)) for _ in range(6)]


N_SCATTER = 11


class Rider:
    kinds = ()

    def bind(self, place, ins, outs, sems):
        self.place, self.r_ins, self.r_outs, self.r_sems = place, ins, outs, sems

    def begin(self):
        pass

    def middle(self):
        pass

    def late(self):
        pass

    def end(self):
        pass


class Exchange(Rider):
    kinds = ("ctx",)

    def __init__(self, sizes, ins, out, pieces, when="begin"):
        self.ins, self.outs, self.pieces, self.when = ins, [out], pieces, when
        count = max(sizes.nc - 1, 1)
        self.sems = [DMA(()), DMA((count,)), DMA((count,))]

    def begin(self):
        if self.when == "begin":
            self.start()

    def middle(self):
        if self.when == "middle":
            self.start()

    def start(self):
        place, nc = self.place, self.place.sizes.nc
        local, send, recv = self.r_sems
        for step in range(1, nc):
            for source_of, target_of in self.pieces:
                push(
                    source_of(self.r_ins, lax.rem(place.c + step, nc)),
                    target_of(self.r_outs[0], place.c),
                    send.at[step - 1],
                    recv.at[step - 1],
                    place.ahead(step),
                ).start()
        for source_of, target_of in self.pieces:
            pltpu.make_async_copy(
                source_of(self.r_ins, place.c), target_of(self.r_outs[0], place.c), local
            ).start()

    def whole(self):
        raise NotImplementedError

    def wait_own(self):
        whole = self.whole()
        pltpu.make_async_copy(whole, whole, self.r_sems[0]).wait()

    def wait_from(self, step):
        whole = self.whole()
        _, send, recv = self.r_sems
        push(whole, whole, send.at[step - 1], recv.at[step - 1], self.place.ahead(step)).wait_recv()

    def wait_sent(self):
        whole = self.whole()
        _, send, recv = self.r_sems
        for step in range(1, self.place.sizes.nc):
            push(whole, whole, send.at[step - 1], recv.at[step - 1], self.place.ahead(step)).wait_send()

    def end(self):
        self.wait_own()
        for step in range(1, self.place.sizes.nc):
            self.wait_from(step)
        self.wait_sent()


class WeightExchange(Exchange):
    def __init__(self, sizes, layer, rows, sources, sub, when="begin"):
        ins, pieces, arrays = [], [], []
        for array, base in sources:
            if not any(array is known for known in arrays):
                arrays.append(array)
            at = [known is array for known in arrays].index(True)
            pieces.append(self.piece(at, layer * rows, rows, base, sub, len(pieces)))
        out = jax.ShapeDtypeStruct((sizes.nc * rows, sub * len(pieces)), BF)
        super().__init__(sizes, arrays, out, pieces, when)
        self.rows = rows

    @staticmethod
    def piece(at, first, rows, base, sub, position):
        def source_of(refs, dest):
            return refs[at].at[pl.ds(first, rows), pl.ds(pl.multiple_of(base + dest * sub, TILE), sub)]

        def target_of(out, source):
            return out.at[pl.ds(pl.multiple_of(source * rows, rows), rows), pl.ds(position * sub, sub)]

        return source_of, target_of

    def whole(self):
        return self.r_outs[0].at[pl.ds(0, self.rows)]


class GradExchange(Exchange):
    def __init__(self, sizes, total, sub, when="begin"):
        rows = total.shape[0] // sizes.nc
        count = total.shape[1] // sub
        out = jax.ShapeDtypeStruct((rows, sizes.nc * total.shape[1]), BF)
        pieces = [self.piece(rows, sub, position, sizes.nc) for position in range(count)]
        super().__init__(sizes, [total], out, pieces, when)
        self.rows = rows

    @staticmethod
    def piece(rows, sub, position, nc):
        def source_of(refs, dest):
            return refs[0].at[pl.ds(pl.multiple_of(dest * rows, rows), rows), pl.ds(position * sub, sub)]

        def target_of(out, source):
            return out.at[:, pl.ds(pl.multiple_of(position * nc * sub + source * sub, TILE), sub)]

        return source_of, target_of

    def whole(self):
        return self.r_ins[0].at[pl.ds(0, self.rows)]


class Spread(Rider):
    kinds = ("fsdp", "twin")

    def __init__(self, sizes, mine, blocks=1):
        if isinstance(mine, Exchange):
            self.source, shape, self.ins = mine, mine.outs[0].shape, []
        else:
            self.source, shape, self.ins = None, mine.shape, [mine]
        rows, width = shape
        self.part, self.blocks, self.rows = rows, blocks, rows // blocks
        self.outs = [jax.ShapeDtypeStruct((sizes.ns, sizes.nf * rows, width), BF)]
        others = max(sizes.nf - 1, 1)
        self.sems = [DMA((blocks,))] + [DMA((blocks, others)) for _ in range(8)] + [DMA((blocks,)) for _ in range(4)]

    def mine(self, block, half, whole=False):
        ref = self.r_ins[0] if self.source is None else self.source.r_outs[0]
        return ref.at[self.span(0, block, half, whole)]

    def span(self, df, block, half, whole=False):
        length = self.rows if whole else self.rows // 2
        at = df * self.part + block * self.rows + half * (self.rows // 2)
        return pl.ds(pl.multiple_of(at, length), length)

    def out(self, ds, df, block, half):
        return self.r_outs[0].at[ds, self.span(df, block, half)]

    def first_copies(self, block):
        place, nf, sems, first = self.place, self.place.sizes.nf, self.r_sems, []
        for step in range(1, nf):
            at, df = step - 1, nf - step
            first.append(
                push(
                    self.mine(block, 0),
                    self.out(0, df, block, 0),
                    sems[1].at[block, at],
                    sems[2].at[block, at],
                    place.across(step),
                )
            )
        first.append(
            push(self.mine(block, 1), self.out(1, 0, block, 1), sems[9].at[block], sems[10].at[block], place.twin())
        )
        return first

    def second_copies(self, block):
        place, nf, sems, second = self.place, self.place.sizes.nf, self.r_sems, []
        for step in range(1, nf):
            at, df = step - 1, nf - step
            across = place.across(step)
            second.append(
                push(
                    self.mine(block, 1), self.out(0, df, block, 1), sems[3].at[block, at], sems[4].at[block, at], across
                )
            )
            second.append(
                push(
                    self.out(1, 0, block, 1),
                    self.out(1, df, block, 1),
                    sems[5].at[block, at],
                    sems[6].at[block, at],
                    across,
                )
            )
            second.append(
                push(
                    self.out(0, df, block, 0),
                    self.out(1, df, block, 0),
                    sems[7].at[block, at],
                    sems[8].at[block, at],
                    place.twin(),
                )
            )
        second.append(
            push(self.mine(block, 0), self.out(1, 0, block, 0), sems[11].at[block], sems[12].at[block], place.twin())
        )
        return second

    def keep(self, block):
        return pltpu.make_async_copy(
            self.mine(block, 0, True), self.r_outs[0].at[0, self.span(0, block, 0, True)], self.r_sems[0].at[block]
        )

    def first(self, block):
        for copy in self.first_copies(block):
            copy.start()
        self.keep(block).start()

    def second(self, block):
        for copy in self.first_copies(block):
            copy.wait_recv()
        for copy in self.second_copies(block):
            copy.start()

    def finish(self, block):
        for copy in self.first_copies(block):
            copy.wait_send()
        for copy in self.second_copies(block):
            copy.wait_recv()
            copy.wait_send()
        self.keep(block).wait()

    def begin(self):
        if self.source is None:
            self.first(0)

    def middle(self):
        if self.source is None:
            self.second(0)
        else:
            self.source.end()
            self.first(0)

    def late(self):
        if self.source is not None:
            self.second(0)

    def end(self):
        self.finish(0)


class Ending(Rider):
    def __init__(self, exchange):
        self.kinds, self.ins, self.outs, self.sems = exchange.kinds, exchange.ins, exchange.outs, exchange.sems
        self.exchange = exchange

    def bind(self, *refs):
        self.exchange.bind(*refs)

    def begin(self):
        self.exchange.begin()


class GradFirst(Rider):
    kinds = ("fsdp", "twin")

    def __init__(self, sizes, grads):
        ns, rows, width = grads.shape
        self.part = rows // sizes.nf
        half = self.half = self.part // 2
        others = max(sizes.nf - 1, 1)
        self.ins = [grads]
        self.outs = [
            jax.ShapeDtypeStruct((others, ns, half, width), BF),
            jax.ShapeDtypeStruct((sizes.nf, half, width), BF),
        ]
        self.sems = [DMA((others, ns)), DMA((others, ns)), DMA((sizes.nf,)), DMA((sizes.nf,))]

    def copies(self):
        place, nf, ns = self.place, self.place.sizes.nf, self.place.sizes.ns
        grads, (low, high) = self.r_ins[0], self.r_outs
        xs, xr, ys, yr = self.r_sems
        out = []
        for step in range(1, nf):
            for ds in range(ns):
                out.append(
                    push(
                        grads.at[ds, pl.ds(step * self.part, self.half)],
                        low.at[step - 1, ds],
                        xs.at[step - 1, ds],
                        xr.at[step - 1, ds],
                        place.across(step),
                    )
                )
        for df in range(nf):
            out.append(
                push(
                    grads.at[1, pl.ds(df * self.part + self.half, self.half)],
                    high.at[df],
                    ys.at[df],
                    yr.at[df],
                    place.twin(),
                )
            )
        return out

    def begin(self):
        for copy in self.copies():
            copy.start()

    def end(self):
        for copy in self.copies():
            copy.wait()


class GradSecond(Rider):
    kinds = ("fsdp", "twin")

    def __init__(self, sizes, low, high):
        self.ins = [low, high]
        others = high.shape[0]
        self.outs = [jax.ShapeDtypeStruct(low.shape, BF), jax.ShapeDtypeStruct(high.shape, BF)]
        self.sems = [DMA(()), DMA(()), DMA((others,)), DMA((others,))]

    def copies(self):
        place, nf = self.place, self.place.sizes.nf
        (low, high), (low_out, high_out) = self.r_ins, self.r_outs
        ys, yr, xs, xr = self.r_sems
        out = [push(low, low_out, ys, yr, place.twin())]
        for step in range(1, nf):
            at = step - 1
            out.append(push(high.at[at], high_out.at[at], xs.at[at], xr.at[at], place.across(step)))
        return out

    def begin(self):
        for copy in self.copies():
            copy.start()

    def end(self):
        for copy in self.copies():
            copy.wait()


def grad_halves(sizes, grads, low, high):
    part = grads.shape[1] // sizes.nf
    half = part // 2
    firsts, seconds = [], []
    for ds in range(sizes.ns):
        own = grads[ds, :half].astype(F32)
        firsts.append(own + sum(low[at, ds].astype(F32) for at in range(sizes.nf - 1)))
    for df in range(sizes.nf):
        own = grads[0, df * part + half : (df + 1) * part].astype(F32)
        seconds.append(own + high[df].astype(F32))
    return firsts, seconds


class Alone:
    kinds, ins, in_specs, outs, out_specs = (), [], [], [], []

    def scratch(self, sizes):
        return []

    def run(self, place, ins, outs, scratch, moment):
        moment("middle")
        moment("late")


class NextNorm:
    kinds = ("mate", "line")

    def __init__(self, sizes, part, stream, gain, shift):
        self.rows, self.width = stream.shape
        self.ins = [part, stream, gain, shift]
        self.in_specs = [VMEM_SPEC] * 4
        self.outs = [jax.ShapeDtypeStruct(part.shape, BF), jax.ShapeDtypeStruct(stream.shape, F32)]
        self.out_specs = [ANY_SPEC, VMEM_SPEC]

    def scratch(self, sizes):
        low = pltpu.VMEM((self.rows, self.width), BF)
        return [low] + scatter_scratch(sizes, self.rows, self.width) + Gather.scratch(sizes)

    def run(self, place, ins, outs, scratch, moment):
        part_ref, stream_ref, gain_ref, shift_ref = ins
        full_ref, new_ref = outs
        low_ref = scratch[0]
        new_rows = stream_ref[...] + scatter_part(place, part_ref, scratch[1 : 1 + N_SCATTER], self.rows)
        new_ref[...] = new_rows
        unit_rows, _ = unit_rows_of(new_rows)
        low_ref[...] = (unit_rows * gain_ref[...] + shift_ref[...]).astype(BF)
        spread_rows(place, low_ref, full_ref, scratch[1 + N_SCATTER :], self.rows, moment)


def spread_rows(place, low_ref, full_ref, sems, rows, moment):
    gather = Gather(place, low_ref, full_ref, sems, rows)
    gather.begin()
    for step in range(1, place.sizes.nc):
        if step == 2 or place.sizes.nc == 2:
            moment("middle")
        gather.forward(step)
    moment("late")
    gather.end()


class LastRows:
    kinds = ("mate", "line")

    def __init__(self, sizes, part, stream):
        self.rows, self.width = stream.shape
        self.ins, self.in_specs = [part, stream], [VMEM_SPEC] * 2
        self.outs, self.out_specs = [jax.ShapeDtypeStruct(stream.shape, F32)], [VMEM_SPEC]

    def scratch(self, sizes):
        return scatter_scratch(sizes, self.rows, self.width)

    def run(self, place, ins, outs, scratch, moment):
        outs[0][...] = ins[1][...] + scatter_part(place, ins[0], scratch, self.rows)
        moment("middle")
        moment("late")


class BackNorm:
    kinds = ("mate", "line")

    def __init__(self, sizes, part, grad, saved, gain, last):
        self.rows, self.width = grad.shape
        self.last = last
        self.ins, self.in_specs = [part, grad, saved, gain], [VMEM_SPEC] * 4
        self.outs = [jax.ShapeDtypeStruct(grad.shape, F32), jax.ShapeDtypeStruct((2, self.width), F32)]
        self.out_specs = [VMEM_SPEC] * 2
        if not last:
            self.outs.append(jax.ShapeDtypeStruct(part.shape, BF))
            self.out_specs.append(ANY_SPEC)

    def scratch(self, sizes):
        low = [] if self.last else [pltpu.VMEM((self.rows, self.width), BF)] + Gather.scratch(sizes)
        return scatter_scratch(sizes, self.rows, self.width) + low

    def run(self, place, ins, outs, scratch, moment):
        part_ref, grad_ref, saved_ref, gain_ref = ins
        new_ref, norm_ref = outs[:2]
        total = scatter_part(place, part_ref, scratch[:N_SCATTER], self.rows)
        inner, gain_grad, shift_grad = norm_back(total, saved_ref[...], gain_ref[...])
        new_rows = grad_ref[...] + inner
        new_ref[...] = new_rows
        norm_ref[0:1] = gain_grad
        norm_ref[1:2] = shift_grad
        if self.last:
            moment("middle")
            moment("late")
            return
        low_ref = scratch[N_SCATTER]
        low_ref[...] = new_rows.astype(BF)
        spread_rows(place, low_ref, outs[2], scratch[N_SCATTER + 1 :], self.rows, moment)


class Start:
    kinds = ("mate", "ctx", "fsdp", "twin")

    def __init__(self, sizes, small, hidden, cotangent, piece, exchange, spread):
        self.sizes, self.piece = sizes, piece
        self.exchange, self.spread = exchange, spread
        lines, lanes = small.shape
        count, self.width = hidden.shape
        self.rows = count // (sizes.ns * sizes.nk)
        group = sizes.nc * sizes.nk * self.rows
        self.ins, self.in_specs = [small, hidden, cotangent], [VMEM_SPEC] * 3
        self.outs = [
            jax.ShapeDtypeStruct((sizes.nf, sizes.nc * lines, lanes), F32),
            jax.ShapeDtypeStruct((lines, lanes), F32),
            jax.ShapeDtypeStruct((lines, self.width), F32),
            jax.ShapeDtypeStruct((self.rows, self.width), F32),
            jax.ShapeDtypeStruct((self.rows, self.width), BF),
            jax.ShapeDtypeStruct((group, self.width), BF),
            jax.ShapeDtypeStruct((group, self.width), BF),
        ]
        self.out_specs = [VMEM_SPEC] * 5 + [ANY_SPEC] * 2

    def scratch(self, sizes):
        others = max(sizes.nf - 1, 1)
        small = [DMA((sizes.nc,)), DMA((sizes.nc,)), DMA((others,)), DMA((others,)), DMA(()), DMA(())]
        return small + [pltpu.VMEM((self.rows, self.width), BF)] + Gather.scratch(sizes) * 2

    def run(self, place, ins, outs, scratch, moment):
        sizes, rows, width = self.sizes, self.rows, self.width
        small_ref, hidden_ref, cotangent_ref = ins
        all_ref, twin_ref, norm_ref, stream_ref, grad_ref, full_ref, grad_full_ref = outs
        cs, cr, fs, fr, ts, tr = scratch[:6]
        low_ref = scratch[6]
        gathers = [scratch[7:12], scratch[12:17]]
        lines = small_ref.shape[0]

        def line_of(c):
            return pl.ds(pl.multiple_of(c * lines, lines), lines)

        to_context = [
            push(
                small_ref, all_ref.at[0, line_of(place.c)], cs.at[step], cr.at[step], place.ahead(step)
            )
            for step in range(1, sizes.nc)
        ]
        to_twin = push(small_ref, twin_ref, ts, tr, place.twin())
        for copy in to_context + [to_twin]:
            copy.start()
        all_ref[0, line_of(place.c)] = small_ref[...]
        own_rows = pl.ds(pl.multiple_of((place.s * sizes.nk + place.k) * rows, rows), rows)
        part = width // sizes.nf
        for df in range(sizes.nf):
            lanes = pl.ds(pl.multiple_of(lax.rem(place.f + df, sizes.nf) * part, part), part)
            stream_ref[:, df * part : (df + 1) * part] = hidden_ref[own_rows, lanes].astype(F32)
            grad_ref[:, df * part : (df + 1) * part] = cotangent_ref[own_rows, lanes]
        unit_rows, _ = unit_rows_of(stream_ref[...])
        for copy in to_context:
            copy.wait()
        to_across = [
            push(all_ref.at[0], all_ref.at[sizes.nf - step], fs.at[step - 1], fr.at[step - 1], place.across(step))
            for step in range(1, sizes.nf)
        ]
        for copy in to_across:
            copy.start()
        for copy in to_across + [to_twin]:
            copy.wait()
        for df in range(sizes.nf):
            for c in range(sizes.nc):
                at = (df * sizes.nc + c) * self.piece
                norm_ref[:, at : at + self.piece] = all_ref[df, c * lines : (c + 1) * lines, : self.piece]
        low_ref[...] = (unit_rows * norm_ref[0:1] + norm_ref[1:2]).astype(BF)
        gather = Gather(place, low_ref, full_ref, gathers[0], rows)
        gather.begin()
        exchange, spread = self.exchange, self.spread
        exchange.wait_own()
        spread.first(place.c)
        for step in range(1, sizes.nc):
            exchange.wait_from(step)
            spread.first(lax.rem(place.c + sizes.nc - step, sizes.nc))
            gather.forward(step)
        moment("middle")
        other = Gather(place, grad_ref, grad_full_ref, gathers[1], rows)
        other.begin()
        for step in range(sizes.nc):
            spread.second(lax.rem(place.c + sizes.nc - step, sizes.nc))
            if step:
                other.forward(step)
        moment("late")
        gather.end()
        other.end()
        exchange.wait_sent()
        for block in range(sizes.nc):
            spread.finish(block)


class Guest(Rider):
    def __init__(self, rider):
        self.kinds, self.ins, self.outs, self.sems = rider.kinds, rider.ins, rider.outs, rider.sems
        self.rider = rider

    def bind(self, *refs):
        self.rider.bind(*refs)


def comm_kernel(sizes, main, riders, kinds, layout, *refs):
    cuts, at = [], 0
    for size in layout:
        cuts.append(refs[at : at + size])
        at += size
    count = len(riders)
    ins, outs, scratch = cuts[: count + 1], cuts[count + 1 : 2 * count + 2], cuts[2 * count + 2 :]
    place = Place(sizes)
    for i, rider in enumerate(riders):
        rider.bind(place, ins[i + 1], outs[i + 1], scratch[i + 1])
    greet(place, kinds)

    def moment(name):
        for rider in riders:
            getattr(rider, name)()

    moment("begin")
    main.run(place, ins[0], outs[0], scratch[0], moment)
    moment("end")


def comm_call(sizes, collective_id, main, riders=(), micros=50):
    kinds = set(main.kinds)
    for rider in riders:
        kinds |= set(rider.kinds)
    main_scratch = main.scratch(sizes)
    operands, in_specs = list(main.ins), list(main.in_specs)
    outs, out_specs = list(main.outs), list(main.out_specs)
    scratch = list(main_scratch)
    for rider in riders:
        operands += rider.ins
        in_specs += [ANY_SPEC] * len(rider.ins)
        outs += rider.outs
        out_specs += [ANY_SPEC] * len(rider.outs)
        scratch += rider.sems
    layout = [len(main.ins)] + [len(rider.ins) for rider in riders]
    layout += [len(main.outs)] + [len(rider.outs) for rider in riders]
    layout += [len(main_scratch)] + [len(rider.sems) for rider in riders]
    results = pl.pallas_call(
        functools.partial(comm_kernel, sizes, main, riders, kinds, layout),
        out_shape=outs,
        in_specs=in_specs,
        out_specs=out_specs,
        scratch_shapes=scratch,
        compiler_params=pltpu.CompilerParams(
            collective_id=collective_id, has_side_effects=True, vmem_limit_bytes=32 * MIB
        ),
        cost_estimate=pl.CostEstimate(flops=0, bytes_accessed=micros * 3 * MIB, transcendentals=0),
    )(*operands)
    groups, at = [], 0
    for size in [len(main.outs)] + [len(rider.outs) for rider in riders]:
        groups.append(list(results[at : at + size]))
        at += size
    return groups[0], groups[1:]


def unit_rows_of(values):
    row_mean = jnp.mean(values, -1, keepdims=True)
    centred = values - row_mean
    row_var = jnp.mean(centred * centred, -1, keepdims=True)
    inverse = lax.rsqrt(row_var + EPS)
    return centred * inverse, inverse


def norm_back(grad_rows, saved_rows, gain_row):
    unit_rows, inverse = unit_rows_of(saved_rows)
    scaled = grad_rows * gain_row
    inner = inverse * (
        scaled
        - jnp.mean(scaled, -1, keepdims=True)
        - unit_rows * jnp.mean(scaled * unit_rows, -1, keepdims=True)
    )
    return inner, jnp.sum(grad_rows * unit_rows, 0, keepdims=True), jnp.sum(grad_rows, 0, keepdims=True)


def swap_lanes(values):
    lane = lax.broadcasted_iota(jnp.int32, values.shape, 1) % HD
    width = values.shape[1]
    up = pltpu.roll(values, width - ROT // 2, 1)
    down = pltpu.roll(values, ROT // 2, 1)
    return jnp.where(lane < ROT // 2, up, jnp.where(lane < ROT, down, 0.0))


def allowed_of(label_col, label_row):
    length = label_col.shape[0]
    row = lax.broadcasted_iota(jnp.int32, (length, length), 0)
    col = lax.broadcasted_iota(jnp.int32, (length, length), 1)
    return (label_col == label_row) & (row >= col)


def attend_kernel(proj_ref, col_ref, row_ref, cos_ref, sin_ref, mix_ref, q_ref, k_ref, lse_ref):
    blocks, length, triple = proj_ref.shape
    width = triple // 3
    heads = width // HD
    allowed = allowed_of(col_ref[...], row_ref[...])
    cosine, sine = cos_ref[...], sin_ref[...]
    scaling = HD ** (-0.5)
    for b in range(blocks):
        for ref, at in ((q_ref, 0), (k_ref, 1)):
            values = proj_ref[b, :, at * width : (at + 1) * width].astype(F32)
            ref[b] = (values * cosine + swap_lanes(values) * sine).astype(BF)
        for h in range(heads):
            span = slice(h * HD, (h + 1) * HD)
            scores = scaling * dot_nt(q_ref[b, :, span], k_ref[b, :, span])
            scores = jnp.where(allowed, scores, NEGATIVE)
            peak = jnp.max(scores, -1, keepdims=True)
            exponent = jnp.exp(scores - peak)
            total = jnp.sum(exponent, -1, keepdims=True)
            probs = (exponent * (1.0 / total)).astype(BF)
            values = proj_ref[b, :, 2 * width + h * HD : 2 * width + (h + 1) * HD]
            mix_ref[b, :, span] = dot_nn(probs, values).astype(BF)
            at = b * heads + h
            lse_ref[:, at : at + 1] = peak + jnp.log(total)


def attend(proj, label_col, label_row, cosine, sine):
    blocks, length, triple = proj.shape
    width = triple // 3
    heads = blocks * width // HD
    return pl.pallas_call(
        attend_kernel,
        out_shape=[
            jax.ShapeDtypeStruct((blocks, length, width), BF),
            jax.ShapeDtypeStruct((blocks, length, width), BF),
            jax.ShapeDtypeStruct((blocks, length, width), BF),
            jax.ShapeDtypeStruct((length, heads), F32),
        ],
        in_specs=[VMEM_SPEC] * 5,
        out_specs=[VMEM_SPEC] * 4,
        compiler_params=pltpu.CompilerParams(vmem_limit_bytes=32 * MIB),
        cost_estimate=pl.CostEstimate(flops=2**30, bytes_accessed=16 * MIB, transcendentals=2**20),
    )(proj, label_col, label_row, cosine, sine)


def attend_back_kernel(
    proj_ref, q_ref, k_ref, lse_ref, grad_ref, col_ref, row_ref, cos_ref, sin_ref, out_ref, bias_ref
):
    blocks, length, triple = proj_ref.shape
    width = triple // 3
    heads = width // HD
    allowed = allowed_of(col_ref[...], row_ref[...])
    cosine, sine = cos_ref[...], sin_ref[...]
    scaling = HD ** (-0.5)
    for b in range(blocks):
        parts = [[], [], []]
        for h in range(heads):
            span = slice(h * HD, (h + 1) * HD)
            at = b * heads + h
            q_rows, k_rows, out_grad = q_ref[b, :, span], k_ref[b, :, span], grad_ref[b, :, span]
            scores = jnp.where(allowed, scaling * dot_nt(q_rows, k_rows), NEGATIVE)
            probs = jnp.exp(scores - lse_ref[:, at : at + 1])
            values = proj_ref[b, :, 2 * width + h * HD : 2 * width + (h + 1) * HD]
            prob_grad = dot_nt(out_grad, values)
            inner = jnp.sum(probs * prob_grad, -1, keepdims=True)
            score_low = (probs * (prob_grad - inner)).astype(BF)
            parts[0].append(scaling * dot_nn(score_low, k_rows))
            parts[1].append(scaling * dot_tn(score_low, q_rows))
            parts[2].append(dot_tn(probs.astype(BF), out_grad))
        for at in range(3):
            rows = jnp.concatenate(parts[at], axis=1)
            if at < 2:
                rows = rows * cosine - swap_lanes(rows) * sine
            low = rows.astype(BF)
            out_ref[b, :, at * width : (at + 1) * width] = low
            bias_ref[b : b + 1, at * width : (at + 1) * width] = jnp.sum(
                low.astype(F32), 0, keepdims=True
            )


def attend_back(proj, q_rot, k_rot, lse, grad, label_col, label_row, cosine, sine):
    blocks, length, triple = proj.shape
    return pl.pallas_call(
        attend_back_kernel,
        out_shape=[
            jax.ShapeDtypeStruct((blocks, length, triple), BF),
            jax.ShapeDtypeStruct((blocks, triple), F32),
        ],
        in_specs=[VMEM_SPEC] * 9,
        out_specs=[VMEM_SPEC] * 2,
        compiler_params=pltpu.CompilerParams(vmem_limit_bytes=40 * MIB),
        cost_estimate=pl.CostEstimate(flops=2**31, bytes_accessed=24 * MIB, transcendentals=2**20),
    )(proj, q_rot, k_rot, lse, grad, label_col, label_row, cosine, sine)


def rotary_tables(labels, width):
    places = jnp.arange(labels.shape[-1], dtype=jnp.int32)
    fresh = jnp.concatenate([jnp.ones((1,), jnp.bool_), labels[1:] != labels[:-1]])
    starts = lax.cummax(jnp.where(fresh, places, 0))
    offsets = (places - starts).astype(F32)
    frequency = jnp.exp(jnp.arange(ROT // 2, dtype=F32) * (-2.0 * math.log(ROPE_BASE) / ROT))
    angles = offsets[:, None] * frequency
    cosine, sine = jnp.cos(angles), jnp.sin(angles)
    rest = jnp.ones((labels.shape[0], HD - ROT), F32)
    cosine = jnp.concatenate([cosine, cosine, rest], 1)
    sine = jnp.concatenate([-sine, sine, 0.0 * rest], 1)
    return jnp.tile(cosine, (1, width // HD)), jnp.tile(sine, (1, width // HD))


def body(
    mesh,
    hidden_in,
    segment_ids,
    norm_gains,
    norm_shifts,
    qkv_weight,
    qkv_bias,
    out_weight,
    gate_up_weight,
    down_weight,
    cotangent,
):
    ns, shard_rows, width = hidden_in.shape
    sizes = Sizes(mesh, ns)
    nf, nc, nk, nt = sizes.nf, sizes.nc, sizes.nk, sizes.nt
    f, c, t = lax.axis_index("fsdp"), lax.axis_index("context"), lax.axis_index("tensor")
    s = t // nk
    layers = qkv_weight.shape[0]
    rows = shard_rows // nk
    part = width // nf
    piece = part // nc
    q_cols = qkv_weight.shape[3]
    q_sub = q_cols // nc
    hidden = gate_up_weight.shape[3]
    f_sub = -(-hidden // (nc * TILE)) * TILE
    f_cols = nc * f_sub

    def move(value, axis, step):
        size = mesh.shape[axis]
        return lax.ppermute(value, axis, [(i, (i + step) % size) for i in range(size)])

    def twin(value):
        return lax.ppermute(value, "tensor", [(i, (i + nk) % nt) for i in range(nt)])

    def context_sum(blocks):
        total = lax.dynamic_index_in_dim(blocks, c, 0, keepdims=False)
        for step in range(1, nc):
            total = total + move(lax.dynamic_index_in_dim(blocks, (c + step) % nc, 0, keepdims=False), "context", step)
        return total

    qkv_flat = qkv_weight.reshape(layers * piece, 3 * q_cols)
    out_flat = out_weight.reshape(layers * piece, q_cols)
    fill = ((0, 0), (0, f_cols - hidden))
    down_flat = jnp.pad(down_weight.reshape(layers * piece, hidden), fill)
    gate_up_flat = jnp.pad(gate_up_weight, ((0, 0), (0, 0)) + fill).reshape(layers * piece, 2 * f_cols)

    def attn_exchange(layer, when="begin"):
        sources = [(qkv_flat, at * q_cols) for at in range(3)] + [(out_flat, 0)]
        return WeightExchange(sizes, layer, piece, sources, q_sub, when)

    def gate_exchange(layer, when="begin"):
        return WeightExchange(sizes, layer, piece, [(gate_up_flat, 0), (gate_up_flat, f_cols)], f_sub, when)

    def down_exchange(layer, when="begin"):
        return WeightExchange(sizes, layer, piece, [(down_flat, 0)], f_sub, when)

    norms = jnp.stack([norm_gains, norm_shifts], axis=2).reshape(4 * layers, piece).astype(F32)
    own_bias = lax.dynamic_slice_in_dim(qkv_bias, c * q_sub, q_sub, 2).reshape(3 * layers, q_sub).astype(F32)
    lines = -(-max(4 * layers, 3 * layers, ns) // 8) * 8

    def lined(value):
        return jnp.pad(value, ((0, lines - value.shape[0]), (0, 0)))

    small = jnp.concatenate([lined(norms), lined(segment_ids.astype(F32)), lined(own_bias)], axis=1)
    first = attn_exchange(0)
    first_spread = Spread(sizes, first, blocks=nc)
    start = Start(
        sizes,
        small,
        hidden_in.reshape(ns * shard_rows, width),
        cotangent.reshape(ns * shard_rows, width),
        piece,
        first,
        first_spread,
    )
    gates_next = gate_exchange(0, "middle")
    results, extra = comm_call(sizes, 1, start, [Ending(first), Guest(first_spread), gates_next], 80)
    small_all, small_twin, norm_rows, stream, grad_low, full_one, grad_full = results
    attn = extra[1][0]
    gate_mine = extra[2][0]
    labels = small_all[0].reshape(nc, lines, -1)[:, :ns, piece : piece + shard_rows]
    labels = lax.dynamic_index_in_dim(labels, s, 1, keepdims=False).reshape(-1).astype(jnp.int32)
    bias_rows = [
        value[: 3 * layers, piece + shard_rows :].reshape(layers, 3 * q_sub) for value in (small, small_twin)
    ]
    bias_rows = jnp.stack(bias_rows, axis=1)[:, :, None]
    cosine, sine = rotary_tables(labels, q_sub)
    label_col, label_row = labels[:, None], labels[None, :]

    def gain_row(layer, which):
        at = (layer * 2 + which) * 2
        return norm_rows[at : at + 1]

    def shift_row(layer, which):
        at = (layer * 2 + which) * 2 + 1
        return norm_rows[at : at + 1]

    kept = []
    attn_mine = None
    for layer in range(layers):
        more = layer + 1 < layers
        proj = [dot_nn(full_one, attn[ds, :, : 3 * q_sub]) + bias_rows[layer, ds] for ds in range(ns)]
        proj = jnp.stack(proj).astype(BF)
        mixed, q_rot, k_rot, lse = attend(proj, label_col, label_row, cosine, sine)
        part_sum = sum(dot_nt(mixed[ds], attn[ds, :, 3 * q_sub :]) for ds in range(ns)).astype(BF)
        down_first = down_exchange(layer)
        riders = [Spread(sizes, gate_mine), Ending(down_first), Spread(sizes, down_first)]
        if more:
            riders.append(attn_exchange(layer + 1, "middle"))
        main = NextNorm(sizes, part_sum, stream, gain_row(layer, 1), shift_row(layer, 1))
        (full_two, middle), extra = comm_call(sizes, 2 + 2 * layer, main, riders, 85)
        gate_up, down = extra[0][0], extra[2][0]
        both = [dot_nn(full_two, gate_up[ds]) for ds in range(ns)]
        acts = [(jax.nn.silu(both[ds][:, :f_sub]) * both[ds][:, f_sub:]).astype(BF) for ds in range(ns)]
        part_sum = sum(dot_nt(acts[ds], down[ds]) for ds in range(ns)).astype(BF)
        kept.append((attn, gate_up, down, stream, middle, full_one, full_two, proj, mixed, q_rot, k_rot, lse, both, acts))
        if more:
            attn_mine = extra[3][0]
            riders = [Spread(sizes, attn_mine), gate_exchange(layer + 1)]
            main = NextNorm(sizes, part_sum, middle, gain_row(layer + 1, 0), shift_row(layer + 1, 0))
            (full_one, stream), extra = comm_call(sizes, 3 + 2 * layer, main, riders, 55)
            attn, gate_mine = extra[0][0], extra[1][0]
        else:
            main = LastRows(sizes, part_sum, middle)
            (stream,), _ = comm_call(sizes, 3 + 2 * layer, main, [], 30)

    def whole_rows(value):
        value = jnp.roll(value.reshape(rows, nf, part), f, axis=1).reshape(rows, width)
        out = jnp.zeros((nt, rows, width), value.dtype)
        out = lax.dynamic_update_index_in_dim(out, value, t, 0)
        for step in range(1, nt):
            out = lax.dynamic_update_index_in_dim(out, move(value, "tensor", step), (t + nt - step) % nt, 0)
        return out.reshape(ns, shard_rows, width)

    block_out = whole_rows(stream.astype(BF))

    first_id = 2 + 2 * layers
    grad = grad_low.astype(F32)
    firsts, seconds, ready = [], [], []
    sums, done = {}, {}
    norm_grads, bias_grads = {}, {}
    calls = [0]

    def run(main, micros, hold=0):
        riders, after = [], []
        for name, grads in firsts:
            riders.append(GradFirst(sizes, grads))
            after.append(("first", name, grads))
        for name, halves in seconds:
            riders.append(GradSecond(sizes, halves[0][1].astype(BF), jnp.stack(halves[1][1:]).astype(BF)))
            after.append(("second", name, halves))
        for name, total in ready:
            riders.append(GradExchange(sizes, total, q_sub if name[0] == "attn" else f_sub))
            after.append(("ready", name, total))
        firsts.clear(), seconds.clear(), ready.clear()
        results, extra = comm_call(sizes, first_id + calls[0], main, riders, micros)
        calls[0] += 1
        for (stage, name, value), out in zip(after, extra):
            if stage == "first":
                seconds.append((name, grad_halves(sizes, value, *out)))
            elif stage == "second":
                low, high = out
                lower = value[0][0] + low.astype(F32)
                upper = value[1][0] + sum(high[at].astype(F32) for at in range(nf - 1))
                ready.append((name, jnp.concatenate([lower, upper], 0).astype(BF)))
            else:
                done[name] = out[0]
        return results

    for layer in range(layers - 1, -1, -1):
        attn, gate_up, down, stream, middle, full_one, full_two, proj, mixed, q_rot, k_rot, lse, both, acts = kept[layer]
        low = []
        for ds in range(ns):
            act_grad = dot_nn(grad_full, down[ds])
            gate, up = both[ds][:, :f_sub], both[ds][:, f_sub:]
            sg = jax.nn.sigmoid(gate)
            gate_grad = act_grad * up * sg * (1.0 + gate * (1.0 - sg))
            low.append(jnp.concatenate([gate_grad, act_grad * gate * sg], 1).astype(BF))
        part_sum = sum(dot_nt(low[ds], gate_up[ds]) for ds in range(ns)).astype(BF)
        firsts.append((("gate", layer), jnp.stack([dot_tn(full_two, low[ds]) for ds in range(ns)]).astype(BF)))
        firsts.append((("down", layer), jnp.stack([dot_tn(grad_full, acts[ds]) for ds in range(ns)]).astype(BF)))
        main = BackNorm(sizes, part_sum, grad, middle, gain_row(layer, 1), False)
        grad, norm_grads[(layer, 1)], middle_full = run(main, 60)
        mixed_grad = jnp.stack([dot_nn(middle_full, attn[ds, :, 3 * q_sub :]) for ds in range(ns)]).astype(BF)
        proj_grad, bias_grads[layer] = attend_back(
            proj, q_rot, k_rot, lse, mixed_grad, label_col, label_row, cosine, sine
        )
        part_sum = sum(dot_nt(proj_grad[ds], attn[ds, :, : 3 * q_sub]) for ds in range(ns)).astype(BF)
        attn_grads = [
            jnp.concatenate([dot_tn(full_one, proj_grad[ds]), dot_tn(middle_full, mixed[ds])], 1) for ds in range(ns)
        ]
        firsts.append((("attn", layer), jnp.stack(attn_grads).astype(BF)))
        main = BackNorm(sizes, part_sum, grad, stream, gain_row(layer, 0), layer == 0)
        results = run(main, 60)
        grad, norm_grads[(layer, 0)] = results[:2]
        if layer > 0:
            grad_full = results[2]
    input_grad = whole_rows(grad.astype(BF)).astype(F32)
    while firsts or seconds or ready:
        run(Alone(), 50)

    norm_part = jnp.stack(
        [jnp.stack([norm_grads[(layer, which)] for which in range(2)], 1) for layer in range(layers)], 1
    )
    norm_part = norm_part.reshape(4 * layers, nf, nc, piece).transpose(2, 0, 1, 3)
    norm_total = context_sum(norm_part)
    norm_total = sum([move(norm_total, "tensor", step) for step in range(1, nt)], norm_total)
    norm_total = sum([move(norm_total[:, step], "fsdp", step) for step in range(1, nf)], norm_total[:, 0])
    norm_total = norm_total.reshape(2, layers, 2, piece)

    bias_part = jnp.stack([bias_grads[layer] for layer in range(layers)])
    bias_total = bias_part[:, 0] + sum(twin(bias_part[:, ds]) for ds in range(1, ns))
    bias_total = sum([move(bias_total, "fsdp", step) for step in range(1, nf)], bias_total)
    blocks = jnp.zeros((nc,) + bias_total.shape, F32)
    blocks = lax.dynamic_update_index_in_dim(blocks, bias_total, c, 0)
    for step in range(1, nc):
        blocks = lax.dynamic_update_index_in_dim(blocks, move(bias_total, "context", step), (c + nc - step) % nc, 0)
    bias_total = blocks.reshape(nc, layers, 3, q_sub).transpose(1, 2, 0, 3).reshape(layers, 3, q_cols)

    qkv_grads, out_grads, gate_up_grads, down_grads = [], [], [], []
    for layer in range(layers):
        flat = done[("attn", layer)].astype(F32)
        qkv_grads.append(flat[:, : 3 * q_cols].reshape(piece, 3, q_cols))
        out_grads.append(flat[:, 3 * q_cols :])
        gate_up_grads.append(done[("gate", layer)].astype(F32).reshape(piece, 2, f_cols)[:, :, :hidden])
        down_grads.append(done[("down", layer)].astype(F32)[:, :hidden])
    return (
        block_out,
        input_grad,
        norm_total[0],
        norm_total[1],
        jnp.stack(qkv_grads),
        bias_total,
        jnp.stack(out_grads),
        jnp.stack(gate_up_grads),
        jnp.stack(down_grads),
    )


def solution(mesh):
    return jax.shard_map(
        functools.partial(body, mesh),
        mesh=mesh,
        in_specs=(
            P("fsdp", "context", None),
            P("fsdp", "context"),
            P(None, None, ("fsdp", "context")),
            P(None, None, ("fsdp", "context")),
            P(None, ("fsdp", "context"), None, "tensor"),
            P(None, None, "tensor"),
            P(None, ("fsdp", "context"), "tensor"),
            P(None, ("fsdp", "context"), None, "tensor"),
            P(None, ("fsdp", "context"), "tensor"),
            P("fsdp", "context", None),
        ),
        out_specs=(
            P("fsdp", "context", None),
            P("fsdp", "context", None),
            P(None, None, ("fsdp", "context")),
            P(None, None, ("fsdp", "context")),
            P(None, ("fsdp", "context"), None, "tensor"),
            P(None, None, "tensor"),
            P(None, ("fsdp", "context"), "tensor"),
            P(None, ("fsdp", "context"), None, "tensor"),
            P(None, ("fsdp", "context"), "tensor"),
        ),
        check_vma=False,
    )
```

```python
import functools
import math

import jax
import jax.numpy as jnp
from jax import lax
from jax.experimental import pallas as pl
from jax.experimental.pallas import tpu as pltpu
from jax.sharding import PartitionSpec as P

HD = 64
ROT = 16
EPS = 1e-05
ROPE_BASE = 10000.0
NEGATIVE = -1e30
MESH = pl.DeviceIdType.MESH
BF = jnp.bfloat16
F32 = jnp.float32
MIB = 2**20
TILE = 128
VMEM_BYTES = 58 * MIB


def dot_nn(a, b):
    return jnp.dot(a, b, preferred_element_type=F32)


def dot_nt(a, b):
    return lax.dot_general(a, b, (((1,), (1,)), ((), ())), preferred_element_type=F32)


def dot_tn(a, b):
    return lax.dot_general(a, b, (((0,), (0,)), ((), ())), preferred_element_type=F32)


class Sizes:
    def __init__(self, mesh, ns):
        self.nf, self.nc, self.nt = mesh.shape["fsdp"], mesh.shape["context"], mesh.shape["tensor"]
        self.ns = ns
        self.nk = self.nt // ns


class Place:
    def __init__(self, sizes):
        self.sizes = sizes
        self.f = lax.axis_index("fsdp")
        self.c = lax.axis_index("context")
        self.t = lax.axis_index("tensor")
        self.s, self.k = self.t // sizes.nk, lax.rem(self.t, sizes.nk)

    def mate(self):
        return {"tensor": self.t + 1 - 2 * self.k}

    def twin(self):
        return {"tensor": self.t + self.sizes.nk * (1 - 2 * self.s)}

    def right(self):
        return {"context": self.c + 1}

    def left(self):
        return {"context": self.c - 1}

    def ahead(self, step):
        return {"context": lax.rem(self.c + step, self.sizes.nc)}

    def across(self, step):
        return {"fsdp": lax.rem(self.f + step, self.sizes.nf)}

    def plane(self, df, dt):
        return {"fsdp": lax.rem(self.f + df, self.sizes.nf), "tensor": lax.rem(self.t + dt, self.sizes.nt)}


def greet(place, kinds):
    barrier = pltpu.get_barrier_semaphore()
    nc, nf = place.sizes.nc, place.sizes.nf

    def signal(device):
        pl.semaphore_signal(barrier, inc=1, device_id=device, device_id_type=MESH)

    count = 0
    if "plane" in kinds:
        for df in range(nf):
            for dt in range(place.sizes.nt):
                if df or dt:
                    signal(place.plane(df, dt))
        count += nf * place.sizes.nt - 1
        kinds = set(kinds) - {"mate", "fsdp", "twin"}
    if "mate" in kinds:
        signal(place.mate())
        count += 1
    if "ctx" in kinds:
        for step in range(1, nc):
            signal(place.ahead(step))
        count += nc - 1
    elif "line" in kinds:

        @pl.when(place.c > 0)
        def _():
            signal(place.left())

        @pl.when(place.c < nc - 1)
        def _():
            signal(place.right())

        count += jnp.minimum(place.c, 1) + jnp.minimum(nc - 1 - place.c, 1)
    if "fsdp" in kinds:
        for step in range(1, nf):
            signal(place.across(step))
        count += nf - 1
    if "twin" in kinds:
        signal(place.twin())
        count += 1
    pl.semaphore_wait(barrier, count)


def push(src, dst, send, recv, device):
    return pltpu.make_async_remote_copy(
        src_ref=src, dst_ref=dst, send_sem=send, recv_sem=recv, device_id=device, device_id_type=MESH
    )


DMA = pltpu.SemaphoreType.DMA
VMEM_SPEC = pl.BlockSpec(memory_space=pltpu.VMEM)
ANY_SPEC = pl.BlockSpec(memory_space=pl.ANY)


HALVES = 2


class Gather:
    def __init__(self, place, own, out, sems, rows):
        self.place, self.own, self.out, self.rows = place, own, out, rows
        self.piece = rows // HALVES
        self.local, self.line_send, self.line_recv, self.mate_send, self.mate_recv = sems

    @staticmethod
    def scratch(sizes):
        nc = sizes.nc
        return [DMA(()), DMA((2, nc, HALVES)), DMA((nc, HALVES)), DMA((nc, HALVES)), DMA((nc, HALVES))]

    def slot(self, source, k, half):
        at = (source * self.place.sizes.nk + k) * self.rows + half * self.piece
        return self.out.at[pl.ds(pl.multiple_of(at, self.piece), self.piece)]

    def origin(self, source, half, first):
        if first:
            return self.own.at[pl.ds(half * self.piece, self.piece)]
        return self.slot(source, self.place.k, half)

    def line(self, source, half, device, first, way):
        return push(
            self.origin(source, half, first),
            self.slot(source, self.place.k, half),
            self.line_send.at[way, source, half],
            self.line_recv.at[source, half],
            device,
        )

    def pass_on(self, source, half, first):
        return push(
            self.origin(source, half, first),
            self.slot(source, self.place.k, half),
            self.mate_send.at[source, half],
            self.mate_recv.at[source, half],
            self.place.mate(),
        )

    def keep(self):
        at = (self.place.c * self.place.sizes.nk + self.place.k) * self.rows
        target = self.out.at[pl.ds(pl.multiple_of(at, self.rows), self.rows)]
        return pltpu.make_async_copy(self.own, target, self.local)

    def begin(self):
        place, c, nc = self.place, self.place.c, self.place.sizes.nc
        for half in range(HALVES):

            @pl.when(c < nc - 1)
            def _():
                self.line(c, half, place.right(), True, 0).start()

            @pl.when(c > 0)
            def _():
                self.line(c, half, place.left(), True, 1).start()

        for half in range(HALVES):
            self.pass_on(c, half, True).start()
        self.keep().start()

    def forward(self, step):
        place, c, nc = self.place, self.place.c, self.place.sizes.nc
        source, other = c - step, c + step
        for half in range(HALVES):

            @pl.when(source >= 0)
            def _():
                self.line(source, half, place.left(), False, 0).wait_recv()

                @pl.when(c < nc - 1)
                def _():
                    self.line(source, half, place.right(), False, 0).start()

                self.pass_on(source, half, False).start()

            @pl.when(other <= nc - 1)
            def _():
                self.line(other, half, place.right(), False, 1).wait_recv()

                @pl.when(c > 0)
                def _():
                    self.line(other, half, place.left(), False, 1).start()

                self.pass_on(other, half, False).start()

    def end(self):
        place, c, nc = self.place, self.place.c, self.place.sizes.nc
        self.keep().wait()
        for source in range(nc):
            for half in range(HALVES):
                arrival = self.slot(source, 1 - place.k, half)
                push(
                    arrival, arrival, self.mate_send.at[source, half], self.mate_recv.at[source, half], place.mate()
                ).wait_recv()
                self.pass_on(source, half, False).wait_send()

                @pl.when((source <= c) & (c < nc - 1))
                def _():
                    self.line(source, half, place.right(), False, 0).wait_send()

                @pl.when((source >= c) & (c > 0))
                def _():
                    self.line(source, half, place.left(), False, 1).wait_send()


def scatter_part(place, part_ref, bufs, rows, moment):
    nc, nk, c, k = place.sizes.nc, place.sizes.nk, place.c, place.k
    piece = rows // HALVES
    mate_buf, to_right, to_left, from_left, from_right = bufs[:5]
    mate_send, mate_recv, right_send, right_recv, left_send, left_recv = bufs[5:]

    def block(dest, kk):
        return part_ref.at[pl.ds(pl.multiple_of((dest * nk + kk) * rows, rows), rows)]

    def mate_copy(dest):
        return push(
            block(dest, 1 - k), mate_buf.at[dest], mate_send.at[dest], mate_recv.at[dest], place.mate()
        )

    def lines(half):
        return slice(half * piece, (half + 1) * piece)

    def right_copy(dest, half):
        return push(
            to_right.at[dest, lines(half)],
            from_left.at[dest, lines(half)],
            right_send.at[dest, half],
            right_recv.at[dest, half],
            place.right(),
        )

    def left_copy(dest, half):
        return push(
            to_left.at[dest, lines(half)],
            from_right.at[dest, lines(half)],
            left_send.at[dest, half],
            left_recv.at[dest, half],
            place.left(),
        )

    def each(visit_right, visit_left, count, after=lambda step: None):
        for step in range(nc - 1):
            far = nc - 1 - step
            for half in range(count):

                @pl.when(far > c)
                def _():
                    visit_right(far, half)

                @pl.when(step < c)
                def _():
                    visit_left(step, half)

            after(step)

    def send_mate(dest, half):
        mate_copy(dest).start()

    each(send_mate, send_mate, 1)
    mate_copy(c).start()
    moment("sent")

    def chip_sum(dest, half):
        if half == 0:
            mate_copy(dest).wait_recv()
        at = pl.multiple_of((dest * nk + k) * rows + half * piece, piece)
        return part_ref[pl.ds(at, piece)].astype(F32) + mate_buf[dest, lines(half)].astype(F32)

    def pass_right(dest, half):
        total = chip_sum(dest, half)
        to_right[dest, lines(half)] = total.astype(BF)

        @pl.when(c > 0)
        def _():
            right_copy(dest, half).wait_recv()
            to_right[dest, lines(half)] = (total + from_left[dest, lines(half)].astype(F32)).astype(BF)

        right_copy(dest, half).start()

    def pass_left(dest, half):
        total = chip_sum(dest, half)
        to_left[dest, lines(half)] = total.astype(BF)

        @pl.when(c < nc - 1)
        def _():
            left_copy(dest, half).wait_recv()
            to_left[dest, lines(half)] = (total + from_right[dest, lines(half)].astype(F32)).astype(BF)

        left_copy(dest, half).start()

    each(pass_right, pass_left, HALVES, lambda step: moment("inside%d" % step))
    totals = []
    for half in range(HALVES):
        total = chip_sum(c, half)

        @pl.when(c > 0)
        def _():
            right_copy(c, half).wait_recv()

        @pl.when(c < nc - 1)
        def _():
            left_copy(c, half).wait_recv()

        total = total + jnp.where(c > 0, from_left[c, lines(half)].astype(F32), 0.0)
        totals.append(total + jnp.where(c < nc - 1, from_right[c, lines(half)].astype(F32), 0.0))
    for dest in range(nc):
        mate_copy(dest).wait_send()
        for half in range(HALVES):

            @pl.when(dest > c)
            def _():
                right_copy(dest, half).wait_send()

            @pl.when(dest < c)
            def _():
                left_copy(dest, half).wait_send()

    return jnp.concatenate(totals, 0)


def scatter_scratch(sizes, rows, width):
    nc = sizes.nc
    return [pltpu.VMEM((nc, rows, width), BF) for _ in range(5)] + [DMA((nc,)) for _ in range(2)] + [
        DMA((nc, HALVES)) for _ in range(4)
    ]


N_SCATTER = 11


class Rider:
    kinds = ()
    ins, outs, sems = [], [], []

    def bind(self, place, ins, outs, sems, main):
        self.place, self.r_ins, self.r_outs, self.r_sems, self.main = place, ins, outs, sems, main

    def at(self, moment):
        pass


class Exchange(Rider):
    kinds = ("ctx",)

    def __init__(self, sizes, ins, out, pieces, when="begin", finish="end"):
        self.ins, self.outs, self.pieces, self.when, self.last = ins, [out], pieces, when, finish
        count = max(sizes.nc - 1, 1)
        self.sems = [DMA(()), DMA((count,)), DMA((count,))]

    def at(self, moment):
        if moment == self.when:
            self.start()
        if moment == self.last:
            self.finish()

    def start(self):
        place, nc = self.place, self.place.sizes.nc
        local, send, recv = self.r_sems
        for step in range(1, nc):
            for source_of, target_of in self.pieces:
                push(
                    source_of(self.r_ins, lax.rem(place.c + step, nc)),
                    target_of(self.r_outs[0], place.c),
                    send.at[step - 1],
                    recv.at[step - 1],
                    place.ahead(step),
                ).start()
        for source_of, target_of in self.pieces:
            pltpu.make_async_copy(
                source_of(self.r_ins, place.c), target_of(self.r_outs[0], place.c), local
            ).start()

    def wait_own(self):
        whole = self.whole()
        pltpu.make_async_copy(whole, whole, self.r_sems[0]).wait()

    def wait_from(self, step):
        whole = self.whole()
        _, send, recv = self.r_sems
        push(whole, whole, send.at[step - 1], recv.at[step - 1], self.place.ahead(step)).wait_recv()

    def wait_sent(self):
        whole = self.whole()
        _, send, recv = self.r_sems
        for step in range(1, self.place.sizes.nc):
            push(whole, whole, send.at[step - 1], recv.at[step - 1], self.place.ahead(step)).wait_send()

    def finish(self):
        self.wait_own()
        for step in range(1, self.place.sizes.nc):
            self.wait_from(step)
        self.wait_sent()


class WeightExchange(Exchange):
    def __init__(self, sizes, rows, array, corners, sub, when="begin", finish="end"):
        pieces = [self.piece(first, rows, base, sub, at) for at, (first, base) in enumerate(corners)]
        out = jax.ShapeDtypeStruct((sizes.nc * rows, sub * len(pieces)), BF)
        super().__init__(sizes, [array], out, pieces, when, finish)
        self.rows = rows

    @staticmethod
    def piece(first, rows, base, sub, position):
        def source_of(refs, dest):
            return refs[0].at[pl.ds(first, rows), pl.ds(pl.multiple_of(base + dest * sub, TILE), sub)]

        def target_of(out, source):
            return out.at[pl.ds(pl.multiple_of(source * rows, rows), rows), pl.ds(position * sub, sub)]

        return source_of, target_of

    def whole(self):
        return self.r_outs[0].at[pl.ds(0, self.rows)]


class GradExchange(Exchange):
    def __init__(self, sizes, total, sub, when="begin", finish="end"):
        rows = total.shape[0] // sizes.nc
        count = total.shape[1] // sub
        out = jax.ShapeDtypeStruct((rows, sizes.nc * total.shape[1]), BF)
        pieces = [self.piece(rows, sub, position, sizes.nc) for position in range(count)]
        super().__init__(sizes, [total], out, pieces, when, finish)
        self.rows = rows

    @staticmethod
    def piece(rows, sub, position, nc):
        def source_of(refs, dest):
            return refs[0].at[pl.ds(pl.multiple_of(dest * rows, rows), rows), pl.ds(position * sub, sub)]

        def target_of(out, source):
            return out.at[:, pl.ds(pl.multiple_of(position * nc * sub + source * sub, TILE), sub)]

        return source_of, target_of

    def whole(self):
        return self.r_ins[0].at[pl.ds(0, self.rows)]


class Spread(Rider):
    kinds = ("fsdp", "twin")

    def __init__(self, sizes, mine, blocks=1, steps=("begin", "inside1")):
        if isinstance(mine, Exchange):
            self.source, shape, self.ins = mine, mine.outs[0].shape, []
        else:
            self.source, shape, self.ins = None, mine.shape, [mine]
        rows, self.width = shape
        self.part, self.blocks, self.rows, self.steps = rows, blocks, rows // blocks, steps
        self.outs = [jax.ShapeDtypeStruct((sizes.nf * rows, sizes.ns * self.width), BF)]
        others = max(sizes.nf - 1, 1)
        self.sems = [DMA((blocks,))] + [DMA((blocks, others)) for _ in range(8)] + [DMA((blocks,)) for _ in range(4)]

    def at(self, moment):
        if moment == self.steps[0]:
            if self.source is not None:
                self.source.finish()
            self.first(0)
        if moment == self.steps[1]:
            self.second(0)
        if moment == "end":
            self.finish(0)

    def span(self, df, block, half, whole=False):
        length = self.rows if whole else self.rows // 2
        at = df * self.part + block * self.rows + half * (self.rows // 2)
        return pl.ds(pl.multiple_of(at, length), length)

    def mine(self, block, half, whole=False):
        ref = self.r_ins[0] if self.source is None else self.source.r_outs[0]
        return ref.at[self.span(0, block, half, whole)]

    def out(self, ds, df, block, half, whole=False):
        return self.r_outs[0].at[self.span(df, block, half, whole), pl.ds(ds * self.width, self.width)]

    def copies(self, block, stage):
        place, nf, sems, out = self.place, self.place.sizes.nf, self.r_sems, []
        for step in range(1, nf):
            at, df = step - 1, nf - step
            across = place.across(step)
            source, target, pair, device = [
                (self.mine(block, 0), self.out(0, df, block, 0), 1, across),
                (self.mine(block, 1), self.out(0, df, block, 1), 3, across),
                (self.out(1, 0, block, 1), self.out(1, df, block, 1), 5, across),
            ][stage]
            out.append(push(source, target, sems[pair].at[block, at], sems[pair + 1].at[block, at], device))
            if stage == 2:
                source, target = self.out(0, df, block, 0), self.out(1, df, block, 0)
                out.append(push(source, target, sems[7].at[block, at], sems[8].at[block, at], place.twin()))
        if stage < 2:
            half, pair = (1, 9) if stage == 0 else (0, 11)
            out.append(
                push(
                    self.mine(block, half),
                    self.out(1, 0, block, half),
                    sems[pair].at[block],
                    sems[pair + 1].at[block],
                    place.twin(),
                )
            )
        return out

    def keep(self, block):
        return pltpu.make_async_copy(
            self.mine(block, 0, True), self.out(0, 0, block, 0, True), self.r_sems[0].at[block]
        )

    def first(self, block):
        for stage in range(2):
            for copy in self.copies(block, stage):
                copy.start()
        self.keep(block).start()

    def second(self, block):
        for copy in self.copies(block, 0):
            copy.wait_recv()
        for copy in self.copies(block, 2):
            copy.start()

    def finish(self, block):
        for copy in self.copies(block, 0):
            copy.wait_send()
        for stage in (1, 2):
            for copy in self.copies(block, stage):
                copy.wait_recv()
                copy.wait_send()
        self.keep(block).wait()


class GradFirst(Rider):
    kinds = ("fsdp", "twin")

    def __init__(self, sizes, name, rows, width, when):
        self.name, self.when = name, when
        self.part = rows // sizes.nf
        self.half = self.part // 2
        self.width = width // sizes.ns
        others = max(sizes.nf - 1, 1)
        self.outs = [
            jax.ShapeDtypeStruct((others, self.half, width), BF),
            jax.ShapeDtypeStruct((sizes.nf, self.half, self.width), BF),
        ]
        self.sems = [DMA((others,)), DMA((others,)), DMA((sizes.nf,)), DMA((sizes.nf,))]

    def copies(self):
        place, nf = self.place, self.place.sizes.nf
        grads, (low, high) = self.main.grads[self.name], self.r_outs
        xs, xr, ys, yr = self.r_sems
        out = []
        for step in range(1, nf):
            at = step - 1
            out.append(
                push(grads.at[pl.ds(step * self.part, self.half)], low.at[at], xs.at[at], xr.at[at], place.across(step))
            )
        for df in range(nf):
            rows = pl.ds(df * self.part + self.half, self.half)
            out.append(
                push(grads.at[rows, pl.ds(self.width, self.width)], high.at[df], ys.at[df], yr.at[df], place.twin())
            )
        return out

    def at(self, moment):
        if moment == self.when:
            for copy in self.copies():
                copy.start()
        if moment == "end":
            for copy in self.copies():
                copy.wait()


class GradSecond(Rider):
    kinds = ("fsdp", "twin")

    def __init__(self, sizes, low, high):
        self.ins = [low, high]
        others = high.shape[0]
        self.outs = [jax.ShapeDtypeStruct(low.shape, BF), jax.ShapeDtypeStruct(high.shape, BF)]
        self.sems = [DMA(()), DMA(()), DMA((others,)), DMA((others,))]

    def copies(self):
        place, nf = self.place, self.place.sizes.nf
        (low, high), (low_out, high_out) = self.r_ins, self.r_outs
        ys, yr, xs, xr = self.r_sems
        out = [push(low, low_out, ys, yr, place.twin())]
        for step in range(1, nf):
            at = step - 1
            out.append(push(high.at[at], high_out.at[at], xs.at[at], xr.at[at], place.across(step)))
        return out

    def at(self, moment):
        if moment == "begin":
            for copy in self.copies():
                copy.start()
        if moment == "end":
            for copy in self.copies():
                copy.wait()


def grad_halves(sizes, grads, low, high):
    part = grads.shape[0] // sizes.nf
    half, width = part // 2, grads.shape[1] // sizes.ns
    firsts, seconds = [], []
    for ds in range(sizes.ns):
        lanes = slice(ds * width, (ds + 1) * width)
        own = grads[:half, lanes].astype(F32)
        firsts.append(own + sum(low[at, :, lanes].astype(F32) for at in range(sizes.nf - 1)))
    for df in range(sizes.nf):
        own = grads[df * part + half : (df + 1) * part, :width].astype(F32)
        seconds.append(own + high[df].astype(F32))
    return firsts, seconds


class Share(Rider):
    def __init__(self, kinds, array, out, count, moves, when="begin"):
        self.kinds, self.moves, self.when = kinds, moves, when
        self.ins, self.outs = [array], [out]
        self.sems = [DMA((count,)), DMA((count,))]

    def copies(self):
        send, recv = self.r_sems
        out = []
        for at, (device, source, target) in enumerate(self.moves(self.place, self.r_ins[0], self.r_outs[0])):
            if device is None:
                out.append(pltpu.make_async_copy(source, target, send.at[at]))
            else:
                out.append(push(source, target, send.at[at], recv.at[at], device))
        return out

    def at(self, moment):
        if moment == self.when:
            for copy in self.copies():
                copy.start()
        if moment == "end":
            for copy in self.copies():
                copy.wait()


def share_rows(sizes, value):
    rows, width = value.shape
    part = width // sizes.nf

    def moves(place, source, out):
        triples = []
        for dt in range(sizes.nt):
            device = place.plane(0, dt) if dt else None
            for df in range(sizes.nf):
                lanes = pl.ds(pl.multiple_of(lax.rem(place.f + df, sizes.nf) * part, part), part)
                triples.append((device, source.at[:, pl.ds(df * part, part)], out.at[place.t, :, lanes]))
        return triples

    out = jax.ShapeDtypeStruct((sizes.nt, rows, width), value.dtype)
    return Share(("plane",), value, out, sizes.nt * sizes.nf, moves)


def share_context(sizes, value, by_dest):
    def moves(place, source, out):
        triples = []
        for step in range(sizes.nc):
            dest = lax.rem(place.c + step, sizes.nc)
            triples.append(
                (place.ahead(step) if step else None, source.at[dest] if by_dest else source, out.at[place.c])
            )
        return triples

    shape = value.shape[1:] if by_dest else value.shape
    return Share(("ctx",), value, jax.ShapeDtypeStruct((sizes.nc,) + shape, value.dtype), sizes.nc, moves)


def share_plane(sizes, value, which):
    def moves(place, source, out):
        return [
            (place.plane(df, dt) if df or dt else None, source.at[at], out.at[slot])
            for slot, (df, dt, at) in enumerate(which)
        ]

    out = jax.ShapeDtypeStruct((len(which),) + value.shape[1:], value.dtype)
    return Share(("plane",), value, out, len(which), moves)


class Moved:
    def __init__(self, hbm, scratch, inward):
        count = len(hbm)
        self.vmem = scratch[:count]
        self.copies = []
        for ref, buffer, sem in zip(hbm, scratch[:count], scratch[count:]):
            ends = (ref, buffer) if inward else (buffer, ref)
            self.copies.append(pltpu.make_async_copy(*ends, sem))

    @staticmethod
    def scratch(arrays):
        return [pltpu.VMEM(a.shape, a.dtype) for a in arrays] + [DMA(()) for _ in arrays]

    def start(self):
        for copy in self.copies:
            copy.start()


class Main:
    kinds = ("mate", "line")
    big, small, results, kept, gathered, work = [], [], [], [], [], []

    def __init__(self, **arrays):
        self.grads = {}

    @property
    def ins(self):
        return list(self.big) + list(self.small)

    @property
    def in_specs(self):
        return [ANY_SPEC] * len(self.big) + [VMEM_SPEC] * len(self.small)

    @property
    def outs(self):
        return list(self.results) + list(self.kept) + list(self.gathered)

    @property
    def out_specs(self):
        return [VMEM_SPEC] * len(self.results) + [ANY_SPEC] * (len(self.kept) + len(self.gathered))

    def scratch(self, sizes):
        self.layout = [
            Moved.scratch(self.big),
            Moved.scratch(self.kept),
            [pltpu.VMEM(a.shape, a.dtype) for a in self.work],
            scatter_scratch(sizes, self.rows, self.width),
        ] + [Gather.scratch(sizes) for _ in self.gathered]
        return [one for group in self.layout for one in group]

    def run(self, place, ins, outs, scratch, moment):
        cuts, at = [], 0
        for group in self.layout:
            cuts.append(scratch[at : at + len(group)])
            at += len(group)
        count = len(self.big)
        self.loads = Moved(ins[:count], cuts[0], True)
        results, kept = outs[: len(self.results)], outs[len(self.results) : len(self.results) + len(self.kept)]
        gathered = outs[len(self.results) + len(self.kept) :]
        self.stores = Moved(kept, cuts[1], False)
        self.work_refs, self.bufs, self.gather_sems = cuts[2], cuts[3], cuts[4:]
        self.loads.start()
        moment("begin")
        self.compute(place, self.loads.vmem, ins[count:], results, self.stores.vmem, gathered, moment)
        for copy in self.stores.copies:
            copy.wait()

    def fetch(self, *which):
        for at in which:
            self.loads.copies[at].wait()

    def store(self, *which):
        for at in which:
            self.stores.copies[at].start()

    def spread(self, place, gathers, moment):
        for gather in gathers:
            gather.begin()
        moment("summed")
        for step in range(1, place.sizes.nc):
            for gather in gathers:
                gather.forward(step)
            if step == 1:
                moment("spread")
        moment("late")
        for gather in gathers:
            gather.end()


def by_rows(count, block, step):
    def one(at, carry):
        step(pl.ds(pl.multiple_of(at * block, block), block))
        return carry

    lax.fori_loop(0, count // block, one, 0)


def unit_rows_of(values):
    row_mean = jnp.mean(values, -1, keepdims=True)
    centred = values - row_mean
    row_var = jnp.mean(centred * centred, -1, keepdims=True)
    inverse = lax.rsqrt(row_var + EPS)
    return centred * inverse, inverse


def norm_back(grad_rows, saved_rows, gain_row):
    unit_rows, inverse = unit_rows_of(saved_rows)
    scaled = grad_rows * gain_row
    inner = inverse * (
        scaled
        - jnp.mean(scaled, -1, keepdims=True)
        - unit_rows * jnp.mean(scaled * unit_rows, -1, keepdims=True)
    )
    return inner, jnp.sum(grad_rows * unit_rows, 0, keepdims=True), jnp.sum(grad_rows, 0, keepdims=True)


def norm_forward(new_rows, gain_ref, shift_ref):
    unit_rows, _ = unit_rows_of(new_rows)
    return (unit_rows * gain_ref[...] + shift_ref[...]).astype(BF)


def swap_lanes(values):
    lane = lax.broadcasted_iota(jnp.int32, values.shape, 1) % HD
    width = values.shape[1]
    up = pltpu.roll(values, width - ROT // 2, 1)
    down = pltpu.roll(values, ROT // 2, 1)
    return jnp.where(lane < ROT // 2, up, jnp.where(lane < ROT, down, 0.0))


def allowed_of(label_col, label_row):
    length = label_col.shape[0]
    row = lax.broadcasted_iota(jnp.int32, (length, length), 0)
    col = lax.broadcasted_iota(jnp.int32, (length, length), 1)
    return (label_col == label_row) & (row >= col)


def like(shape, dtype):
    return jax.ShapeDtypeStruct(shape, dtype)


ROW_BLOCK = 128
OUT_BLOCK = 256


class AttnForward(Main):
    def __init__(self, full, w_qkv, w_out, bias, tables, stream, gain, shift):
        super().__init__()
        self.rows, self.width = stream.shape
        length = full.shape[0]
        self.big = [full, w_qkv, w_out]
        self.small = [bias, *tables, stream, gain, shift]
        heads = w_out.shape[1] // HD
        self.results = [like(stream.shape, F32), like((length, heads), F32)]
        mixed = like((length, w_out.shape[1]), BF)
        self.kept = [like((length, w_qkv.shape[1]), BF), mixed, mixed, mixed]
        self.gathered = [like(full.shape, BF)]
        self.work = [like(full.shape, BF), like(stream.shape, BF)]

    def compute(self, place, big, small, results, kept, gathered, moment):
        full, w_qkv, w_out = big
        bias_ref, col_ref, row_ref, cos_ref, sin_ref, stream_ref, gain_ref, shift_ref = small
        new_ref, lse_ref = results
        proj_ref, mix_ref, q_ref, k_ref = kept
        part_ref, low_ref = self.work_refs
        length = full.shape[0]
        ns = place.sizes.ns
        width = w_out.shape[1] // ns
        self.fetch(0, 1)

        def project(rows):
            proj_ref[rows] = (dot_nn(full[rows], w_qkv[...]) + bias_ref[...]).astype(BF)

        by_rows(length, ROW_BLOCK, project)
        self.store(0)
        allowed = allowed_of(col_ref[...], row_ref[...])
        cosine, sine = cos_ref[...], sin_ref[...]
        scaling = HD ** (-0.5)
        for b in range(ns):
            base, own = 3 * width * b, slice(b * width, (b + 1) * width)
            for ref, at in ((q_ref, 0), (k_ref, 1)):
                values = proj_ref[:, base + at * width : base + (at + 1) * width].astype(F32)
                ref[:, own] = (values * cosine + swap_lanes(values) * sine).astype(BF)
            for h in range(width // HD):
                span = slice(b * width + h * HD, b * width + (h + 1) * HD)
                scores = scaling * dot_nt(q_ref[:, span], k_ref[:, span])
                scores = jnp.where(allowed, scores, NEGATIVE)
                peak = jnp.max(scores, -1, keepdims=True)
                exponent = jnp.exp(scores - peak)
                total = jnp.sum(exponent, -1, keepdims=True)
                probs = (exponent * (1.0 / total)).astype(BF)
                at = base + 2 * width + h * HD
                mix_ref[:, span] = dot_nn(probs, proj_ref[:, at : at + HD]).astype(BF)
                at = b * (width // HD) + h
                lse_ref[:, at : at + 1] = peak + jnp.log(total)
        self.store(1, 2, 3)
        self.fetch(2)
        for at in range(0, self.width, OUT_BLOCK):
            part_ref[:, at : at + OUT_BLOCK] = dot_nt(mix_ref[...], w_out[at : at + OUT_BLOCK]).astype(BF)
        moment("ready")
        new_rows = stream_ref[...] + scatter_part(place, part_ref, self.bufs, self.rows, moment)
        new_ref[...] = new_rows
        low_ref[...] = norm_forward(new_rows, gain_ref, shift_ref)
        self.spread(place, [Gather(place, low_ref, gathered[0], self.gather_sems[0], self.rows)], moment)


class FfnForward(Main):
    def __init__(self, full, w_gate_up, w_down, stream, gain, shift, cotangent=None):
        super().__init__()
        self.rows, self.width = stream.shape
        length = full.shape[0]
        self.last = cotangent is not None
        self.big = [full, w_gate_up, w_down]
        self.small = [stream, cotangent] if self.last else [stream, gain, shift]
        self.results = [like(stream.shape, F32)]
        self.kept = [like((length, w_gate_up.shape[1]), F32), like((length, w_down.shape[1]), BF)]
        self.gathered = [like(full.shape, BF)]
        self.work = [like(full.shape, BF), like(stream.shape, BF)]

    def compute(self, place, big, small, results, kept, gathered, moment):
        full, w_gate_up, w_down = big
        stream_ref = small[0]
        both_ref, act_ref = kept
        part_ref, low_ref = self.work_refs
        ns = place.sizes.ns
        width = w_down.shape[1] // ns
        gather = None
        if self.last:
            gather = Gather(place, small[1], gathered[0], self.gather_sems[0], self.rows)
            gather.begin()
        self.fetch(0, 1)

        def gates(rows):
            both = dot_nn(full[rows], w_gate_up[...])
            both_ref[rows] = both
            for b in range(ns):
                gate = both[:, 2 * b * width : (2 * b + 1) * width]
                up = both[:, (2 * b + 1) * width : (2 * b + 2) * width]
                act_ref[rows, b * width : (b + 1) * width] = (gate * jax.nn.sigmoid(gate) * up).astype(BF)

        by_rows(full.shape[0], ROW_BLOCK, gates)
        self.store(0, 1)
        self.fetch(2)
        for at in range(0, self.width, OUT_BLOCK):
            part_ref[:, at : at + OUT_BLOCK] = dot_nt(act_ref[...], w_down[at : at + OUT_BLOCK]).astype(BF)
        moment("ready")
        new_rows = stream_ref[...] + scatter_part(place, part_ref, self.bufs, self.rows, moment)
        results[0][...] = new_rows
        if self.last:
            moment("summed")
            for step in range(1, place.sizes.nc):
                gather.forward(step)
            moment("spread")
            moment("late")
            gather.end()
            return
        low_ref[...] = norm_forward(new_rows, small[1], small[2])
        self.spread(place, [Gather(place, low_ref, gathered[0], self.gather_sems[0], self.rows)], moment)


class FfnBack(Main):
    def __init__(self, grad_full, w_gate_up, w_down, both, acts, full, grad, saved, gain):
        super().__init__()
        self.rows, self.width = grad.shape
        self.big = [grad_full, w_down, both, w_gate_up, acts, full]
        self.small = [grad, saved, gain]
        self.results = [like(grad.shape, F32), like((2, self.width), F32)]
        self.kept = [like(w_down.shape, BF), like(w_gate_up.shape, BF)]
        self.gathered = [like(full.shape, BF)]
        self.work = [like(both.shape, BF), like(full.shape, BF), like(grad.shape, BF)]

    def compute(self, place, big, small, results, kept, gathered, moment):
        grad_full, w_down, both_ref, w_gate_up, act_ref, full = big
        grad_ref, saved_ref, gain_ref = small
        new_ref, norm_ref = results
        down_ref, gate_up_ref = kept
        low_ref, part_ref, grad_low_ref = self.work_refs
        ns = place.sizes.ns
        width = w_down.shape[1] // ns
        self.grads = {"down": down_ref, "gate": gate_up_ref}
        self.fetch(0, 1, 2)

        def gates(rows):
            act_grad = dot_nn(grad_full[rows], w_down[...])
            for b in range(ns):
                first, second = 2 * b * width, (2 * b + 1) * width
                gate, up = both_ref[rows, first : first + width], both_ref[rows, second : second + width]
                mine = act_grad[:, b * width : (b + 1) * width]
                sg = jax.nn.sigmoid(gate)
                low_ref[rows, first : first + width] = (mine * up * sg * (1.0 + gate * (1.0 - sg))).astype(BF)
                low_ref[rows, second : second + width] = (mine * gate * sg).astype(BF)

        by_rows(full.shape[0], ROW_BLOCK, gates)
        self.fetch(3)
        for at in range(0, self.width, OUT_BLOCK):
            part_ref[:, at : at + OUT_BLOCK] = dot_nt(low_ref[...], w_gate_up[at : at + OUT_BLOCK]).astype(BF)
        moment("ready")
        self.fetch(4, 5)

        def weights(name):
            if name == "sent":
                for at in range(0, self.width, OUT_BLOCK):
                    down_ref[at : at + OUT_BLOCK] = dot_tn(grad_full[:, at : at + OUT_BLOCK], act_ref[...]).astype(BF)
                self.store(0)
                moment("downs")
                for at in range(0, self.width, OUT_BLOCK):
                    gate_up_ref[at : at + OUT_BLOCK] = dot_tn(full[:, at : at + OUT_BLOCK], low_ref[...]).astype(BF)
                self.store(1)
                moment("gates")
            moment(name)

        total = scatter_part(place, part_ref, self.bufs, self.rows, weights)
        inner, gain_grad, shift_grad = norm_back(total, saved_ref[...], gain_ref[...])
        new_rows = grad_ref[...] + inner
        new_ref[...] = new_rows
        grad_low_ref[...] = new_rows.astype(BF)
        norm_ref[0:1] = gain_grad
        norm_ref[1:2] = shift_grad
        self.spread(place, [Gather(place, grad_low_ref, gathered[0], self.gather_sems[0], self.rows)], moment)


class AttnBack(Main):
    def __init__(self, grad_full, w_qkv, w_out, kept, full, tables, lse, grad, saved, gain, last):
        super().__init__()
        proj, mixed, q_rot, k_rot = kept
        self.rows, self.width = grad.shape
        self.last = last
        self.big = [grad_full, w_out, q_rot, k_rot, proj, w_qkv, full, mixed]
        self.small = [*tables, lse, grad, saved, gain]
        self.results = [like(grad.shape, F32), like((2, self.width), F32), like((1, w_qkv.shape[1]), F32)]
        self.kept = [like(w_qkv.shape, BF), like(w_out.shape, BF)]
        self.gathered = [] if last else [like(full.shape, BF)]
        self.work = [like(proj.shape, BF), like(full.shape, BF), like(grad.shape, BF), like(mixed.shape, BF)]

    def compute(self, place, big, small, results, kept, gathered, moment):
        grad_full, w_out, q_ref, k_ref, proj_ref, w_qkv, full, mix_ref = big
        col_ref, row_ref, cos_ref, sin_ref, lse_ref, grad_ref, saved_ref, gain_ref = small
        new_ref, norm_ref, bias_ref = results
        qkv_ref, out_ref = kept
        low_ref, part_ref, grad_low_ref, mix_grad_ref = self.work_refs
        ns = place.sizes.ns
        width = w_out.shape[1] // ns
        self.grads = {"qkv": qkv_ref, "out": out_ref}
        self.fetch(0, 1)

        def mixed_grad(rows):
            mix_grad_ref[rows] = dot_nn(grad_full[rows], w_out[...]).astype(BF)

        by_rows(full.shape[0], ROW_BLOCK, mixed_grad)
        self.fetch(2, 3, 4)
        allowed = allowed_of(col_ref[...], row_ref[...])
        cosine, sine = cos_ref[...], sin_ref[...]
        scaling = HD ** (-0.5)
        for b in range(ns):
            parts = [[], [], []]
            base = 3 * width * b
            for h in range(width // HD):
                span = slice(b * width + h * HD, b * width + (h + 1) * HD)
                at = b * (width // HD) + h
                q_rows, k_rows, out_grad = q_ref[:, span], k_ref[:, span], mix_grad_ref[:, span]
                scores = jnp.where(allowed, scaling * dot_nt(q_rows, k_rows), NEGATIVE)
                probs = jnp.exp(scores - lse_ref[:, at : at + 1])
                first = base + 2 * width + h * HD
                prob_grad = dot_nt(out_grad, proj_ref[:, first : first + HD])
                inner = jnp.sum(probs * prob_grad, -1, keepdims=True)
                score_low = (probs * (prob_grad - inner)).astype(BF)
                parts[0].append(scaling * dot_nn(score_low, k_rows))
                parts[1].append(scaling * dot_tn(score_low, q_rows))
                parts[2].append(dot_tn(probs.astype(BF), out_grad))
            for at in range(3):
                values = jnp.concatenate(parts[at], axis=1)
                if at < 2:
                    values = values * cosine - swap_lanes(values) * sine
                low = values.astype(BF)
                lanes = slice(base + at * width, base + (at + 1) * width)
                low_ref[:, lanes] = low
                bias_ref[:, lanes] = jnp.sum(low.astype(F32), 0, keepdims=True)
        self.fetch(5)
        for at in range(0, self.width, OUT_BLOCK):
            part_ref[:, at : at + OUT_BLOCK] = dot_nt(low_ref[...], w_qkv[at : at + OUT_BLOCK]).astype(BF)
        moment("ready")
        self.fetch(6, 7)

        def weights(name):
            if name == "sent":
                for at in range(0, self.width, OUT_BLOCK):
                    span = slice(at, at + OUT_BLOCK)
                    qkv_ref[span] = dot_tn(full[:, span], low_ref[...]).astype(BF)
                    out_ref[span] = dot_tn(grad_full[:, span], mix_ref[...]).astype(BF)
                self.store(0, 1)
                moment("attns")
            moment(name)

        total = scatter_part(place, part_ref, self.bufs, self.rows, weights)
        inner, gain_grad, shift_grad = norm_back(total, saved_ref[...], gain_ref[...])
        new_rows = grad_ref[...] + inner
        new_ref[...] = new_rows
        norm_ref[0:1] = gain_grad
        norm_ref[1:2] = shift_grad
        if self.last:
            for name in ("summed", "spread", "late"):
                moment(name)
            return
        grad_low_ref[...] = new_rows.astype(BF)
        self.spread(place, [Gather(place, grad_low_ref, gathered[0], self.gather_sems[0], self.rows)], moment)


class Alone:
    kinds, ins, in_specs, outs, out_specs = (), [], [], [], []

    def scratch(self, sizes):
        return []

    def run(self, place, ins, outs, scratch, moment):
        moment("begin")


class Start:
    kinds = ("mate", "ctx", "fsdp", "twin")

    def __init__(self, sizes, small, hidden, cotangent, piece, chains):
        self.sizes, self.piece, self.chains = sizes, piece, chains
        lines, lanes = small.shape
        count, self.width = hidden.shape
        self.rows = count // (sizes.ns * sizes.nk)
        group = sizes.nc * sizes.nk * self.rows
        self.ins, self.in_specs = [small, hidden, cotangent], [VMEM_SPEC] * 3
        self.outs = [
            like((sizes.nf, sizes.nc * lines, lanes), F32),
            like((lines, lanes), F32),
            like((lines, self.width), F32),
            like((self.rows, self.width), F32),
            like((self.rows, self.width), BF),
            like((group, self.width), BF),
        ]
        self.out_specs = [VMEM_SPEC] * 5 + [ANY_SPEC]

    def scratch(self, sizes):
        others = max(sizes.nf - 1, 1)
        small = [DMA((sizes.nc,)), DMA((sizes.nc,)), DMA((others,)), DMA((others,)), DMA(()), DMA(())]
        return small + [pltpu.VMEM((self.rows, self.width), BF)] + Gather.scratch(sizes)

    def run(self, place, ins, outs, scratch, moment):
        sizes, rows, width = self.sizes, self.rows, self.width
        small_ref, hidden_ref, cotangent_ref = ins
        all_ref, twin_ref, norm_ref, stream_ref, grad_ref, full_ref = outs
        cs, cr, fs, fr, ts, tr = scratch[:6]
        low_ref = scratch[6]
        lines = small_ref.shape[0]

        def line_of(c):
            return pl.ds(pl.multiple_of(c * lines, lines), lines)

        to_context = [
            push(small_ref, all_ref.at[0, line_of(place.c)], cs.at[step], cr.at[step], place.ahead(step))
            for step in range(1, sizes.nc)
        ]
        to_twin = push(small_ref, twin_ref, ts, tr, place.twin())
        for copy in to_context + [to_twin]:
            copy.start()
        moment("begin")
        all_ref[0, line_of(place.c)] = small_ref[...]
        own_rows = pl.ds(pl.multiple_of((place.s * sizes.nk + place.k) * rows, rows), rows)
        part = width // sizes.nf
        for df in range(sizes.nf):
            lanes = pl.ds(pl.multiple_of(lax.rem(place.f + df, sizes.nf) * part, part), part)
            stream_ref[:, df * part : (df + 1) * part] = hidden_ref[own_rows, lanes].astype(F32)
            grad_ref[:, df * part : (df + 1) * part] = cotangent_ref[own_rows, lanes]
        unit_rows, _ = unit_rows_of(stream_ref[...])
        for copy in to_context:
            copy.wait()
        to_across = [
            push(all_ref.at[0], all_ref.at[sizes.nf - step], fs.at[step - 1], fr.at[step - 1], place.across(step))
            for step in range(1, sizes.nf)
        ]
        for copy in to_across:
            copy.start()
        for copy in to_across + [to_twin]:
            copy.wait()
        for df in range(sizes.nf):
            for c in range(sizes.nc):
                at = (df * sizes.nc + c) * self.piece
                norm_ref[:, at : at + self.piece] = all_ref[df, c * lines : (c + 1) * lines, : self.piece]
        low_ref[...] = (unit_rows * norm_ref[0:1] + norm_ref[1:2]).astype(BF)
        gather = Gather(place, low_ref, full_ref, scratch[7:12], rows)
        gather.begin()
        for exchange, spread in self.chains:
            exchange.wait_own()
            spread.first(place.c)
        for step in range(1, sizes.nc):
            for exchange, spread in self.chains:
                exchange.wait_from(step)
                spread.first(lax.rem(place.c + sizes.nc - step, sizes.nc))
            gather.forward(step)
        moment("spread")
        for step in range(sizes.nc):
            for exchange, spread in self.chains:
                spread.second(lax.rem(place.c + sizes.nc - step, sizes.nc))
        moment("late")
        gather.end()
        for exchange, spread in self.chains:
            exchange.wait_sent()
            for block in range(sizes.nc):
                spread.finish(block)


class Guest(Rider):
    def __init__(self, rider):
        self.kinds, self.ins, self.outs, self.sems = rider.kinds, rider.ins, rider.outs, rider.sems
        self.rider = rider

    def bind(self, *refs):
        self.rider.bind(*refs)

    def at(self, moment):
        if moment == "begin" and isinstance(self.rider, Exchange):
            self.rider.start()


def comm_kernel(sizes, main, riders, kinds, layout, *refs):
    cuts, at = [], 0
    for size in layout:
        cuts.append(refs[at : at + size])
        at += size
    count = len(riders)
    ins, outs, scratch = cuts[: count + 1], cuts[count + 1 : 2 * count + 2], cuts[2 * count + 2 :]
    place = Place(sizes)
    for i, rider in enumerate(riders):
        rider.bind(place, ins[i + 1], outs[i + 1], scratch[i + 1], main)
    greet(place, kinds)

    def moment(name):
        for rider in riders:
            rider.at(name)

    main.run(place, ins[0], outs[0], scratch[0], moment)
    moment("end")


def comm_call(sizes, collective_id, main, riders=(), micros=50):
    kinds = set(main.kinds)
    for rider in riders:
        kinds |= set(rider.kinds)
    main_scratch = main.scratch(sizes)
    operands, in_specs = list(main.ins), list(main.in_specs)
    outs, out_specs = list(main.outs), list(main.out_specs)
    scratch = list(main_scratch)
    for rider in riders:
        operands += rider.ins
        in_specs += [ANY_SPEC] * len(rider.ins)
        outs += rider.outs
        out_specs += [ANY_SPEC] * len(rider.outs)
        scratch += rider.sems
    layout = [len(main.ins)] + [len(rider.ins) for rider in riders]
    layout += [len(main.outs)] + [len(rider.outs) for rider in riders]
    layout += [len(main_scratch)] + [len(rider.sems) for rider in riders]
    results = pl.pallas_call(
        functools.partial(comm_kernel, sizes, main, riders, kinds, layout),
        out_shape=outs,
        in_specs=in_specs,
        out_specs=out_specs,
        scratch_shapes=scratch,
        compiler_params=pltpu.CompilerParams(
            collective_id=collective_id, has_side_effects=True, vmem_limit_bytes=VMEM_BYTES
        ),
        cost_estimate=pl.CostEstimate(flops=0, bytes_accessed=micros * 3 * MIB, transcendentals=0),
    )(*operands)
    groups, at = [], 0
    for size in [len(main.outs)] + [len(rider.outs) for rider in riders]:
        groups.append(list(results[at : at + size]))
        at += size
    return groups[0], groups[1:]


def finish_kernel(count, hidden, *refs):
    ins, (qkv_out, out_out, gate_up_out, down_out) = refs[: 4 * count], refs[4 * count :]
    triple, rows, q_cols = qkv_out.shape[1:]
    for layer in range(count):

        @pl.when(pl.program_id(0) == layer)
        def _():
            qkv, out, gate, down = ins[4 * layer : 4 * layer + 4]
            f_cols = gate.shape[1] // 2

            def some(span):
                for at in range(triple):
                    qkv_out[0, at, span] = qkv[span, at * q_cols : (at + 1) * q_cols].astype(F32)
                out_out[0, span] = out[span].astype(F32)
                for at in range(2):
                    gate_up_out[0, span, at] = gate[span, at * f_cols : at * f_cols + hidden].astype(F32)
                down_out[0, span] = down[span, :hidden].astype(F32)

            by_rows(rows, 64, some)


def finish(grads, q_cols, hidden):
    count = len(grads)
    rows = grads[0][0].shape[0]
    shapes = [(3, rows, q_cols), (rows, q_cols), (rows, 2, hidden), (rows, hidden)]

    def block(shape):
        return pl.BlockSpec((1,) + shape, lambda layer: (layer,) + (0,) * len(shape))

    return pl.pallas_call(
        functools.partial(finish_kernel, count, hidden),
        grid=(count,),
        out_shape=[jax.ShapeDtypeStruct((count,) + shape, F32) for shape in shapes],
        in_specs=[VMEM_SPEC] * (4 * count),
        out_specs=[block(shape) for shape in shapes],
        compiler_params=pltpu.CompilerParams(vmem_limit_bytes=VMEM_BYTES),
    )(*[one for layer in grads for one in layer])


def rotary_tables(labels, width):
    places = jnp.arange(labels.shape[-1], dtype=jnp.int32)
    fresh = jnp.concatenate([jnp.ones((1,), jnp.bool_), labels[1:] != labels[:-1]])
    starts = lax.cummax(jnp.where(fresh, places, 0))
    offsets = (places - starts).astype(F32)
    frequency = jnp.exp(jnp.arange(ROT // 2, dtype=F32) * (-2.0 * math.log(ROPE_BASE) / ROT))
    angles = offsets[:, None] * frequency
    cosine, sine = jnp.cos(angles), jnp.sin(angles)
    rest = jnp.ones((labels.shape[0], HD - ROT), F32)
    cosine = jnp.concatenate([cosine, cosine, rest], 1)
    sine = jnp.concatenate([-sine, sine, 0.0 * rest], 1)
    return jnp.tile(cosine, (1, width // HD)), jnp.tile(sine, (1, width // HD))


def body(
    mesh,
    hidden_in,
    segment_ids,
    norm_gains,
    norm_shifts,
    qkv_weight,
    qkv_bias,
    out_weight,
    gate_up_weight,
    down_weight,
    cotangent,
):
    ns, shard_rows, width = hidden_in.shape
    sizes = Sizes(mesh, ns)
    nf, nc, nk, nt = sizes.nf, sizes.nc, sizes.nk, sizes.nt
    f, c, t = lax.axis_index("fsdp"), lax.axis_index("context"), lax.axis_index("tensor")
    s = t // nk
    layers = qkv_weight.shape[0]
    rows = shard_rows // nk
    part = width // nf
    piece = part // nc
    q_cols = qkv_weight.shape[3]
    q_sub = q_cols // nc
    hidden = gate_up_weight.shape[3]
    f_sub = -(-hidden // (nc * TILE)) * TILE
    f_cols = nc * f_sub

    qkv_flat = qkv_weight.transpose(0, 2, 1, 3).reshape(layers * 3 * piece, q_cols)
    out_flat = out_weight.reshape(layers * piece, q_cols)
    fill = ((0, 0), (0, f_cols - hidden))
    down_flat = jnp.pad(down_weight.reshape(layers * piece, hidden), fill)
    gate_up_flat = jnp.pad(gate_up_weight, ((0, 0), (0, 0)) + fill).reshape(layers * piece, 2 * f_cols)

    def exchange(name, layer, when="begin", finish="end"):
        first = layer * piece
        array, corners, sub = {
            "qkv": (qkv_flat, [((3 * layer + at) * piece, 0) for at in range(3)], q_sub),
            "out": (out_flat, [(first, 0)], q_sub),
            "gate": (gate_up_flat, [(first, 0), (first, f_cols)], f_sub),
            "down": (down_flat, [(first, 0)], f_sub),
        }[name]
        return WeightExchange(sizes, piece, array, corners, sub, when, finish)

    norms = jnp.stack([norm_gains, norm_shifts], axis=2).reshape(4 * layers, piece).astype(F32)
    own_bias = lax.dynamic_slice_in_dim(qkv_bias, c * q_sub, q_sub, 2).reshape(3 * layers, q_sub).astype(F32)
    lines = -(-max(4 * layers, 3 * layers, ns) // 8) * 8

    def lined(value):
        return jnp.pad(value, ((0, lines - value.shape[0]), (0, 0)))

    small = jnp.concatenate([lined(norms), lined(segment_ids.astype(F32)), lined(own_bias)], axis=1)
    chains = []
    for name in ("qkv", "out"):
        moved = exchange(name, 0, finish=None)
        chains.append((moved, Spread(sizes, moved, blocks=nc, steps=(None, None))))
    start = Start(
        sizes,
        small,
        hidden_in.reshape(ns * shard_rows, width),
        cotangent.reshape(ns * shard_rows, width),
        piece,
        chains,
    )
    guests = [Guest(one) for chain in chains for one in chain]
    results, extra = comm_call(sizes, 1, start, guests + [exchange("gate", 0, "spread")], 80)
    small_all, small_twin, norm_rows, stream, grad_low, full_one = results
    w_qkv, w_out, gate_mine = extra[1][0], extra[3][0], extra[4][0]
    labels = small_all[0].reshape(nc, lines, -1)[:, :ns, piece : piece + shard_rows]
    labels = lax.dynamic_index_in_dim(labels, s, 1, keepdims=False).reshape(-1).astype(jnp.int32)
    bias_rows = [
        value[: 3 * layers, piece + shard_rows :].reshape(layers, 3 * q_sub) for value in (small, small_twin)
    ]
    bias_rows = jnp.concatenate(bias_rows, axis=1)
    cosine, sine = rotary_tables(labels, q_sub)
    tables = [labels[:, None], labels[None, :], cosine, sine]

    def gain_row(layer, which):
        at = (layer * 2 + which) * 2
        return norm_rows[at : at + 1]

    def shift_row(layer, which):
        at = (layer * 2 + which) * 2 + 1
        return norm_rows[at : at + 1]

    kept = []
    for layer in range(layers):
        more = layer + 1 < layers
        down_first = exchange("down", layer, finish=None)
        riders = [Spread(sizes, gate_mine), down_first, Spread(sizes, down_first, steps=("inside1", "spread"))]
        if more:
            riders += [exchange("qkv", layer + 1), exchange("out", layer + 1)]
        main = AttnForward(
            full_one, w_qkv, w_out, bias_rows[layer : layer + 1], tables, stream, gain_row(layer, 1), shift_row(layer, 1)
        )
        results, extra = comm_call(sizes, 2 + 2 * layer, main, riders, 85)
        middle, lse, proj, mixed, q_rot, k_rot, full_two = results
        w_gate_up, w_down = extra[0][0], extra[2][0]
        attn_kept = (full_one, w_qkv, w_out, (proj, mixed, q_rot, k_rot), lse, stream)
        if more:
            riders = [Spread(sizes, extra[3][0]), Spread(sizes, extra[4][0]), exchange("gate", layer + 1)]
            main = FfnForward(
                full_two, w_gate_up, w_down, middle, gain_row(layer + 1, 0), shift_row(layer + 1, 0)
            )
        else:
            riders = []
            main = FfnForward(full_two, w_gate_up, w_down, middle, None, None, grad_low)
        results, extra = comm_call(sizes, 3 + 2 * layer, main, riders, 55)
        stream, both, acts, full = results
        kept.append(attn_kept + (full_two, w_gate_up, w_down, both, acts, middle))
        if more:
            full_one = full
            w_qkv, w_out, gate_mine = (one[0] for one in extra)
        else:
            grad_full = full

    first_id = 2 + 2 * layers
    grad = grad_low.astype(F32)
    seconds, ready = [], []
    done, norm_grads, bias_grads = {}, {}, {}
    calls = [0]
    shares = [("block_out", share_rows(sizes, stream.astype(BF)))]

    def run(main, names, micros):
        riders, after = [], []
        for name, halves in seconds:
            riders.append(GradSecond(sizes, halves[0][1].astype(BF), jnp.stack(halves[1][1:]).astype(BF)))
            after.append(("second", name, halves))
        for name, total in ready:
            riders.append(GradExchange(sizes, total, q_sub if name[0] in ("qkv", "out") else f_sub))
            after.append(("ready", name, total))
        for layer, name, when, at in names:
            shape = main.kept[at].shape
            riders.append(GradFirst(sizes, name, *shape, when))
            after.append(("first", (name, layer), at))
        for name, rider in shares:
            riders.append(rider)
            after.append(("share", name, None))
        seconds.clear(), ready.clear(), shares.clear()
        results, extra = comm_call(sizes, first_id + calls[0], main, riders, micros)
        calls[0] += 1
        for (stage, name, value), out in zip(after, extra):
            if stage == "first":
                own = results[len(main.results) + value]
                seconds.append((name, grad_halves(sizes, own, *out)))
            elif stage == "second":
                low, high = out
                lower = value[0][0] + low.astype(F32)
                upper = value[1][0] + sum(high[at].astype(F32) for at in range(nf - 1))
                ready.append((name, jnp.concatenate([lower, upper], 0).astype(BF)))
            else:
                done[name] = out[0]
        return results

    for layer in range(layers - 1, -1, -1):
        full_one, w_qkv, w_out, attn_kept, lse, stream, full_two, w_gate_up, w_down, both, acts, middle = kept[layer]
        main = FfnBack(grad_full, w_gate_up, w_down, both, acts, full_two, grad, middle, gain_row(layer, 1))
        names = [(layer, "down", "downs", 0), (layer, "gate", "gates", 1)]
        grad, norm_grads[(layer, 1)], _, _, middle_full = run(main, names, 60)
        main = AttnBack(
            middle_full, w_qkv, w_out, attn_kept, full_one, tables, lse, grad, stream, gain_row(layer, 0), layer == 0
        )
        names = [(layer, "qkv", "attns", 0), (layer, "out", "attns", 1)]
        results = run(main, names, 60)
        grad, norm_grads[(layer, 0)], bias_grads[layer] = results[:3]
        if layer > 0:
            grad_full = results[5]
    norm_part = jnp.stack(
        [jnp.stack([norm_grads[(layer, which)] for which in range(2)], 1) for layer in range(layers)], 1
    )
    norm_part = norm_part.reshape(4 * layers, nf, nc, piece).transpose(2, 1, 0, 3)
    bias_part = jnp.concatenate([bias_grads[layer] for layer in range(layers)]).reshape(layers, ns, 3, q_sub)
    bias_part = bias_part.transpose(1, 0, 2, 3).reshape(ns, 3 * layers, q_sub)
    bias_part = jnp.pad(bias_part, ((0, 0), (0, -3 * layers % 8), (0, 0)))
    shares.append(("input_grad", share_rows(sizes, grad.astype(BF))))
    shares.append(("norm", share_context(sizes, norm_part, True)))
    around = [(df, ds * nk, ds) for df in range(nf) for ds in range(ns)]
    shares.append(("bias", share_plane(sizes, bias_part, around)))
    run(Alone(), [], 50)
    around = [(df, dt, df) for df in range(nf) for dt in range(nt)]
    shares.append(("norm", share_plane(sizes, jnp.sum(done["norm"], 0), around)))
    shares.append(("bias", share_context(sizes, jnp.sum(done["bias"], 0), False)))
    run(Alone(), [], 50)
    while seconds or ready:
        run(Alone(), [], 50)
    block_out = done["block_out"].reshape(ns, shard_rows, width)
    input_grad = done["input_grad"].reshape(ns, shard_rows, width).astype(F32)
    norm_total = jnp.sum(done["norm"], 0).reshape(2, layers, 2, piece)
    bias_total = done["bias"][:, : 3 * layers].reshape(nc, layers, 3, q_sub)
    bias_total = bias_total.transpose(1, 2, 0, 3).reshape(layers, 3, q_cols)

    grads = [[done[(name, layer)] for name in ("qkv", "out", "gate", "down")] for layer in range(layers)]
    qkv_grad, out_grad, gate_up_grad, down_grad = finish(grads, q_cols, hidden)
    return (
        block_out,
        input_grad,
        norm_total[0],
        norm_total[1],
        qkv_grad.transpose(0, 2, 1, 3),
        bias_total,
        out_grad,
        gate_up_grad,
        down_grad,
    )


def solution(mesh):
    return jax.shard_map(
        functools.partial(body, mesh),
        mesh=mesh,
        in_specs=(
            P("fsdp", "context", None),
            P("fsdp", "context"),
            P(None, None, ("fsdp", "context")),
            P(None, None, ("fsdp", "context")),
            P(None, ("fsdp", "context"), None, "tensor"),
            P(None, None, "tensor"),
            P(None, ("fsdp", "context"), "tensor"),
            P(None, ("fsdp", "context"), None, "tensor"),
            P(None, ("fsdp", "context"), "tensor"),
            P("fsdp", "context", None),
        ),
        out_specs=(
            P("fsdp", "context", None),
            P("fsdp", "context", None),
            P(None, None, ("fsdp", "context")),
            P(None, None, ("fsdp", "context")),
            P(None, ("fsdp", "context"), None, "tensor"),
            P(None, None, "tensor"),
            P(None, ("fsdp", "context"), "tensor"),
            P(None, ("fsdp", "context"), None, "tensor"),
            P(None, ("fsdp", "context"), "tensor"),
        ),
        check_vma=False,
    )
```

```python
import functools
import math

import jax
import jax.numpy as jnp
from jax import lax
from jax.experimental import pallas as pl
from jax.experimental.pallas import tpu as pltpu
from jax.sharding import PartitionSpec as P

HD = 64
ROT = 16
EPS = 1e-05
ROPE_BASE = 10000.0
NEGATIVE = -1e30
MESH = pl.DeviceIdType.MESH
BF = jnp.bfloat16
F32 = jnp.float32
MIB = 2**20
TILE = 128
VMEM_BYTES = 58 * MIB


def dot_nn(a, b):
    return jnp.dot(a, b, preferred_element_type=F32)


def dot_nt(a, b):
    return lax.dot_general(a, b, (((1,), (1,)), ((), ())), preferred_element_type=F32)


def dot_tn(a, b):
    return lax.dot_general(a, b, (((0,), (0,)), ((), ())), preferred_element_type=F32)


class Sizes:
    def __init__(self, mesh, ns):
        self.nf, self.nc, self.nt = mesh.shape["fsdp"], mesh.shape["context"], mesh.shape["tensor"]
        self.ns = ns
        self.nk = self.nt // ns


class Place:
    def __init__(self, sizes):
        self.sizes = sizes
        self.f = lax.axis_index("fsdp")
        self.c = lax.axis_index("context")
        self.t = lax.axis_index("tensor")
        self.s, self.k = self.t // sizes.nk, lax.rem(self.t, sizes.nk)

    def mate(self):
        return {"tensor": self.t + 1 - 2 * self.k}

    def twin(self):
        return {"tensor": self.t + self.sizes.nk * (1 - 2 * self.s)}

    def right(self):
        return {"context": self.c + 1}

    def left(self):
        return {"context": self.c - 1}

    def ahead(self, step):
        return {"context": lax.rem(self.c + step, self.sizes.nc)}

    def across(self, step):
        return {"fsdp": lax.rem(self.f + step, self.sizes.nf)}

    def plane(self, df, dt):
        return {"fsdp": lax.rem(self.f + df, self.sizes.nf), "tensor": lax.rem(self.t + dt, self.sizes.nt)}


def greet(place, kinds):
    barrier = pltpu.get_barrier_semaphore()
    nc, nf = place.sizes.nc, place.sizes.nf

    def signal(device):
        pl.semaphore_signal(barrier, inc=1, device_id=device, device_id_type=MESH)

    count = 0
    if "plane" in kinds:
        for df in range(nf):
            for dt in range(place.sizes.nt):
                if df or dt:
                    signal(place.plane(df, dt))
        count += nf * place.sizes.nt - 1
        kinds = set(kinds) - {"mate", "fsdp", "twin"}
    if "mate" in kinds:
        signal(place.mate())
        count += 1
    if "ctx" in kinds:
        for step in range(1, nc):
            signal(place.ahead(step))
        count += nc - 1
    elif "line" in kinds:

        @pl.when(place.c > 0)
        def _():
            signal(place.left())

        @pl.when(place.c < nc - 1)
        def _():
            signal(place.right())

        count += jnp.minimum(place.c, 1) + jnp.minimum(nc - 1 - place.c, 1)
    if "fsdp" in kinds:
        for step in range(1, nf):
            signal(place.across(step))
        count += nf - 1
    if "twin" in kinds:
        signal(place.twin())
        count += 1
    return count


def push(src, dst, send, recv, device):
    return pltpu.make_async_remote_copy(
        src_ref=src, dst_ref=dst, send_sem=send, recv_sem=recv, device_id=device, device_id_type=MESH
    )


DMA = pltpu.SemaphoreType.DMA
VMEM_SPEC = pl.BlockSpec(memory_space=pltpu.VMEM)
ANY_SPEC = pl.BlockSpec(memory_space=pl.ANY)


HALVES = 2


class Gather:
    def __init__(self, place, own, out, sems, rows):
        self.place, self.own, self.out, self.rows = place, own, out, rows
        self.piece = rows // HALVES
        self.local, self.line_send, self.line_recv, self.mate_send, self.mate_recv = sems

    @staticmethod
    def scratch(sizes):
        nc = sizes.nc
        return [DMA(()), DMA((2, nc, HALVES)), DMA((nc, HALVES)), DMA((nc, HALVES)), DMA((nc, HALVES))]

    def slot(self, source, k, half):
        at = (source * self.place.sizes.nk + k) * self.rows + half * self.piece
        return self.out.at[pl.ds(pl.multiple_of(at, self.piece), self.piece)]

    def origin(self, source, half, first):
        if first:
            return self.own.at[pl.ds(half * self.piece, self.piece)]
        return self.slot(source, self.place.k, half)

    def line(self, source, half, device, first, way):
        return push(
            self.origin(source, half, first),
            self.slot(source, self.place.k, half),
            self.line_send.at[way, source, half],
            self.line_recv.at[source, half],
            device,
        )

    def pass_on(self, source, half, first):
        return push(
            self.origin(source, half, first),
            self.slot(source, self.place.k, half),
            self.mate_send.at[source, half],
            self.mate_recv.at[source, half],
            self.place.mate(),
        )

    def keep(self):
        at = (self.place.c * self.place.sizes.nk + self.place.k) * self.rows
        target = self.out.at[pl.ds(pl.multiple_of(at, self.rows), self.rows)]
        return pltpu.make_async_copy(self.own, target, self.local)

    def begin(self):
        place, c, nc = self.place, self.place.c, self.place.sizes.nc
        for half in range(HALVES):

            @pl.when(c < nc - 1)
            def _():
                self.line(c, half, place.right(), True, 0).start()

            @pl.when(c > 0)
            def _():
                self.line(c, half, place.left(), True, 1).start()

        for half in range(HALVES):
            self.pass_on(c, half, True).start()
        self.keep().start()

    def forward(self, step):
        place, c, nc = self.place, self.place.c, self.place.sizes.nc
        source, other = c - step, c + step
        for half in range(HALVES):

            @pl.when(source >= 0)
            def _():
                self.line(source, half, place.left(), False, 0).wait_recv()

                @pl.when(c < nc - 1)
                def _():
                    self.line(source, half, place.right(), False, 0).start()

                self.pass_on(source, half, False).start()

            @pl.when(other <= nc - 1)
            def _():
                self.line(other, half, place.right(), False, 1).wait_recv()

                @pl.when(c > 0)
                def _():
                    self.line(other, half, place.left(), False, 1).start()

                self.pass_on(other, half, False).start()

    def end(self):
        place, c, nc = self.place, self.place.c, self.place.sizes.nc
        self.keep().wait()
        for source in range(nc):
            for half in range(HALVES):
                arrival = self.slot(source, 1 - place.k, half)
                push(
                    arrival, arrival, self.mate_send.at[source, half], self.mate_recv.at[source, half], place.mate()
                ).wait_recv()
                self.pass_on(source, half, False).wait_send()

                @pl.when((source <= c) & (c < nc - 1))
                def _():
                    self.line(source, half, place.right(), False, 0).wait_send()

                @pl.when((source >= c) & (c > 0))
                def _():
                    self.line(source, half, place.left(), False, 1).wait_send()


def scatter_part(place, part_ref, bufs, rows, moment):
    nc, nk, c, k = place.sizes.nc, place.sizes.nk, place.c, place.k
    piece = rows // HALVES
    mate_buf, to_right, to_left, from_left, from_right = bufs[:5]
    mate_send, mate_recv, right_send, right_recv, left_send, left_recv = bufs[5:]

    def block(dest, kk):
        return part_ref.at[pl.ds(pl.multiple_of((dest * nk + kk) * rows, rows), rows)]

    def mate_copy(dest):
        return push(
            block(dest, 1 - k), mate_buf.at[dest], mate_send.at[dest], mate_recv.at[dest], place.mate()
        )

    def lines(half):
        return slice(half * piece, (half + 1) * piece)

    def right_copy(dest, half):
        return push(
            to_right.at[dest, lines(half)],
            from_left.at[dest, lines(half)],
            right_send.at[dest, half],
            right_recv.at[dest, half],
            place.right(),
        )

    def left_copy(dest, half):
        return push(
            to_left.at[dest, lines(half)],
            from_right.at[dest, lines(half)],
            left_send.at[dest, half],
            left_recv.at[dest, half],
            place.left(),
        )

    def each(visit_right, visit_left, count, after=lambda step: None):
        for step in range(nc - 1):
            far = nc - 1 - step
            for half in range(count):

                @pl.when(far > c)
                def _():
                    visit_right(far, half)

                @pl.when(step < c)
                def _():
                    visit_left(step, half)

            after(step)

    def send_mate(dest, half):
        mate_copy(dest).start()

    each(send_mate, send_mate, 1)
    mate_copy(c).start()
    moment("sent")

    def chip_sum(dest, half):
        if half == 0:
            mate_copy(dest).wait_recv()
        at = pl.multiple_of((dest * nk + k) * rows + half * piece, piece)
        return part_ref[pl.ds(at, piece)].astype(F32) + mate_buf[dest, lines(half)].astype(F32)

    def pass_right(dest, half):
        total = chip_sum(dest, half)
        to_right[dest, lines(half)] = total.astype(BF)

        @pl.when(c > 0)
        def _():
            right_copy(dest, half).wait_recv()
            to_right[dest, lines(half)] = (total + from_left[dest, lines(half)].astype(F32)).astype(BF)

        right_copy(dest, half).start()

    def pass_left(dest, half):
        total = chip_sum(dest, half)
        to_left[dest, lines(half)] = total.astype(BF)

        @pl.when(c < nc - 1)
        def _():
            left_copy(dest, half).wait_recv()
            to_left[dest, lines(half)] = (total + from_right[dest, lines(half)].astype(F32)).astype(BF)

        left_copy(dest, half).start()

    each(pass_right, pass_left, HALVES, lambda step: moment("inside%d" % step))
    totals = []
    for half in range(HALVES):
        total = chip_sum(c, half)

        @pl.when(c > 0)
        def _():
            right_copy(c, half).wait_recv()

        @pl.when(c < nc - 1)
        def _():
            left_copy(c, half).wait_recv()

        total = total + jnp.where(c > 0, from_left[c, lines(half)].astype(F32), 0.0)
        totals.append(total + jnp.where(c < nc - 1, from_right[c, lines(half)].astype(F32), 0.0))
    def sent():
        for dest in range(nc):
            mate_copy(dest).wait_send()
            for half in range(HALVES):

                @pl.when(dest > c)
                def _():
                    right_copy(dest, half).wait_send()

                @pl.when(dest < c)
                def _():
                    left_copy(dest, half).wait_send()

    return jnp.concatenate(totals, 0), sent


def scatter_scratch(sizes, rows, width):
    nc = sizes.nc
    return [pltpu.VMEM((nc, rows, width), BF) for _ in range(5)] + [DMA((nc,)) for _ in range(2)] + [
        DMA((nc, HALVES)) for _ in range(4)
    ]


N_SCATTER = 11


class Rider:
    kinds = ()
    ins, outs, sems = [], [], []
    aliased = False

    def bind(self, place, ins, outs, sems, main):
        self.place, self.r_ins, self.r_outs, self.r_sems, self.main = place, ins, outs, sems, main

    def at(self, moment):
        pass


class Exchange(Rider):
    kinds = ("ctx",)

    def __init__(self, sizes, ins, out, pieces, rows, sub, when="begin", finish="end"):
        self.ins, self.outs, self.pieces, self.when, self.last = ins, [out], pieces, when, finish
        count = max(sizes.nc - 1, 1)
        self.sub = sub
        self.sems = [DMA(()), DMA((count,)), DMA((count,)), pltpu.VMEM((rows, sub * len(pieces)), BF)]

    def at(self, moment):
        if moment == self.when:
            self.start()
        if moment == self.last:
            self.finish()

    def start(self):
        place, nc = self.place, self.place.sizes.nc
        local, send, recv, held = self.r_sems
        for step in range(1, nc):
            for source_of, target_of in self.pieces:
                push(
                    source_of(self.r_ins, lax.rem(place.c + step, nc)),
                    target_of(self.r_outs[0], place.c),
                    send.at[step - 1],
                    recv.at[step - 1],
                    place.ahead(step),
                ).start()
        for at, (source_of, _) in enumerate(self.pieces):
            lanes = pl.ds(at * self.sub, self.sub)
            pltpu.make_async_copy(source_of(self.r_ins, place.c), held.at[:, lanes], local).start()

    def wait_own(self):
        local, _, _, held = self.r_sems
        pltpu.make_async_copy(held, held, local).wait()
        for at, (_, target_of) in enumerate(self.pieces):
            lanes = pl.ds(at * self.sub, self.sub)
            pltpu.make_async_copy(held.at[:, lanes], target_of(self.r_outs[0], self.place.c), local).start()
        pltpu.make_async_copy(held, held, local).wait()

    def wait_from(self, step):
        whole = self.whole()
        _, send, recv, _ = self.r_sems
        push(whole, whole, send.at[step - 1], recv.at[step - 1], self.place.ahead(step)).wait_recv()

    def wait_sent(self):
        whole = self.whole()
        _, send, recv, _ = self.r_sems
        for step in range(1, self.place.sizes.nc):
            push(whole, whole, send.at[step - 1], recv.at[step - 1], self.place.ahead(step)).wait_send()

    def finish(self):
        self.wait_own()
        for step in range(1, self.place.sizes.nc):
            self.wait_from(step)
        self.wait_sent()


class WeightExchange(Exchange):
    def __init__(self, sizes, rows, array, corners, sub, when="begin", finish="end"):
        pieces = [self.piece(first, rows, base, sub, at) for at, (first, base) in enumerate(corners)]
        out = jax.ShapeDtypeStruct((sizes.nc * rows, sub * len(pieces)), BF)
        super().__init__(sizes, [array], out, pieces, rows, sub, when, finish)
        self.rows = rows

    @staticmethod
    def piece(first, rows, base, sub, position):
        def source_of(refs, dest):
            return refs[0].at[pl.ds(first, rows), pl.ds(pl.multiple_of(base + dest * sub, TILE), sub)]

        def target_of(out, source):
            return out.at[pl.ds(pl.multiple_of(source * rows, rows), rows), pl.ds(position * sub, sub)]

        return source_of, target_of

    def whole(self):
        return self.r_outs[0].at[pl.ds(0, self.rows)]


class GradExchange(Exchange):
    def __init__(self, sizes, total, sub, when="begin", finish="end"):
        self.middle = total if isinstance(total, GradMiddle) else None
        shape = self.middle.outs[0].shape if self.middle else total.shape
        rows = shape[0] // sizes.nc
        count = shape[1] // sub
        out = jax.ShapeDtypeStruct((rows, sizes.nc * shape[1]), BF)
        pieces = [self.piece(rows, sub, position, sizes.nc) for position in range(count)]
        super().__init__(sizes, [] if self.middle else [total], out, pieces, rows, sub, when, finish)
        self.rows = rows

    def start(self):
        if self.middle:
            self.r_ins = [self.middle.total]
        super().start()

    @staticmethod
    def piece(rows, sub, position, nc):
        def source_of(refs, dest):
            return refs[0].at[pl.ds(pl.multiple_of(dest * rows, rows), rows), pl.ds(position * sub, sub)]

        def target_of(out, source):
            return out.at[:, pl.ds(pl.multiple_of(position * nc * sub + source * sub, TILE), sub)]

        return source_of, target_of

    def whole(self):
        return self.r_ins[0].at[pl.ds(0, self.rows)]


class Spread(Rider):
    kinds = ("fsdp", "twin")

    def __init__(self, sizes, mine, blocks=1, steps=("begin", "inside1")):
        if isinstance(mine, Exchange):
            self.source, shape, self.ins = mine, mine.outs[0].shape, []
        else:
            self.source, shape, self.ins = None, mine.shape, [mine]
        rows, self.width = shape
        self.part, self.blocks, self.rows, self.steps = rows, blocks, rows // blocks, steps
        self.outs = [jax.ShapeDtypeStruct((sizes.nf * rows, sizes.ns * self.width), BF)]
        others = max(sizes.nf - 1, 1)
        self.sems = [DMA((blocks,))] + [DMA((blocks, others)) for _ in range(8)] + [DMA((blocks,)) for _ in range(4)]
        self.sems.append(pltpu.VMEM((rows, self.width), BF))

    def at(self, moment):
        if moment == self.steps[0]:
            if self.source is not None:
                self.source.finish()
            for block in range(self.blocks):
                self.first(block)
        if moment == self.steps[1]:
            for block in range(self.blocks):
                self.second(block)
        if moment == "end":
            for block in range(self.blocks):
                self.finish(block)

    def span(self, df, block, half, whole=False):
        length = self.rows if whole else self.rows // 2
        at = df * self.part + block * self.rows + half * (self.rows // 2)
        return pl.ds(pl.multiple_of(at, length), length)

    def mine(self, block, half, whole=False):
        ref = self.r_ins[0] if self.source is None else self.source.r_outs[0]
        return ref.at[self.span(0, block, half, whole)]

    def out(self, ds, df, block, half, whole=False):
        return self.r_outs[0].at[self.span(df, block, half, whole), pl.ds(ds * self.width, self.width)]

    def copies(self, block, stage):
        place, nf, sems, out = self.place, self.place.sizes.nf, self.r_sems, []
        for step in range(1, nf):
            at, df = step - 1, nf - step
            across = place.across(step)
            source, target, pair, device = [
                (self.mine(block, 0), self.out(0, df, block, 0), 1, across),
                (self.mine(block, 1), self.out(0, df, block, 1), 3, across),
                (self.out(1, 0, block, 1), self.out(1, df, block, 1), 5, across),
            ][stage]
            out.append(push(source, target, sems[pair].at[block, at], sems[pair + 1].at[block, at], device))
            if stage == 2:
                source, target = self.out(0, df, block, 0), self.out(1, df, block, 0)
                out.append(push(source, target, sems[7].at[block, at], sems[8].at[block, at], place.twin()))
        if stage < 2:
            half, pair = (1, 9) if stage == 0 else (0, 11)
            out.append(
                push(
                    self.mine(block, half),
                    self.out(1, 0, block, half),
                    sems[pair].at[block],
                    sems[pair + 1].at[block],
                    place.twin(),
                )
            )
        return out

    def keep(self, block, inward):
        held = self.r_sems[13].at[self.span(0, block, 0, True)]
        ends = (self.mine(block, 0, True), held) if inward else (held, self.out(0, 0, block, 0, True))
        return pltpu.make_async_copy(*ends, self.r_sems[0].at[block])

    def first(self, block):
        for stage in range(2):
            for copy in self.copies(block, stage):
                copy.start()
        self.keep(block, True).start()

    def second(self, block):
        for copy in self.copies(block, 0):
            copy.wait_recv()
        for copy in self.copies(block, 2):
            copy.start()
        self.keep(block, True).wait()
        self.keep(block, False).start()

    def finish(self, block):
        for copy in self.copies(block, 0):
            copy.wait_send()
        for stage in (1, 2):
            for copy in self.copies(block, stage):
                copy.wait_recv()
                copy.wait_send()
        self.keep(block, False).wait()


class SpreadOwn(Spread):
    def at(self, moment):
        if moment == self.steps[0]:
            if self.source is not None:
                self.source.finish()
            for block in range(self.blocks):
                self.first(block)
        if moment == "end" and self.steps[0] is not None:
            for block in range(self.blocks):
                self.finish(block)

    def finish(self, block):
        self.keep(block, True).wait()
        self.keep(block, False).start()
        for stage in range(2):
            for copy in self.copies(block, stage):
                copy.wait_recv()
                copy.wait_send()
        self.keep(block, False).wait()


class SpreadRelay(Rider):
    kinds = ("fsdp", "twin")
    aliased = True

    def __init__(self, sizes, whole, when="begin"):
        self.ins, self.outs, self.when = [whole], [jax.ShapeDtypeStruct(whole.shape, BF)], when
        self.part, self.width = whole.shape[0] // sizes.nf, whole.shape[1] // sizes.ns
        others = max(sizes.nf - 1, 1)
        self.sems = [DMA((others,)) for _ in range(4)]
        self.blocks = sizes.nc

    def copies(self):
        out, place, nf = [], self.place, self.place.sizes.nf
        rows, half = self.part // self.blocks, self.part // self.blocks // 2
        for step in range(1, nf):
            at, df = step - 1, nf - step
            for block in range(self.blocks):
                low, high = block * rows, block * rows + half
                lanes = pl.ds(self.width, self.width)
                first = pl.ds(df * self.part + low, half)
                second = pl.ds(df * self.part + high, half)
                whole = self.r_outs[0]
                out.append(
                    push(
                        whole.at[pl.ds(high, half), lanes],
                        whole.at[second, lanes],
                        self.sems_of(0, at),
                        self.sems_of(1, at),
                        place.across(step),
                    )
                )
                out.append(
                    push(
                        whole.at[first, pl.ds(0, self.width)],
                        whole.at[first, lanes],
                        self.sems_of(2, at),
                        self.sems_of(3, at),
                        place.twin(),
                    )
                )
        return out

    def sems_of(self, kind, at):
        return self.r_sems[kind].at[at]

    def at(self, moment):
        if moment == self.when:
            for copy in self.copies():
                copy.start()
        if moment == "end":
            place, half = self.place, self.part // 2
            for step in range(1, place.sizes.nf):
                at = step - 1
                bytes_of = self.r_outs[0].at[pl.ds(0, half), pl.ds(0, self.width)]
                for kind, device in ((0, place.across(step)), (2, place.twin())):
                    push(bytes_of, bytes_of, self.sems_of(kind, at), self.sems_of(kind + 1, at), device).wait()


class GradFirst(Rider):
    kinds = ("fsdp", "twin")

    def __init__(self, sizes, name, rows, width, when):
        self.name, self.when, self.taken = name, when, False
        self.part = rows // sizes.nf
        self.half = self.part // 2
        self.width = width // sizes.ns
        others = max(sizes.nf - 1, 1)
        self.outs = [
            jax.ShapeDtypeStruct((others, self.half, width), BF),
            jax.ShapeDtypeStruct((sizes.nf, self.half, self.width), BF),
        ]
        self.sems = [DMA((others,)), DMA((others,)), DMA((sizes.nf,)), DMA((sizes.nf,))]

    def copies(self):
        place, nf = self.place, self.place.sizes.nf
        grads, (low, high) = self.main.grads[self.name], self.r_outs
        xs, xr, ys, yr = self.r_sems
        out = []
        for step in range(1, nf):
            at = step - 1
            out.append(
                push(grads.at[pl.ds(step * self.part, self.half)], low.at[at], xs.at[at], xr.at[at], place.across(step))
            )
        for df in range(nf):
            rows = pl.ds(df * self.part + self.half, self.half)
            out.append(
                push(grads.at[rows, pl.ds(self.width, self.width)], high.at[df], ys.at[df], yr.at[df], place.twin())
            )
        return out

    def at(self, moment):
        if moment == self.when:
            for copy in self.copies():
                copy.start()
        if moment == "end":
            if not self.taken:
                self.wait_recv()
            for copy in self.copies():
                copy.wait_send()

    def wait_recv(self):
        self.taken = True
        for copy in self.copies():
            copy.wait_recv()


class GradMiddle(Rider):
    kinds = ("fsdp", "twin")

    def __init__(self, sizes, source, steps=("begin", "sent", "late")):
        self.steps = steps
        if isinstance(source, GradFirst):
            self.source, self.ins = source, []
            low, high = source.outs
            part = source.part
        else:
            self.source, self.ins = None, list(source)
            low, high = source[1:]
            part = source[0].shape[0] // sizes.nf
        self.part, self.half, self.width = part, part // 2, high.shape[2]
        nf, others = sizes.nf, low.shape[0]
        self.outs = [jax.ShapeDtypeStruct((part, self.width), BF)]
        piece = (self.half, self.width)
        self.sems = [
            pltpu.VMEM((self.half, sizes.ns * self.width), BF),
            pltpu.VMEM((nf,) + piece, BF),
            pltpu.VMEM(low.shape, BF),
            pltpu.VMEM(high.shape, BF),
            pltpu.VMEM(piece, BF),
            pltpu.VMEM((others,) + piece, BF),
            pltpu.VMEM((part, self.width), BF),
            DMA((nf + 3,)),
            DMA(()),
            DMA(()),
            DMA((others,)),
            DMA((others,)),
            DMA(()),
        ]

    @property
    def total(self):
        return self.r_sems[6]

    def loads(self):
        nf = self.place.sizes.nf
        if self.source is None:
            grads, low, high = self.r_ins
        else:
            grads = self.main.grads[self.source.name]
            low, high = self.source.r_outs
        g_low, g_high, r_low, r_high = self.r_sems[:4]
        sem = self.r_sems[7]
        out = [
            pltpu.make_async_copy(grads.at[pl.ds(0, self.half)], g_low, sem.at[nf]),
            pltpu.make_async_copy(low, r_low, sem.at[nf + 1]),
            pltpu.make_async_copy(high, r_high, sem.at[nf + 2]),
        ]
        for df in range(nf):
            rows = pl.ds(df * self.part + self.half, self.half)
            out.append(pltpu.make_async_copy(grads.at[rows, pl.ds(0, self.width)], g_high.at[df], sem.at[df]))
        return out

    def copies(self):
        place, nf, width = self.place, self.place.sizes.nf, self.width
        g_low, g_high, _, _, low, high = self.r_sems[:6]
        ys, yr, xs, xr = self.r_sems[8:12]
        out = [push(g_low.at[:, pl.ds(width, width)], low, ys, yr, place.twin())]
        for step in range(1, nf):
            at = step - 1
            out.append(push(g_high.at[step], high.at[at], xs.at[at], xr.at[at], place.across(step)))
        return out

    def store(self):
        return pltpu.make_async_copy(self.total, self.r_outs[0], self.r_sems[12])

    def at(self, moment):
        nf, width, half = self.place.sizes.nf, self.width, self.half
        g_low, g_high, r_low, r_high, low, high, total = self.r_sems[:7]
        if moment == self.steps[0]:
            if self.source is not None:
                self.source.wait_recv()
            for copy in self.loads():
                copy.start()
        if moment == self.steps[1]:
            for copy in self.loads():
                copy.wait()
            lanes = slice(width, 2 * width)

            def first(rows):
                value = g_low[rows, lanes].astype(F32)
                for at in range(nf - 1):
                    value = value + r_low[at, rows, lanes].astype(F32)
                g_low[rows, lanes] = value.astype(BF)
                for df in range(1, nf):
                    g_high[df, rows] = (g_high[df, rows].astype(F32) + r_high[df, rows].astype(F32)).astype(BF)

            by_rows(half, 32, first)
            for copy in self.copies():
                copy.start()
        if moment == self.steps[2]:
            for copy in self.copies():
                copy.wait_recv()
            lanes = slice(0, width)

            def second(rows):
                value = g_low[rows, lanes].astype(F32) + low[rows].astype(F32)
                for at in range(nf - 1):
                    value = value + r_low[at, rows, lanes].astype(F32)
                total[rows] = value.astype(BF)

            def third(rows):
                value = g_high[0, rows].astype(F32) + r_high[0, rows].astype(F32)
                for at in range(nf - 1):
                    value = value + high[at, rows].astype(F32)
                total[pl.ds(pl.multiple_of(rows.start + half, 32), 32)] = value.astype(BF)

            by_rows(half, 32, second)
            by_rows(half, 32, third)
            self.store().start()
        if moment == "end":
            for copy in self.copies():
                copy.wait_send()
            self.store().wait()


class Share(Rider):
    def __init__(self, kinds, array, out, count, moves, when="begin"):
        self.kinds, self.moves, self.when = kinds, moves, when
        self.ins, self.outs = [array], [out]
        self.sems = [DMA((count,)), DMA((count,))]

    def copies(self):
        send, recv = self.r_sems
        out = []
        for at, (device, source, target) in enumerate(self.moves(self.place, self.r_ins[0], self.r_outs[0])):
            if device is None:
                out.append(pltpu.make_async_copy(source, target, send.at[at]))
            else:
                out.append(push(source, target, send.at[at], recv.at[at], device))
        return out

    def at(self, moment):
        if moment == self.when:
            for copy in self.copies():
                copy.start()
        if moment == "end":
            for copy in self.copies():
                copy.wait()


def share_rows(sizes, value):
    rows, width = value.shape
    part = width // sizes.nf

    def moves(place, source, out):
        triples = []
        for dt in range(sizes.nt):
            device = place.plane(0, dt) if dt else None
            for df in range(sizes.nf):
                lanes = pl.ds(pl.multiple_of(lax.rem(place.f + df, sizes.nf) * part, part), part)
                triples.append((device, source.at[:, pl.ds(df * part, part)], out.at[place.t, :, lanes]))
        return triples

    out = jax.ShapeDtypeStruct((sizes.nt, rows, width), value.dtype)
    return Share(("plane",), value, out, sizes.nt * sizes.nf, moves)


class MainRows(Share):
    def __init__(self, sizes, rows, width, when):
        share = share_rows(sizes, jax.ShapeDtypeStruct((rows, width), BF))
        super().__init__(share.kinds, None, share.outs[0], share.sems[0].shape[0], share.moves, when)
        self.ins = []

    def copies(self):
        self.r_ins = [self.main.rows_ref]
        return super().copies()


class NormSum(Rider):
    kinds = ("ctx", "plane")

    def __init__(self, sizes, lines, places, piece, steps):
        self.ins, self.places, self.piece, self.steps = [lines], places, piece, steps
        count = lines.shape[0]
        self.outs = [jax.ShapeDtypeStruct((count, piece), F32)]
        self.around = [(df, dt) for df in range(sizes.nf) for dt in range(sizes.nt)][1:]
        block = (sizes.nf, count, piece)
        self.sems = [
            pltpu.VMEM(lines.shape, F32),
            pltpu.VMEM((sizes.nc,) + block, F32),
            pltpu.VMEM(block, F32),
            pltpu.VMEM((len(self.around), count, piece), F32),
            pltpu.VMEM((count, piece), F32),
            DMA(()),
            DMA((sizes.nc,)),
            DMA((sizes.nc,)),
            DMA((len(self.around),)),
            DMA((len(self.around),)),
            pltpu.VMEM((sizes.nc,) + block, F32),
        ]

    def rounds(self):
        place = self.place
        _, _, sums, _, _, _, _, _, send, recv, _ = self.r_sems
        return [
            push(sums.at[df], self.r_sems[3].at[at], send.at[at], recv.at[at], place.plane(df, dt))
            for at, (df, dt) in enumerate(self.around)
        ]

    def whole(self, step):
        box = self.r_sems[1].at[step]
        return push(box, box, self.r_sems[6].at[step], self.r_sems[7].at[step], self.place.ahead(step))

    def at(self, moment):
        place, sizes = self.place, self.place.sizes
        lines, first, sums, second, result, load, send, recv = self.r_sems[:8]

        def keep():
            return pltpu.make_async_copy(self.r_ins[0], lines, load)

        if moment == "begin":
            keep().start()
        if moment == self.steps[0]:
            keep().wait()
            for at, line in enumerate(self.places):
                lines[line : line + 1] = self.main.norm_ref[at : at + 1]
            blocks = self.r_sems[10]
            for dest in range(sizes.nc):
                for df in range(sizes.nf):
                    lane = (df * sizes.nc + dest) * self.piece
                    blocks[dest, df] = lines[:, lane : lane + self.piece]
            for step in range(1, sizes.nc):
                push(
                    blocks.at[lax.rem(place.c + step, sizes.nc)],
                    first.at[step],
                    send.at[step],
                    recv.at[step],
                    place.ahead(step),
                ).start()
            first[0] = blocks[place.c]
        if moment == self.steps[1]:
            for step in range(1, sizes.nc):
                self.whole(step).wait_recv()
            sums[...] = sum(first[step] for step in range(sizes.nc))
            for copy in self.rounds():
                copy.start()
        if moment == "end":
            for copy in self.rounds():
                copy.wait()
            for step in range(1, sizes.nc):
                self.whole(step).wait_send()
            result[...] = sums[0] + sum(second[at] for at in range(len(self.around)))
            out = pltpu.make_async_copy(result, self.r_outs[0], load)
            out.start()
            out.wait()


class BiasSum(Rider):
    kinds = ("ctx", "plane")

    def __init__(self, sizes, value, own, steps):
        self.ins, self.own, self.steps = [value], own, steps
        ns, count, width = value.shape
        self.width = width
        self.outs = [jax.ShapeDtypeStruct((sizes.nc, count, width), F32)]
        self.around = [(df, ds) for df in range(sizes.nf) for ds in range(ns)][1:]
        self.sems = [
            pltpu.VMEM(value.shape, F32),
            pltpu.VMEM((len(self.around), count, width), F32),
            pltpu.VMEM((count, width), F32),
            DMA(()),
            DMA((len(self.around),)),
            DMA((len(self.around),)),
            DMA((sizes.nc,)),
            DMA((sizes.nc,)),
        ]

    def rounds(self):
        lines, first, _, _, send, recv = self.r_sems[:6]
        nk = self.place.sizes.nk
        return [
            push(lines.at[ds], first.at[at], send.at[at], recv.at[at], self.place.plane(df, ds * nk))
            for at, (df, ds) in enumerate(self.around)
        ]

    def spreads(self):
        place, nc = self.place, self.place.sizes.nc
        sums, target = self.r_sems[2], self.r_outs[0].at[self.place.c]
        send, recv = self.r_sems[6:]
        return [push(sums, target, send.at[step], recv.at[step], place.ahead(step)) for step in range(1, nc)]

    def at(self, moment):
        lines, first, sums, load = self.r_sems[:4]

        def keep():
            return pltpu.make_async_copy(self.r_ins[0], lines, load)

        def mine():
            return pltpu.make_async_copy(sums, self.r_outs[0].at[self.place.c], load)

        if moment == "begin":
            keep().start()
        if moment == self.steps[0]:
            keep().wait()
            for ds in range(self.place.sizes.ns):
                for line in range(self.own):
                    at = (ds * self.own + line) * self.width
                    lines[ds, line : line + 1] = self.main.bias_ref[:, at : at + self.width]
            for copy in self.rounds():
                copy.start()
        if moment == self.steps[1]:
            for copy in self.rounds():
                copy.wait()
            sums[...] = lines[0] + sum(first[at] for at in range(len(self.around)))
            for copy in self.spreads() + [mine()]:
                copy.start()
        if moment == "end":
            for copy in self.spreads() + [mine()]:
                copy.wait()


class Moved:
    def __init__(self, hbm, scratch, inward):
        count = len(hbm)
        self.vmem = scratch[:count]
        self.copies = []
        for ref, buffer, sem in zip(hbm, scratch[:count], scratch[count:]):
            ends = (ref, buffer) if inward else (buffer, ref)
            self.copies.append(pltpu.make_async_copy(*ends, sem))

    @staticmethod
    def scratch(arrays):
        return [pltpu.VMEM(a.shape, a.dtype) for a in arrays] + [DMA(()) for _ in arrays]

    def start(self):
        for copy in self.copies:
            copy.start()


class Main:
    kinds = ("mate", "line")
    big, small, results, kept, gathered, work = [], [], [], [], [], []

    def __init__(self, **arrays):
        self.grads = {}

    @property
    def ins(self):
        return list(self.big) + list(self.small)

    @property
    def in_specs(self):
        return [ANY_SPEC] * len(self.big) + [VMEM_SPEC] * len(self.small)

    @property
    def outs(self):
        return list(self.results) + list(self.kept) + list(self.gathered)

    @property
    def out_specs(self):
        return [VMEM_SPEC] * len(self.results) + [ANY_SPEC] * (len(self.kept) + len(self.gathered))

    def scratch(self, sizes):
        self.layout = [
            Moved.scratch(self.big),
            Moved.scratch(self.kept),
            [pltpu.VMEM(a.shape, a.dtype) for a in self.work],
            scatter_scratch(sizes, self.rows, self.width),
        ] + [Gather.scratch(sizes) for _ in self.gathered]
        return [one for group in self.layout for one in group]

    def run(self, place, ins, outs, scratch, moment):
        cuts, at = [], 0
        for group in self.layout:
            cuts.append(scratch[at : at + len(group)])
            at += len(group)
        count = len(self.big)
        self.loads = Moved(ins[:count], cuts[0], True)
        results, kept = outs[: len(self.results)], outs[len(self.results) : len(self.results) + len(self.kept)]
        gathered = outs[len(self.results) + len(self.kept) :]
        self.stores = Moved(kept, cuts[1], False)
        self.work_refs, self.bufs, self.gather_sems = cuts[2], cuts[3], cuts[4:]
        self.loads.start()
        moment("begin")
        self.compute(place, self.loads.vmem, ins[count:], results, self.stores.vmem, gathered, moment)
        self.sent()
        for copy in self.stores.copies:
            copy.wait()

    def fetch(self, *which):
        for at in which:
            self.loads.copies[at].wait()

    def store(self, *which):
        for at in which:
            self.stores.copies[at].start()

    def spread(self, place, gathers, moment):
        for gather in gathers:
            gather.begin()
        moment("summed")
        for step in range(1, place.sizes.nc):
            for gather in gathers:
                gather.forward(step)
            if step == 1:
                moment("spread")
        moment("late")
        for gather in gathers:
            gather.end()


def by_rows(count, block, step):
    def one(at, carry):
        step(pl.ds(pl.multiple_of(at * block, block), block))
        return carry

    lax.fori_loop(0, count // block, one, 0)


def unit_rows_of(values):
    row_mean = jnp.mean(values, -1, keepdims=True)
    centred = values - row_mean
    row_var = jnp.mean(centred * centred, -1, keepdims=True)
    inverse = lax.rsqrt(row_var + EPS)
    return centred * inverse, inverse


def norm_back(grad_rows, saved_rows, gain_row):
    unit_rows, inverse = unit_rows_of(saved_rows)
    scaled = grad_rows * gain_row
    inner = inverse * (
        scaled
        - jnp.mean(scaled, -1, keepdims=True)
        - unit_rows * jnp.mean(scaled * unit_rows, -1, keepdims=True)
    )
    return inner, jnp.sum(grad_rows * unit_rows, 0, keepdims=True), jnp.sum(grad_rows, 0, keepdims=True)


def norm_forward(new_rows, norm_ref, at):
    unit_rows, _ = unit_rows_of(new_rows)
    return (unit_rows * norm_ref[at : at + 1] + norm_ref[at + 1 : at + 2]).astype(BF)


def swap_lanes(values):
    lane = lax.broadcasted_iota(jnp.int32, values.shape, 1) % HD
    width = values.shape[1]
    up = pltpu.roll(values, width - ROT // 2, 1)
    down = pltpu.roll(values, ROT // 2, 1)
    return jnp.where(lane < ROT // 2, up, jnp.where(lane < ROT, down, 0.0))


def allowed_of(label_col, label_row):
    length = label_col.shape[0]
    row = lax.broadcasted_iota(jnp.int32, (length, length), 0)
    col = lax.broadcasted_iota(jnp.int32, (length, length), 1)
    return (label_col == label_row) & (row >= col)


def like(shape, dtype):
    return jax.ShapeDtypeStruct(shape, dtype)


ROW_BLOCK = 128
OUT_BLOCK = 256


class AttnForward(Main):
    def __init__(self, full, w_qkv, w_out, bias, tables, stream, norm):
        super().__init__()
        self.rows, self.width = stream.shape
        length = full.shape[0]
        self.big = [full, w_qkv, w_out]
        self.small, self.norm_at = [bias[0], *tables, stream, norm[0]], norm[1]
        self.bias_at = bias[1]
        heads = w_out.shape[1] // HD
        self.results = [like(stream.shape, F32), like((length, heads), F32)]
        mixed = like((length, w_out.shape[1]), BF)
        self.kept = [like((length, w_qkv.shape[1]), BF), mixed, mixed, mixed]
        self.gathered = [like(full.shape, BF)]
        self.work = [like(full.shape, BF), like(stream.shape, BF)]

    def compute(self, place, big, small, results, kept, gathered, moment):
        full, w_qkv, w_out = big
        bias_ref, col_ref, row_ref, cos_ref, sin_ref, stream_ref, norm_ref = small
        new_ref, lse_ref = results
        proj_ref, mix_ref, q_ref, k_ref = kept
        part_ref, low_ref = self.work_refs
        length = full.shape[0]
        ns = place.sizes.ns
        width = w_out.shape[1] // ns
        self.fetch(0, 1)

        def project(rows):
            proj_ref[rows] = (dot_nn(full[rows], w_qkv[...]) + bias_ref[self.bias_at : self.bias_at + 1]).astype(BF)

        by_rows(length, ROW_BLOCK, project)
        self.store(0)
        allowed = allowed_of(col_ref[...], row_ref[...])
        cosine, sine = cos_ref[...], sin_ref[...]
        scaling = HD ** (-0.5)
        for b in range(ns):
            base, own = 3 * width * b, slice(b * width, (b + 1) * width)
            for ref, at in ((q_ref, 0), (k_ref, 1)):
                values = proj_ref[:, base + at * width : base + (at + 1) * width].astype(F32)
                ref[:, own] = (values * cosine + swap_lanes(values) * sine).astype(BF)
            for h in range(width // HD):
                span = slice(b * width + h * HD, b * width + (h + 1) * HD)
                scores = scaling * dot_nt(q_ref[:, span], k_ref[:, span])
                scores = jnp.where(allowed, scores, NEGATIVE)
                peak = jnp.max(scores, -1, keepdims=True)
                exponent = jnp.exp(scores - peak)
                total = jnp.sum(exponent, -1, keepdims=True)
                probs = (exponent * (1.0 / total)).astype(BF)
                at = base + 2 * width + h * HD
                mix_ref[:, span] = dot_nn(probs, proj_ref[:, at : at + HD]).astype(BF)
                at = b * (width // HD) + h
                lse_ref[:, at : at + 1] = peak + jnp.log(total)
        self.store(1, 2, 3)
        self.fetch(2)
        for at in range(0, self.width, OUT_BLOCK):
            part_ref[:, at : at + OUT_BLOCK] = dot_nt(mix_ref[...], w_out[at : at + OUT_BLOCK]).astype(BF)
        moment("ready")
        total, self.sent = scatter_part(place, part_ref, self.bufs, self.rows, moment)
        new_rows = stream_ref[...] + total
        new_ref[...] = new_rows
        low_ref[...] = norm_forward(new_rows, norm_ref, self.norm_at)
        self.spread(place, [Gather(place, low_ref, gathered[0], self.gather_sems[0], self.rows)], moment)


class FfnForward(Main):
    def __init__(self, full, w_gate, w_up, w_down, stream, norm, cotangent=None):
        super().__init__()
        self.rows, self.width = stream.shape
        length = full.shape[0]
        self.last = cotangent is not None
        self.big = [full, w_gate, w_up, w_down]
        self.small = [stream, cotangent if self.last else norm[0]]
        self.norm_at = norm and norm[1]
        self.results = [like(stream.shape, F32)]
        hidden = (length, w_gate.shape[1])
        self.kept = [like(hidden, F32), like(hidden, F32), like(hidden, BF)]
        self.gathered = [like(full.shape, BF)]
        self.work = [like(full.shape, BF), like(stream.shape, BF)]

    def compute(self, place, big, small, results, kept, gathered, moment):
        full, w_gate, w_up, w_down = big
        stream_ref = small[0]
        gate_ref, up_ref, act_ref = kept
        part_ref, low_ref = self.work_refs
        gather = None
        if self.last:
            gather = Gather(place, small[1], gathered[0], self.gather_sems[0], self.rows)
            gather.begin()
        self.fetch(0, 1, 2)

        def gates(rows):
            gate = dot_nn(full[rows], w_gate[...])
            up = dot_nn(full[rows], w_up[...])
            gate_ref[rows] = gate
            up_ref[rows] = up
            act_ref[rows] = (gate * jax.nn.sigmoid(gate) * up).astype(BF)

        by_rows(full.shape[0], ROW_BLOCK, gates)
        self.store(0, 1, 2)
        self.fetch(3)
        for at in range(0, self.width, OUT_BLOCK):
            part_ref[:, at : at + OUT_BLOCK] = dot_nt(act_ref[...], w_down[at : at + OUT_BLOCK]).astype(BF)
        moment("ready")
        total, self.sent = scatter_part(place, part_ref, self.bufs, self.rows, moment)
        new_rows = stream_ref[...] + total
        results[0][...] = new_rows
        if self.last:
            moment("summed")
            for step in range(1, place.sizes.nc):
                gather.forward(step)
            moment("spread")
            moment("late")
            gather.end()
            return
        low_ref[...] = norm_forward(new_rows, small[1], self.norm_at)
        self.spread(place, [Gather(place, low_ref, gathered[0], self.gather_sems[0], self.rows)], moment)


class FfnBack(Main):
    names = ["down", "gate", "up"]

    def __init__(self, grad_full, w_gate, w_up, w_down, gates, ups, acts, full, grad, saved, norm):
        super().__init__()
        self.rows, self.width = grad.shape
        self.big = [grad_full, acts, w_down, gates, ups, w_gate, w_up, full]
        self.small, self.norm_at = [grad, saved, norm[0]], norm[1]
        self.results = [like(grad.shape, F32), like((2, self.width), F32)]
        self.kept = [like(w_down.shape, BF), like(w_gate.shape, BF), like(w_up.shape, BF)]
        self.gathered = [like(full.shape, BF)]
        hidden = like(acts.shape, BF)
        self.work = [hidden, hidden, like(full.shape, BF), like(grad.shape, BF)]

    def compute(self, place, big, small, results, kept, gathered, moment):
        grad_full, act_ref, w_down, gate_ref, up_ref, w_gate, w_up, full = big
        grad_ref, saved_ref, norms_ref = small
        new_ref, norm_ref = results
        down_grad, gate_grad, up_grad = kept
        low_gate, low_up, part_ref, grad_low_ref = self.work_refs
        self.grads = {"down": down_grad, "gate": gate_grad, "up": up_grad}

        def weights_of(which, target, left, right, name):
            for at in range(0, self.width, OUT_BLOCK):
                span = slice(at, at + OUT_BLOCK)
                target[span] = dot_tn(left[:, span], right[...]).astype(BF)
            self.store(which)
            moment(name)

        self.fetch(0, 1)
        weights_of(0, down_grad, grad_full, act_ref, "downs")
        self.fetch(2, 3, 4)

        def gates(rows):
            act_grad = dot_nn(grad_full[rows], w_down[...])
            gate, up = gate_ref[rows], up_ref[rows]
            sg = jax.nn.sigmoid(gate)
            low_gate[rows] = (act_grad * up * sg * (1.0 + gate * (1.0 - sg))).astype(BF)
            low_up[rows] = (act_grad * gate * sg).astype(BF)

        by_rows(full.shape[0], ROW_BLOCK, gates)
        self.fetch(5, 6)
        for at in range(0, self.width, OUT_BLOCK):
            span = slice(at, at + OUT_BLOCK)
            part_ref[:, span] = (dot_nt(low_gate[...], w_gate[span]) + dot_nt(low_up[...], w_up[span])).astype(BF)
        moment("ready")
        self.fetch(7)

        def weights(name):
            if name == "sent":
                weights_of(1, gate_grad, full, low_gate, "gates")
                weights_of(2, up_grad, full, low_up, "ups")
            moment(name)

        total, self.sent = scatter_part(place, part_ref, self.bufs, self.rows, weights)
        inner, gain_grad, shift_grad = norm_back(total, saved_ref[...], norms_ref[self.norm_at : self.norm_at + 1])
        new_rows = grad_ref[...] + inner
        new_ref[...] = new_rows
        grad_low_ref[...] = new_rows.astype(BF)
        norm_ref[0:1] = gain_grad
        norm_ref[1:2] = shift_grad
        self.spread(place, [Gather(place, grad_low_ref, gathered[0], self.gather_sems[0], self.rows)], moment)


class AttnBack(Main):
    names = ["qkv", "out"]

    def __init__(self, grad_full, w_qkv, w_out, kept, full, tables, lse, grad, saved, norm, last):
        super().__init__()
        proj, mixed, q_rot, k_rot = kept
        self.rows, self.width = grad.shape
        self.last = last
        self.big = [grad_full, w_out, q_rot, k_rot, proj, w_qkv, full, mixed]
        self.small, self.norm_at = [*tables, lse, grad, saved, norm[0]], norm[1]
        self.results = [like(grad.shape, F32), like((2, self.width), F32), like((1, w_qkv.shape[1]), F32)]
        self.kept = [like(w_qkv.shape, BF), like(w_out.shape, BF)]
        self.gathered = [] if last else [like(full.shape, BF)]
        self.work = [like(proj.shape, BF), like(full.shape, BF), like(grad.shape, BF), like(mixed.shape, BF)]

    def compute(self, place, big, small, results, kept, gathered, moment):
        grad_full, w_out, q_ref, k_ref, proj_ref, w_qkv, full, mix_ref = big
        col_ref, row_ref, cos_ref, sin_ref, lse_ref, grad_ref, saved_ref, norms_ref = small
        new_ref, norm_ref, bias_ref = results
        qkv_ref, out_ref = kept
        self.norm_ref, self.bias_ref, self.rows_ref = norm_ref, bias_ref, self.work_refs[2]
        low_ref, part_ref, grad_low_ref, mix_grad_ref = self.work_refs
        ns = place.sizes.ns
        width = w_out.shape[1] // ns
        self.grads = {"qkv": qkv_ref, "out": out_ref}
        self.fetch(0, 1)

        def mixed_grad(rows):
            mix_grad_ref[rows] = dot_nn(grad_full[rows], w_out[...]).astype(BF)

        by_rows(full.shape[0], ROW_BLOCK, mixed_grad)
        self.fetch(2, 3, 4)
        allowed = allowed_of(col_ref[...], row_ref[...])
        cosine, sine = cos_ref[...], sin_ref[...]
        scaling = HD ** (-0.5)
        for b in range(ns):
            parts = [[], [], []]
            base = 3 * width * b
            for h in range(width // HD):
                span = slice(b * width + h * HD, b * width + (h + 1) * HD)
                at = b * (width // HD) + h
                q_rows, k_rows, out_grad = q_ref[:, span], k_ref[:, span], mix_grad_ref[:, span]
                scores = jnp.where(allowed, scaling * dot_nt(q_rows, k_rows), NEGATIVE)
                probs = jnp.exp(scores - lse_ref[:, at : at + 1])
                first = base + 2 * width + h * HD
                prob_grad = dot_nt(out_grad, proj_ref[:, first : first + HD])
                inner = jnp.sum(probs * prob_grad, -1, keepdims=True)
                score_low = (probs * (prob_grad - inner)).astype(BF)
                parts[0].append(scaling * dot_nn(score_low, k_rows))
                parts[1].append(scaling * dot_tn(score_low, q_rows))
                parts[2].append(dot_tn(probs.astype(BF), out_grad))
            for at in range(3):
                values = jnp.concatenate(parts[at], axis=1)
                if at < 2:
                    values = values * cosine - swap_lanes(values) * sine
                low = values.astype(BF)
                lanes = slice(base + at * width, base + (at + 1) * width)
                low_ref[:, lanes] = low
                bias_ref[:, lanes] = jnp.sum(low.astype(F32), 0, keepdims=True)
        self.fetch(5)
        for at in range(0, self.width, OUT_BLOCK):
            part_ref[:, at : at + OUT_BLOCK] = dot_nt(low_ref[...], w_qkv[at : at + OUT_BLOCK]).astype(BF)
        moment("ready")
        self.fetch(6, 7)

        def weights(name):
            if name == "sent":
                for at in range(0, self.width, OUT_BLOCK):
                    span = slice(at, at + OUT_BLOCK)
                    qkv_ref[span] = dot_tn(full[:, span], low_ref[...]).astype(BF)
                    out_ref[span] = dot_tn(grad_full[:, span], mix_ref[...]).astype(BF)
                self.store(0, 1)
                moment("attns")
            moment(name)

        total, self.sent = scatter_part(place, part_ref, self.bufs, self.rows, weights)
        inner, gain_grad, shift_grad = norm_back(total, saved_ref[...], norms_ref[self.norm_at : self.norm_at + 1])
        new_rows = grad_ref[...] + inner
        new_ref[...] = new_rows
        norm_ref[0:1] = gain_grad
        norm_ref[1:2] = shift_grad
        grad_low_ref[...] = new_rows.astype(BF)
        if self.last:
            for name in ("summed", "spread", "late"):
                moment(name)
            return
        self.spread(place, [Gather(place, grad_low_ref, gathered[0], self.gather_sems[0], self.rows)], moment)


class Alone:
    kinds, ins, in_specs, outs, out_specs = (), [], [], [], []

    def scratch(self, sizes):
        return []

    def run(self, place, ins, outs, scratch, moment):
        moment("begin")


class Start:
    kinds = ("mate", "ctx", "fsdp", "twin")

    def __init__(self, sizes, small, hidden, cotangent, piece, q_sub, layers, chains, following):
        self.sizes, self.piece, self.chains, self.following = sizes, piece, chains, following
        self.q_sub, self.layers = q_sub, layers
        lines, lanes = small.shape
        count, self.width = hidden.shape
        self.rows = count // (sizes.ns * sizes.nk)
        group = sizes.nc * sizes.nk * self.rows
        self.ins, self.in_specs = [small, hidden, cotangent], [VMEM_SPEC] * 3
        self.outs = [
            like((sizes.nf, sizes.nc * lines, lanes), F32),
            like((lines, lanes), F32),
            like((lines, self.width), F32),
            like((self.rows, self.width), F32),
            like((self.rows, self.width), BF),
            like((group, 1), jnp.int32),
            like((1, group), jnp.int32),
            like((group, q_sub), F32),
            like((group, q_sub), F32),
            like((layers, sizes.ns * 3 * q_sub), F32),
            like((group, self.width), BF),
        ]
        self.out_specs = [VMEM_SPEC] * 10 + [ANY_SPEC]

    def scratch(self, sizes):
        others = max(sizes.nf - 1, 1)
        small = [DMA((sizes.nc,)), DMA((sizes.nc,)), DMA((others,)), DMA((others,)), DMA(()), DMA(())]
        return small + [pltpu.VMEM((self.rows, self.width), BF)] + Gather.scratch(sizes)

    def run(self, place, ins, outs, scratch, moment):
        sizes, rows, width = self.sizes, self.rows, self.width
        small_ref, hidden_ref, cotangent_ref = ins
        all_ref, twin_ref, norm_ref, stream_ref, grad_ref = outs[:5]
        full_ref = outs[10]
        cs, cr, fs, fr, ts, tr = scratch[:6]
        low_ref = scratch[6]
        lines = small_ref.shape[0]

        def line_of(c):
            return pl.ds(pl.multiple_of(c * lines, lines), lines)

        to_context = [
            push(small_ref, all_ref.at[0, line_of(place.c)], cs.at[step], cr.at[step], place.ahead(step))
            for step in range(1, sizes.nc)
        ]
        to_twin = push(small_ref, twin_ref, ts, tr, place.twin())
        moment("begin")
        for copy in to_context + [to_twin]:
            copy.start()
        for exchange, _ in self.chains:
            exchange.start()
        all_ref[0, line_of(place.c)] = small_ref[...]
        own_rows = pl.ds(pl.multiple_of((place.s * sizes.nk + place.k) * rows, rows), rows)
        part = width // sizes.nf
        for df in range(sizes.nf):
            lanes = pl.ds(pl.multiple_of(lax.rem(place.f + df, sizes.nf) * part, part), part)
            stream_ref[:, df * part : (df + 1) * part] = hidden_ref[own_rows, lanes].astype(F32)
            grad_ref[:, df * part : (df + 1) * part] = cotangent_ref[own_rows, lanes]
        unit_rows, _ = unit_rows_of(stream_ref[...])
        for copy in to_context:
            copy.wait()
        to_across = [
            push(all_ref.at[0], all_ref.at[sizes.nf - step], fs.at[step - 1], fr.at[step - 1], place.across(step))
            for step in range(1, sizes.nf)
        ]
        for copy in to_across:
            copy.start()
        for copy in to_across + [to_twin]:
            copy.wait()
        for df in range(sizes.nf):
            for c in range(sizes.nc):
                at = (df * sizes.nc + c) * self.piece
                norm_ref[:, at : at + self.piece] = all_ref[df, c * lines : (c + 1) * lines, : self.piece]
        low_ref[...] = (unit_rows * norm_ref[0:1] + norm_ref[1:2]).astype(BF)
        gather = Gather(place, low_ref, full_ref, scratch[7:12], rows)
        for exchange, spread in self.chains:
            exchange.wait_own()
            spread.first(place.c)
        for step in range(1, sizes.nc):
            for exchange, spread in self.chains:
                exchange.wait_from(step)
                spread.first(lax.rem(place.c + sizes.nc - step, sizes.nc))
        gather.begin()
        for exchange in self.following:
            exchange.start()
        self.tables(place, small_ref, all_ref, twin_ref, *outs[5:10])
        for step in range(sizes.nc):
            for _, chain in self.chains:
                chain.second(lax.rem(place.c + sizes.nc - step, sizes.nc))
            if step:
                gather.forward(step)
        gather.end()
        for exchange, spread in self.chains:
            exchange.wait_sent()
            for block in range(sizes.nc):
                spread.finish(block)
        for exchange in self.following:
            exchange.finish()


    def tables(self, place, small_ref, all_ref, twin_ref, col_ref, row_ref, cos_ref, sin_ref, bias_ref):
        sizes, q_sub = self.sizes, self.q_sub
        lines = small_ref.shape[0]
        shard = sizes.nk * self.rows
        for c in range(sizes.nc):
            mine = jnp.zeros((1, shard), F32)
            for at in range(sizes.ns):
                line = c * lines + at
                found = all_ref[0, line : line + 1, self.piece : self.piece + shard]
                mine = jnp.where(place.s == at, found, mine)
            row_ref[:, c * shard : (c + 1) * shard] = mine.astype(jnp.int32)
        length = row_ref.shape[1]
        row = row_ref[...].astype(F32)
        at_row = lax.broadcasted_iota(jnp.int32, (length, length), 0)
        at_col = lax.broadcasted_iota(jnp.int32, (length, length), 1)
        col = jnp.sum(jnp.where(at_row == at_col, row, 0.0), -1, keepdims=True)
        col_ref[...] = col.astype(jnp.int32)
        before = jnp.sum(jnp.where(row < col, 1.0, 0.0), -1, keepdims=True)
        places = lax.broadcasted_iota(jnp.int32, (length, 1), 0).astype(F32)
        lane = lax.broadcasted_iota(jnp.int32, (1, q_sub), 1) % HD
        turn = jnp.exp((lane % (ROT // 2)).astype(F32) * (-2.0 * math.log(ROPE_BASE) / ROT))
        angles = (places - before) * jnp.where(lane < ROT, turn, 0.0)
        sine = jnp.sin(angles)
        cos_ref[...] = jnp.cos(angles)
        sin_ref[...] = jnp.where(lane < ROT // 2, -sine, sine)
        for layer in range(self.layers):
            for ds, source in enumerate((small_ref, twin_ref)):
                for at in range(3):
                    line = 3 * layer + at
                    lanes = slice((ds * 3 + at) * q_sub, (ds * 3 + at + 1) * q_sub)
                    bias_ref[layer : layer + 1, lanes] = source[line : line + 1, self.piece + shard :]


class Guest(Rider):
    def __init__(self, rider):
        self.kinds, self.ins, self.outs, self.sems = rider.kinds, rider.ins, rider.outs, rider.sems
        self.rider = rider

    def bind(self, *refs):
        self.rider.bind(*refs)


def comm_kernel(sizes, main, riders, kinds, layout, *refs):
    cuts, at = [], 0
    for size in layout:
        cuts.append(refs[at : at + size])
        at += size
    count = len(riders)
    ins, outs, scratch = cuts[: count + 1], cuts[count + 1 : 2 * count + 2], cuts[2 * count + 2 :]
    place = Place(sizes)
    for i, rider in enumerate(riders):
        rider.bind(place, ins[i + 1], outs[i + 1], scratch[i + 1], main)
    count = greet(place, kinds)

    def moment(name):
        if name == "begin":
            pl.semaphore_wait(pltpu.get_barrier_semaphore(), count)
        for rider in riders:
            rider.at(name)

    main.run(place, ins[0], outs[0], scratch[0], moment)
    moment("end")


def comm_call(sizes, collective_id, main, riders=(), micros=50):
    kinds = set(main.kinds)
    for rider in riders:
        kinds |= set(rider.kinds)
    main_scratch = main.scratch(sizes)
    operands, in_specs = list(main.ins), list(main.in_specs)
    outs, out_specs = list(main.outs), list(main.out_specs)
    scratch = list(main_scratch)
    aliases = {}
    for rider in riders:
        if rider.aliased:
            aliases[len(operands)] = len(outs)
        operands += rider.ins
        in_specs += [ANY_SPEC] * len(rider.ins)
        outs += rider.outs
        out_specs += [ANY_SPEC] * len(rider.outs)
        scratch += rider.sems
    layout = [len(main.ins)] + [len(rider.ins) for rider in riders]
    layout += [len(main.outs)] + [len(rider.outs) for rider in riders]
    layout += [len(main_scratch)] + [len(rider.sems) for rider in riders]
    results = pl.pallas_call(
        functools.partial(comm_kernel, sizes, main, riders, kinds, layout),
        out_shape=outs,
        in_specs=in_specs,
        out_specs=out_specs,
        scratch_shapes=scratch,
        input_output_aliases=aliases,
        compiler_params=pltpu.CompilerParams(
            collective_id=collective_id, has_side_effects=True, vmem_limit_bytes=VMEM_BYTES
        ),
        cost_estimate=pl.CostEstimate(flops=0, bytes_accessed=micros * 3 * MIB, transcendentals=0),
    )(*operands)
    groups, at = [], 0
    for size in [len(main.outs)] + [len(rider.outs) for rider in riders]:
        groups.append(list(results[at : at + size]))
        at += size
    return groups[0], groups[1:]


def finish_kernel(count, hidden, *refs):
    ins, (qkv_out, out_out, gate_up_out, down_out) = refs[: 5 * count], refs[5 * count :]
    triple, rows, q_cols = qkv_out.shape[1:]
    for layer in range(count):

        @pl.when(pl.program_id(0) == layer)
        def _():
            qkv, out, gate, up, down = ins[5 * layer : 5 * layer + 5]

            def some(span):
                for at in range(triple):
                    qkv_out[0, at, span] = qkv[span, at * q_cols : (at + 1) * q_cols].astype(F32)
                out_out[0, span] = out[span].astype(F32)
                gate_up_out[0, span, 0] = gate[span, :hidden].astype(F32)
                gate_up_out[0, span, 1] = up[span, :hidden].astype(F32)
                down_out[0, span] = down[span, :hidden].astype(F32)

            by_rows(rows, 64, some)


def finish(grads, q_cols, hidden):
    count = len(grads)
    rows = grads[0][0].shape[0]
    shapes = [(3, rows, q_cols), (rows, q_cols), (rows, 2, hidden), (rows, hidden)]

    def block(shape):
        return pl.BlockSpec((1,) + shape, lambda layer: (layer,) + (0,) * len(shape))

    return pl.pallas_call(
        functools.partial(finish_kernel, count, hidden),
        grid=(count,),
        out_shape=[jax.ShapeDtypeStruct((count,) + shape, F32) for shape in shapes],
        in_specs=[VMEM_SPEC] * (5 * count),
        out_specs=[block(shape) for shape in shapes],
        compiler_params=pltpu.CompilerParams(vmem_limit_bytes=VMEM_BYTES),
    )(*[one for layer in grads for one in layer])


def body(
    mesh,
    hidden_in,
    segment_ids,
    norm_gains,
    norm_shifts,
    qkv_weight,
    qkv_bias,
    out_weight,
    gate_up_weight,
    down_weight,
    cotangent,
):
    ns, shard_rows, width = hidden_in.shape
    sizes = Sizes(mesh, ns)
    nf, nc, nk, nt = sizes.nf, sizes.nc, sizes.nk, sizes.nt
    f, c, t = lax.axis_index("fsdp"), lax.axis_index("context"), lax.axis_index("tensor")
    s = t // nk
    layers = qkv_weight.shape[0]
    rows = shard_rows // nk
    part = width // nf
    piece = part // nc
    q_cols = qkv_weight.shape[3]
    q_sub = q_cols // nc
    hidden = gate_up_weight.shape[3]
    f_sub = -(-hidden // (nc * TILE)) * TILE
    f_cols = nc * f_sub

    qkv_flat = qkv_weight.transpose(0, 2, 1, 3).reshape(layers * 3 * piece, q_cols)
    out_flat = out_weight.reshape(layers * piece, q_cols)
    fill = ((0, 0), (0, f_cols - hidden))
    down_flat = jnp.pad(down_weight.reshape(layers * piece, hidden), fill)
    gate_up_flat = jnp.pad(gate_up_weight, ((0, 0), (0, 0)) + fill).reshape(layers * piece, 2 * f_cols)

    def exchange(name, layer, when="begin", finish="end"):
        first = layer * piece
        array, corners, sub = {
            "qkv": (qkv_flat, [((3 * layer + at) * piece, 0) for at in range(3)], q_sub),
            "out": (out_flat, [(first, 0)], q_sub),
            "gate": (gate_up_flat, [(first, 0)], f_sub),
            "up": (gate_up_flat, [(first, f_cols)], f_sub),
            "down": (down_flat, [(first, 0)], f_sub),
        }[name]
        return WeightExchange(sizes, piece, array, corners, sub, when, finish)

    norms = jnp.stack([norm_gains, norm_shifts], axis=2).reshape(4 * layers, piece).astype(F32)
    own_bias = lax.dynamic_slice_in_dim(qkv_bias, c * q_sub, q_sub, 2).reshape(3 * layers, q_sub).astype(F32)
    lines = -(-max(4 * layers, 3 * layers, ns) // 8) * 8

    def lined(value):
        return jnp.pad(value, ((0, lines - value.shape[0]), (0, 0)))

    small = jnp.concatenate([lined(norms), lined(segment_ids.astype(F32)), lined(own_bias)], axis=1)
    chains = []
    for name in ("qkv", "out"):
        moved = exchange(name, 0, finish=None)
        chains.append((moved, Spread(sizes, moved, blocks=nc, steps=(None, None))))
    following = [exchange(name, 0, finish=None) for name in ("gate", "up")]
    start = Start(
        sizes,
        small,
        hidden_in.reshape(ns * shard_rows, width),
        cotangent.reshape(ns * shard_rows, width),
        piece,
        q_sub,
        layers,
        chains,
        following,
    )
    guests = [Guest(one) for chain in chains for one in chain] + [Guest(one) for one in following]
    results, extra = comm_call(sizes, 1, start, guests, 80)
    norm_rows, stream, grad_low = results[2:5]
    tables, bias_rows, full_one = results[5:9], results[9], results[10]
    w_qkv, w_out, gate_mine, up_mine = (extra[at][0] for at in (1, 3, 4, 5))

    def norm_of(layer, which):
        return (norm_rows, (layer * 2 + which) * 2)

    kept = []
    gate_own = None
    for layer in range(layers):
        more = layer + 1 < layers
        down_first = exchange("down", layer, finish=None)
        riders = [Spread(sizes, gate_mine) if gate_own is None else SpreadRelay(sizes, gate_own), Spread(sizes, up_mine)]
        riders += [down_first, Spread(sizes, down_first, steps=("inside0", "spread"))]
        if more:
            riders += [exchange("qkv", layer + 1), exchange("out", layer + 1)]
        main = AttnForward(
            full_one, w_qkv, w_out, (bias_rows, layer), tables, stream, norm_of(layer, 1)
        )
        results, extra = comm_call(sizes, 2 + 2 * layer, main, riders, 85)
        middle, lse, proj, mixed, q_rot, k_rot, full_two = results
        w_gate, w_up, w_down = extra[0][0], extra[1][0], extra[3][0]
        attn_kept = (full_one, w_qkv, w_out, (proj, mixed, q_rot, k_rot), lse, stream)
        if more:
            gate_first = exchange("gate", layer + 1, finish=None)
            riders = [Spread(sizes, extra[4][0]), Spread(sizes, extra[5][0])]
            riders += [gate_first, SpreadOwn(sizes, gate_first, blocks=nc, steps=("inside1",))]
            riders.append(exchange("up", layer + 1, "spread"))
            main = FfnForward(
                full_two, w_gate, w_up, w_down, middle, norm_of(layer + 1, 0)
            )
        else:
            riders = []
            main = FfnForward(full_two, w_gate, w_up, w_down, middle, None, grad_low)
        results, extra = comm_call(sizes, 3 + 2 * layer, main, riders, 55)
        stream, gates, ups, acts, full = results
        kept.append(attn_kept + (full_two, w_gate, w_up, w_down, gates, ups, acts, middle))
        if more:
            full_one = full
            w_qkv, w_out, _, gate_own, up_mine = (one[0] for one in extra)
        else:
            grad_full = full

    first_id = 2 + 2 * layers
    stream_out = stream
    grad = grad_low.astype(F32)
    firsts, totals = {}, {}
    done, norm_grads, bias_grads = {}, {}, {}
    calls = [0]

    def sub_of(name):
        return q_sub if name in ("qkv", "out") else f_sub

    def run(main, steps, others, micros):
        riders, after = [], []
        here = {}

        def ride(rider, what, name):
            here[(what, name)] = rider
            riders.append(rider)
            after.append((what, name))

        for what, name, layer, when in steps:
            at = (name, layer)
            if what == "first":
                ride(GradFirst(sizes, name, *main.kept[main.names.index(name)].shape, when), what, at)
            elif what == "middle":
                ride(GradMiddle(sizes, here.get(("first", at)) or firsts[at], when), what, at)
            else:
                ride(GradExchange(sizes, here.get(("middle", at)) or totals[at], sub_of(name), when), what, at)
        for name, rider in others:
            ride(rider, "other", name)
        results, extra = comm_call(sizes, first_id + calls[0], main, riders, micros)
        calls[0] += 1
        for (what, at), out in zip(after, extra):
            if what == "first":
                firsts[at] = (results[len(main.results) + main.names.index(at[0])], *out)
            elif what == "middle":
                totals[at] = out[0]
            else:
                done[at] = out[0]
        return results

    attn, ffn = ("qkv", "out"), ("gate", "up")
    for layer in range(layers - 1, -1, -1):
        full_one, w_qkv, w_out, attn_kept, lse, stream, full_two, w_gate, w_up, w_down, gates, ups, acts, middle = kept[
            layer
        ]
        main = FfnBack(grad_full, w_gate, w_up, w_down, gates, ups, acts, full_two, grad, middle, norm_of(layer, 1))
        top = layer + 1 == layers
        steps, others = [], []
        if top:
            others.append(("block_out", share_rows(sizes, stream_out.astype(BF))))
        else:
            steps += [("exchange", name, layer + 1, "begin") for name in ffn]
            steps += [("exchange", name, layer + 1, "spread") for name in attn]
        steps += [("first", "down", layer, "downs"), ("first", "gate", layer, "gates"), ("first", "up", layer, "ups")]
        steps += [("middle", "down", layer, ("summed", "summed", "late"))]
        if not top:
            steps += [("middle", name, layer, ("late", "late", "end")) for name in ffn]
        grad, norm_grads[(layer, 1)], _, _, _, middle_full = run(main, steps, others, 60)
        main = AttnBack(
            middle_full, w_qkv, w_out, attn_kept, full_one, tables, lse, grad, stream, norm_of(layer, 0), layer == 0
        )
        steps, others = [("exchange", "down", layer, "begin")], []
        if not top:
            steps += [("exchange", name, layer, "begin") for name in ffn]
        if layer == 0:
            none = jnp.zeros((2, width), F32)
            pairs = [[norm_grads.get((at, which), none) for which in range(2)] for at in range(layers)]
            lines = jnp.stack([jnp.stack(pair, 1) for pair in pairs], 1).reshape(4 * layers, width)
            none = jnp.zeros((1, ns * 3 * q_sub), F32)
            bias = jnp.concatenate([bias_grads.get(at, none) for at in range(layers)]).reshape(layers, ns, 3, q_sub)
            bias = bias.transpose(1, 0, 2, 3).reshape(ns, 3 * layers, q_sub)
            bias = jnp.pad(bias, ((0, 0), (0, -3 * layers % 8), (0, 0)))
            others = [
                ("input_grad", MainRows(sizes, rows, width, "summed")),
                ("norm", NormSum(sizes, lines, (0, 2 * layers), piece, ("summed", "spread"))),
                ("bias", BiasSum(sizes, bias, 3, ("attns", "inside0"))),
            ]
            steps += [("first", name, 0, "attns") for name in attn]
            steps += [("middle", name, 0, ("inside0", "inside0", "inside%d" % (nc - 2))) for name in attn]
            steps += [("exchange", name, 0, "inside%d" % (nc - 2)) for name in attn]
        else:
            steps += [("middle", name, layer, ("begin", "sent", "late")) for name in (ffn if top else ())]
            steps += [("first", name, layer, "attns") for name in attn]
            steps += [("middle", name, layer, ("spread", "spread", "late")) for name in attn]
        results = run(main, steps, others, 60)
        grad, norm_grads[(layer, 0)], bias_grads[layer] = results[:3]
        if layer > 0:
            grad_full = results[5]
    block_out = done["block_out"].reshape(ns, shard_rows, width)
    input_grad = done["input_grad"].reshape(ns, shard_rows, width).astype(F32)
    norm_total = done["norm"].reshape(2, layers, 2, piece)
    bias_total = done["bias"][:, : 3 * layers].reshape(nc, layers, 3, q_sub)
    bias_total = bias_total.transpose(1, 2, 0, 3).reshape(layers, 3, q_cols)

    grads = [[done[(name, layer)] for name in ("qkv", "out", "gate", "up", "down")] for layer in range(layers)]
    qkv_grad, out_grad, gate_up_grad, down_grad = finish(grads, q_cols, hidden)
    return (
        block_out,
        input_grad,
        norm_total[0],
        norm_total[1],
        qkv_grad.transpose(0, 2, 1, 3),
        bias_total,
        out_grad,
        gate_up_grad,
        down_grad,
    )


def solution(mesh):
    return jax.shard_map(
        functools.partial(body, mesh),
        mesh=mesh,
        in_specs=(
            P("fsdp", "context", None),
            P("fsdp", "context"),
            P(None, None, ("fsdp", "context")),
            P(None, None, ("fsdp", "context")),
            P(None, ("fsdp", "context"), None, "tensor"),
            P(None, None, "tensor"),
            P(None, ("fsdp", "context"), "tensor"),
            P(None, ("fsdp", "context"), None, "tensor"),
            P(None, ("fsdp", "context"), "tensor"),
            P("fsdp", "context", None),
        ),
        out_specs=(
            P("fsdp", "context", None),
            P("fsdp", "context", None),
            P(None, None, ("fsdp", "context")),
            P(None, None, ("fsdp", "context")),
            P(None, ("fsdp", "context"), None, "tensor"),
            P(None, None, "tensor"),
            P(None, ("fsdp", "context"), "tensor"),
            P(None, ("fsdp", "context"), None, "tensor"),
            P(None, ("fsdp", "context"), "tensor"),
        ),
        check_vma=False,
    )
```

```python
import functools
import math

import jax
import jax.numpy as jnp
from jax import lax
from jax.experimental import pallas as pl
from jax.experimental.pallas import tpu as pltpu
from jax.sharding import PartitionSpec as P

HD = 64
ROT = 16
EPS = 1e-05
ROPE_BASE = 10000.0
NEGATIVE = -1e30
MESH = pl.DeviceIdType.MESH
BF = jnp.bfloat16
F32 = jnp.float32
MIB = 2**20
TILE = 128
VMEM_BYTES = 58 * MIB


def dot_nn(a, b):
    return jnp.dot(a, b, preferred_element_type=F32)


def dot_nt(a, b):
    return lax.dot_general(a, b, (((1,), (1,)), ((), ())), preferred_element_type=F32)


def dot_tn(a, b):
    return lax.dot_general(a, b, (((0,), (0,)), ((), ())), preferred_element_type=F32)


class Sizes:
    def __init__(self, mesh, ns):
        self.nf, self.nc, self.nt = mesh.shape["fsdp"], mesh.shape["context"], mesh.shape["tensor"]
        self.ns = ns
        self.nk = self.nt // ns


class Place:
    def __init__(self, sizes):
        self.sizes = sizes
        self.f = lax.axis_index("fsdp")
        self.c = lax.axis_index("context")
        self.t = lax.axis_index("tensor")
        self.s, self.k = self.t // sizes.nk, lax.rem(self.t, sizes.nk)

    def mate(self):
        return {"tensor": self.t + 1 - 2 * self.k}

    def twin(self):
        return {"tensor": self.t + self.sizes.nk * (1 - 2 * self.s)}

    def right(self):
        return {"context": self.c + 1}

    def left(self):
        return {"context": self.c - 1}

    def ahead(self, step):
        return {"context": lax.rem(self.c + step, self.sizes.nc)}

    def across(self, step):
        return {"fsdp": lax.rem(self.f + step, self.sizes.nf)}

    def plane(self, df, dt):
        return {"fsdp": lax.rem(self.f + df, self.sizes.nf), "tensor": lax.rem(self.t + dt, self.sizes.nt)}


def greet(place, kinds):
    barrier = pltpu.get_barrier_semaphore()
    nc, nf = place.sizes.nc, place.sizes.nf

    def signal(device):
        pl.semaphore_signal(barrier, inc=1, device_id=device, device_id_type=MESH)

    count = 0
    if "plane" in kinds:
        for df in range(nf):
            for dt in range(place.sizes.nt):
                if df or dt:
                    signal(place.plane(df, dt))
        count += nf * place.sizes.nt - 1
        kinds = set(kinds) - {"mate", "fsdp", "twin"}
    if "mate" in kinds:
        signal(place.mate())
        count += 1
    if "ctx" in kinds:
        for step in range(1, nc):
            signal(place.ahead(step))
        count += nc - 1
    elif "line" in kinds:

        @pl.when(place.c > 0)
        def _():
            signal(place.left())

        @pl.when(place.c < nc - 1)
        def _():
            signal(place.right())

        count += jnp.minimum(place.c, 1) + jnp.minimum(nc - 1 - place.c, 1)
    if "fsdp" in kinds:
        for step in range(1, nf):
            signal(place.across(step))
        count += nf - 1
    if "twin" in kinds:
        signal(place.twin())
        count += 1
    return count


def push(src, dst, send, recv, device):
    return pltpu.make_async_remote_copy(
        src_ref=src, dst_ref=dst, send_sem=send, recv_sem=recv, device_id=device, device_id_type=MESH
    )


DMA = pltpu.SemaphoreType.DMA
VMEM_SPEC = pl.BlockSpec(memory_space=pltpu.VMEM)
ANY_SPEC = pl.BlockSpec(memory_space=pl.ANY)


HALVES = 2


class Gather:
    def __init__(self, place, own, out, sems, rows):
        self.place, self.own, self.out, self.rows = place, own, out, rows
        self.piece = rows // HALVES
        self.local, self.line_send, self.line_recv, self.mate_send, self.mate_recv = sems

    @staticmethod
    def scratch(sizes):
        nc = sizes.nc
        return [DMA(()), DMA((2, nc, HALVES)), DMA((nc, HALVES)), DMA((nc, HALVES)), DMA((nc, HALVES))]

    def slot(self, source, k, half):
        at = (source * self.place.sizes.nk + k) * self.rows + half * self.piece
        return self.out.at[pl.ds(pl.multiple_of(at, self.piece), self.piece)]

    def origin(self, source, half, first):
        if first:
            return self.own.at[pl.ds(half * self.piece, self.piece)]
        return self.slot(source, self.place.k, half)

    def line(self, source, half, device, first, way):
        return push(
            self.origin(source, half, first),
            self.slot(source, self.place.k, half),
            self.line_send.at[way, source, half],
            self.line_recv.at[source, half],
            device,
        )

    def pass_on(self, source, half, first):
        return push(
            self.origin(source, half, first),
            self.slot(source, self.place.k, half),
            self.mate_send.at[source, half],
            self.mate_recv.at[source, half],
            self.place.mate(),
        )

    def keep(self):
        at = (self.place.c * self.place.sizes.nk + self.place.k) * self.rows
        target = self.out.at[pl.ds(pl.multiple_of(at, self.rows), self.rows)]
        return pltpu.make_async_copy(self.own, target, self.local)

    def begin(self):
        place, c, nc = self.place, self.place.c, self.place.sizes.nc
        for half in range(HALVES):

            @pl.when(c < nc - 1)
            def _():
                self.line(c, half, place.right(), True, 0).start()

            @pl.when(c > 0)
            def _():
                self.line(c, half, place.left(), True, 1).start()

        for half in range(HALVES):
            self.pass_on(c, half, True).start()
        self.keep().start()

    def forward(self, step):
        place, c, nc = self.place, self.place.c, self.place.sizes.nc
        source, other = c - step, c + step
        for half in range(HALVES):

            @pl.when(source >= 0)
            def _():
                self.line(source, half, place.left(), False, 0).wait_recv()

                @pl.when(c < nc - 1)
                def _():
                    self.line(source, half, place.right(), False, 0).start()

                self.pass_on(source, half, False).start()

            @pl.when(other <= nc - 1)
            def _():
                self.line(other, half, place.right(), False, 1).wait_recv()

                @pl.when(c > 0)
                def _():
                    self.line(other, half, place.left(), False, 1).start()

                self.pass_on(other, half, False).start()

    def end(self):
        place, c, nc = self.place, self.place.c, self.place.sizes.nc
        self.keep().wait()
        for source in range(nc):
            for half in range(HALVES):
                arrival = self.slot(source, 1 - place.k, half)
                push(
                    arrival, arrival, self.mate_send.at[source, half], self.mate_recv.at[source, half], place.mate()
                ).wait_recv()
                self.pass_on(source, half, False).wait_send()

                @pl.when((source <= c) & (c < nc - 1))
                def _():
                    self.line(source, half, place.right(), False, 0).wait_send()

                @pl.when((source >= c) & (c > 0))
                def _():
                    self.line(source, half, place.left(), False, 1).wait_send()


def scatter_part(place, part_ref, bufs, rows, moment):
    nc, nk, c, k = place.sizes.nc, place.sizes.nk, place.c, place.k
    piece = rows // HALVES
    mate_buf, to_right, to_left, from_left, from_right = bufs[:5]
    mate_send, mate_recv, right_send, right_recv, left_send, left_recv = bufs[5:]

    def block(dest, kk):
        return part_ref.at[pl.ds(pl.multiple_of((dest * nk + kk) * rows, rows), rows)]

    def mate_copy(dest):
        return push(
            block(dest, 1 - k), mate_buf.at[dest], mate_send.at[dest], mate_recv.at[dest], place.mate()
        )

    def lines(half):
        return slice(half * piece, (half + 1) * piece)

    def right_copy(dest, half):
        return push(
            to_right.at[dest, lines(half)],
            from_left.at[dest, lines(half)],
            right_send.at[dest, half],
            right_recv.at[dest, half],
            place.right(),
        )

    def left_copy(dest, half):
        return push(
            to_left.at[dest, lines(half)],
            from_right.at[dest, lines(half)],
            left_send.at[dest, half],
            left_recv.at[dest, half],
            place.left(),
        )

    def each(visit_right, visit_left, count, after=lambda step: None):
        for step in range(nc - 1):
            far = nc - 1 - step
            for half in range(count):

                @pl.when(far > c)
                def _():
                    visit_right(far, half)

                @pl.when(step < c)
                def _():
                    visit_left(step, half)

            after(step)

    def send_mate(dest, half):
        mate_copy(dest).start()

    each(send_mate, send_mate, 1)
    mate_copy(c).start()
    moment("sent")

    def chip_sum(dest, half):
        if half == 0:
            mate_copy(dest).wait_recv()
        at = pl.multiple_of((dest * nk + k) * rows + half * piece, piece)
        return part_ref[pl.ds(at, piece)].astype(F32) + mate_buf[dest, lines(half)].astype(F32)

    def pass_right(dest, half):
        total = chip_sum(dest, half)
        to_right[dest, lines(half)] = total.astype(BF)

        @pl.when(c > 0)
        def _():
            right_copy(dest, half).wait_recv()
            to_right[dest, lines(half)] = (total + from_left[dest, lines(half)].astype(F32)).astype(BF)

        right_copy(dest, half).start()

    def pass_left(dest, half):
        total = chip_sum(dest, half)
        to_left[dest, lines(half)] = total.astype(BF)

        @pl.when(c < nc - 1)
        def _():
            left_copy(dest, half).wait_recv()
            to_left[dest, lines(half)] = (total + from_right[dest, lines(half)].astype(F32)).astype(BF)

        left_copy(dest, half).start()

    def inside(step):
        for at in range(3):
            if at * (nc - 1) // 3 == step:
                moment("inside%d" % at)

    each(pass_right, pass_left, HALVES, inside)
    totals = []
    for half in range(HALVES):
        total = chip_sum(c, half)

        @pl.when(c > 0)
        def _():
            right_copy(c, half).wait_recv()

        @pl.when(c < nc - 1)
        def _():
            left_copy(c, half).wait_recv()

        total = total + jnp.where(c > 0, from_left[c, lines(half)].astype(F32), 0.0)
        totals.append(total + jnp.where(c < nc - 1, from_right[c, lines(half)].astype(F32), 0.0))
    def sent():
        for dest in range(nc):
            mate_copy(dest).wait_send()
            for half in range(HALVES):

                @pl.when(dest > c)
                def _():
                    right_copy(dest, half).wait_send()

                @pl.when(dest < c)
                def _():
                    left_copy(dest, half).wait_send()

    return jnp.concatenate(totals, 0), sent


def scatter_scratch(sizes, rows, width):
    nc = sizes.nc
    return [pltpu.VMEM((nc, rows, width), BF) for _ in range(5)] + [DMA((nc,)) for _ in range(2)] + [
        DMA((nc, HALVES)) for _ in range(4)
    ]


N_SCATTER = 11


class Rider:
    kinds = ()
    ins, outs, sems = [], [], []
    aliased = False

    def bind(self, place, ins, outs, sems, main):
        self.place, self.r_ins, self.r_outs, self.r_sems, self.main = place, ins, outs, sems, main

    def at(self, moment):
        pass


class Exchange(Rider):
    kinds = ("ctx",)

    def __init__(self, sizes, ins, out, pieces, rows, sub, when="begin", finish="end"):
        self.ins, self.outs, self.pieces, self.when, self.last = ins, [out], pieces, when, finish
        count = max(sizes.nc - 1, 1)
        self.sub = sub
        self.sems = [DMA(()), DMA((count,)), DMA((count,)), pltpu.VMEM((rows, sub * len(pieces)), BF)]

    def at(self, moment):
        if moment == self.when:
            self.start()
        if moment == self.last:
            self.finish()

    def start(self):
        place, nc = self.place, self.place.sizes.nc
        local, send, recv, held = self.r_sems
        for step in range(1, nc):
            for source_of, target_of in self.pieces:
                push(
                    source_of(self.r_ins, lax.rem(place.c + step, nc)),
                    target_of(self.r_outs[0], place.c),
                    send.at[step - 1],
                    recv.at[step - 1],
                    place.ahead(step),
                ).start()
        for at, (source_of, _) in enumerate(self.pieces):
            lanes = pl.ds(at * self.sub, self.sub)
            pltpu.make_async_copy(source_of(self.r_ins, place.c), held.at[:, lanes], local).start()

    def wait_own(self):
        local, _, _, held = self.r_sems
        pltpu.make_async_copy(held, held, local).wait()
        for at, (_, target_of) in enumerate(self.pieces):
            lanes = pl.ds(at * self.sub, self.sub)
            pltpu.make_async_copy(held.at[:, lanes], target_of(self.r_outs[0], self.place.c), local).start()
        pltpu.make_async_copy(held, held, local).wait()

    def wait_from(self, step):
        whole = self.whole()
        _, send, recv, _ = self.r_sems
        push(whole, whole, send.at[step - 1], recv.at[step - 1], self.place.ahead(step)).wait_recv()

    def wait_sent(self):
        whole = self.whole()
        _, send, recv, _ = self.r_sems
        for step in range(1, self.place.sizes.nc):
            push(whole, whole, send.at[step - 1], recv.at[step - 1], self.place.ahead(step)).wait_send()

    def finish(self):
        self.wait_own()
        for step in range(1, self.place.sizes.nc):
            self.wait_from(step)
        self.wait_sent()


class WeightExchange(Exchange):
    def __init__(self, sizes, rows, array, corners, sub, when="begin", finish="end"):
        pieces = [self.piece(first, rows, base, sub, at) for at, (first, base) in enumerate(corners)]
        out = jax.ShapeDtypeStruct((sizes.nc * rows, sub * len(pieces)), BF)
        super().__init__(sizes, [array], out, pieces, rows, sub, when, finish)
        self.rows = rows

    @staticmethod
    def piece(first, rows, base, sub, position):
        def source_of(refs, dest):
            return refs[0].at[pl.ds(first, rows), pl.ds(pl.multiple_of(base + dest * sub, TILE), sub)]

        def target_of(out, source):
            return out.at[pl.ds(pl.multiple_of(source * rows, rows), rows), pl.ds(position * sub, sub)]

        return source_of, target_of

    def whole(self):
        return self.r_outs[0].at[pl.ds(0, self.rows)]


class GradExchange(Exchange):
    def __init__(self, sizes, total, sub, when="begin", finish="end"):
        self.middle = total if isinstance(total, GradMiddle) else None
        shape = self.middle.outs[0].shape if self.middle else total.shape
        rows = shape[0] // sizes.nc
        count = shape[1] // sub
        out = jax.ShapeDtypeStruct((rows, sizes.nc * shape[1]), BF)
        pieces = [self.piece(rows, sub, position, sizes.nc) for position in range(count)]
        super().__init__(sizes, [] if self.middle else [total], out, pieces, rows, sub, when, finish)
        self.rows = rows

    def start(self):
        if self.middle:
            self.r_ins = [self.middle.total]
        super().start()

    @staticmethod
    def piece(rows, sub, position, nc):
        def source_of(refs, dest):
            return refs[0].at[pl.ds(pl.multiple_of(dest * rows, rows), rows), pl.ds(position * sub, sub)]

        def target_of(out, source):
            return out.at[:, pl.ds(pl.multiple_of(position * nc * sub + source * sub, TILE), sub)]

        return source_of, target_of

    def whole(self):
        return self.r_ins[0].at[pl.ds(0, self.rows)]


class Spread(Rider):
    kinds = ("fsdp", "twin")

    def __init__(self, sizes, mine, blocks=1, steps=("begin", "inside1")):
        if isinstance(mine, Exchange):
            self.source, shape, self.ins = mine, mine.outs[0].shape, []
        else:
            self.source, shape, self.ins = None, mine.shape, [mine]
        rows, self.width = shape
        self.part, self.blocks, self.rows, self.steps = rows, blocks, rows // blocks, steps
        self.outs = [jax.ShapeDtypeStruct((sizes.nf * rows, sizes.ns * self.width), BF)]
        others = max(sizes.nf - 1, 1)
        self.sems = [DMA((blocks,))] + [DMA((blocks, others)) for _ in range(8)] + [DMA((blocks,)) for _ in range(4)]
        self.sems.append(pltpu.VMEM((rows, self.width), BF))

    def at(self, moment):
        if moment == self.steps[0]:
            if self.source is not None:
                self.source.finish()
            for block in range(self.blocks):
                self.first(block)
        if moment == self.steps[1]:
            for block in range(self.blocks):
                self.second(block)
        if moment == "end":
            for block in range(self.blocks):
                self.finish(block)

    def span(self, df, block, half, whole=False):
        length = self.rows if whole else self.rows // 2
        at = df * self.part + block * self.rows + half * (self.rows // 2)
        return pl.ds(pl.multiple_of(at, length), length)

    def mine(self, block, half, whole=False):
        ref = self.r_ins[0] if self.source is None else self.source.r_outs[0]
        return ref.at[self.span(0, block, half, whole)]

    def out(self, ds, df, block, half, whole=False):
        return self.r_outs[0].at[self.span(df, block, half, whole), pl.ds(ds * self.width, self.width)]

    def copies(self, block, stage):
        place, nf, sems, out = self.place, self.place.sizes.nf, self.r_sems, []
        for step in range(1, nf):
            at, df = step - 1, nf - step
            across = place.across(step)
            source, target, pair, device = [
                (self.mine(block, 0), self.out(0, df, block, 0), 1, across),
                (self.mine(block, 1), self.out(0, df, block, 1), 3, across),
                (self.out(1, 0, block, 1), self.out(1, df, block, 1), 5, across),
            ][stage]
            out.append(push(source, target, sems[pair].at[block, at], sems[pair + 1].at[block, at], device))
            if stage == 2:
                source, target = self.out(0, df, block, 0), self.out(1, df, block, 0)
                out.append(push(source, target, sems[7].at[block, at], sems[8].at[block, at], place.twin()))
        if stage < 2:
            half, pair = (1, 9) if stage == 0 else (0, 11)
            out.append(
                push(
                    self.mine(block, half),
                    self.out(1, 0, block, half),
                    sems[pair].at[block],
                    sems[pair + 1].at[block],
                    place.twin(),
                )
            )
        return out

    def keep(self, block, inward):
        held = self.r_sems[13].at[self.span(0, block, 0, True)]
        ends = (self.mine(block, 0, True), held) if inward else (held, self.out(0, 0, block, 0, True))
        return pltpu.make_async_copy(*ends, self.r_sems[0].at[block])

    def first(self, block):
        for stage in range(2):
            for copy in self.copies(block, stage):
                copy.start()
        self.keep(block, True).start()

    def second(self, block):
        for copy in self.copies(block, 0):
            copy.wait_recv()
        for copy in self.copies(block, 2):
            copy.start()
        self.keep(block, True).wait()
        self.keep(block, False).start()

    def finish(self, block):
        for copy in self.copies(block, 0):
            copy.wait_send()
        for stage in (1, 2):
            for copy in self.copies(block, stage):
                copy.wait_recv()
                copy.wait_send()
        self.keep(block, False).wait()


class SpreadOwn(Spread):
    def at(self, moment):
        if moment == self.steps[0]:
            if self.source is not None:
                self.source.finish()
            for block in range(self.blocks):
                self.first(block)
        if moment == "end" and self.steps[0] is not None:
            for block in range(self.blocks):
                self.finish(block)

    def finish(self, block):
        self.keep(block, True).wait()
        self.keep(block, False).start()
        for stage in range(2):
            for copy in self.copies(block, stage):
                copy.wait_recv()
                copy.wait_send()
        self.keep(block, False).wait()


class SpreadRelay(Rider):
    kinds = ("fsdp", "twin")
    aliased = True

    def __init__(self, sizes, whole, when="begin"):
        self.ins, self.outs, self.when = [whole], [jax.ShapeDtypeStruct(whole.shape, BF)], when
        self.part, self.width = whole.shape[0] // sizes.nf, whole.shape[1] // sizes.ns
        others = max(sizes.nf - 1, 1)
        self.sems = [DMA((others,)) for _ in range(4)]
        self.blocks = sizes.nc

    def copies(self):
        out, place, nf = [], self.place, self.place.sizes.nf
        rows, half = self.part // self.blocks, self.part // self.blocks // 2
        for step in range(1, nf):
            at, df = step - 1, nf - step
            for block in range(self.blocks):
                low, high = block * rows, block * rows + half
                lanes = pl.ds(self.width, self.width)
                first = pl.ds(df * self.part + low, half)
                second = pl.ds(df * self.part + high, half)
                whole = self.r_outs[0]
                out.append(
                    push(
                        whole.at[pl.ds(high, half), lanes],
                        whole.at[second, lanes],
                        self.sems_of(0, at),
                        self.sems_of(1, at),
                        place.across(step),
                    )
                )
                out.append(
                    push(
                        whole.at[first, pl.ds(0, self.width)],
                        whole.at[first, lanes],
                        self.sems_of(2, at),
                        self.sems_of(3, at),
                        place.twin(),
                    )
                )
        return out

    def sems_of(self, kind, at):
        return self.r_sems[kind].at[at]

    def at(self, moment):
        if moment == self.when:
            for copy in self.copies():
                copy.start()
        if moment == "end":
            place, half = self.place, self.part // 2
            for step in range(1, place.sizes.nf):
                at = step - 1
                bytes_of = self.r_outs[0].at[pl.ds(0, half), pl.ds(0, self.width)]
                for kind, device in ((0, place.across(step)), (2, place.twin())):
                    push(bytes_of, bytes_of, self.sems_of(kind, at), self.sems_of(kind + 1, at), device).wait()


class GradFirst(Rider):
    kinds = ("fsdp", "twin")

    def __init__(self, sizes, name, rows, width, when):
        self.name, self.when, self.taken = name, when, False
        self.part = rows // sizes.nf
        self.half = self.part // 2
        self.width = width // sizes.ns
        others = max(sizes.nf - 1, 1)
        self.outs = [
            jax.ShapeDtypeStruct((others, self.half, width), BF),
            jax.ShapeDtypeStruct((sizes.nf, self.half, self.width), BF),
        ]
        self.sems = [DMA((others,)), DMA((others,)), DMA((sizes.nf,)), DMA((sizes.nf,))]

    def copies(self):
        place, nf = self.place, self.place.sizes.nf
        grads, (low, high) = self.main.grads[self.name], self.r_outs
        xs, xr, ys, yr = self.r_sems
        out = []
        for step in range(1, nf):
            at = step - 1
            out.append(
                push(grads.at[pl.ds(step * self.part, self.half)], low.at[at], xs.at[at], xr.at[at], place.across(step))
            )
        for df in range(nf):
            rows = pl.ds(df * self.part + self.half, self.half)
            out.append(
                push(grads.at[rows, pl.ds(self.width, self.width)], high.at[df], ys.at[df], yr.at[df], place.twin())
            )
        return out

    def at(self, moment):
        if moment == self.when:
            for copy in self.copies():
                copy.start()
        if moment == "end":
            if not self.taken:
                self.wait_recv()
            for copy in self.copies():
                copy.wait_send()

    def wait_recv(self):
        self.taken = True
        for copy in self.copies():
            copy.wait_recv()


class GradMiddle(Rider):
    kinds = ("fsdp", "twin")

    def __init__(self, sizes, source, steps=("begin", "sent", "late")):
        self.steps = steps
        if isinstance(source, GradFirst):
            self.source, self.ins = source, []
            low, high = source.outs
            part = source.part
        else:
            self.source, self.ins = None, list(source)
            low, high = source[1:]
            part = source[0].shape[0] // sizes.nf
        self.part, self.half, self.width = part, part // 2, high.shape[2]
        nf, others = sizes.nf, low.shape[0]
        self.outs = [jax.ShapeDtypeStruct((part, self.width), BF)]
        piece = (self.half, self.width)
        self.sems = [
            pltpu.VMEM((self.half, sizes.ns * self.width), BF),
            pltpu.VMEM((nf,) + piece, BF),
            pltpu.VMEM(low.shape, BF),
            pltpu.VMEM(high.shape, BF),
            pltpu.VMEM(piece, BF),
            pltpu.VMEM((others,) + piece, BF),
            pltpu.VMEM((part, self.width), BF),
            DMA((nf + 3,)),
            DMA(()),
            DMA(()),
            DMA((others,)),
            DMA((others,)),
            DMA(()),
        ]

    @property
    def total(self):
        return self.r_sems[6]

    def loads(self):
        nf = self.place.sizes.nf
        if self.source is None:
            grads, low, high = self.r_ins
        else:
            grads = self.main.grads[self.source.name]
            low, high = self.source.r_outs
        g_low, g_high, r_low, r_high = self.r_sems[:4]
        sem = self.r_sems[7]
        out = [
            pltpu.make_async_copy(grads.at[pl.ds(0, self.half)], g_low, sem.at[nf]),
            pltpu.make_async_copy(low, r_low, sem.at[nf + 1]),
            pltpu.make_async_copy(high, r_high, sem.at[nf + 2]),
        ]
        for df in range(nf):
            rows = pl.ds(df * self.part + self.half, self.half)
            out.append(pltpu.make_async_copy(grads.at[rows, pl.ds(0, self.width)], g_high.at[df], sem.at[df]))
        return out

    def copies(self):
        place, nf, width = self.place, self.place.sizes.nf, self.width
        g_low, g_high, _, _, low, high = self.r_sems[:6]
        ys, yr, xs, xr = self.r_sems[8:12]
        out = [push(g_low.at[:, pl.ds(width, width)], low, ys, yr, place.twin())]
        for step in range(1, nf):
            at = step - 1
            out.append(push(g_high.at[step], high.at[at], xs.at[at], xr.at[at], place.across(step)))
        return out

    def store(self):
        return pltpu.make_async_copy(self.total, self.r_outs[0], self.r_sems[12])

    def at(self, moment):
        nf, width, half = self.place.sizes.nf, self.width, self.half
        g_low, g_high, r_low, r_high, low, high, total = self.r_sems[:7]
        if moment == self.steps[0]:
            if self.source is not None:
                self.source.wait_recv()
            for copy in self.loads():
                copy.start()
        if moment == self.steps[1]:
            for copy in self.loads():
                copy.wait()
            lanes = slice(width, 2 * width)

            def first(rows):
                value = g_low[rows, lanes].astype(F32)
                for at in range(nf - 1):
                    value = value + r_low[at, rows, lanes].astype(F32)
                g_low[rows, lanes] = value.astype(BF)
                for df in range(1, nf):
                    g_high[df, rows] = (g_high[df, rows].astype(F32) + r_high[df, rows].astype(F32)).astype(BF)

            by_rows(half, 32, first)
            for copy in self.copies():
                copy.start()
        if moment == self.steps[2]:
            for copy in self.copies():
                copy.wait_recv()
            lanes = slice(0, width)

            def second(rows):
                value = g_low[rows, lanes].astype(F32) + low[rows].astype(F32)
                for at in range(nf - 1):
                    value = value + r_low[at, rows, lanes].astype(F32)
                total[rows] = value.astype(BF)

            def third(rows):
                value = g_high[0, rows].astype(F32) + r_high[0, rows].astype(F32)
                for at in range(nf - 1):
                    value = value + high[at, rows].astype(F32)
                total[pl.ds(pl.multiple_of(rows.start + half, 32), 32)] = value.astype(BF)

            by_rows(half, 32, second)
            by_rows(half, 32, third)
            self.store().start()
        if moment == "end":
            for copy in self.copies():
                copy.wait_send()
            self.store().wait()


class Share(Rider):
    def __init__(self, kinds, array, out, count, moves, when="begin"):
        self.kinds, self.moves, self.when = kinds, moves, when
        self.ins, self.outs = [array], [out]
        self.sems = [DMA((count,)), DMA((count,))]

    def copies(self):
        send, recv = self.r_sems
        out = []
        for at, (device, source, target) in enumerate(self.moves(self.place, self.r_ins[0], self.r_outs[0])):
            if device is None:
                out.append(pltpu.make_async_copy(source, target, send.at[at]))
            else:
                out.append(push(source, target, send.at[at], recv.at[at], device))
        return out

    def at(self, moment):
        if moment == self.when:
            for copy in self.copies():
                copy.start()
        if moment == "end":
            for copy in self.copies():
                copy.wait()


def share_rows(sizes, value):
    rows, width = value.shape
    part = width // sizes.nf

    def moves(place, source, out):
        triples = []
        for dt in range(sizes.nt):
            device = place.plane(0, dt) if dt else None
            for df in range(sizes.nf):
                lanes = pl.ds(pl.multiple_of(lax.rem(place.f + df, sizes.nf) * part, part), part)
                triples.append((device, source.at[:, pl.ds(df * part, part)], out.at[place.t, :, lanes]))
        return triples

    out = jax.ShapeDtypeStruct((sizes.nt, rows, width), value.dtype)
    return Share(("plane",), value, out, sizes.nt * sizes.nf, moves)


class MainRows(Share):
    def __init__(self, sizes, rows, width, when):
        share = share_rows(sizes, jax.ShapeDtypeStruct((rows, width), BF))
        super().__init__(share.kinds, None, share.outs[0], share.sems[0].shape[0], share.moves, when)
        self.ins = []

    def copies(self):
        self.r_ins = [self.main.rows_ref]
        return super().copies()


class NormSum(Rider):
    kinds = ("ctx", "plane")

    def __init__(self, sizes, lines, places, piece, steps):
        self.ins, self.places, self.piece, self.steps = [lines], places, piece, steps
        count = lines.shape[0]
        self.outs = [jax.ShapeDtypeStruct((count, piece), F32)]
        self.around = [(df, dt) for df in range(sizes.nf) for dt in range(sizes.nt)][1:]
        block = (sizes.nf, count, piece)
        self.sems = [
            pltpu.VMEM(lines.shape, F32),
            pltpu.VMEM((sizes.nc,) + block, F32),
            pltpu.VMEM(block, F32),
            pltpu.VMEM((len(self.around), count, piece), F32),
            pltpu.VMEM((count, piece), F32),
            DMA(()),
            DMA((sizes.nc,)),
            DMA((sizes.nc,)),
            DMA((len(self.around),)),
            DMA((len(self.around),)),
            pltpu.VMEM((sizes.nc,) + block, F32),
        ]

    def rounds(self):
        place = self.place
        _, _, sums, _, _, _, _, _, send, recv, _ = self.r_sems
        return [
            push(sums.at[df], self.r_sems[3].at[at], send.at[at], recv.at[at], place.plane(df, dt))
            for at, (df, dt) in enumerate(self.around)
        ]

    def whole(self, step):
        box = self.r_sems[1].at[step]
        return push(box, box, self.r_sems[6].at[step], self.r_sems[7].at[step], self.place.ahead(step))

    def at(self, moment):
        place, sizes = self.place, self.place.sizes
        lines, first, sums, second, result, load, send, recv = self.r_sems[:8]

        def keep():
            return pltpu.make_async_copy(self.r_ins[0], lines, load)

        if moment == "begin":
            keep().start()
        if moment == self.steps[0]:
            keep().wait()
            for at, line in enumerate(self.places):
                lines[line : line + 1] = self.main.norm_ref[at : at + 1]
            blocks = self.r_sems[10]
            for dest in range(sizes.nc):
                for df in range(sizes.nf):
                    lane = (df * sizes.nc + dest) * self.piece
                    blocks[dest, df] = lines[:, lane : lane + self.piece]
            for step in range(1, sizes.nc):
                push(
                    blocks.at[lax.rem(place.c + step, sizes.nc)],
                    first.at[step],
                    send.at[step],
                    recv.at[step],
                    place.ahead(step),
                ).start()
            first[0] = blocks[place.c]
        if moment == self.steps[1]:
            for step in range(1, sizes.nc):
                self.whole(step).wait_recv()
            sums[...] = sum(first[step] for step in range(sizes.nc))
            for copy in self.rounds():
                copy.start()
        if moment == "end":
            for copy in self.rounds():
                copy.wait()
            for step in range(1, sizes.nc):
                self.whole(step).wait_send()
            result[...] = sums[0] + sum(second[at] for at in range(len(self.around)))
            out = pltpu.make_async_copy(result, self.r_outs[0], load)
            out.start()
            out.wait()


class BiasSum(Rider):
    kinds = ("ctx", "plane")

    def __init__(self, sizes, value, own, steps):
        self.ins, self.own, self.steps = [value], own, steps
        ns, count, width = value.shape
        self.width = width
        self.outs = [jax.ShapeDtypeStruct((sizes.nc, count, width), F32)]
        self.around = [(df, ds) for df in range(sizes.nf) for ds in range(ns)][1:]
        self.sems = [
            pltpu.VMEM(value.shape, F32),
            pltpu.VMEM((len(self.around), count, width), F32),
            pltpu.VMEM((count, width), F32),
            DMA(()),
            DMA((len(self.around),)),
            DMA((len(self.around),)),
            DMA((sizes.nc,)),
            DMA((sizes.nc,)),
        ]

    def rounds(self):
        lines, first, _, _, send, recv = self.r_sems[:6]
        nk = self.place.sizes.nk
        return [
            push(lines.at[ds], first.at[at], send.at[at], recv.at[at], self.place.plane(df, ds * nk))
            for at, (df, ds) in enumerate(self.around)
        ]

    def spreads(self):
        place, nc = self.place, self.place.sizes.nc
        sums, target = self.r_sems[2], self.r_outs[0].at[self.place.c]
        send, recv = self.r_sems[6:]
        return [push(sums, target, send.at[step], recv.at[step], place.ahead(step)) for step in range(1, nc)]

    def at(self, moment):
        lines, first, sums, load = self.r_sems[:4]

        def keep():
            return pltpu.make_async_copy(self.r_ins[0], lines, load)

        def mine():
            return pltpu.make_async_copy(sums, self.r_outs[0].at[self.place.c], load)

        if moment == "begin":
            keep().start()
        if moment == self.steps[0]:
            keep().wait()
            for ds in range(self.place.sizes.ns):
                for line in range(self.own):
                    at = (ds * self.own + line) * self.width
                    lines[ds, line : line + 1] = self.main.bias_ref[:, at : at + self.width]
            for copy in self.rounds():
                copy.start()
        if moment == self.steps[1]:
            for copy in self.rounds():
                copy.wait()
            sums[...] = lines[0] + sum(first[at] for at in range(len(self.around)))
            for copy in self.spreads() + [mine()]:
                copy.start()
        if moment == "end":
            for copy in self.spreads() + [mine()]:
                copy.wait()


class Moved:
    def __init__(self, hbm, scratch, inward):
        count = len(hbm)
        self.vmem = scratch[:count]
        self.copies = []
        for ref, buffer, sem in zip(hbm, scratch[:count], scratch[count:]):
            ends = (ref, buffer) if inward else (buffer, ref)
            self.copies.append(pltpu.make_async_copy(*ends, sem))

    @staticmethod
    def scratch(arrays):
        return [pltpu.VMEM(a.shape, a.dtype) for a in arrays] + [DMA(()) for _ in arrays]

    def start(self):
        for copy in self.copies:
            copy.start()


class Main:
    kinds = ("mate", "line")
    big, small, results, kept, gathered, work = [], [], [], [], [], []

    def __init__(self, **arrays):
        self.grads = {}

    @property
    def ins(self):
        return list(self.big) + list(self.small)

    @property
    def in_specs(self):
        return [ANY_SPEC] * len(self.big) + [VMEM_SPEC] * len(self.small)

    @property
    def outs(self):
        return list(self.results) + list(self.kept) + list(self.gathered)

    @property
    def out_specs(self):
        return [VMEM_SPEC] * len(self.results) + [ANY_SPEC] * (len(self.kept) + len(self.gathered))

    def scratch(self, sizes):
        self.layout = [
            Moved.scratch(self.big),
            Moved.scratch(self.kept),
            [pltpu.VMEM(a.shape, a.dtype) for a in self.work],
            scatter_scratch(sizes, self.rows, self.width),
        ] + [Gather.scratch(sizes) for _ in self.gathered]
        return [one for group in self.layout for one in group]

    def run(self, place, ins, outs, scratch, moment):
        cuts, at = [], 0
        for group in self.layout:
            cuts.append(scratch[at : at + len(group)])
            at += len(group)
        count = len(self.big)
        self.loads = Moved(ins[:count], cuts[0], True)
        results, kept = outs[: len(self.results)], outs[len(self.results) : len(self.results) + len(self.kept)]
        gathered = outs[len(self.results) + len(self.kept) :]
        self.stores = Moved(kept, cuts[1], False)
        self.work_refs, self.bufs, self.gather_sems = cuts[2], cuts[3], cuts[4:]
        self.loads.start()
        moment("begin")
        self.compute(place, self.loads.vmem, ins[count:], results, self.stores.vmem, gathered, moment)
        self.sent()
        for copy in self.stores.copies:
            copy.wait()

    def fetch(self, *which):
        for at in which:
            self.loads.copies[at].wait()

    def store(self, *which):
        for at in which:
            self.stores.copies[at].start()

    def spread(self, place, gathers, moment):
        for gather in gathers:
            gather.begin()
        moment("summed")
        for step in range(1, place.sizes.nc):
            for gather in gathers:
                gather.forward(step)
            if step == 1:
                moment("spread")
        moment("late")
        for gather in gathers:
            gather.end()


def by_rows(count, block, step):
    def one(at, carry):
        step(pl.ds(pl.multiple_of(at * block, block), block))
        return carry

    lax.fori_loop(0, count // block, one, 0)


def unit_rows_of(values):
    row_mean = jnp.mean(values, -1, keepdims=True)
    centred = values - row_mean
    row_var = jnp.mean(centred * centred, -1, keepdims=True)
    inverse = lax.rsqrt(row_var + EPS)
    return centred * inverse, inverse


def norm_back(grad_rows, saved_rows, gain_row):
    unit_rows, inverse = unit_rows_of(saved_rows)
    scaled = grad_rows * gain_row
    inner = inverse * (
        scaled
        - jnp.mean(scaled, -1, keepdims=True)
        - unit_rows * jnp.mean(scaled * unit_rows, -1, keepdims=True)
    )
    return inner, jnp.sum(grad_rows * unit_rows, 0, keepdims=True), jnp.sum(grad_rows, 0, keepdims=True)


def norm_forward(new_rows, norm_ref, at):
    unit_rows, _ = unit_rows_of(new_rows)
    return (unit_rows * norm_ref[at : at + 1] + norm_ref[at + 1 : at + 2]).astype(BF)


def swap_lanes(values):
    lane = lax.broadcasted_iota(jnp.int32, values.shape, 1) % HD
    width = values.shape[1]
    up = pltpu.roll(values, width - ROT // 2, 1)
    down = pltpu.roll(values, ROT // 2, 1)
    return jnp.where(lane < ROT // 2, up, jnp.where(lane < ROT, down, 0.0))


def allowed_of(label_col, label_row):
    length = label_col.shape[0]
    row = lax.broadcasted_iota(jnp.int32, (length, length), 0)
    col = lax.broadcasted_iota(jnp.int32, (length, length), 1)
    return (label_col == label_row) & (row >= col)


def like(shape, dtype):
    return jax.ShapeDtypeStruct(shape, dtype)


ROW_BLOCK = 128
OUT_BLOCK = 256


class AttnForward(Main):
    def __init__(self, full, w_qkv, w_out, bias, tables, stream, norm):
        super().__init__()
        self.rows, self.width = stream.shape
        length = full.shape[0]
        self.big = [full, w_qkv, w_out]
        self.small, self.norm_at = [bias[0], *tables, stream, norm[0]], norm[1]
        self.bias_at = bias[1]
        heads = w_out.shape[1] // HD
        self.results = [like(stream.shape, F32), like((length, heads), F32)]
        mixed = like((length, w_out.shape[1]), BF)
        self.kept = [like((length, w_qkv.shape[1]), BF), mixed, mixed, mixed]
        self.gathered = [like(full.shape, BF)]
        self.work = [like(full.shape, BF), like(stream.shape, BF)]

    def compute(self, place, big, small, results, kept, gathered, moment):
        full, w_qkv, w_out = big
        bias_ref, col_ref, row_ref, cos_ref, sin_ref, stream_ref, norm_ref = small
        new_ref, lse_ref = results
        proj_ref, mix_ref, q_ref, k_ref = kept
        part_ref, low_ref = self.work_refs
        length = full.shape[0]
        ns = place.sizes.ns
        width = w_out.shape[1] // ns
        self.fetch(0, 1)

        def project(rows):
            proj_ref[rows] = (dot_nn(full[rows], w_qkv[...]) + bias_ref[self.bias_at : self.bias_at + 1]).astype(BF)

        by_rows(length, ROW_BLOCK, project)
        self.store(0)
        allowed = allowed_of(col_ref[...], row_ref[...])
        cosine, sine = cos_ref[...], sin_ref[...]
        scaling = HD ** (-0.5)
        for b in range(ns):
            base, own = 3 * width * b, slice(b * width, (b + 1) * width)
            for ref, at in ((q_ref, 0), (k_ref, 1)):
                values = proj_ref[:, base + at * width : base + (at + 1) * width].astype(F32)
                ref[:, own] = (values * cosine + swap_lanes(values) * sine).astype(BF)
            for h in range(width // HD):
                span = slice(b * width + h * HD, b * width + (h + 1) * HD)
                scores = scaling * dot_nt(q_ref[:, span], k_ref[:, span])
                scores = jnp.where(allowed, scores, NEGATIVE)
                peak = jnp.max(scores, -1, keepdims=True)
                exponent = jnp.exp(scores - peak)
                total = jnp.sum(exponent, -1, keepdims=True)
                probs = (exponent * (1.0 / total)).astype(BF)
                at = base + 2 * width + h * HD
                mix_ref[:, span] = dot_nn(probs, proj_ref[:, at : at + HD]).astype(BF)
                at = b * (width // HD) + h
                lse_ref[:, at : at + 1] = peak + jnp.log(total)
        self.store(1, 2, 3)
        self.fetch(2)
        for at in range(0, self.width, OUT_BLOCK):
            part_ref[:, at : at + OUT_BLOCK] = dot_nt(mix_ref[...], w_out[at : at + OUT_BLOCK]).astype(BF)
        moment("ready")
        total, self.sent = scatter_part(place, part_ref, self.bufs, self.rows, moment)
        new_rows = stream_ref[...] + total
        new_ref[...] = new_rows
        low_ref[...] = norm_forward(new_rows, norm_ref, self.norm_at)
        self.spread(place, [Gather(place, low_ref, gathered[0], self.gather_sems[0], self.rows)], moment)


class FfnForward(Main):
    def __init__(self, full, w_gate, w_up, w_down, stream, norm, cotangent=None):
        super().__init__()
        self.rows, self.width = stream.shape
        length = full.shape[0]
        self.last = cotangent is not None
        self.big = [full, w_gate, w_up, w_down]
        self.small = [stream, cotangent if self.last else norm[0]]
        self.norm_at = norm and norm[1]
        self.results = [like(stream.shape, F32)]
        hidden = (length, w_gate.shape[1])
        self.kept = [like(hidden, F32), like(hidden, F32), like(hidden, BF)]
        self.gathered = [like(full.shape, BF)]
        self.work = [like(full.shape, BF), like(stream.shape, BF)]

    def compute(self, place, big, small, results, kept, gathered, moment):
        full, w_gate, w_up, w_down = big
        stream_ref = small[0]
        gate_ref, up_ref, act_ref = kept
        part_ref, low_ref = self.work_refs
        gather = None
        if self.last:
            gather = Gather(place, small[1], gathered[0], self.gather_sems[0], self.rows)
            gather.begin()
        self.fetch(0, 1, 2)

        def gates(rows):
            gate = dot_nn(full[rows], w_gate[...])
            up = dot_nn(full[rows], w_up[...])
            gate_ref[rows] = gate
            up_ref[rows] = up
            act_ref[rows] = (gate * jax.nn.sigmoid(gate) * up).astype(BF)

        by_rows(full.shape[0], ROW_BLOCK, gates)
        self.store(0, 1, 2)
        self.fetch(3)
        for at in range(0, self.width, OUT_BLOCK):
            part_ref[:, at : at + OUT_BLOCK] = dot_nt(act_ref[...], w_down[at : at + OUT_BLOCK]).astype(BF)
        moment("ready")
        steps = list(range(1, place.sizes.nc)) if self.last else []

        def meanwhile(name):
            if steps and name in ("sent", "inside1", "inside2"):
                gather.forward(steps.pop(0))
            moment(name)

        total, self.sent = scatter_part(place, part_ref, self.bufs, self.rows, meanwhile)
        new_rows = stream_ref[...] + total
        results[0][...] = new_rows
        if self.last:
            moment("summed")
            for step in steps:
                gather.forward(step)
            moment("spread")
            moment("late")
            gather.end()
            return
        low_ref[...] = norm_forward(new_rows, small[1], self.norm_at)
        self.spread(place, [Gather(place, low_ref, gathered[0], self.gather_sems[0], self.rows)], moment)


class FfnBack(Main):
    names = ["down", "gate", "up"]

    def __init__(self, grad_full, w_gate, w_up, w_down, gates, ups, acts, full, grad, saved, norm):
        super().__init__()
        self.rows, self.width = grad.shape
        self.big = [grad_full, acts, w_down, gates, ups, w_gate, w_up, full]
        self.small, self.norm_at = [grad, saved, norm[0]], norm[1]
        self.results = [like(grad.shape, F32), like((2, self.width), F32)]
        self.kept = [like(w_down.shape, BF), like(w_gate.shape, BF), like(w_up.shape, BF)]
        self.gathered = [like(full.shape, BF)]
        hidden = like(acts.shape, BF)
        self.work = [hidden, hidden, like(full.shape, BF), like(grad.shape, BF)]

    def compute(self, place, big, small, results, kept, gathered, moment):
        grad_full, act_ref, w_down, gate_ref, up_ref, w_gate, w_up, full = big
        grad_ref, saved_ref, norms_ref = small
        new_ref, norm_ref = results
        down_grad, gate_grad, up_grad = kept
        low_gate, low_up, part_ref, grad_low_ref = self.work_refs
        self.grads = {"down": down_grad, "gate": gate_grad, "up": up_grad}

        def weights_of(which, target, left, right, name):
            for at in range(0, self.width, OUT_BLOCK):
                span = slice(at, at + OUT_BLOCK)
                target[span] = dot_tn(left[:, span], right[...]).astype(BF)
            self.store(which)
            moment(name)

        self.fetch(0, 1)
        weights_of(0, down_grad, grad_full, act_ref, "downs")
        self.fetch(2, 3, 4)

        def gates(rows):
            act_grad = dot_nn(grad_full[rows], w_down[...])
            gate, up = gate_ref[rows], up_ref[rows]
            sg = jax.nn.sigmoid(gate)
            low_gate[rows] = (act_grad * up * sg * (1.0 + gate * (1.0 - sg))).astype(BF)
            low_up[rows] = (act_grad * gate * sg).astype(BF)

        by_rows(full.shape[0], ROW_BLOCK, gates)
        self.fetch(5, 6)
        for at in range(0, self.width, OUT_BLOCK):
            span = slice(at, at + OUT_BLOCK)
            part_ref[:, span] = (dot_nt(low_gate[...], w_gate[span]) + dot_nt(low_up[...], w_up[span])).astype(BF)
        moment("ready")
        self.fetch(7)

        def weights(name):
            if name == "sent":
                weights_of(1, gate_grad, full, low_gate, "gates")
            if name == "inside0":
                weights_of(2, up_grad, full, low_up, "ups")
            moment(name)

        total, self.sent = scatter_part(place, part_ref, self.bufs, self.rows, weights)
        inner, gain_grad, shift_grad = norm_back(total, saved_ref[...], norms_ref[self.norm_at : self.norm_at + 1])
        new_rows = grad_ref[...] + inner
        new_ref[...] = new_rows
        grad_low_ref[...] = new_rows.astype(BF)
        norm_ref[0:1] = gain_grad
        norm_ref[1:2] = shift_grad
        self.spread(place, [Gather(place, grad_low_ref, gathered[0], self.gather_sems[0], self.rows)], moment)


class AttnBack(Main):
    names = ["qkv", "out"]

    def __init__(self, grad_full, w_qkv, w_out, kept, full, tables, lse, grad, saved, norm, last):
        super().__init__()
        proj, mixed, q_rot, k_rot = kept
        self.rows, self.width = grad.shape
        self.last = last
        self.big = [grad_full, w_out, q_rot, k_rot, proj, w_qkv, full, mixed]
        self.small, self.norm_at = [*tables, lse, grad, saved, norm[0]], norm[1]
        self.results = [like(grad.shape, F32), like((2, self.width), F32), like((1, w_qkv.shape[1]), F32)]
        self.kept = [like(w_qkv.shape, BF), like(w_out.shape, BF)]
        self.gathered = [] if last else [like(full.shape, BF)]
        self.work = [like(proj.shape, BF), like(full.shape, BF), like(grad.shape, BF), like(mixed.shape, BF)]

    def compute(self, place, big, small, results, kept, gathered, moment):
        grad_full, w_out, q_ref, k_ref, proj_ref, w_qkv, full, mix_ref = big
        col_ref, row_ref, cos_ref, sin_ref, lse_ref, grad_ref, saved_ref, norms_ref = small
        new_ref, norm_ref, bias_ref = results
        qkv_ref, out_ref = kept
        self.norm_ref, self.bias_ref, self.rows_ref = norm_ref, bias_ref, self.work_refs[2]
        low_ref, part_ref, grad_low_ref, mix_grad_ref = self.work_refs
        ns = place.sizes.ns
        width = w_out.shape[1] // ns
        self.grads = {"qkv": qkv_ref, "out": out_ref}
        self.fetch(0, 1)

        def mixed_grad(rows):
            mix_grad_ref[rows] = dot_nn(grad_full[rows], w_out[...]).astype(BF)

        by_rows(full.shape[0], ROW_BLOCK, mixed_grad)
        self.fetch(2, 3, 4)
        allowed = allowed_of(col_ref[...], row_ref[...])
        cosine, sine = cos_ref[...], sin_ref[...]
        scaling = HD ** (-0.5)
        for b in range(ns):
            parts = [[], [], []]
            base = 3 * width * b
            for h in range(width // HD):
                span = slice(b * width + h * HD, b * width + (h + 1) * HD)
                at = b * (width // HD) + h
                q_rows, k_rows, out_grad = q_ref[:, span], k_ref[:, span], mix_grad_ref[:, span]
                scores = jnp.where(allowed, scaling * dot_nt(q_rows, k_rows), NEGATIVE)
                probs = jnp.exp(scores - lse_ref[:, at : at + 1])
                first = base + 2 * width + h * HD
                prob_grad = dot_nt(out_grad, proj_ref[:, first : first + HD])
                inner = jnp.sum(probs * prob_grad, -1, keepdims=True)
                score_low = (probs * (prob_grad - inner)).astype(BF)
                parts[0].append(scaling * dot_nn(score_low, k_rows))
                parts[1].append(scaling * dot_tn(score_low, q_rows))
                parts[2].append(dot_tn(probs.astype(BF), out_grad))
            for at in range(3):
                values = jnp.concatenate(parts[at], axis=1)
                if at < 2:
                    values = values * cosine - swap_lanes(values) * sine
                low = values.astype(BF)
                lanes = slice(base + at * width, base + (at + 1) * width)
                low_ref[:, lanes] = low
                bias_ref[:, lanes] = jnp.sum(low.astype(F32), 0, keepdims=True)
        self.fetch(5)
        for at in range(0, self.width, OUT_BLOCK):
            part_ref[:, at : at + OUT_BLOCK] = dot_nt(low_ref[...], w_qkv[at : at + OUT_BLOCK]).astype(BF)
        moment("ready")
        self.fetch(6, 7)

        def weights(name):
            if name == "sent":
                for at in range(0, self.width, OUT_BLOCK):
                    span = slice(at, at + OUT_BLOCK)
                    qkv_ref[span] = dot_tn(full[:, span], low_ref[...]).astype(BF)
                    out_ref[span] = dot_tn(grad_full[:, span], mix_ref[...]).astype(BF)
                self.store(0, 1)
                moment("attns")
            moment(name)

        total, self.sent = scatter_part(place, part_ref, self.bufs, self.rows, weights)
        inner, gain_grad, shift_grad = norm_back(total, saved_ref[...], norms_ref[self.norm_at : self.norm_at + 1])
        new_rows = grad_ref[...] + inner
        new_ref[...] = new_rows
        norm_ref[0:1] = gain_grad
        norm_ref[1:2] = shift_grad
        grad_low_ref[...] = new_rows.astype(BF)
        if self.last:
            for name in ("summed", "spread", "late"):
                moment(name)
            return
        self.spread(place, [Gather(place, grad_low_ref, gathered[0], self.gather_sems[0], self.rows)], moment)


class Alone:
    kinds, ins, in_specs, outs, out_specs = (), [], [], [], []

    def scratch(self, sizes):
        return []

    def run(self, place, ins, outs, scratch, moment):
        moment("begin")


class Start:
    kinds = ("mate", "ctx", "fsdp", "twin")

    def __init__(self, sizes, small, hidden, cotangent, piece, q_sub, layers, chains, following):
        self.sizes, self.piece, self.chains, self.following = sizes, piece, chains, following
        self.q_sub, self.layers = q_sub, layers
        lines, lanes = small.shape
        count, self.width = hidden.shape
        self.rows = count // (sizes.ns * sizes.nk)
        group = sizes.nc * sizes.nk * self.rows
        self.ins, self.in_specs = [small, hidden, cotangent], [VMEM_SPEC] * 3
        self.outs = [
            like((sizes.nf, sizes.nc * lines, lanes), F32),
            like((lines, lanes), F32),
            like((lines, self.width), F32),
            like((self.rows, self.width), F32),
            like((self.rows, self.width), BF),
            like((group, 1), jnp.int32),
            like((1, group), jnp.int32),
            like((group, q_sub), F32),
            like((group, q_sub), F32),
            like((layers, sizes.ns * 3 * q_sub), F32),
            like((group, self.width), BF),
        ]
        self.out_specs = [VMEM_SPEC] * 10 + [ANY_SPEC]

    def scratch(self, sizes):
        others = max(sizes.nf - 1, 1)
        small = [DMA((sizes.nc,)), DMA((sizes.nc,)), DMA((others,)), DMA((others,)), DMA(()), DMA(())]
        return small + [pltpu.VMEM((self.rows, self.width), BF)] + Gather.scratch(sizes)

    def run(self, place, ins, outs, scratch, moment):
        sizes, rows, width = self.sizes, self.rows, self.width
        small_ref, hidden_ref, cotangent_ref = ins
        all_ref, twin_ref, norm_ref, stream_ref, grad_ref = outs[:5]
        full_ref = outs[10]
        cs, cr, fs, fr, ts, tr = scratch[:6]
        low_ref = scratch[6]
        lines = small_ref.shape[0]

        def line_of(c):
            return pl.ds(pl.multiple_of(c * lines, lines), lines)

        to_context = [
            push(small_ref, all_ref.at[0, line_of(place.c)], cs.at[step], cr.at[step], place.ahead(step))
            for step in range(1, sizes.nc)
        ]
        to_twin = push(small_ref, twin_ref, ts, tr, place.twin())
        moment("begin")
        for copy in to_context + [to_twin]:
            copy.start()
        for exchange, _ in self.chains:
            exchange.start()
        all_ref[0, line_of(place.c)] = small_ref[...]
        own_rows = pl.ds(pl.multiple_of((place.s * sizes.nk + place.k) * rows, rows), rows)
        part = width // sizes.nf
        for df in range(sizes.nf):
            lanes = pl.ds(pl.multiple_of(lax.rem(place.f + df, sizes.nf) * part, part), part)
            stream_ref[:, df * part : (df + 1) * part] = hidden_ref[own_rows, lanes].astype(F32)
            grad_ref[:, df * part : (df + 1) * part] = cotangent_ref[own_rows, lanes]
        unit_rows, _ = unit_rows_of(stream_ref[...])
        for copy in to_context:
            copy.wait()
        to_across = [
            push(all_ref.at[0], all_ref.at[sizes.nf - step], fs.at[step - 1], fr.at[step - 1], place.across(step))
            for step in range(1, sizes.nf)
        ]
        for copy in to_across:
            copy.start()
        for copy in to_across + [to_twin]:
            copy.wait()
        for df in range(sizes.nf):
            for c in range(sizes.nc):
                at = (df * sizes.nc + c) * self.piece
                norm_ref[:, at : at + self.piece] = all_ref[df, c * lines : (c + 1) * lines, : self.piece]
        low_ref[...] = (unit_rows * norm_ref[0:1] + norm_ref[1:2]).astype(BF)
        gather = Gather(place, low_ref, full_ref, scratch[7:12], rows)
        for exchange, spread in self.chains:
            exchange.wait_own()
            spread.first(place.c)
        for step in range(1, sizes.nc):
            for exchange, spread in self.chains:
                exchange.wait_from(step)
                spread.first(lax.rem(place.c + sizes.nc - step, sizes.nc))
        gather.begin()
        for exchange in self.following:
            exchange.start()
        self.tables(place, small_ref, all_ref, twin_ref, *outs[5:10])
        for step in range(sizes.nc):
            for _, chain in self.chains:
                chain.second(lax.rem(place.c + sizes.nc - step, sizes.nc))
            if step:
                gather.forward(step)
        gather.end()
        for exchange, spread in self.chains:
            exchange.wait_sent()
            for block in range(sizes.nc):
                spread.finish(block)
        for exchange in self.following:
            exchange.finish()


    def tables(self, place, small_ref, all_ref, twin_ref, col_ref, row_ref, cos_ref, sin_ref, bias_ref):
        sizes, q_sub = self.sizes, self.q_sub
        lines = small_ref.shape[0]
        shard = sizes.nk * self.rows
        for c in range(sizes.nc):
            mine = jnp.zeros((1, shard), F32)
            for at in range(sizes.ns):
                line = c * lines + at
                found = all_ref[0, line : line + 1, self.piece : self.piece + shard]
                mine = jnp.where(place.s == at, found, mine)
            row_ref[:, c * shard : (c + 1) * shard] = mine.astype(jnp.int32)
        length = row_ref.shape[1]
        row = row_ref[...].astype(F32)
        at_row = lax.broadcasted_iota(jnp.int32, (length, length), 0)
        at_col = lax.broadcasted_iota(jnp.int32, (length, length), 1)
        col = jnp.sum(jnp.where(at_row == at_col, row, 0.0), -1, keepdims=True)
        col_ref[...] = col.astype(jnp.int32)
        before = jnp.sum(jnp.where(row < col, 1.0, 0.0), -1, keepdims=True)
        places = lax.broadcasted_iota(jnp.int32, (length, 1), 0).astype(F32)
        lane = lax.broadcasted_iota(jnp.int32, (1, q_sub), 1) % HD
        turn = jnp.exp((lane % (ROT // 2)).astype(F32) * (-2.0 * math.log(ROPE_BASE) / ROT))
        angles = (places - before) * jnp.where(lane < ROT, turn, 0.0)
        sine = jnp.sin(angles)
        cos_ref[...] = jnp.cos(angles)
        sin_ref[...] = jnp.where(lane < ROT // 2, -sine, sine)
        for layer in range(self.layers):
            for ds, source in enumerate((small_ref, twin_ref)):
                for at in range(3):
                    line = 3 * layer + at
                    lanes = slice((ds * 3 + at) * q_sub, (ds * 3 + at + 1) * q_sub)
                    bias_ref[layer : layer + 1, lanes] = source[line : line + 1, self.piece + shard :]


class Guest(Rider):
    def __init__(self, rider):
        self.kinds, self.ins, self.outs, self.sems = rider.kinds, rider.ins, rider.outs, rider.sems
        self.rider = rider

    def bind(self, *refs):
        self.rider.bind(*refs)


def comm_kernel(sizes, main, riders, kinds, layout, *refs):
    cuts, at = [], 0
    for size in layout:
        cuts.append(refs[at : at + size])
        at += size
    count = len(riders)
    ins, outs, scratch = cuts[: count + 1], cuts[count + 1 : 2 * count + 2], cuts[2 * count + 2 :]
    place = Place(sizes)
    for i, rider in enumerate(riders):
        rider.bind(place, ins[i + 1], outs[i + 1], scratch[i + 1], main)
    count = greet(place, kinds)

    def moment(name):
        if name == "begin":
            pl.semaphore_wait(pltpu.get_barrier_semaphore(), count)
        for rider in riders:
            rider.at(name)

    main.run(place, ins[0], outs[0], scratch[0], moment)
    moment("end")


def comm_call(sizes, collective_id, main, riders=(), micros=50):
    kinds = set(main.kinds)
    for rider in riders:
        kinds |= set(rider.kinds)
    main_scratch = main.scratch(sizes)
    operands, in_specs = list(main.ins), list(main.in_specs)
    outs, out_specs = list(main.outs), list(main.out_specs)
    scratch = list(main_scratch)
    aliases = {}
    for rider in riders:
        if rider.aliased:
            aliases[len(operands)] = len(outs)
        operands += rider.ins
        in_specs += [ANY_SPEC] * len(rider.ins)
        outs += rider.outs
        out_specs += [ANY_SPEC] * len(rider.outs)
        scratch += rider.sems
    layout = [len(main.ins)] + [len(rider.ins) for rider in riders]
    layout += [len(main.outs)] + [len(rider.outs) for rider in riders]
    layout += [len(main_scratch)] + [len(rider.sems) for rider in riders]
    results = pl.pallas_call(
        functools.partial(comm_kernel, sizes, main, riders, kinds, layout),
        out_shape=outs,
        in_specs=in_specs,
        out_specs=out_specs,
        scratch_shapes=scratch,
        input_output_aliases=aliases,
        compiler_params=pltpu.CompilerParams(
            collective_id=collective_id, has_side_effects=True, vmem_limit_bytes=VMEM_BYTES
        ),
        cost_estimate=pl.CostEstimate(flops=0, bytes_accessed=micros * 3 * MIB, transcendentals=0),
    )(*operands)
    groups, at = [], 0
    for size in [len(main.outs)] + [len(rider.outs) for rider in riders]:
        groups.append(list(results[at : at + size]))
        at += size
    return groups[0], groups[1:]


def finish_kernel(count, hidden, *refs):
    ins, (qkv_out, out_out, gate_up_out, down_out) = refs[: 5 * count], refs[5 * count :]
    triple, rows, q_cols = qkv_out.shape[1:]
    for layer in range(count):

        @pl.when(pl.program_id(0) == layer)
        def _():
            qkv, out, gate, up, down = ins[5 * layer : 5 * layer + 5]

            def some(span):
                for at in range(triple):
                    qkv_out[0, at, span] = qkv[span, at * q_cols : (at + 1) * q_cols].astype(F32)
                out_out[0, span] = out[span].astype(F32)
                gate_up_out[0, span, 0] = gate[span, :hidden].astype(F32)
                gate_up_out[0, span, 1] = up[span, :hidden].astype(F32)
                down_out[0, span] = down[span, :hidden].astype(F32)

            by_rows(rows, 64, some)


def finish(grads, q_cols, hidden):
    count = len(grads)
    rows = grads[0][0].shape[0]
    shapes = [(3, rows, q_cols), (rows, q_cols), (rows, 2, hidden), (rows, hidden)]

    def block(shape):
        return pl.BlockSpec((1,) + shape, lambda layer: (layer,) + (0,) * len(shape))

    return pl.pallas_call(
        functools.partial(finish_kernel, count, hidden),
        grid=(count,),
        out_shape=[jax.ShapeDtypeStruct((count,) + shape, F32) for shape in shapes],
        in_specs=[VMEM_SPEC] * (5 * count),
        out_specs=[block(shape) for shape in shapes],
        compiler_params=pltpu.CompilerParams(vmem_limit_bytes=VMEM_BYTES),
    )(*[one for layer in grads for one in layer])


def body(
    mesh,
    hidden_in,
    segment_ids,
    norm_gains,
    norm_shifts,
    qkv_weight,
    qkv_bias,
    out_weight,
    gate_up_weight,
    down_weight,
    cotangent,
):
    ns, shard_rows, width = hidden_in.shape
    sizes = Sizes(mesh, ns)
    nf, nc, nk, nt = sizes.nf, sizes.nc, sizes.nk, sizes.nt
    f, c, t = lax.axis_index("fsdp"), lax.axis_index("context"), lax.axis_index("tensor")
    s = t // nk
    layers = qkv_weight.shape[0]
    rows = shard_rows // nk
    part = width // nf
    piece = part // nc
    q_cols = qkv_weight.shape[3]
    q_sub = q_cols // nc
    hidden = gate_up_weight.shape[3]
    f_sub = -(-hidden // (nc * TILE)) * TILE
    f_cols = nc * f_sub

    qkv_flat = qkv_weight.transpose(0, 2, 1, 3).reshape(layers * 3 * piece, q_cols)
    out_flat = out_weight.reshape(layers * piece, q_cols)
    fill = ((0, 0), (0, f_cols - hidden))
    down_flat = jnp.pad(down_weight.reshape(layers * piece, hidden), fill)
    gate_up_flat = jnp.pad(gate_up_weight, ((0, 0), (0, 0)) + fill).reshape(layers * piece, 2 * f_cols)

    def exchange(name, layer, when="begin", finish="end"):
        first = layer * piece
        array, corners, sub = {
            "qkv": (qkv_flat, [((3 * layer + at) * piece, 0) for at in range(3)], q_sub),
            "out": (out_flat, [(first, 0)], q_sub),
            "gate": (gate_up_flat, [(first, 0)], f_sub),
            "up": (gate_up_flat, [(first, f_cols)], f_sub),
            "down": (down_flat, [(first, 0)], f_sub),
        }[name]
        return WeightExchange(sizes, piece, array, corners, sub, when, finish)

    norms = jnp.stack([norm_gains, norm_shifts], axis=2).reshape(4 * layers, piece).astype(F32)
    own_bias = lax.dynamic_slice_in_dim(qkv_bias, c * q_sub, q_sub, 2).reshape(3 * layers, q_sub).astype(F32)
    lines = -(-max(4 * layers, 3 * layers, ns) // 8) * 8

    def lined(value):
        return jnp.pad(value, ((0, lines - value.shape[0]), (0, 0)))

    small = jnp.concatenate([lined(norms), lined(segment_ids.astype(F32)), lined(own_bias)], axis=1)
    chains = []
    for name in ("qkv", "out"):
        moved = exchange(name, 0, finish=None)
        chains.append((moved, Spread(sizes, moved, blocks=nc, steps=(None, None))))
    following = [exchange(name, 0, finish=None) for name in ("gate", "up")]
    start = Start(
        sizes,
        small,
        hidden_in.reshape(ns * shard_rows, width),
        cotangent.reshape(ns * shard_rows, width),
        piece,
        q_sub,
        layers,
        chains,
        following,
    )
    guests = [Guest(one) for chain in chains for one in chain] + [Guest(one) for one in following]
    results, extra = comm_call(sizes, 1, start, guests, 80)
    norm_rows, stream, grad_low = results[2:5]
    tables, bias_rows, full_one = results[5:9], results[9], results[10]
    w_qkv, w_out, gate_mine, up_mine = (extra[at][0] for at in (1, 3, 4, 5))

    def norm_of(layer, which):
        return (norm_rows, (layer * 2 + which) * 2)

    kept = []
    gate_own = None
    for layer in range(layers):
        more = layer + 1 < layers
        down_first = exchange("down", layer, finish=None)
        riders = [Spread(sizes, gate_mine) if gate_own is None else SpreadRelay(sizes, gate_own), Spread(sizes, up_mine)]
        riders += [down_first, Spread(sizes, down_first, steps=("inside0", "spread"))]
        if more:
            riders += [exchange("qkv", layer + 1, "spread"), exchange("out", layer + 1, "spread")]
        main = AttnForward(
            full_one, w_qkv, w_out, (bias_rows, layer), tables, stream, norm_of(layer, 1)
        )
        results, extra = comm_call(sizes, 2 + 2 * layer, main, riders, 85)
        middle, lse, proj, mixed, q_rot, k_rot, full_two = results
        w_gate, w_up, w_down = extra[0][0], extra[1][0], extra[3][0]
        attn_kept = (full_one, w_qkv, w_out, (proj, mixed, q_rot, k_rot), lse, stream)
        if more:
            gate_first = exchange("gate", layer + 1, finish=None)
            riders = [Spread(sizes, extra[4][0]), Spread(sizes, extra[5][0])]
            riders += [gate_first, SpreadOwn(sizes, gate_first, blocks=nc, steps=("summed",))]
            riders.append(exchange("up", layer + 1, "spread"))
            main = FfnForward(
                full_two, w_gate, w_up, w_down, middle, norm_of(layer + 1, 0)
            )
        else:
            riders = []
            main = FfnForward(full_two, w_gate, w_up, w_down, middle, None, grad_low)
        results, extra = comm_call(sizes, 3 + 2 * layer, main, riders, 55)
        stream, gates, ups, acts, full = results
        kept.append(attn_kept + (full_two, w_gate, w_up, w_down, gates, ups, acts, middle))
        if more:
            full_one = full
            w_qkv, w_out, _, gate_own, up_mine = (one[0] for one in extra)
        else:
            grad_full = full

    first_id = 2 + 2 * layers
    stream_out = stream
    grad = grad_low.astype(F32)
    firsts, totals = {}, {}
    done, norm_grads, bias_grads = {}, {}, {}
    calls = [0]

    def sub_of(name):
        return q_sub if name in ("qkv", "out") else f_sub

    def run(main, steps, others, micros):
        riders, after = [], []
        here = {}

        def ride(rider, what, name):
            here[(what, name)] = rider
            riders.append(rider)
            after.append((what, name))

        for what, name, layer, when in steps:
            at = (name, layer)
            if what == "first":
                ride(GradFirst(sizes, name, *main.kept[main.names.index(name)].shape, when), what, at)
            elif what == "middle":
                ride(GradMiddle(sizes, here.get(("first", at)) or firsts[at], when), what, at)
            else:
                ride(GradExchange(sizes, here.get(("middle", at)) or totals[at], sub_of(name), when), what, at)
        for name, rider in others:
            ride(rider, "other", name)
        results, extra = comm_call(sizes, first_id + calls[0], main, riders, micros)
        calls[0] += 1
        for (what, at), out in zip(after, extra):
            if what == "first":
                firsts[at] = (results[len(main.results) + main.names.index(at[0])], *out)
            elif what == "middle":
                totals[at] = out[0]
            else:
                done[at] = out[0]
        return results

    attn, ffn = ("qkv", "out"), ("gate", "up")
    for layer in range(layers - 1, -1, -1):
        full_one, w_qkv, w_out, attn_kept, lse, stream, full_two, w_gate, w_up, w_down, gates, ups, acts, middle = kept[
            layer
        ]
        main = FfnBack(grad_full, w_gate, w_up, w_down, gates, ups, acts, full_two, grad, middle, norm_of(layer, 1))
        top = layer + 1 == layers
        steps, others = [], []
        if top:
            others.append(("block_out", share_rows(sizes, stream_out.astype(BF))))
        else:
            steps += [("exchange", "gate", layer + 1, "begin"), ("exchange", "up", layer + 1, "spread")]
            steps += [("exchange", name, layer + 1, "late") for name in attn]
        steps += [("first", "down", layer, "downs"), ("first", "gate", layer, "gates"), ("first", "up", layer, "ups")]
        steps += [("middle", "down", layer, ("summed", "summed", "late"))]
        if not top:
            steps += [("middle", name, layer, ("late", "late", "end")) for name in ffn]
        grad, norm_grads[(layer, 1)], _, _, _, middle_full = run(main, steps, others, 60)
        main = AttnBack(
            middle_full, w_qkv, w_out, attn_kept, full_one, tables, lse, grad, stream, norm_of(layer, 0), layer == 0
        )
        steps, others = [("exchange", "down", layer, "begin")], []
        if not top:
            steps += [("exchange", "gate", layer, "begin"), ("exchange", "up", layer, "inside2")]
        if layer == 0:
            none = jnp.zeros((2, width), F32)
            pairs = [[norm_grads.get((at, which), none) for which in range(2)] for at in range(layers)]
            lines = jnp.stack([jnp.stack(pair, 1) for pair in pairs], 1).reshape(4 * layers, width)
            none = jnp.zeros((1, ns * 3 * q_sub), F32)
            bias = jnp.concatenate([bias_grads.get(at, none) for at in range(layers)]).reshape(layers, ns, 3, q_sub)
            bias = bias.transpose(1, 0, 2, 3).reshape(ns, 3 * layers, q_sub)
            bias = jnp.pad(bias, ((0, 0), (0, -3 * layers % 8), (0, 0)))
            others = [
                ("input_grad", MainRows(sizes, rows, width, "summed")),
                ("norm", NormSum(sizes, lines, (0, 2 * layers), piece, ("summed", "spread"))),
                ("bias", BiasSum(sizes, bias, 3, ("attns", "inside0"))),
            ]
            steps += [("first", name, 0, "attns") for name in attn]
            steps += [("middle", name, 0, ("inside0", "inside0", "inside2")) for name in attn]
            steps += [("exchange", name, 0, "inside2") for name in attn]
        else:
            steps += [("middle", name, layer, ("begin", "inside0", "late")) for name in (ffn if top else ())]
            steps += [("first", name, layer, "attns") for name in attn]
            steps += [("middle", name, layer, ("spread", "spread", "late")) for name in attn]
        results = run(main, steps, others, 60)
        grad, norm_grads[(layer, 0)], bias_grads[layer] = results[:3]
        if layer > 0:
            grad_full = results[5]
    block_out = done["block_out"].reshape(ns, shard_rows, width)
    input_grad = done["input_grad"].reshape(ns, shard_rows, width).astype(F32)
    norm_total = done["norm"].reshape(2, layers, 2, piece)
    bias_total = done["bias"][:, : 3 * layers].reshape(nc, layers, 3, q_sub)
    bias_total = bias_total.transpose(1, 2, 0, 3).reshape(layers, 3, q_cols)

    grads = [[done[(name, layer)] for name in ("qkv", "out", "gate", "up", "down")] for layer in range(layers)]
    qkv_grad, out_grad, gate_up_grad, down_grad = finish(grads, q_cols, hidden)
    return (
        block_out,
        input_grad,
        norm_total[0],
        norm_total[1],
        qkv_grad.transpose(0, 2, 1, 3),
        bias_total,
        out_grad,
        gate_up_grad,
        down_grad,
    )


def solution(mesh):
    return jax.shard_map(
        functools.partial(body, mesh),
        mesh=mesh,
        in_specs=(
            P("fsdp", "context", None),
            P("fsdp", "context"),
            P(None, None, ("fsdp", "context")),
            P(None, None, ("fsdp", "context")),
            P(None, ("fsdp", "context"), None, "tensor"),
            P(None, None, "tensor"),
            P(None, ("fsdp", "context"), "tensor"),
            P(None, ("fsdp", "context"), None, "tensor"),
            P(None, ("fsdp", "context"), "tensor"),
            P("fsdp", "context", None),
        ),
        out_specs=(
            P("fsdp", "context", None),
            P("fsdp", "context", None),
            P(None, None, ("fsdp", "context")),
            P(None, None, ("fsdp", "context")),
            P(None, ("fsdp", "context"), None, "tensor"),
            P(None, None, "tensor"),
            P(None, ("fsdp", "context"), "tensor"),
            P(None, ("fsdp", "context"), None, "tensor"),
            P(None, ("fsdp", "context"), "tensor"),
        ),
        check_vma=False,
    )
```

```python
import functools
import math

import jax
import jax.numpy as jnp
from jax import lax
from jax.experimental import pallas as pl
from jax.experimental.pallas import tpu as pltpu
from jax.sharding import PartitionSpec as P

HD = 64
ROT = 16
EPS = 1e-05
ROPE_BASE = 10000.0
NEGATIVE = -1e30
MESH = pl.DeviceIdType.MESH
BF = jnp.bfloat16
F32 = jnp.float32
MIB = 2**20
TILE = 128
VMEM_BYTES = 58 * MIB


def dot_nn(a, b):
    return jnp.dot(a, b, preferred_element_type=F32)


def dot_nt(a, b):
    return lax.dot_general(a, b, (((1,), (1,)), ((), ())), preferred_element_type=F32)


def dot_tn(a, b):
    return lax.dot_general(a, b, (((0,), (0,)), ((), ())), preferred_element_type=F32)


class Sizes:
    def __init__(self, mesh, ns):
        self.nf, self.nc, self.nt = mesh.shape["fsdp"], mesh.shape["context"], mesh.shape["tensor"]
        self.ns = ns
        self.nk = self.nt // ns


class Place:
    def __init__(self, sizes):
        self.sizes = sizes
        self.f = lax.axis_index("fsdp")
        self.c = lax.axis_index("context")
        self.t = lax.axis_index("tensor")
        self.s, self.k = self.t // sizes.nk, lax.rem(self.t, sizes.nk)

    def mate(self):
        return {"tensor": self.t + 1 - 2 * self.k}

    def twin(self):
        return {"tensor": self.t + self.sizes.nk * (1 - 2 * self.s)}

    def right(self):
        return {"context": self.c + 1}

    def left(self):
        return {"context": self.c - 1}

    def ahead(self, step):
        return {"context": lax.rem(self.c + step, self.sizes.nc)}

    def across(self, step):
        return {"fsdp": lax.rem(self.f + step, self.sizes.nf)}

    def plane(self, df, dt):
        return {"fsdp": lax.rem(self.f + df, self.sizes.nf), "tensor": lax.rem(self.t + dt, self.sizes.nt)}


def greet(place, kinds):
    barrier = pltpu.get_barrier_semaphore()
    nc, nf = place.sizes.nc, place.sizes.nf

    def signal(device):
        pl.semaphore_signal(barrier, inc=1, device_id=device, device_id_type=MESH)

    count = 0
    if "plane" in kinds:
        for df in range(nf):
            for dt in range(place.sizes.nt):
                if df or dt:
                    signal(place.plane(df, dt))
        count += nf * place.sizes.nt - 1
        kinds = set(kinds) - {"mate", "fsdp", "twin"}
    if "mate" in kinds:
        signal(place.mate())
        count += 1
    if "ctx" in kinds:
        for step in range(1, nc):
            signal(place.ahead(step))
        count += nc - 1
    elif "line" in kinds:

        @pl.when(place.c > 0)
        def _():
            signal(place.left())

        @pl.when(place.c < nc - 1)
        def _():
            signal(place.right())

        count += jnp.minimum(place.c, 1) + jnp.minimum(nc - 1 - place.c, 1)
    if "fsdp" in kinds:
        for step in range(1, nf):
            signal(place.across(step))
        count += nf - 1
    if "twin" in kinds:
        signal(place.twin())
        count += 1
    return count


def push(src, dst, send, recv, device):
    return pltpu.make_async_remote_copy(
        src_ref=src, dst_ref=dst, send_sem=send, recv_sem=recv, device_id=device, device_id_type=MESH
    )


DMA = pltpu.SemaphoreType.DMA
VMEM_SPEC = pl.BlockSpec(memory_space=pltpu.VMEM)
ANY_SPEC = pl.BlockSpec(memory_space=pl.ANY)


HALVES = 2


class Gather:
    def __init__(self, place, own, out, sems, rows):
        self.place, self.own, self.out, self.rows = place, own, out, rows
        self.piece = rows // HALVES
        self.local, self.line_send, self.line_recv, self.mate_send, self.mate_recv = sems

    @staticmethod
    def scratch(sizes):
        nc = sizes.nc
        return [DMA(()), DMA((2, nc, HALVES)), DMA((nc, HALVES)), DMA((nc, HALVES)), DMA((nc, HALVES))]

    def slot(self, source, k, half):
        at = (source * self.place.sizes.nk + k) * self.rows + half * self.piece
        return self.out.at[pl.ds(pl.multiple_of(at, self.piece), self.piece)]

    def origin(self, source, half, first):
        if first:
            return self.own.at[pl.ds(half * self.piece, self.piece)]
        return self.slot(source, self.place.k, half)

    def line(self, source, half, device, first, way):
        return push(
            self.origin(source, half, first),
            self.slot(source, self.place.k, half),
            self.line_send.at[way, source, half],
            self.line_recv.at[source, half],
            device,
        )

    def pass_on(self, source, half, first):
        return push(
            self.origin(source, half, first),
            self.slot(source, self.place.k, half),
            self.mate_send.at[source, half],
            self.mate_recv.at[source, half],
            self.place.mate(),
        )

    def keep(self):
        at = (self.place.c * self.place.sizes.nk + self.place.k) * self.rows
        target = self.out.at[pl.ds(pl.multiple_of(at, self.rows), self.rows)]
        return pltpu.make_async_copy(self.own, target, self.local)

    def begin(self):
        place, c, nc = self.place, self.place.c, self.place.sizes.nc
        for half in range(HALVES):

            @pl.when(c < nc - 1)
            def _():
                self.line(c, half, place.right(), True, 0).start()

            @pl.when(c > 0)
            def _():
                self.line(c, half, place.left(), True, 1).start()

        for half in range(HALVES):
            self.pass_on(c, half, True).start()
        self.keep().start()

    def forward(self, step):
        place, c, nc = self.place, self.place.c, self.place.sizes.nc
        source, other = c - step, c + step
        for half in range(HALVES):

            @pl.when(source >= 0)
            def _():
                self.line(source, half, place.left(), False, 0).wait_recv()

                @pl.when(c < nc - 1)
                def _():
                    self.line(source, half, place.right(), False, 0).start()

                self.pass_on(source, half, False).start()

            @pl.when(other <= nc - 1)
            def _():
                self.line(other, half, place.right(), False, 1).wait_recv()

                @pl.when(c > 0)
                def _():
                    self.line(other, half, place.left(), False, 1).start()

                self.pass_on(other, half, False).start()

    def end(self):
        place, c, nc = self.place, self.place.c, self.place.sizes.nc
        self.keep().wait()
        for source in range(nc):
            for half in range(HALVES):
                arrival = self.slot(source, 1 - place.k, half)
                push(
                    arrival, arrival, self.mate_send.at[source, half], self.mate_recv.at[source, half], place.mate()
                ).wait_recv()
                self.pass_on(source, half, False).wait_send()

                @pl.when((source <= c) & (c < nc - 1))
                def _():
                    self.line(source, half, place.right(), False, 0).wait_send()

                @pl.when((source >= c) & (c > 0))
                def _():
                    self.line(source, half, place.left(), False, 1).wait_send()


def scatter_part(place, part_ref, bufs, rows, moment):
    nc, nk, c, k = place.sizes.nc, place.sizes.nk, place.c, place.k
    piece = rows // HALVES
    mate_buf, to_right, to_left, from_left, from_right = bufs[:5]
    mate_send, mate_recv, right_send, right_recv, left_send, left_recv = bufs[5:]

    def block(dest, kk):
        return part_ref.at[pl.ds(pl.multiple_of((dest * nk + kk) * rows, rows), rows)]

    def mate_copy(dest):
        return push(
            block(dest, 1 - k), mate_buf.at[dest], mate_send.at[dest], mate_recv.at[dest], place.mate()
        )

    def lines(half):
        return slice(half * piece, (half + 1) * piece)

    def right_copy(dest, half):
        return push(
            to_right.at[dest, lines(half)],
            from_left.at[dest, lines(half)],
            right_send.at[dest, half],
            right_recv.at[dest, half],
            place.right(),
        )

    def left_copy(dest, half):
        return push(
            to_left.at[dest, lines(half)],
            from_right.at[dest, lines(half)],
            left_send.at[dest, half],
            left_recv.at[dest, half],
            place.left(),
        )

    def each(visit_right, visit_left, count, after=lambda step: None):
        for step in range(nc - 1):
            far = nc - 1 - step
            for half in range(count):

                @pl.when(far > c)
                def _():
                    visit_right(far, half)

                @pl.when(step < c)
                def _():
                    visit_left(step, half)

            after(step)

    def send_mate(dest, half):
        mate_copy(dest).start()

    each(send_mate, send_mate, 1)
    mate_copy(c).start()
    moment("sent")

    def chip_sum(dest, half):
        if half == 0:
            mate_copy(dest).wait_recv()
        at = pl.multiple_of((dest * nk + k) * rows + half * piece, piece)
        return part_ref[pl.ds(at, piece)].astype(F32) + mate_buf[dest, lines(half)].astype(F32)

    def pass_right(dest, half):
        total = chip_sum(dest, half)
        to_right[dest, lines(half)] = total.astype(BF)

        @pl.when(c > 0)
        def _():
            right_copy(dest, half).wait_recv()
            to_right[dest, lines(half)] = (total + from_left[dest, lines(half)].astype(F32)).astype(BF)

        right_copy(dest, half).start()

    def pass_left(dest, half):
        total = chip_sum(dest, half)
        to_left[dest, lines(half)] = total.astype(BF)

        @pl.when(c < nc - 1)
        def _():
            left_copy(dest, half).wait_recv()
            to_left[dest, lines(half)] = (total + from_right[dest, lines(half)].astype(F32)).astype(BF)

        left_copy(dest, half).start()

    def inside(step):
        for at in range(3):
            if at * (nc - 1) // 3 == step:
                moment("inside%d" % at)

    each(pass_right, pass_left, HALVES, inside)
    totals = []
    for half in range(HALVES):
        total = chip_sum(c, half)

        @pl.when(c > 0)
        def _():
            right_copy(c, half).wait_recv()

        @pl.when(c < nc - 1)
        def _():
            left_copy(c, half).wait_recv()

        total = total + jnp.where(c > 0, from_left[c, lines(half)].astype(F32), 0.0)
        totals.append(total + jnp.where(c < nc - 1, from_right[c, lines(half)].astype(F32), 0.0))
    def sent():
        for dest in range(nc):
            mate_copy(dest).wait_send()
            for half in range(HALVES):

                @pl.when(dest > c)
                def _():
                    right_copy(dest, half).wait_send()

                @pl.when(dest < c)
                def _():
                    left_copy(dest, half).wait_send()

    return jnp.concatenate(totals, 0), sent


def scatter_scratch(sizes, rows, width):
    nc = sizes.nc
    return [pltpu.VMEM((nc, rows, width), BF) for _ in range(5)] + [DMA((nc,)) for _ in range(2)] + [
        DMA((nc, HALVES)) for _ in range(4)
    ]


N_SCATTER = 11


class Rider:
    kinds = ()
    ins, outs, sems = [], [], []
    aliased = False

    def bind(self, place, ins, outs, sems, main):
        self.place, self.r_ins, self.r_outs, self.r_sems, self.main = place, ins, outs, sems, main

    def at(self, moment):
        pass


class Exchange(Rider):
    kinds = ("ctx",)

    def __init__(self, sizes, ins, out, pieces, rows, sub, when="begin", finish="end"):
        self.ins, self.outs, self.pieces, self.when, self.last = ins, [out], pieces, when, finish
        count = max(sizes.nc - 1, 1)
        self.sub = sub
        self.sems = [DMA(()), DMA((count,)), DMA((count,)), pltpu.VMEM((rows, sub * len(pieces)), BF)]

    def at(self, moment):
        if moment == self.when:
            self.start()
        if moment == self.last:
            self.finish()

    def start(self):
        place, nc = self.place, self.place.sizes.nc
        local, send, recv, held = self.r_sems
        for step in range(1, nc):
            for source_of, target_of in self.pieces:
                push(
                    source_of(self.r_ins, lax.rem(place.c + step, nc)),
                    target_of(self.r_outs[0], place.c),
                    send.at[step - 1],
                    recv.at[step - 1],
                    place.ahead(step),
                ).start()
        for at, (source_of, _) in enumerate(self.pieces):
            lanes = pl.ds(at * self.sub, self.sub)
            pltpu.make_async_copy(source_of(self.r_ins, place.c), held.at[:, lanes], local).start()

    def wait_own(self):
        local, _, _, held = self.r_sems
        pltpu.make_async_copy(held, held, local).wait()
        for at, (_, target_of) in enumerate(self.pieces):
            lanes = pl.ds(at * self.sub, self.sub)
            pltpu.make_async_copy(held.at[:, lanes], target_of(self.r_outs[0], self.place.c), local).start()
        pltpu.make_async_copy(held, held, local).wait()

    def wait_from(self, step):
        whole = self.whole()
        _, send, recv, _ = self.r_sems
        push(whole, whole, send.at[step - 1], recv.at[step - 1], self.place.ahead(step)).wait_recv()

    def wait_sent(self):
        whole = self.whole()
        _, send, recv, _ = self.r_sems
        for step in range(1, self.place.sizes.nc):
            push(whole, whole, send.at[step - 1], recv.at[step - 1], self.place.ahead(step)).wait_send()

    def finish(self):
        self.wait_own()
        for step in range(1, self.place.sizes.nc):
            self.wait_from(step)
        self.wait_sent()


class WeightExchange(Exchange):
    def __init__(self, sizes, rows, array, corners, sub, when="begin", finish="end"):
        pieces = [self.piece(first, rows, base, sub, at) for at, (first, base) in enumerate(corners)]
        out = jax.ShapeDtypeStruct((sizes.nc * rows, sub * len(pieces)), BF)
        super().__init__(sizes, [array], out, pieces, rows, sub, when, finish)
        self.rows = rows

    @staticmethod
    def piece(first, rows, base, sub, position):
        def source_of(refs, dest):
            return refs[0].at[pl.ds(first, rows), pl.ds(pl.multiple_of(base + dest * sub, TILE), sub)]

        def target_of(out, source):
            return out.at[pl.ds(pl.multiple_of(source * rows, rows), rows), pl.ds(position * sub, sub)]

        return source_of, target_of

    def whole(self):
        return self.r_outs[0].at[pl.ds(0, self.rows)]


class GradExchange(Exchange):
    def __init__(self, sizes, total, sub, when="begin", finish="end"):
        self.middle = total if isinstance(total, GradMiddle) else None
        shape = self.middle.outs[0].shape if self.middle else total.shape
        rows = shape[0] // sizes.nc
        count = shape[1] // sub
        out = jax.ShapeDtypeStruct((rows, sizes.nc * shape[1]), BF)
        pieces = [self.piece(rows, sub, position, sizes.nc) for position in range(count)]
        super().__init__(sizes, [] if self.middle else [total], out, pieces, rows, sub, when, finish)
        self.rows = rows

    def start(self):
        if self.middle:
            self.r_ins = [self.middle.total]
        super().start()

    @staticmethod
    def piece(rows, sub, position, nc):
        def source_of(refs, dest):
            return refs[0].at[pl.ds(pl.multiple_of(dest * rows, rows), rows), pl.ds(position * sub, sub)]

        def target_of(out, source):
            return out.at[:, pl.ds(pl.multiple_of(position * nc * sub + source * sub, TILE), sub)]

        return source_of, target_of

    def whole(self):
        return self.r_ins[0].at[pl.ds(0, self.rows)]


class Spread(Rider):
    kinds = ("fsdp", "twin")

    def __init__(self, sizes, mine, blocks=1, steps=("begin", "inside1")):
        if isinstance(mine, Exchange):
            self.source, shape, self.ins = mine, mine.outs[0].shape, []
        else:
            self.source, shape, self.ins = None, mine.shape, [mine]
        rows, self.width = shape
        self.part, self.blocks, self.rows, self.steps = rows, blocks, rows // blocks, steps
        self.outs = [jax.ShapeDtypeStruct((sizes.nf * rows, sizes.ns * self.width), BF)]
        others = max(sizes.nf - 1, 1)
        self.sems = [DMA((blocks,))] + [DMA((blocks, others)) for _ in range(8)] + [DMA((blocks,)) for _ in range(4)]
        self.sems.append(pltpu.VMEM((rows, self.width), BF))

    def at(self, moment):
        if moment == self.steps[0]:
            if self.source is not None:
                self.source.finish()
            for block in range(self.blocks):
                self.first(block)
        if moment == self.steps[1]:
            for block in range(self.blocks):
                self.second(block)
        if moment == "end":
            for block in range(self.blocks):
                self.finish(block)

    def span(self, df, block, half, whole=False):
        length = self.rows if whole else self.rows // 2
        at = df * self.part + block * self.rows + half * (self.rows // 2)
        return pl.ds(pl.multiple_of(at, length), length)

    def mine(self, block, half, whole=False):
        ref = self.r_ins[0] if self.source is None else self.source.r_outs[0]
        return ref.at[self.span(0, block, half, whole)]

    def out(self, ds, df, block, half, whole=False):
        return self.r_outs[0].at[self.span(df, block, half, whole), pl.ds(ds * self.width, self.width)]

    def copies(self, block, stage):
        place, nf, sems, out = self.place, self.place.sizes.nf, self.r_sems, []
        for step in range(1, nf):
            at, df = step - 1, nf - step
            across = place.across(step)
            source, target, pair, device = [
                (self.mine(block, 0), self.out(0, df, block, 0), 1, across),
                (self.mine(block, 1), self.out(0, df, block, 1), 3, across),
                (self.out(1, 0, block, 1), self.out(1, df, block, 1), 5, across),
            ][stage]
            out.append(push(source, target, sems[pair].at[block, at], sems[pair + 1].at[block, at], device))
            if stage == 2:
                source, target = self.out(0, df, block, 0), self.out(1, df, block, 0)
                out.append(push(source, target, sems[7].at[block, at], sems[8].at[block, at], place.twin()))
        if stage < 2:
            half, pair = (1, 9) if stage == 0 else (0, 11)
            out.append(
                push(
                    self.mine(block, half),
                    self.out(1, 0, block, half),
                    sems[pair].at[block],
                    sems[pair + 1].at[block],
                    place.twin(),
                )
            )
        return out

    def keep(self, block, inward):
        held = self.r_sems[13].at[self.span(0, block, 0, True)]
        ends = (self.mine(block, 0, True), held) if inward else (held, self.out(0, 0, block, 0, True))
        return pltpu.make_async_copy(*ends, self.r_sems[0].at[block])

    def first(self, block):
        for stage in range(2):
            for copy in self.copies(block, stage):
                copy.start()
        self.keep(block, True).start()

    def second(self, block):
        for copy in self.copies(block, 0):
            copy.wait_recv()
        for copy in self.copies(block, 2):
            copy.start()
        self.keep(block, True).wait()
        self.keep(block, False).start()

    def finish(self, block):
        for copy in self.copies(block, 0):
            copy.wait_send()
        for stage in (1, 2):
            for copy in self.copies(block, stage):
                copy.wait_recv()
                copy.wait_send()
        self.keep(block, False).wait()


class SpreadOwn(Spread):
    def at(self, moment):
        if moment == self.steps[0]:
            if self.source is not None:
                self.source.finish()
            for block in range(self.blocks):
                self.first(block)
        if moment == "end" and self.steps[0] is not None:
            for block in range(self.blocks):
                self.finish(block)

    def finish(self, block):
        self.keep(block, True).wait()
        self.keep(block, False).start()
        for stage in range(2):
            for copy in self.copies(block, stage):
                copy.wait_recv()
                copy.wait_send()
        self.keep(block, False).wait()


class SpreadRelay(Rider):
    kinds = ("fsdp", "twin")
    aliased = True

    def __init__(self, sizes, whole, when="begin"):
        self.ins, self.outs, self.when = [whole], [jax.ShapeDtypeStruct(whole.shape, BF)], when
        self.part, self.width = whole.shape[0] // sizes.nf, whole.shape[1] // sizes.ns
        others = max(sizes.nf - 1, 1)
        self.sems = [DMA((others,)) for _ in range(4)]
        self.blocks = sizes.nc

    def copies(self):
        out, place, nf = [], self.place, self.place.sizes.nf
        rows, half = self.part // self.blocks, self.part // self.blocks // 2
        for step in range(1, nf):
            at, df = step - 1, nf - step
            for block in range(self.blocks):
                low, high = block * rows, block * rows + half
                lanes = pl.ds(self.width, self.width)
                first = pl.ds(df * self.part + low, half)
                second = pl.ds(df * self.part + high, half)
                whole = self.r_outs[0]
                out.append(
                    push(
                        whole.at[pl.ds(high, half), lanes],
                        whole.at[second, lanes],
                        self.sems_of(0, at),
                        self.sems_of(1, at),
                        place.across(step),
                    )
                )
                out.append(
                    push(
                        whole.at[first, pl.ds(0, self.width)],
                        whole.at[first, lanes],
                        self.sems_of(2, at),
                        self.sems_of(3, at),
                        place.twin(),
                    )
                )
        return out

    def sems_of(self, kind, at):
        return self.r_sems[kind].at[at]

    def at(self, moment):
        if moment == self.when:
            for copy in self.copies():
                copy.start()
        if moment == "end":
            place, half = self.place, self.part // 2
            for step in range(1, place.sizes.nf):
                at = step - 1
                bytes_of = self.r_outs[0].at[pl.ds(0, half), pl.ds(0, self.width)]
                for kind, device in ((0, place.across(step)), (2, place.twin())):
                    push(bytes_of, bytes_of, self.sems_of(kind, at), self.sems_of(kind + 1, at), device).wait()


class GradFirst(Rider):
    kinds = ("fsdp", "twin")

    def __init__(self, sizes, name, rows, width, when):
        self.name, self.when, self.taken = name, when, False
        self.part = rows // sizes.nf
        self.half = self.part // 2
        self.width = width // sizes.ns
        others = max(sizes.nf - 1, 1)
        self.outs = [
            jax.ShapeDtypeStruct((others, self.half, width), BF),
            jax.ShapeDtypeStruct((sizes.nf, self.half, self.width), BF),
        ]
        self.sems = [DMA((others,)), DMA((others,)), DMA((sizes.nf,)), DMA((sizes.nf,))]

    def copies(self):
        place, nf = self.place, self.place.sizes.nf
        grads, (low, high) = self.main.grads[self.name], self.r_outs
        xs, xr, ys, yr = self.r_sems
        out = []
        for step in range(1, nf):
            at = step - 1
            out.append(
                push(grads.at[pl.ds(step * self.part, self.half)], low.at[at], xs.at[at], xr.at[at], place.across(step))
            )
        for df in range(nf):
            rows = pl.ds(df * self.part + self.half, self.half)
            out.append(
                push(grads.at[rows, pl.ds(self.width, self.width)], high.at[df], ys.at[df], yr.at[df], place.twin())
            )
        return out

    def at(self, moment):
        if moment == self.when:
            for copy in self.copies():
                copy.start()
        if moment == "end":
            if not self.taken:
                self.wait_recv()
            for copy in self.copies():
                copy.wait_send()

    def wait_recv(self):
        self.taken = True
        for copy in self.copies():
            copy.wait_recv()


class GradMiddle(Rider):
    kinds = ("fsdp", "twin")

    def __init__(self, sizes, source, steps=("begin", "sent", "late")):
        self.steps = steps
        if isinstance(source, GradFirst):
            self.source, self.ins = source, []
            low, high = source.outs
            part = source.part
        else:
            self.source, self.ins = None, list(source)
            low, high = source[1:]
            part = source[0].shape[0] // sizes.nf
        self.part, self.half, self.width = part, part // 2, high.shape[2]
        nf, others = sizes.nf, low.shape[0]
        self.outs = [jax.ShapeDtypeStruct((part, self.width), BF)]
        piece = (self.half, self.width)
        self.sems = [
            pltpu.VMEM((self.half, sizes.ns * self.width), BF),
            pltpu.VMEM((nf,) + piece, BF),
            pltpu.VMEM(low.shape, BF),
            pltpu.VMEM(high.shape, BF),
            pltpu.VMEM(piece, BF),
            pltpu.VMEM((others,) + piece, BF),
            pltpu.VMEM((part, self.width), BF),
            DMA((nf + 3,)),
            DMA(()),
            DMA(()),
            DMA((others,)),
            DMA((others,)),
            DMA(()),
        ]

    @property
    def total(self):
        return self.r_sems[6]

    def loads(self):
        nf = self.place.sizes.nf
        if self.source is None:
            grads, low, high = self.r_ins
        else:
            grads = self.main.grads[self.source.name]
            low, high = self.source.r_outs
        g_low, g_high, r_low, r_high = self.r_sems[:4]
        sem = self.r_sems[7]
        out = [
            pltpu.make_async_copy(grads.at[pl.ds(0, self.half)], g_low, sem.at[nf]),
            pltpu.make_async_copy(low, r_low, sem.at[nf + 1]),
            pltpu.make_async_copy(high, r_high, sem.at[nf + 2]),
        ]
        for df in range(nf):
            rows = pl.ds(df * self.part + self.half, self.half)
            out.append(pltpu.make_async_copy(grads.at[rows, pl.ds(0, self.width)], g_high.at[df], sem.at[df]))
        return out

    def copies(self):
        place, nf, width = self.place, self.place.sizes.nf, self.width
        g_low, g_high, _, _, low, high = self.r_sems[:6]
        ys, yr, xs, xr = self.r_sems[8:12]
        out = [push(g_low.at[:, pl.ds(width, width)], low, ys, yr, place.twin())]
        for step in range(1, nf):
            at = step - 1
            out.append(push(g_high.at[step], high.at[at], xs.at[at], xr.at[at], place.across(step)))
        return out

    def store(self):
        return pltpu.make_async_copy(self.total, self.r_outs[0], self.r_sems[12])

    def at(self, moment):
        nf, width, half = self.place.sizes.nf, self.width, self.half
        g_low, g_high, r_low, r_high, low, high, total = self.r_sems[:7]
        if moment == self.steps[0]:
            if self.source is not None:
                self.source.wait_recv()
            for copy in self.loads():
                copy.start()
        if moment == self.steps[1]:
            for copy in self.loads():
                copy.wait()
            lanes = slice(width, 2 * width)

            def first(rows):
                value = g_low[rows, lanes].astype(F32)
                for at in range(nf - 1):
                    value = value + r_low[at, rows, lanes].astype(F32)
                g_low[rows, lanes] = value.astype(BF)
                for df in range(1, nf):
                    g_high[df, rows] = (g_high[df, rows].astype(F32) + r_high[df, rows].astype(F32)).astype(BF)

            by_rows(half, 32, first)
            for copy in self.copies():
                copy.start()
        if moment == self.steps[2]:
            for copy in self.copies():
                copy.wait_recv()
            lanes = slice(0, width)

            def second(rows):
                value = g_low[rows, lanes].astype(F32) + low[rows].astype(F32)
                for at in range(nf - 1):
                    value = value + r_low[at, rows, lanes].astype(F32)
                total[rows] = value.astype(BF)

            def third(rows):
                value = g_high[0, rows].astype(F32) + r_high[0, rows].astype(F32)
                for at in range(nf - 1):
                    value = value + high[at, rows].astype(F32)
                total[pl.ds(pl.multiple_of(rows.start + half, 32), 32)] = value.astype(BF)

            by_rows(half, 32, second)
            by_rows(half, 32, third)
            self.store().start()
        if moment == "end":
            for copy in self.copies():
                copy.wait_send()
            self.store().wait()


class Share(Rider):
    def __init__(self, kinds, array, out, count, moves, when="begin"):
        self.kinds, self.moves, self.when = kinds, moves, when
        self.ins, self.outs = [array], [out]
        self.sems = [DMA((count,)), DMA((count,))]

    def copies(self):
        send, recv = self.r_sems
        out = []
        for at, (device, source, target) in enumerate(self.moves(self.place, self.r_ins[0], self.r_outs[0])):
            if device is None:
                out.append(pltpu.make_async_copy(source, target, send.at[at]))
            else:
                out.append(push(source, target, send.at[at], recv.at[at], device))
        return out

    def at(self, moment):
        if moment == self.when:
            for copy in self.copies():
                copy.start()
        if moment == "end":
            for copy in self.copies():
                copy.wait()


def share_rows(sizes, value):
    rows, width = value.shape
    part = width // sizes.nf

    def moves(place, source, out):
        triples = []
        for dt in range(sizes.nt):
            device = place.plane(0, dt) if dt else None
            for df in range(sizes.nf):
                lanes = pl.ds(pl.multiple_of(lax.rem(place.f + df, sizes.nf) * part, part), part)
                triples.append((device, source.at[:, pl.ds(df * part, part)], out.at[place.t, :, lanes]))
        return triples

    out = jax.ShapeDtypeStruct((sizes.nt, rows, width), value.dtype)
    return Share(("plane",), value, out, sizes.nt * sizes.nf, moves)


class MainRows(Share):
    def __init__(self, sizes, rows, width, when):
        share = share_rows(sizes, jax.ShapeDtypeStruct((rows, width), BF))
        super().__init__(share.kinds, None, share.outs[0], share.sems[0].shape[0], share.moves, when)
        self.ins = []

    def copies(self):
        self.r_ins = [self.main.rows_ref]
        return super().copies()


class NormSum(Rider):
    kinds = ("ctx", "plane")

    def __init__(self, sizes, lines, places, piece, steps):
        self.ins, self.places, self.piece, self.steps = [lines], places, piece, steps
        count = lines.shape[0]
        self.outs = [jax.ShapeDtypeStruct((count, piece), F32)]
        self.around = [(df, dt) for df in range(sizes.nf) for dt in range(sizes.nt)][1:]
        block = (sizes.nf, count, piece)
        self.sems = [
            pltpu.VMEM(lines.shape, F32),
            pltpu.VMEM((sizes.nc,) + block, F32),
            pltpu.VMEM(block, F32),
            pltpu.VMEM((len(self.around), count, piece), F32),
            pltpu.VMEM((count, piece), F32),
            DMA(()),
            DMA((sizes.nc,)),
            DMA((sizes.nc,)),
            DMA((len(self.around),)),
            DMA((len(self.around),)),
            pltpu.VMEM((sizes.nc,) + block, F32),
        ]

    def rounds(self):
        place = self.place
        _, _, sums, _, _, _, _, _, send, recv, _ = self.r_sems
        return [
            push(sums.at[df], self.r_sems[3].at[at], send.at[at], recv.at[at], place.plane(df, dt))
            for at, (df, dt) in enumerate(self.around)
        ]

    def whole(self, step):
        box = self.r_sems[1].at[step]
        return push(box, box, self.r_sems[6].at[step], self.r_sems[7].at[step], self.place.ahead(step))

    def at(self, moment):
        place, sizes = self.place, self.place.sizes
        lines, first, sums, second, result, load, send, recv = self.r_sems[:8]

        def keep():
            return pltpu.make_async_copy(self.r_ins[0], lines, load)

        if moment == "begin":
            keep().start()
        if moment == self.steps[0]:
            keep().wait()
            for at, line in enumerate(self.places):
                lines[line : line + 1] = self.main.norm_ref[at : at + 1]
            blocks = self.r_sems[10]
            for dest in range(sizes.nc):
                for df in range(sizes.nf):
                    lane = (df * sizes.nc + dest) * self.piece
                    blocks[dest, df] = lines[:, lane : lane + self.piece]
            for step in range(1, sizes.nc):
                push(
                    blocks.at[lax.rem(place.c + step, sizes.nc)],
                    first.at[step],
                    send.at[step],
                    recv.at[step],
                    place.ahead(step),
                ).start()
            first[0] = blocks[place.c]
        if moment == self.steps[1]:
            for step in range(1, sizes.nc):
                self.whole(step).wait_recv()
            sums[...] = sum(first[step] for step in range(sizes.nc))
            for copy in self.rounds():
                copy.start()
        if moment == "end":
            for copy in self.rounds():
                copy.wait()
            for step in range(1, sizes.nc):
                self.whole(step).wait_send()
            result[...] = sums[0] + sum(second[at] for at in range(len(self.around)))
            out = pltpu.make_async_copy(result, self.r_outs[0], load)
            out.start()
            out.wait()


class BiasSum(Rider):
    kinds = ("ctx", "plane")

    def __init__(self, sizes, value, own, steps):
        self.ins, self.own, self.steps = [value], own, steps
        ns, count, width = value.shape
        self.width = width
        self.outs = [jax.ShapeDtypeStruct((sizes.nc, count, width), F32)]
        self.around = [(df, ds) for df in range(sizes.nf) for ds in range(ns)][1:]
        self.sems = [
            pltpu.VMEM(value.shape, F32),
            pltpu.VMEM((len(self.around), count, width), F32),
            pltpu.VMEM((count, width), F32),
            DMA(()),
            DMA((len(self.around),)),
            DMA((len(self.around),)),
            DMA((sizes.nc,)),
            DMA((sizes.nc,)),
        ]

    def rounds(self):
        lines, first, _, _, send, recv = self.r_sems[:6]
        nk = self.place.sizes.nk
        return [
            push(lines.at[ds], first.at[at], send.at[at], recv.at[at], self.place.plane(df, ds * nk))
            for at, (df, ds) in enumerate(self.around)
        ]

    def spreads(self):
        place, nc = self.place, self.place.sizes.nc
        sums, target = self.r_sems[2], self.r_outs[0].at[self.place.c]
        send, recv = self.r_sems[6:]
        return [push(sums, target, send.at[step], recv.at[step], place.ahead(step)) for step in range(1, nc)]

    def at(self, moment):
        lines, first, sums, load = self.r_sems[:4]

        def keep():
            return pltpu.make_async_copy(self.r_ins[0], lines, load)

        def mine():
            return pltpu.make_async_copy(sums, self.r_outs[0].at[self.place.c], load)

        if moment == "begin":
            keep().start()
        if moment == self.steps[0]:
            keep().wait()
            for ds in range(self.place.sizes.ns):
                for line in range(self.own):
                    at = (ds * self.own + line) * self.width
                    lines[ds, line : line + 1] = self.main.bias_ref[:, at : at + self.width]
            for copy in self.rounds():
                copy.start()
        if moment == self.steps[1]:
            for copy in self.rounds():
                copy.wait()
            sums[...] = lines[0] + sum(first[at] for at in range(len(self.around)))
            for copy in self.spreads() + [mine()]:
                copy.start()
        if moment == "end":
            for copy in self.spreads() + [mine()]:
                copy.wait()


class Moved:
    def __init__(self, hbm, scratch, inward):
        count = len(hbm)
        self.vmem = scratch[:count]
        self.copies = []
        for ref, buffer, sem in zip(hbm, scratch[:count], scratch[count:]):
            ends = (ref, buffer) if inward else (buffer, ref)
            self.copies.append(pltpu.make_async_copy(*ends, sem))

    @staticmethod
    def scratch(arrays):
        return [pltpu.VMEM(a.shape, a.dtype) for a in arrays] + [DMA(()) for _ in arrays]

    def start(self):
        for copy in self.copies:
            copy.start()


class Main:
    kinds = ("mate", "line")
    big, small, results, kept, gathered, work = [], [], [], [], [], []

    def __init__(self, **arrays):
        self.grads = {}

    @property
    def ins(self):
        return list(self.big) + list(self.small)

    @property
    def in_specs(self):
        return [ANY_SPEC] * len(self.big) + [VMEM_SPEC] * len(self.small)

    @property
    def outs(self):
        return list(self.results) + list(self.kept) + list(self.gathered)

    @property
    def out_specs(self):
        return [VMEM_SPEC] * len(self.results) + [ANY_SPEC] * (len(self.kept) + len(self.gathered))

    def scratch(self, sizes):
        self.layout = [
            Moved.scratch(self.big),
            Moved.scratch(self.kept),
            [pltpu.VMEM(a.shape, a.dtype) for a in self.work],
            scatter_scratch(sizes, self.rows, self.width),
        ] + [Gather.scratch(sizes) for _ in self.gathered]
        return [one for group in self.layout for one in group]

    def run(self, place, ins, outs, scratch, moment):
        cuts, at = [], 0
        for group in self.layout:
            cuts.append(scratch[at : at + len(group)])
            at += len(group)
        count = len(self.big)
        self.loads = Moved(ins[:count], cuts[0], True)
        results, kept = outs[: len(self.results)], outs[len(self.results) : len(self.results) + len(self.kept)]
        gathered = outs[len(self.results) + len(self.kept) :]
        self.stores = Moved(kept, cuts[1], False)
        self.work_refs, self.bufs, self.gather_sems = cuts[2], cuts[3], cuts[4:]
        self.loads.start()
        moment("begin")
        self.compute(place, self.loads.vmem, ins[count:], results, self.stores.vmem, gathered, moment)
        self.sent()
        for copy in self.stores.copies:
            copy.wait()

    def fetch(self, *which):
        for at in which:
            self.loads.copies[at].wait()

    def store(self, *which):
        for at in which:
            self.stores.copies[at].start()

    def spread(self, place, gathers, moment):
        for gather in gathers:
            gather.begin()
        moment("summed")
        for step in range(1, place.sizes.nc):
            for gather in gathers:
                gather.forward(step)
            if step == 1:
                moment("spread")
        moment("late")
        for gather in gathers:
            gather.end()


def by_rows(count, block, step):
    def one(at, carry):
        step(pl.ds(pl.multiple_of(at * block, block), block))
        return carry

    lax.fori_loop(0, count // block, one, 0)


def unit_rows_of(values):
    row_mean = jnp.mean(values, -1, keepdims=True)
    centred = values - row_mean
    row_var = jnp.mean(centred * centred, -1, keepdims=True)
    inverse = lax.rsqrt(row_var + EPS)
    return centred * inverse, inverse


def norm_back(grad_rows, saved_rows, gain_row):
    unit_rows, inverse = unit_rows_of(saved_rows)
    scaled = grad_rows * gain_row
    inner = inverse * (
        scaled
        - jnp.mean(scaled, -1, keepdims=True)
        - unit_rows * jnp.mean(scaled * unit_rows, -1, keepdims=True)
    )
    return inner, jnp.sum(grad_rows * unit_rows, 0, keepdims=True), jnp.sum(grad_rows, 0, keepdims=True)


def norm_forward(new_rows, norm_ref, at):
    unit_rows, _ = unit_rows_of(new_rows)
    return (unit_rows * norm_ref[at : at + 1] + norm_ref[at + 1 : at + 2]).astype(BF)


def swap_lanes(values):
    lane = lax.broadcasted_iota(jnp.int32, values.shape, 1) % HD
    width = values.shape[1]
    up = pltpu.roll(values, width - ROT // 2, 1)
    down = pltpu.roll(values, ROT // 2, 1)
    return jnp.where(lane < ROT // 2, up, jnp.where(lane < ROT, down, 0.0))


def allowed_of(label_col, label_row):
    length = label_col.shape[0]
    row = lax.broadcasted_iota(jnp.int32, (length, length), 0)
    col = lax.broadcasted_iota(jnp.int32, (length, length), 1)
    return (label_col == label_row) & (row >= col)


def like(shape, dtype):
    return jax.ShapeDtypeStruct(shape, dtype)


ROW_BLOCK = 128
OUT_BLOCK = 256


class AttnForward(Main):
    def __init__(self, full, w_qkv, w_out, bias, tables, stream, norm):
        super().__init__()
        self.rows, self.width = stream.shape
        length = full.shape[0]
        self.big = [full, w_qkv, w_out]
        self.small, self.norm_at = [bias[0], *tables, stream, norm[0]], norm[1]
        self.bias_at = bias[1]
        heads = w_out.shape[1] // HD
        self.results = [like(stream.shape, F32), like((length, heads), F32)]
        mixed = like((length, w_out.shape[1]), BF)
        self.kept = [like((length, w_qkv.shape[1]), BF), mixed, mixed, mixed]
        self.gathered = [like(full.shape, BF)]
        self.work = [like(full.shape, BF), like(stream.shape, BF)]

    def compute(self, place, big, small, results, kept, gathered, moment):
        full, w_qkv, w_out = big
        bias_ref, col_ref, row_ref, cos_ref, sin_ref, stream_ref, norm_ref = small
        new_ref, lse_ref = results
        proj_ref, mix_ref, q_ref, k_ref = kept
        part_ref, low_ref = self.work_refs
        length = full.shape[0]
        ns = place.sizes.ns
        width = w_out.shape[1] // ns
        self.fetch(0, 1)

        def project(rows):
            proj_ref[rows] = (dot_nn(full[rows], w_qkv[...]) + bias_ref[self.bias_at : self.bias_at + 1]).astype(BF)

        by_rows(length, ROW_BLOCK, project)
        self.store(0)
        allowed = allowed_of(col_ref[...], row_ref[...])
        cosine, sine = cos_ref[...], sin_ref[...]
        scaling = HD ** (-0.5)
        for b in range(ns):
            base, own = 3 * width * b, slice(b * width, (b + 1) * width)
            for ref, at in ((q_ref, 0), (k_ref, 1)):
                values = proj_ref[:, base + at * width : base + (at + 1) * width].astype(F32)
                ref[:, own] = (values * cosine + swap_lanes(values) * sine).astype(BF)
            for h in range(width // HD):
                span = slice(b * width + h * HD, b * width + (h + 1) * HD)
                scores = scaling * dot_nt(q_ref[:, span], k_ref[:, span])
                scores = jnp.where(allowed, scores, NEGATIVE)
                peak = jnp.max(scores, -1, keepdims=True)
                exponent = jnp.exp(scores - peak)
                total = jnp.sum(exponent, -1, keepdims=True)
                probs = (exponent * (1.0 / total)).astype(BF)
                at = base + 2 * width + h * HD
                mix_ref[:, span] = dot_nn(probs, proj_ref[:, at : at + HD]).astype(BF)
                at = b * (width // HD) + h
                lse_ref[:, at : at + 1] = peak + jnp.log(total)
        self.store(1, 2, 3)
        self.fetch(2)
        for at in range(0, self.width, OUT_BLOCK):
            part_ref[:, at : at + OUT_BLOCK] = dot_nt(mix_ref[...], w_out[at : at + OUT_BLOCK]).astype(BF)
        moment("ready")
        total, self.sent = scatter_part(place, part_ref, self.bufs, self.rows, moment)
        new_rows = stream_ref[...] + total
        new_ref[...] = new_rows
        low_ref[...] = norm_forward(new_rows, norm_ref, self.norm_at)
        self.spread(place, [Gather(place, low_ref, gathered[0], self.gather_sems[0], self.rows)], moment)


class FfnForward(Main):
    def __init__(self, full, w_gate, w_up, w_down, stream, norm, cotangent=None):
        super().__init__()
        self.rows, self.width = stream.shape
        length = full.shape[0]
        self.last = cotangent is not None
        self.big = [full, w_gate, w_up, w_down]
        self.small = [stream, cotangent if self.last else norm[0]]
        self.norm_at = norm and norm[1]
        self.results = [like(stream.shape, F32)]
        hidden = (length, w_gate.shape[1])
        self.kept = [like(hidden, F32), like(hidden, F32), like(hidden, BF)]
        self.gathered = [like(full.shape, BF)]
        self.work = [like(full.shape, BF), like(stream.shape, BF)]

    def compute(self, place, big, small, results, kept, gathered, moment):
        full, w_gate, w_up, w_down = big
        stream_ref = small[0]
        gate_ref, up_ref, act_ref = kept
        part_ref, low_ref = self.work_refs
        gather = None
        if self.last:
            gather = Gather(place, small[1], gathered[0], self.gather_sems[0], self.rows)
            gather.begin()
        self.fetch(0, 1, 2)

        def gates(rows):
            gate = dot_nn(full[rows], w_gate[...])
            up = dot_nn(full[rows], w_up[...])
            gate_ref[rows] = gate
            up_ref[rows] = up
            act_ref[rows] = (gate * jax.nn.sigmoid(gate) * up).astype(BF)

        by_rows(full.shape[0], ROW_BLOCK, gates)
        self.store(0, 1, 2)
        self.fetch(3)
        for at in range(0, self.width, OUT_BLOCK):
            part_ref[:, at : at + OUT_BLOCK] = dot_nt(act_ref[...], w_down[at : at + OUT_BLOCK]).astype(BF)
        moment("ready")
        steps = list(range(1, place.sizes.nc)) if self.last else []

        def meanwhile(name):
            if steps and name in ("sent", "inside1", "inside2"):
                gather.forward(steps.pop(0))
            moment(name)

        total, self.sent = scatter_part(place, part_ref, self.bufs, self.rows, meanwhile)
        new_rows = stream_ref[...] + total
        results[0][...] = new_rows
        if self.last:
            moment("summed")
            for step in steps:
                gather.forward(step)
            moment("spread")
            moment("late")
            gather.end()
            return
        low_ref[...] = norm_forward(new_rows, small[1], self.norm_at)
        self.spread(place, [Gather(place, low_ref, gathered[0], self.gather_sems[0], self.rows)], moment)


class FfnBack(Main):
    names = ["down", "gate", "up"]

    def __init__(self, grad_full, w_gate, w_up, w_down, gates, ups, acts, full, grad, saved, norm):
        super().__init__()
        self.rows, self.width = grad.shape
        self.big = [grad_full, acts, w_down, gates, ups, w_gate, w_up, full]
        self.small, self.norm_at = [grad, saved, norm[0]], norm[1]
        self.results = [like(grad.shape, F32), like((2, self.width), F32)]
        self.kept = [like(w_down.shape, BF), like(w_gate.shape, BF), like(w_up.shape, BF)]
        self.gathered = [like(full.shape, BF)]
        hidden = like(acts.shape, BF)
        self.work = [hidden, hidden, like(full.shape, BF), like(grad.shape, BF)]

    def compute(self, place, big, small, results, kept, gathered, moment):
        grad_full, act_ref, w_down, gate_ref, up_ref, w_gate, w_up, full = big
        grad_ref, saved_ref, norms_ref = small
        new_ref, norm_ref = results
        down_grad, gate_grad, up_grad = kept
        low_gate, low_up, part_ref, grad_low_ref = self.work_refs
        self.grads = {"down": down_grad, "gate": gate_grad, "up": up_grad}

        def weights_of(which, target, left, right, name):
            for at in range(0, self.width, OUT_BLOCK):
                span = slice(at, at + OUT_BLOCK)
                target[span] = dot_tn(left[:, span], right[...]).astype(BF)
            self.store(which)
            moment(name)

        self.fetch(0, 1)
        weights_of(0, down_grad, grad_full, act_ref, "downs")
        self.fetch(2, 3, 4)

        def gates(rows):
            act_grad = dot_nn(grad_full[rows], w_down[...])
            gate, up = gate_ref[rows], up_ref[rows]
            sg = jax.nn.sigmoid(gate)
            low_gate[rows] = (act_grad * up * sg * (1.0 + gate * (1.0 - sg))).astype(BF)
            low_up[rows] = (act_grad * gate * sg).astype(BF)

        by_rows(full.shape[0], ROW_BLOCK, gates)
        self.fetch(5, 6)
        for at in range(0, self.width, OUT_BLOCK):
            span = slice(at, at + OUT_BLOCK)
            part_ref[:, span] = (dot_nt(low_gate[...], w_gate[span]) + dot_nt(low_up[...], w_up[span])).astype(BF)
        moment("ready")
        self.fetch(7)

        def weights(name):
            if name == "sent":
                weights_of(1, gate_grad, full, low_gate, "gates")
            if name == "inside0":
                weights_of(2, up_grad, full, low_up, "ups")
            moment(name)

        total, self.sent = scatter_part(place, part_ref, self.bufs, self.rows, weights)
        inner, gain_grad, shift_grad = norm_back(total, saved_ref[...], norms_ref[self.norm_at : self.norm_at + 1])
        new_rows = grad_ref[...] + inner
        new_ref[...] = new_rows
        grad_low_ref[...] = new_rows.astype(BF)
        norm_ref[0:1] = gain_grad
        norm_ref[1:2] = shift_grad
        self.spread(place, [Gather(place, grad_low_ref, gathered[0], self.gather_sems[0], self.rows)], moment)


class AttnBack(Main):
    names = ["qkv", "out"]

    def __init__(self, grad_full, w_qkv, w_out, kept, full, tables, lse, grad, saved, norm, last):
        super().__init__()
        proj, mixed, q_rot, k_rot = kept
        self.rows, self.width = grad.shape
        self.last = last
        self.big = [grad_full, w_out, q_rot, k_rot, proj, w_qkv, full, mixed]
        self.small, self.norm_at = [*tables, lse, grad, saved, norm[0]], norm[1]
        self.results = [like(grad.shape, F32), like((2, self.width), F32), like((1, w_qkv.shape[1]), F32)]
        self.kept = [like(w_qkv.shape, BF), like(w_out.shape, BF)]
        self.gathered = [] if last else [like(full.shape, BF)]
        self.work = [like(proj.shape, BF), like(full.shape, BF), like(grad.shape, BF), like(mixed.shape, BF)]

    def compute(self, place, big, small, results, kept, gathered, moment):
        grad_full, w_out, q_ref, k_ref, proj_ref, w_qkv, full, mix_ref = big
        col_ref, row_ref, cos_ref, sin_ref, lse_ref, grad_ref, saved_ref, norms_ref = small
        new_ref, norm_ref, bias_ref = results
        qkv_ref, out_ref = kept
        self.norm_ref, self.bias_ref, self.rows_ref = norm_ref, bias_ref, self.work_refs[2]
        low_ref, part_ref, grad_low_ref, mix_grad_ref = self.work_refs
        ns = place.sizes.ns
        width = w_out.shape[1] // ns
        self.grads = {"qkv": qkv_ref, "out": out_ref}
        self.fetch(0, 1)

        def mixed_grad(rows):
            mix_grad_ref[rows] = dot_nn(grad_full[rows], w_out[...]).astype(BF)

        by_rows(full.shape[0], ROW_BLOCK, mixed_grad)
        self.fetch(2, 3, 4)
        allowed = allowed_of(col_ref[...], row_ref[...])
        cosine, sine = cos_ref[...], sin_ref[...]
        scaling = HD ** (-0.5)
        for b in range(ns):
            parts = [[], [], []]
            base = 3 * width * b
            for h in range(width // HD):
                span = slice(b * width + h * HD, b * width + (h + 1) * HD)
                at = b * (width // HD) + h
                q_rows, k_rows, out_grad = q_ref[:, span], k_ref[:, span], mix_grad_ref[:, span]
                scores = jnp.where(allowed, scaling * dot_nt(q_rows, k_rows), NEGATIVE)
                probs = jnp.exp(scores - lse_ref[:, at : at + 1])
                first = base + 2 * width + h * HD
                prob_grad = dot_nt(out_grad, proj_ref[:, first : first + HD])
                inner = jnp.sum(probs * prob_grad, -1, keepdims=True)
                score_low = (probs * (prob_grad - inner)).astype(BF)
                parts[0].append(scaling * dot_nn(score_low, k_rows))
                parts[1].append(scaling * dot_tn(score_low, q_rows))
                parts[2].append(dot_tn(probs.astype(BF), out_grad))
            for at in range(3):
                values = jnp.concatenate(parts[at], axis=1)
                if at < 2:
                    values = values * cosine - swap_lanes(values) * sine
                low = values.astype(BF)
                lanes = slice(base + at * width, base + (at + 1) * width)
                low_ref[:, lanes] = low
                bias_ref[:, lanes] = jnp.sum(low.astype(F32), 0, keepdims=True)
        self.fetch(5)
        for at in range(0, self.width, OUT_BLOCK):
            part_ref[:, at : at + OUT_BLOCK] = dot_nt(low_ref[...], w_qkv[at : at + OUT_BLOCK]).astype(BF)
        moment("ready")
        self.fetch(6, 7)

        def weights(name):
            if name == "sent":
                for at in range(0, self.width, OUT_BLOCK):
                    span = slice(at, at + OUT_BLOCK)
                    qkv_ref[span] = dot_tn(full[:, span], low_ref[...]).astype(BF)
                    out_ref[span] = dot_tn(grad_full[:, span], mix_ref[...]).astype(BF)
                self.store(0, 1)
                moment("attns")
            moment(name)

        total, self.sent = scatter_part(place, part_ref, self.bufs, self.rows, weights)
        inner, gain_grad, shift_grad = norm_back(total, saved_ref[...], norms_ref[self.norm_at : self.norm_at + 1])
        new_rows = grad_ref[...] + inner
        new_ref[...] = new_rows
        norm_ref[0:1] = gain_grad
        norm_ref[1:2] = shift_grad
        grad_low_ref[...] = new_rows.astype(BF)
        if self.last:
            for name in ("summed", "spread", "late"):
                moment(name)
            return
        self.spread(place, [Gather(place, grad_low_ref, gathered[0], self.gather_sems[0], self.rows)], moment)


class Alone:
    kinds, ins, in_specs, outs, out_specs = (), [], [], [], []

    def scratch(self, sizes):
        return []

    def run(self, place, ins, outs, scratch, moment):
        moment("begin")


class Start:
    kinds = ("mate", "ctx", "fsdp", "twin")

    def __init__(self, sizes, small, hidden, cotangent, piece, q_sub, layers, chains, following):
        self.sizes, self.piece, self.chains, self.following = sizes, piece, chains, following
        self.q_sub, self.layers = q_sub, layers
        lines, lanes = small.shape
        count, self.width = hidden.shape
        self.rows = count // (sizes.ns * sizes.nk)
        group = sizes.nc * sizes.nk * self.rows
        self.ins, self.in_specs = [small, hidden, cotangent], [VMEM_SPEC] * 3
        self.outs = [
            like((sizes.nf, sizes.nc * lines, lanes), F32),
            like((lines, lanes), F32),
            like((lines, self.width), F32),
            like((self.rows, self.width), F32),
            like((self.rows, self.width), BF),
            like((group, 1), jnp.int32),
            like((1, group), jnp.int32),
            like((group, q_sub), F32),
            like((group, q_sub), F32),
            like((layers, sizes.ns * 3 * q_sub), F32),
            like((group, self.width), BF),
        ]
        self.out_specs = [VMEM_SPEC] * 10 + [ANY_SPEC]

    def scratch(self, sizes):
        others = max(sizes.nf - 1, 1)
        small = [DMA((sizes.nc,)), DMA((sizes.nc,)), DMA((others,)), DMA((others,)), DMA(()), DMA(())]
        return small + [pltpu.VMEM((self.rows, self.width), BF)] + Gather.scratch(sizes)

    def run(self, place, ins, outs, scratch, moment):
        sizes, rows, width = self.sizes, self.rows, self.width
        small_ref, hidden_ref, cotangent_ref = ins
        all_ref, twin_ref, norm_ref, stream_ref, grad_ref = outs[:5]
        full_ref = outs[10]
        cs, cr, fs, fr, ts, tr = scratch[:6]
        low_ref = scratch[6]
        lines = small_ref.shape[0]

        def line_of(c):
            return pl.ds(pl.multiple_of(c * lines, lines), lines)

        to_context = [
            push(small_ref, all_ref.at[0, line_of(place.c)], cs.at[step], cr.at[step], place.ahead(step))
            for step in range(1, sizes.nc)
        ]
        to_twin = push(small_ref, twin_ref, ts, tr, place.twin())
        moment("begin")
        for copy in to_context + [to_twin]:
            copy.start()
        for exchange, _ in self.chains:
            exchange.start()
        all_ref[0, line_of(place.c)] = small_ref[...]
        own_rows = pl.ds(pl.multiple_of((place.s * sizes.nk + place.k) * rows, rows), rows)
        part = width // sizes.nf
        for df in range(sizes.nf):
            lanes = pl.ds(pl.multiple_of(lax.rem(place.f + df, sizes.nf) * part, part), part)
            stream_ref[:, df * part : (df + 1) * part] = hidden_ref[own_rows, lanes].astype(F32)
            grad_ref[:, df * part : (df + 1) * part] = cotangent_ref[own_rows, lanes]
        unit_rows, _ = unit_rows_of(stream_ref[...])
        for copy in to_context:
            copy.wait()
        to_across = [
            push(all_ref.at[0], all_ref.at[sizes.nf - step], fs.at[step - 1], fr.at[step - 1], place.across(step))
            for step in range(1, sizes.nf)
        ]
        for copy in to_across:
            copy.start()
        for copy in to_across + [to_twin]:
            copy.wait()
        for df in range(sizes.nf):
            for c in range(sizes.nc):
                at = (df * sizes.nc + c) * self.piece
                norm_ref[:, at : at + self.piece] = all_ref[df, c * lines : (c + 1) * lines, : self.piece]
        low_ref[...] = (unit_rows * norm_ref[0:1] + norm_ref[1:2]).astype(BF)
        gather = Gather(place, low_ref, full_ref, scratch[7:12], rows)
        for exchange, spread in self.chains:
            exchange.wait_own()
            spread.first(place.c)
        for step in range(1, sizes.nc):
            for exchange, spread in self.chains:
                exchange.wait_from(step)
                spread.first(lax.rem(place.c + sizes.nc - step, sizes.nc))
        gather.begin()
        for exchange in self.following:
            exchange.start()
        self.tables(place, small_ref, all_ref, twin_ref, *outs[5:10])
        for step in range(sizes.nc):
            for _, chain in self.chains:
                chain.second(lax.rem(place.c + sizes.nc - step, sizes.nc))
            if step:
                gather.forward(step)
        gather.end()
        for exchange, spread in self.chains:
            exchange.wait_sent()
            for block in range(sizes.nc):
                spread.finish(block)
        for exchange in self.following:
            exchange.finish()


    def tables(self, place, small_ref, all_ref, twin_ref, col_ref, row_ref, cos_ref, sin_ref, bias_ref):
        sizes, q_sub = self.sizes, self.q_sub
        lines = small_ref.shape[0]
        shard = sizes.nk * self.rows
        for c in range(sizes.nc):
            mine = jnp.zeros((1, shard), F32)
            for at in range(sizes.ns):
                line = c * lines + at
                found = all_ref[0, line : line + 1, self.piece : self.piece + shard]
                mine = jnp.where(place.s == at, found, mine)
            row_ref[:, c * shard : (c + 1) * shard] = mine.astype(jnp.int32)
        length = row_ref.shape[1]
        row = row_ref[...].astype(F32)
        at_row = lax.broadcasted_iota(jnp.int32, (length, length), 0)
        at_col = lax.broadcasted_iota(jnp.int32, (length, length), 1)
        col = jnp.sum(jnp.where(at_row == at_col, row, 0.0), -1, keepdims=True)
        col_ref[...] = col.astype(jnp.int32)
        before = jnp.sum(jnp.where(row < col, 1.0, 0.0), -1, keepdims=True)
        places = lax.broadcasted_iota(jnp.int32, (length, 1), 0).astype(F32)
        lane = lax.broadcasted_iota(jnp.int32, (1, q_sub), 1) % HD
        turn = jnp.exp((lane % (ROT // 2)).astype(F32) * (-2.0 * math.log(ROPE_BASE) / ROT))
        angles = (places - before) * jnp.where(lane < ROT, turn, 0.0)
        sine = jnp.sin(angles)
        cos_ref[...] = jnp.cos(angles)
        sin_ref[...] = jnp.where(lane < ROT // 2, -sine, sine)
        for layer in range(self.layers):
            for ds, source in enumerate((small_ref, twin_ref)):
                for at in range(3):
                    line = 3 * layer + at
                    lanes = slice((ds * 3 + at) * q_sub, (ds * 3 + at + 1) * q_sub)
                    bias_ref[layer : layer + 1, lanes] = source[line : line + 1, self.piece + shard :]


class Guest(Rider):
    def __init__(self, rider):
        self.kinds, self.ins, self.outs, self.sems = rider.kinds, rider.ins, rider.outs, rider.sems
        self.rider = rider

    def bind(self, *refs):
        self.rider.bind(*refs)


def comm_kernel(sizes, main, riders, kinds, layout, *refs):
    cuts, at = [], 0
    for size in layout:
        cuts.append(refs[at : at + size])
        at += size
    count = len(riders)
    ins, outs, scratch = cuts[: count + 1], cuts[count + 1 : 2 * count + 2], cuts[2 * count + 2 :]
    place = Place(sizes)
    for i, rider in enumerate(riders):
        rider.bind(place, ins[i + 1], outs[i + 1], scratch[i + 1], main)
    count = greet(place, kinds)

    def moment(name):
        if name == "begin":
            pl.semaphore_wait(pltpu.get_barrier_semaphore(), count)
        for rider in riders:
            rider.at(name)

    main.run(place, ins[0], outs[0], scratch[0], moment)
    moment("end")


def comm_call(sizes, collective_id, main, riders=(), micros=50):
    kinds = set(main.kinds)
    for rider in riders:
        kinds |= set(rider.kinds)
    main_scratch = main.scratch(sizes)
    operands, in_specs = list(main.ins), list(main.in_specs)
    outs, out_specs = list(main.outs), list(main.out_specs)
    scratch = list(main_scratch)
    aliases = {}
    for rider in riders:
        if rider.aliased:
            aliases[len(operands)] = len(outs)
        operands += rider.ins
        in_specs += [ANY_SPEC] * len(rider.ins)
        outs += rider.outs
        out_specs += [ANY_SPEC] * len(rider.outs)
        scratch += rider.sems
    layout = [len(main.ins)] + [len(rider.ins) for rider in riders]
    layout += [len(main.outs)] + [len(rider.outs) for rider in riders]
    layout += [len(main_scratch)] + [len(rider.sems) for rider in riders]
    results = pl.pallas_call(
        functools.partial(comm_kernel, sizes, main, riders, kinds, layout),
        out_shape=outs,
        in_specs=in_specs,
        out_specs=out_specs,
        scratch_shapes=scratch,
        input_output_aliases=aliases,
        compiler_params=pltpu.CompilerParams(
            collective_id=collective_id, has_side_effects=True, vmem_limit_bytes=VMEM_BYTES
        ),
        cost_estimate=pl.CostEstimate(flops=0, bytes_accessed=micros * 3 * MIB, transcendentals=0),
    )(*operands)
    groups, at = [], 0
    for size in [len(main.outs)] + [len(rider.outs) for rider in riders]:
        groups.append(list(results[at : at + size]))
        at += size
    return groups[0], groups[1:]


def finish_kernel(count, hidden, *refs):
    ins, (qkv_out, out_out, gate_up_out, down_out) = refs[: 5 * count], refs[5 * count :]
    triple, rows, q_cols = qkv_out.shape[1:]
    for layer in range(count):

        @pl.when(pl.program_id(0) == layer)
        def _():
            qkv, out, gate, up, down = ins[5 * layer : 5 * layer + 5]

            def some(span):
                for at in range(triple):
                    qkv_out[0, at, span] = qkv[span, at * q_cols : (at + 1) * q_cols].astype(F32)
                out_out[0, span] = out[span].astype(F32)
                gate_up_out[0, span, 0] = gate[span, :hidden].astype(F32)
                gate_up_out[0, span, 1] = up[span, :hidden].astype(F32)
                down_out[0, span] = down[span, :hidden].astype(F32)

            by_rows(rows, 64, some)


def finish(grads, q_cols, hidden):
    count = len(grads)
    rows = grads[0][0].shape[0]
    shapes = [(3, rows, q_cols), (rows, q_cols), (rows, 2, hidden), (rows, hidden)]

    def block(shape):
        return pl.BlockSpec((1,) + shape, lambda layer: (layer,) + (0,) * len(shape))

    return pl.pallas_call(
        functools.partial(finish_kernel, count, hidden),
        grid=(count,),
        out_shape=[jax.ShapeDtypeStruct((count,) + shape, F32) for shape in shapes],
        in_specs=[VMEM_SPEC] * (5 * count),
        out_specs=[block(shape) for shape in shapes],
        compiler_params=pltpu.CompilerParams(vmem_limit_bytes=VMEM_BYTES),
    )(*[one for layer in grads for one in layer])


def body(
    mesh,
    hidden_in,
    segment_ids,
    norm_gains,
    norm_shifts,
    qkv_weight,
    qkv_bias,
    out_weight,
    gate_up_weight,
    down_weight,
    cotangent,
):
    ns, shard_rows, width = hidden_in.shape
    sizes = Sizes(mesh, ns)
    nf, nc, nk, nt = sizes.nf, sizes.nc, sizes.nk, sizes.nt
    f, c, t = lax.axis_index("fsdp"), lax.axis_index("context"), lax.axis_index("tensor")
    s = t // nk
    layers = qkv_weight.shape[0]
    rows = shard_rows // nk
    part = width // nf
    piece = part // nc
    q_cols = qkv_weight.shape[3]
    q_sub = q_cols // nc
    hidden = gate_up_weight.shape[3]
    f_sub = -(-hidden // (nc * TILE)) * TILE
    f_cols = nc * f_sub

    qkv_flat = qkv_weight.transpose(0, 2, 1, 3).reshape(layers * 3 * piece, q_cols)
    out_flat = out_weight.reshape(layers * piece, q_cols)
    fill = ((0, 0), (0, f_cols - hidden))
    down_flat = jnp.pad(down_weight.reshape(layers * piece, hidden), fill)
    gate_up_flat = jnp.pad(gate_up_weight, ((0, 0), (0, 0)) + fill).reshape(layers * piece, 2 * f_cols)

    def exchange(name, layer, when="begin", finish="end"):
        first = layer * piece
        array, corners, sub = {
            "qkv": (qkv_flat, [((3 * layer + at) * piece, 0) for at in range(3)], q_sub),
            "out": (out_flat, [(first, 0)], q_sub),
            "gate": (gate_up_flat, [(first, 0)], f_sub),
            "up": (gate_up_flat, [(first, f_cols)], f_sub),
            "down": (down_flat, [(first, 0)], f_sub),
        }[name]
        return WeightExchange(sizes, piece, array, corners, sub, when, finish)

    norms = jnp.stack([norm_gains, norm_shifts], axis=2).reshape(4 * layers, piece).astype(F32)
    own_bias = lax.dynamic_slice_in_dim(qkv_bias, c * q_sub, q_sub, 2).reshape(3 * layers, q_sub).astype(F32)
    lines = -(-max(4 * layers, 3 * layers, ns) // 8) * 8

    def lined(value):
        return jnp.pad(value, ((0, lines - value.shape[0]), (0, 0)))

    small = jnp.concatenate([lined(norms), lined(segment_ids.astype(F32)), lined(own_bias)], axis=1)
    chains = []
    for name in ("qkv", "out"):
        moved = exchange(name, 0, finish=None)
        chains.append((moved, Spread(sizes, moved, blocks=nc, steps=(None, None))))
    following = [exchange(name, 0, finish=None) for name in ("gate", "up")]
    start = Start(
        sizes,
        small,
        hidden_in.reshape(ns * shard_rows, width),
        cotangent.reshape(ns * shard_rows, width),
        piece,
        q_sub,
        layers,
        chains,
        following,
    )
    guests = [Guest(one) for chain in chains for one in chain] + [Guest(one) for one in following]
    results, extra = comm_call(sizes, 1, start, guests, 80)
    norm_rows, stream, grad_low = results[2:5]
    tables, bias_rows, full_one = results[5:9], results[9], results[10]
    w_qkv, w_out, gate_mine, up_mine = (extra[at][0] for at in (1, 3, 4, 5))

    def norm_of(layer, which):
        return (norm_rows, (layer * 2 + which) * 2)

    kept = []
    gate_own = None
    for layer in range(layers):
        more = layer + 1 < layers
        down_first = exchange("down", layer, finish=None)
        riders = [Spread(sizes, gate_mine) if gate_own is None else SpreadRelay(sizes, gate_own), Spread(sizes, up_mine)]
        riders += [down_first, Spread(sizes, down_first, steps=("inside0", "spread"))]
        if more:
            riders += [exchange("qkv", layer + 1, "spread"), exchange("out", layer + 1, "spread")]
        main = AttnForward(
            full_one, w_qkv, w_out, (bias_rows, layer), tables, stream, norm_of(layer, 1)
        )
        results, extra = comm_call(sizes, 2 + 2 * layer, main, riders, 85)
        middle, lse, proj, mixed, q_rot, k_rot, full_two = results
        w_gate, w_up, w_down = extra[0][0], extra[1][0], extra[3][0]
        attn_kept = (full_one, w_qkv, w_out, (proj, mixed, q_rot, k_rot), lse, stream)
        if more:
            gate_first = exchange("gate", layer + 1, finish=None)
            riders = [Spread(sizes, extra[4][0]), Spread(sizes, extra[5][0])]
            riders += [gate_first, SpreadOwn(sizes, gate_first, blocks=nc, steps=("summed",))]
            riders.append(exchange("up", layer + 1, "spread"))
            main = FfnForward(
                full_two, w_gate, w_up, w_down, middle, norm_of(layer + 1, 0)
            )
        else:
            riders = []
            main = FfnForward(full_two, w_gate, w_up, w_down, middle, None, grad_low)
        results, extra = comm_call(sizes, 3 + 2 * layer, main, riders, 55)
        stream, gates, ups, acts, full = results
        kept.append(attn_kept + (full_two, w_gate, w_up, w_down, gates, ups, acts, middle))
        if more:
            full_one = full
            w_qkv, w_out, _, gate_own, up_mine = (one[0] for one in extra)
        else:
            grad_full = full

    first_id = 2 + 2 * layers
    stream_out = stream
    grad = grad_low.astype(F32)
    firsts, totals = {}, {}
    done, norm_grads, bias_grads = {}, {}, {}
    calls = [0]

    def sub_of(name):
        return q_sub if name in ("qkv", "out") else f_sub

    def run(main, steps, others, micros):
        riders, after = [], []
        here = {}

        def ride(rider, what, name):
            here[(what, name)] = rider
            riders.append(rider)
            after.append((what, name))

        for what, name, layer, when in steps:
            at = (name, layer)
            if what == "first":
                ride(GradFirst(sizes, name, *main.kept[main.names.index(name)].shape, when), what, at)
            elif what == "middle":
                ride(GradMiddle(sizes, here.get(("first", at)) or firsts[at], when), what, at)
            else:
                ride(GradExchange(sizes, here.get(("middle", at)) or totals[at], sub_of(name), when), what, at)
        for name, rider in others:
            ride(rider, "other", name)
        results, extra = comm_call(sizes, first_id + calls[0], main, riders, micros)
        calls[0] += 1
        for (what, at), out in zip(after, extra):
            if what == "first":
                firsts[at] = (results[len(main.results) + main.names.index(at[0])], *out)
            elif what == "middle":
                totals[at] = out[0]
            else:
                done[at] = out[0]
        return results

    attn, ffn = ("qkv", "out"), ("gate", "up")
    for layer in range(layers - 1, -1, -1):
        full_one, w_qkv, w_out, attn_kept, lse, stream, full_two, w_gate, w_up, w_down, gates, ups, acts, middle = kept[
            layer
        ]
        main = FfnBack(grad_full, w_gate, w_up, w_down, gates, ups, acts, full_two, grad, middle, norm_of(layer, 1))
        top = layer + 1 == layers
        steps, others = [], []
        if not top:
            steps += [("exchange", "gate", layer + 1, "begin"), ("exchange", "up", layer + 1, "spread")]
            steps += [("exchange", name, layer + 1, "late") for name in attn]
        steps += [("first", "down", layer, "downs"), ("first", "gate", layer, "gates"), ("first", "up", layer, "ups")]
        steps += [("middle", "down", layer, ("inside1", "inside2", "late"))]
        if not top:
            steps += [("middle", name, layer, ("late", "late", "end")) for name in ffn]
        grad, norm_grads[(layer, 1)], _, _, _, middle_full = run(main, steps, others, 60)
        main = AttnBack(
            middle_full, w_qkv, w_out, attn_kept, full_one, tables, lse, grad, stream, norm_of(layer, 0), layer == 0
        )
        steps, others = [("exchange", "down", layer, "begin")], []
        if top:
            others.append(("block_out", share_rows(sizes, stream_out.astype(BF))))
        if not top:
            steps += [("exchange", "gate", layer, "begin"), ("exchange", "up", layer, "inside0")]
        if layer == 0:
            none = jnp.zeros((2, width), F32)
            pairs = [[norm_grads.get((at, which), none) for which in range(2)] for at in range(layers)]
            lines = jnp.stack([jnp.stack(pair, 1) for pair in pairs], 1).reshape(4 * layers, width)
            none = jnp.zeros((1, ns * 3 * q_sub), F32)
            bias = jnp.concatenate([bias_grads.get(at, none) for at in range(layers)]).reshape(layers, ns, 3, q_sub)
            bias = bias.transpose(1, 0, 2, 3).reshape(ns, 3 * layers, q_sub)
            bias = jnp.pad(bias, ((0, 0), (0, -3 * layers % 8), (0, 0)))
            others += [
                ("input_grad", MainRows(sizes, rows, width, "summed")),
                ("norm", NormSum(sizes, lines, (0, 2 * layers), piece, ("summed", "spread"))),
                ("bias", BiasSum(sizes, bias, 3, ("attns", "inside0"))),
            ]
            steps += [("first", name, 0, "attns") for name in attn]
            steps += [("middle", name, 0, ("inside0", "inside0", "inside2")) for name in attn]
            steps += [("exchange", name, 0, "inside2") for name in attn]
        else:
            steps += [("middle", name, layer, ("begin", "inside0", "late")) for name in (ffn if top else ())]
            steps += [("first", name, layer, "attns") for name in attn]
            steps += [("middle", name, layer, ("spread", "spread", "late")) for name in attn]
        results = run(main, steps, others, 60)
        grad, norm_grads[(layer, 0)], bias_grads[layer] = results[:3]
        if layer > 0:
            grad_full = results[5]
    block_out = done["block_out"].reshape(ns, shard_rows, width)
    input_grad = done["input_grad"].reshape(ns, shard_rows, width).astype(F32)
    norm_total = done["norm"].reshape(2, layers, 2, piece)
    bias_total = done["bias"][:, : 3 * layers].reshape(nc, layers, 3, q_sub)
    bias_total = bias_total.transpose(1, 2, 0, 3).reshape(layers, 3, q_cols)

    grads = [[done[(name, layer)] for name in ("qkv", "out", "gate", "up", "down")] for layer in range(layers)]
    qkv_grad, out_grad, gate_up_grad, down_grad = finish(grads, q_cols, hidden)
    return (
        block_out,
        input_grad,
        norm_total[0],
        norm_total[1],
        qkv_grad.transpose(0, 2, 1, 3),
        bias_total,
        out_grad,
        gate_up_grad,
        down_grad,
    )


def solution(mesh):
    return jax.shard_map(
        functools.partial(body, mesh),
        mesh=mesh,
        in_specs=(
            P("fsdp", "context", None),
            P("fsdp", "context"),
            P(None, None, ("fsdp", "context")),
            P(None, None, ("fsdp", "context")),
            P(None, ("fsdp", "context"), None, "tensor"),
            P(None, None, "tensor"),
            P(None, ("fsdp", "context"), "tensor"),
            P(None, ("fsdp", "context"), None, "tensor"),
            P(None, ("fsdp", "context"), "tensor"),
            P("fsdp", "context", None),
        ),
        out_specs=(
            P("fsdp", "context", None),
            P("fsdp", "context", None),
            P(None, None, ("fsdp", "context")),
            P(None, None, ("fsdp", "context")),
            P(None, ("fsdp", "context"), None, "tensor"),
            P(None, None, "tensor"),
            P(None, ("fsdp", "context"), "tensor"),
            P(None, ("fsdp", "context"), None, "tensor"),
            P(None, ("fsdp", "context"), "tensor"),
        ),
        check_vma=False,
    )
```

```python
import functools
import math

import jax
import jax.numpy as jnp
from jax import lax
from jax.experimental import pallas as pl
from jax.experimental.pallas import tpu as pltpu
from jax.sharding import PartitionSpec as P

HD = 64
ROT = 16
EPS = 1e-05
ROPE_BASE = 10000.0
NEGATIVE = -1e30
MESH = pl.DeviceIdType.MESH
BF = jnp.bfloat16
F32 = jnp.float32
MIB = 2**20
TILE = 128
VMEM_BYTES = 58 * MIB


def dot_nn(a, b):
    return jnp.dot(a, b, preferred_element_type=F32)


def dot_nt(a, b):
    return lax.dot_general(a, b, (((1,), (1,)), ((), ())), preferred_element_type=F32)


def dot_tn(a, b):
    return lax.dot_general(a, b, (((0,), (0,)), ((), ())), preferred_element_type=F32)


class Sizes:
    def __init__(self, mesh, ns):
        self.nf, self.nc, self.nt = mesh.shape["fsdp"], mesh.shape["context"], mesh.shape["tensor"]
        self.ns = ns
        self.nk = self.nt // ns


class Place:
    def __init__(self, sizes):
        self.sizes = sizes
        self.f = lax.axis_index("fsdp")
        self.c = lax.axis_index("context")
        self.t = lax.axis_index("tensor")
        self.s, self.k = self.t // sizes.nk, lax.rem(self.t, sizes.nk)

    def mate(self):
        return {"tensor": self.t + 1 - 2 * self.k}

    def twin(self):
        return {"tensor": self.t + self.sizes.nk * (1 - 2 * self.s)}

    def right(self):
        return {"context": self.c + 1}

    def left(self):
        return {"context": self.c - 1}

    def ahead(self, step):
        return {"context": lax.rem(self.c + step, self.sizes.nc)}

    def across(self, step):
        return {"fsdp": lax.rem(self.f + step, self.sizes.nf)}

    def plane(self, df, dt):
        return {"fsdp": lax.rem(self.f + df, self.sizes.nf), "tensor": lax.rem(self.t + dt, self.sizes.nt)}


def greet(place, kinds):
    barrier = pltpu.get_barrier_semaphore()
    nc, nf = place.sizes.nc, place.sizes.nf

    def signal(device):
        pl.semaphore_signal(barrier, inc=1, device_id=device, device_id_type=MESH)

    count = 0
    if "plane" in kinds:
        for df in range(nf):
            for dt in range(place.sizes.nt):
                if df or dt:
                    signal(place.plane(df, dt))
        count += nf * place.sizes.nt - 1
        kinds = set(kinds) - {"mate", "fsdp", "twin"}
    if "mate" in kinds:
        signal(place.mate())
        count += 1
    if "ctx" in kinds:
        for step in range(1, nc):
            signal(place.ahead(step))
        count += nc - 1
    elif "line" in kinds:

        @pl.when(place.c > 0)
        def _():
            signal(place.left())

        @pl.when(place.c < nc - 1)
        def _():
            signal(place.right())

        count += jnp.minimum(place.c, 1) + jnp.minimum(nc - 1 - place.c, 1)
    if "fsdp" in kinds:
        for step in range(1, nf):
            signal(place.across(step))
        count += nf - 1
    if "twin" in kinds:
        signal(place.twin())
        count += 1
    return count


def push(src, dst, send, recv, device):
    return pltpu.make_async_remote_copy(
        src_ref=src, dst_ref=dst, send_sem=send, recv_sem=recv, device_id=device, device_id_type=MESH
    )


DMA = pltpu.SemaphoreType.DMA
VMEM_SPEC = pl.BlockSpec(memory_space=pltpu.VMEM)
ANY_SPEC = pl.BlockSpec(memory_space=pl.ANY)


HALVES = 2


class Gather:
    def __init__(self, place, own, out, sems, rows):
        self.place, self.own, self.out, self.rows = place, own, out, rows
        self.piece = rows // HALVES
        self.local, self.line_send, self.line_recv, self.mate_send, self.mate_recv = sems

    @staticmethod
    def scratch(sizes):
        nc = sizes.nc
        return [DMA(()), DMA((2, nc, HALVES)), DMA((nc, HALVES)), DMA((nc, HALVES)), DMA((nc, HALVES))]

    def slot(self, source, k, half):
        at = (source * self.place.sizes.nk + k) * self.rows + half * self.piece
        return self.out.at[pl.ds(pl.multiple_of(at, self.piece), self.piece)]

    def origin(self, source, half, first):
        if first:
            return self.own.at[pl.ds(half * self.piece, self.piece)]
        return self.slot(source, self.place.k, half)

    def line(self, source, half, device, first, way):
        return push(
            self.origin(source, half, first),
            self.slot(source, self.place.k, half),
            self.line_send.at[way, source, half],
            self.line_recv.at[source, half],
            device,
        )

    def pass_on(self, source, half, first):
        return push(
            self.origin(source, half, first),
            self.slot(source, self.place.k, half),
            self.mate_send.at[source, half],
            self.mate_recv.at[source, half],
            self.place.mate(),
        )

    def keep(self):
        at = (self.place.c * self.place.sizes.nk + self.place.k) * self.rows
        target = self.out.at[pl.ds(pl.multiple_of(at, self.rows), self.rows)]
        return pltpu.make_async_copy(self.own, target, self.local)

    def begin(self):
        place, c, nc = self.place, self.place.c, self.place.sizes.nc
        for half in range(HALVES):

            @pl.when(c < nc - 1)
            def _():
                self.line(c, half, place.right(), True, 0).start()

            @pl.when(c > 0)
            def _():
                self.line(c, half, place.left(), True, 1).start()

        for half in range(HALVES):
            self.pass_on(c, half, True).start()
        self.keep().start()

    def forward(self, step):
        place, c, nc = self.place, self.place.c, self.place.sizes.nc
        source, other = c - step, c + step
        for half in range(HALVES):

            @pl.when(source >= 0)
            def _():
                self.line(source, half, place.left(), False, 0).wait_recv()

                @pl.when(c < nc - 1)
                def _():
                    self.line(source, half, place.right(), False, 0).start()

                self.pass_on(source, half, False).start()

            @pl.when(other <= nc - 1)
            def _():
                self.line(other, half, place.right(), False, 1).wait_recv()

                @pl.when(c > 0)
                def _():
                    self.line(other, half, place.left(), False, 1).start()

                self.pass_on(other, half, False).start()

    def end(self):
        place, c, nc = self.place, self.place.c, self.place.sizes.nc
        self.keep().wait()
        for source in range(nc):
            for half in range(HALVES):
                arrival = self.slot(source, 1 - place.k, half)
                push(
                    arrival, arrival, self.mate_send.at[source, half], self.mate_recv.at[source, half], place.mate()
                ).wait_recv()
                self.pass_on(source, half, False).wait_send()

                @pl.when((source <= c) & (c < nc - 1))
                def _():
                    self.line(source, half, place.right(), False, 0).wait_send()

                @pl.when((source >= c) & (c > 0))
                def _():
                    self.line(source, half, place.left(), False, 1).wait_send()


def scatter_part(place, part_ref, bufs, rows, moment):
    nc, nk, c, k = place.sizes.nc, place.sizes.nk, place.c, place.k
    piece = rows // HALVES
    mate_buf, to_right, to_left, from_left, from_right = bufs[:5]
    mate_send, mate_recv, right_send, right_recv, left_send, left_recv = bufs[5:]

    def block(dest, kk):
        return part_ref.at[pl.ds(pl.multiple_of((dest * nk + kk) * rows, rows), rows)]

    def mate_copy(dest):
        return push(
            block(dest, 1 - k), mate_buf.at[dest], mate_send.at[dest], mate_recv.at[dest], place.mate()
        )

    def lines(half):
        return slice(half * piece, (half + 1) * piece)

    def right_copy(dest, half):
        return push(
            to_right.at[dest, lines(half)],
            from_left.at[dest, lines(half)],
            right_send.at[dest, half],
            right_recv.at[dest, half],
            place.right(),
        )

    def left_copy(dest, half):
        return push(
            to_left.at[dest, lines(half)],
            from_right.at[dest, lines(half)],
            left_send.at[dest, half],
            left_recv.at[dest, half],
            place.left(),
        )

    def each(visit_right, visit_left, count, after=lambda step: None):
        for step in range(nc - 1):
            far = nc - 1 - step
            for half in range(count):

                @pl.when(far > c)
                def _():
                    visit_right(far, half)

                @pl.when(step < c)
                def _():
                    visit_left(step, half)

            after(step)

    def send_mate(dest, half):
        mate_copy(dest).start()

    each(send_mate, send_mate, 1)
    mate_copy(c).start()
    moment("sent")

    def chip_sum(dest, half):
        if half == 0:
            mate_copy(dest).wait_recv()
        at = pl.multiple_of((dest * nk + k) * rows + half * piece, piece)
        return part_ref[pl.ds(at, piece)].astype(F32) + mate_buf[dest, lines(half)].astype(F32)

    def pass_right(dest, half):
        total = chip_sum(dest, half)
        to_right[dest, lines(half)] = total.astype(BF)

        @pl.when(c > 0)
        def _():
            right_copy(dest, half).wait_recv()
            to_right[dest, lines(half)] = (total + from_left[dest, lines(half)].astype(F32)).astype(BF)

        right_copy(dest, half).start()

    def pass_left(dest, half):
        total = chip_sum(dest, half)
        to_left[dest, lines(half)] = total.astype(BF)

        @pl.when(c < nc - 1)
        def _():
            left_copy(dest, half).wait_recv()
            to_left[dest, lines(half)] = (total + from_right[dest, lines(half)].astype(F32)).astype(BF)

        left_copy(dest, half).start()

    def inside(step):
        for at in range(3):
            if at * (nc - 1) // 3 == step:
                moment("inside%d" % at)

    each(pass_right, pass_left, HALVES, inside)
    totals = []
    for half in range(HALVES):
        total = chip_sum(c, half)

        @pl.when(c > 0)
        def _():
            right_copy(c, half).wait_recv()

        @pl.when(c < nc - 1)
        def _():
            left_copy(c, half).wait_recv()

        total = total + jnp.where(c > 0, from_left[c, lines(half)].astype(F32), 0.0)
        totals.append(total + jnp.where(c < nc - 1, from_right[c, lines(half)].astype(F32), 0.0))
    def sent():
        for dest in range(nc):
            mate_copy(dest).wait_send()
            for half in range(HALVES):

                @pl.when(dest > c)
                def _():
                    right_copy(dest, half).wait_send()

                @pl.when(dest < c)
                def _():
                    left_copy(dest, half).wait_send()

    return jnp.concatenate(totals, 0), sent


def scatter_scratch(sizes, rows, width):
    nc = sizes.nc
    return [pltpu.VMEM((nc, rows, width), BF) for _ in range(5)] + [DMA((nc,)) for _ in range(2)] + [
        DMA((nc, HALVES)) for _ in range(4)
    ]


N_SCATTER = 11


class Rider:
    kinds = ()
    ins, outs, sems = [], [], []
    aliased = False

    def bind(self, place, ins, outs, sems, main):
        self.place, self.r_ins, self.r_outs, self.r_sems, self.main = place, ins, outs, sems, main

    def at(self, moment):
        pass


class Exchange(Rider):
    kinds = ("ctx",)

    def __init__(self, sizes, ins, out, pieces, rows, sub, when="begin", finish="end"):
        self.ins, self.outs, self.pieces, self.when, self.last = ins, [out], pieces, when, finish
        count = max(sizes.nc - 1, 1)
        self.sub = sub
        self.sems = [DMA(()), DMA((count,)), DMA((count,)), pltpu.VMEM((rows, sub * len(pieces)), BF)]

    def at(self, moment):
        if moment == self.when:
            self.start()
        if moment == self.last:
            self.finish()

    def start(self):
        place, nc = self.place, self.place.sizes.nc
        local, send, recv, held = self.r_sems
        for step in range(1, nc):
            for source_of, target_of in self.pieces:
                push(
                    source_of(self.r_ins, lax.rem(place.c + step, nc)),
                    target_of(self.r_outs[0], place.c),
                    send.at[step - 1],
                    recv.at[step - 1],
                    place.ahead(step),
                ).start()
        for at, (source_of, _) in enumerate(self.pieces):
            lanes = pl.ds(at * self.sub, self.sub)
            pltpu.make_async_copy(source_of(self.r_ins, place.c), held.at[:, lanes], local).start()

    def wait_own(self):
        local, _, _, held = self.r_sems
        pltpu.make_async_copy(held, held, local).wait()
        for at, (_, target_of) in enumerate(self.pieces):
            lanes = pl.ds(at * self.sub, self.sub)
            pltpu.make_async_copy(held.at[:, lanes], target_of(self.r_outs[0], self.place.c), local).start()
        pltpu.make_async_copy(held, held, local).wait()

    def wait_from(self, step):
        whole = self.whole()
        _, send, recv, _ = self.r_sems
        push(whole, whole, send.at[step - 1], recv.at[step - 1], self.place.ahead(step)).wait_recv()

    def wait_sent(self):
        whole = self.whole()
        _, send, recv, _ = self.r_sems
        for step in range(1, self.place.sizes.nc):
            push(whole, whole, send.at[step - 1], recv.at[step - 1], self.place.ahead(step)).wait_send()

    def finish(self):
        self.wait_own()
        for step in range(1, self.place.sizes.nc):
            self.wait_from(step)
        self.wait_sent()


class WeightExchange(Exchange):
    def __init__(self, sizes, rows, array, corners, sub, when="begin", finish="end"):
        pieces = [self.piece(first, rows, base, sub, at) for at, (first, base) in enumerate(corners)]
        out = jax.ShapeDtypeStruct((sizes.nc * rows, sub * len(pieces)), BF)
        super().__init__(sizes, [array], out, pieces, rows, sub, when, finish)
        self.rows = rows

    @staticmethod
    def piece(first, rows, base, sub, position):
        def source_of(refs, dest):
            return refs[0].at[pl.ds(first, rows), pl.ds(pl.multiple_of(base + dest * sub, TILE), sub)]

        def target_of(out, source):
            return out.at[pl.ds(pl.multiple_of(source * rows, rows), rows), pl.ds(position * sub, sub)]

        return source_of, target_of

    def whole(self):
        return self.r_outs[0].at[pl.ds(0, self.rows)]


class GradExchange(Exchange):
    def __init__(self, sizes, total, sub, when="begin", finish="end"):
        self.middle = total if isinstance(total, GradMiddle) else None
        shape = self.middle.outs[0].shape if self.middle else total.shape
        rows = shape[0] // sizes.nc
        count = shape[1] // sub
        out = jax.ShapeDtypeStruct((rows, sizes.nc * shape[1]), BF)
        pieces = [self.piece(rows, sub, position, sizes.nc) for position in range(count)]
        super().__init__(sizes, [] if self.middle else [total], out, pieces, rows, sub, when, finish)
        self.rows = rows

    def start(self):
        if self.middle:
            self.r_ins = [self.middle.total]
        super().start()

    @staticmethod
    def piece(rows, sub, position, nc):
        def source_of(refs, dest):
            return refs[0].at[pl.ds(pl.multiple_of(dest * rows, rows), rows), pl.ds(position * sub, sub)]

        def target_of(out, source):
            return out.at[:, pl.ds(pl.multiple_of(position * nc * sub + source * sub, TILE), sub)]

        return source_of, target_of

    def whole(self):
        return self.r_ins[0].at[pl.ds(0, self.rows)]


class Spread(Rider):
    kinds = ("fsdp", "twin")

    def __init__(self, sizes, mine, blocks=1, steps=("begin", "inside1")):
        if isinstance(mine, Exchange):
            self.source, shape, self.ins = mine, mine.outs[0].shape, []
        else:
            self.source, shape, self.ins = None, mine.shape, [mine]
        rows, self.width = shape
        self.part, self.blocks, self.rows, self.steps = rows, blocks, rows // blocks, steps
        self.outs = [jax.ShapeDtypeStruct((sizes.nf * rows, sizes.ns * self.width), BF)]
        others = max(sizes.nf - 1, 1)
        self.sems = [DMA((blocks,))] + [DMA((blocks, others)) for _ in range(8)] + [DMA((blocks,)) for _ in range(4)]
        self.sems.append(pltpu.VMEM((rows, self.width), BF))

    def at(self, moment):
        if moment == self.steps[0]:
            if self.source is not None:
                self.source.finish()
            for block in range(self.blocks):
                self.first(block)
        if moment == self.steps[1]:
            for block in range(self.blocks):
                self.second(block)
        if moment == "end":
            for block in range(self.blocks):
                self.finish(block)

    def span(self, df, block, half, whole=False):
        length = self.rows if whole else self.rows // 2
        at = df * self.part + block * self.rows + half * (self.rows // 2)
        return pl.ds(pl.multiple_of(at, length), length)

    def mine(self, block, half, whole=False):
        ref = self.r_ins[0] if self.source is None else self.source.r_outs[0]
        return ref.at[self.span(0, block, half, whole)]

    def out(self, ds, df, block, half, whole=False):
        return self.r_outs[0].at[self.span(df, block, half, whole), pl.ds(ds * self.width, self.width)]

    def copies(self, block, stage):
        place, nf, sems, out = self.place, self.place.sizes.nf, self.r_sems, []
        for step in range(1, nf):
            at, df = step - 1, nf - step
            across = place.across(step)
            source, target, pair, device = [
                (self.mine(block, 0), self.out(0, df, block, 0), 1, across),
                (self.mine(block, 1), self.out(0, df, block, 1), 3, across),
                (self.out(1, 0, block, 1), self.out(1, df, block, 1), 5, across),
            ][stage]
            out.append(push(source, target, sems[pair].at[block, at], sems[pair + 1].at[block, at], device))
            if stage == 2:
                source, target = self.out(0, df, block, 0), self.out(1, df, block, 0)
                out.append(push(source, target, sems[7].at[block, at], sems[8].at[block, at], place.twin()))
        if stage < 2:
            half, pair = (1, 9) if stage == 0 else (0, 11)
            out.append(
                push(
                    self.mine(block, half),
                    self.out(1, 0, block, half),
                    sems[pair].at[block],
                    sems[pair + 1].at[block],
                    place.twin(),
                )
            )
        return out

    def keep(self, block, inward):
        held = self.r_sems[13].at[self.span(0, block, 0, True)]
        ends = (self.mine(block, 0, True), held) if inward else (held, self.out(0, 0, block, 0, True))
        return pltpu.make_async_copy(*ends, self.r_sems[0].at[block])

    def first(self, block):
        for stage in range(2):
            for copy in self.copies(block, stage):
                copy.start()
        self.keep(block, True).start()

    def second(self, block):
        for copy in self.copies(block, 0):
            copy.wait_recv()
        for copy in self.copies(block, 2):
            copy.start()
        self.keep(block, True).wait()
        self.keep(block, False).start()

    def finish(self, block):
        for copy in self.copies(block, 0):
            copy.wait_send()
        for stage in (1, 2):
            for copy in self.copies(block, stage):
                copy.wait_recv()
                copy.wait_send()
        self.keep(block, False).wait()


class SpreadOwn(Spread):
    def at(self, moment):
        if moment == self.steps[0]:
            if self.source is not None:
                self.source.finish()
            for block in range(self.blocks):
                self.first(block)
        if moment == "end" and self.steps[0] is not None:
            for block in range(self.blocks):
                self.finish(block)

    def finish(self, block):
        self.keep(block, True).wait()
        self.keep(block, False).start()
        for stage in range(2):
            for copy in self.copies(block, stage):
                copy.wait_recv()
                copy.wait_send()
        self.keep(block, False).wait()


class SpreadRelay(Rider):
    kinds = ("fsdp", "twin")
    aliased = True

    def __init__(self, sizes, whole, when="begin"):
        self.ins, self.outs, self.when = [whole], [jax.ShapeDtypeStruct(whole.shape, BF)], when
        self.part, self.width = whole.shape[0] // sizes.nf, whole.shape[1] // sizes.ns
        others = max(sizes.nf - 1, 1)
        self.sems = [DMA((others,)) for _ in range(4)]
        self.blocks = sizes.nc

    def copies(self):
        out, place, nf = [], self.place, self.place.sizes.nf
        rows, half = self.part // self.blocks, self.part // self.blocks // 2
        for step in range(1, nf):
            at, df = step - 1, nf - step
            for block in range(self.blocks):
                low, high = block * rows, block * rows + half
                lanes = pl.ds(self.width, self.width)
                first = pl.ds(df * self.part + low, half)
                second = pl.ds(df * self.part + high, half)
                whole = self.r_outs[0]
                out.append(
                    push(
                        whole.at[pl.ds(high, half), lanes],
                        whole.at[second, lanes],
                        self.sems_of(0, at),
                        self.sems_of(1, at),
                        place.across(step),
                    )
                )
                out.append(
                    push(
                        whole.at[first, pl.ds(0, self.width)],
                        whole.at[first, lanes],
                        self.sems_of(2, at),
                        self.sems_of(3, at),
                        place.twin(),
                    )
                )
        return out

    def sems_of(self, kind, at):
        return self.r_sems[kind].at[at]

    def at(self, moment):
        if moment == self.when:
            for copy in self.copies():
                copy.start()
        if moment == "end":
            place, half = self.place, self.part // 2
            for step in range(1, place.sizes.nf):
                at = step - 1
                bytes_of = self.r_outs[0].at[pl.ds(0, half), pl.ds(0, self.width)]
                for kind, device in ((0, place.across(step)), (2, place.twin())):
                    push(bytes_of, bytes_of, self.sems_of(kind, at), self.sems_of(kind + 1, at), device).wait()


class GradFirst(Rider):
    kinds = ("fsdp", "twin")

    def __init__(self, sizes, name, rows, width, when):
        self.name, self.when, self.taken = name, when, False
        self.part = rows // sizes.nf
        self.half = self.part // 2
        self.width = width // sizes.ns
        others = max(sizes.nf - 1, 1)
        self.outs = [
            jax.ShapeDtypeStruct((others, self.half, width), BF),
            jax.ShapeDtypeStruct((sizes.nf, self.half, self.width), BF),
        ]
        self.sems = [DMA((others,)), DMA((others,)), DMA((sizes.nf,)), DMA((sizes.nf,))]

    def copies(self):
        place, nf = self.place, self.place.sizes.nf
        grads, (low, high) = self.main.grads[self.name], self.r_outs
        xs, xr, ys, yr = self.r_sems
        out = []
        for step in range(1, nf):
            at = step - 1
            out.append(
                push(grads.at[pl.ds(step * self.part, self.half)], low.at[at], xs.at[at], xr.at[at], place.across(step))
            )
        for df in range(nf):
            rows = pl.ds(df * self.part + self.half, self.half)
            out.append(
                push(grads.at[rows, pl.ds(self.width, self.width)], high.at[df], ys.at[df], yr.at[df], place.twin())
            )
        return out

    def at(self, moment):
        if moment == self.when:
            for copy in self.copies():
                copy.start()
        if moment == "end":
            if not self.taken:
                self.wait_recv()
            for copy in self.copies():
                copy.wait_send()

    def wait_recv(self):
        self.taken = True
        for copy in self.copies():
            copy.wait_recv()


class GradMiddle(Rider):
    kinds = ("fsdp", "twin")

    def __init__(self, sizes, source, steps=("begin", "sent", "late")):
        self.steps = steps
        if isinstance(source, GradFirst):
            self.source, self.ins = source, []
            low, high = source.outs
            part = source.part
        else:
            self.source, self.ins = None, list(source)
            low, high = source[1:]
            part = source[0].shape[0] // sizes.nf
        self.part, self.half, self.width = part, part // 2, high.shape[2]
        nf, others = sizes.nf, low.shape[0]
        self.outs = [jax.ShapeDtypeStruct((part, self.width), BF)]
        piece = (self.half, self.width)
        self.sems = [
            pltpu.VMEM((self.half, sizes.ns * self.width), BF),
            pltpu.VMEM((nf,) + piece, BF),
            pltpu.VMEM(low.shape, BF),
            pltpu.VMEM(high.shape, BF),
            pltpu.VMEM(piece, BF),
            pltpu.VMEM((others,) + piece, BF),
            pltpu.VMEM((part, self.width), BF),
            DMA((nf + 3,)),
            DMA(()),
            DMA(()),
            DMA((others,)),
            DMA((others,)),
            DMA(()),
        ]

    @property
    def total(self):
        return self.r_sems[6]

    def loads(self):
        nf = self.place.sizes.nf
        if self.source is None:
            grads, low, high = self.r_ins
        else:
            grads = self.main.grads[self.source.name]
            low, high = self.source.r_outs
        g_low, g_high, r_low, r_high = self.r_sems[:4]
        sem = self.r_sems[7]
        out = [
            pltpu.make_async_copy(grads.at[pl.ds(0, self.half)], g_low, sem.at[nf]),
            pltpu.make_async_copy(low, r_low, sem.at[nf + 1]),
            pltpu.make_async_copy(high, r_high, sem.at[nf + 2]),
        ]
        for df in range(nf):
            rows = pl.ds(df * self.part + self.half, self.half)
            out.append(pltpu.make_async_copy(grads.at[rows, pl.ds(0, self.width)], g_high.at[df], sem.at[df]))
        return out

    def copies(self):
        place, nf, width = self.place, self.place.sizes.nf, self.width
        g_low, g_high, _, _, low, high = self.r_sems[:6]
        ys, yr, xs, xr = self.r_sems[8:12]
        out = [push(g_low.at[:, pl.ds(width, width)], low, ys, yr, place.twin())]
        for step in range(1, nf):
            at = step - 1
            out.append(push(g_high.at[step], high.at[at], xs.at[at], xr.at[at], place.across(step)))
        return out

    def store(self):
        return pltpu.make_async_copy(self.total, self.r_outs[0], self.r_sems[12])

    def at(self, moment):
        nf, width, half = self.place.sizes.nf, self.width, self.half
        g_low, g_high, r_low, r_high, low, high, total = self.r_sems[:7]
        if moment == self.steps[0]:
            if self.source is not None:
                self.source.wait_recv()
            for copy in self.loads():
                copy.start()
        if moment == self.steps[1]:
            for copy in self.loads():
                copy.wait()
            lanes = slice(width, 2 * width)

            def first(rows):
                value = g_low[rows, lanes].astype(F32)
                for at in range(nf - 1):
                    value = value + r_low[at, rows, lanes].astype(F32)
                g_low[rows, lanes] = value.astype(BF)
                for df in range(1, nf):
                    g_high[df, rows] = (g_high[df, rows].astype(F32) + r_high[df, rows].astype(F32)).astype(BF)

            by_rows(half, 32, first)
            for copy in self.copies():
                copy.start()
        if moment == self.steps[2]:
            for copy in self.copies():
                copy.wait_recv()
            lanes = slice(0, width)

            def second(rows):
                value = g_low[rows, lanes].astype(F32) + low[rows].astype(F32)
                for at in range(nf - 1):
                    value = value + r_low[at, rows, lanes].astype(F32)
                total[rows] = value.astype(BF)

            def third(rows):
                value = g_high[0, rows].astype(F32) + r_high[0, rows].astype(F32)
                for at in range(nf - 1):
                    value = value + high[at, rows].astype(F32)
                total[pl.ds(pl.multiple_of(rows.start + half, 32), 32)] = value.astype(BF)

            by_rows(half, 32, second)
            by_rows(half, 32, third)
            self.store().start()
        if moment == "end":
            for copy in self.copies():
                copy.wait_send()
            self.store().wait()


class Share(Rider):
    def __init__(self, kinds, array, out, count, moves, when="begin"):
        self.kinds, self.moves, self.when = kinds, moves, when
        self.ins, self.outs = [array], [out]
        self.sems = [DMA((count,)), DMA((count,))]

    def copies(self):
        send, recv = self.r_sems
        out = []
        for at, (device, source, target) in enumerate(self.moves(self.place, self.r_ins[0], self.r_outs[0])):
            if device is None:
                out.append(pltpu.make_async_copy(source, target, send.at[at]))
            else:
                out.append(push(source, target, send.at[at], recv.at[at], device))
        return out

    def at(self, moment):
        if moment == self.when:
            for copy in self.copies():
                copy.start()
        if moment == "end":
            for copy in self.copies():
                copy.wait()


def share_rows(sizes, value):
    rows, width = value.shape
    part = width // sizes.nf

    def moves(place, source, out):
        triples = []
        for dt in range(sizes.nt):
            device = place.plane(0, dt) if dt else None
            for df in range(sizes.nf):
                lanes = pl.ds(pl.multiple_of(lax.rem(place.f + df, sizes.nf) * part, part), part)
                triples.append((device, source.at[:, pl.ds(df * part, part)], out.at[place.t, :, lanes]))
        return triples

    out = jax.ShapeDtypeStruct((sizes.nt, rows, width), value.dtype)
    return Share(("plane",), value, out, sizes.nt * sizes.nf, moves)


class MainRows(Share):
    def __init__(self, sizes, rows, width, when):
        share = share_rows(sizes, jax.ShapeDtypeStruct((rows, width), BF))
        super().__init__(share.kinds, None, share.outs[0], share.sems[0].shape[0], share.moves, when)
        self.ins = []

    def copies(self):
        self.r_ins = [self.main.rows_ref]
        return super().copies()


class NormSum(Rider):
    kinds = ("ctx", "plane")

    def __init__(self, sizes, lines, places, piece, steps):
        self.ins, self.places, self.piece, self.steps = [lines], places, piece, steps
        count = lines.shape[0]
        self.outs = [jax.ShapeDtypeStruct((count, piece), F32)]
        self.around = [(df, dt) for df in range(sizes.nf) for dt in range(sizes.nt)][1:]
        block = (sizes.nf, count, piece)
        self.sems = [
            pltpu.VMEM(lines.shape, F32),
            pltpu.VMEM((sizes.nc,) + block, F32),
            pltpu.VMEM(block, F32),
            pltpu.VMEM((len(self.around), count, piece), F32),
            pltpu.VMEM((count, piece), F32),
            DMA(()),
            DMA((sizes.nc,)),
            DMA((sizes.nc,)),
            DMA((len(self.around),)),
            DMA((len(self.around),)),
            pltpu.VMEM((sizes.nc,) + block, F32),
        ]

    def rounds(self):
        place = self.place
        _, _, sums, _, _, _, _, _, send, recv, _ = self.r_sems
        return [
            push(sums.at[df], self.r_sems[3].at[at], send.at[at], recv.at[at], place.plane(df, dt))
            for at, (df, dt) in enumerate(self.around)
        ]

    def whole(self, step):
        box = self.r_sems[1].at[step]
        return push(box, box, self.r_sems[6].at[step], self.r_sems[7].at[step], self.place.ahead(step))

    def at(self, moment):
        place, sizes = self.place, self.place.sizes
        lines, first, sums, second, result, load, send, recv = self.r_sems[:8]

        def keep():
            return pltpu.make_async_copy(self.r_ins[0], lines, load)

        if moment == "begin":
            keep().start()
        if moment == self.steps[0]:
            keep().wait()
            for at, line in enumerate(self.places):
                lines[line : line + 1] = self.main.norm_ref[at : at + 1]
            blocks = self.r_sems[10]
            for dest in range(sizes.nc):
                for df in range(sizes.nf):
                    lane = (df * sizes.nc + dest) * self.piece
                    blocks[dest, df] = lines[:, lane : lane + self.piece]
            for step in range(1, sizes.nc):
                push(
                    blocks.at[lax.rem(place.c + step, sizes.nc)],
                    first.at[step],
                    send.at[step],
                    recv.at[step],
                    place.ahead(step),
                ).start()
            first[0] = blocks[place.c]
        if moment == self.steps[1]:
            for step in range(1, sizes.nc):
                self.whole(step).wait_recv()
            sums[...] = sum(first[step] for step in range(sizes.nc))
            for copy in self.rounds():
                copy.start()
        if moment == "end":
            for copy in self.rounds():
                copy.wait()
            for step in range(1, sizes.nc):
                self.whole(step).wait_send()
            result[...] = sums[0] + sum(second[at] for at in range(len(self.around)))
            out = pltpu.make_async_copy(result, self.r_outs[0], load)
            out.start()
            out.wait()


class BiasSum(Rider):
    kinds = ("ctx", "plane")

    def __init__(self, sizes, value, own, steps):
        self.ins, self.own, self.steps = [value], own, steps
        ns, count, width = value.shape
        self.width = width
        self.outs = [jax.ShapeDtypeStruct((sizes.nc, count, width), F32)]
        self.around = [(df, ds) for df in range(sizes.nf) for ds in range(ns)][1:]
        self.sems = [
            pltpu.VMEM(value.shape, F32),
            pltpu.VMEM((len(self.around), count, width), F32),
            pltpu.VMEM((count, width), F32),
            DMA(()),
            DMA((len(self.around),)),
            DMA((len(self.around),)),
            DMA((sizes.nc,)),
            DMA((sizes.nc,)),
        ]

    def rounds(self):
        lines, first, _, _, send, recv = self.r_sems[:6]
        nk = self.place.sizes.nk
        return [
            push(lines.at[ds], first.at[at], send.at[at], recv.at[at], self.place.plane(df, ds * nk))
            for at, (df, ds) in enumerate(self.around)
        ]

    def spreads(self):
        place, nc = self.place, self.place.sizes.nc
        sums, target = self.r_sems[2], self.r_outs[0].at[self.place.c]
        send, recv = self.r_sems[6:]
        return [push(sums, target, send.at[step], recv.at[step], place.ahead(step)) for step in range(1, nc)]

    def at(self, moment):
        lines, first, sums, load = self.r_sems[:4]

        def keep():
            return pltpu.make_async_copy(self.r_ins[0], lines, load)

        def mine():
            return pltpu.make_async_copy(sums, self.r_outs[0].at[self.place.c], load)

        if moment == "begin":
            keep().start()
        if moment == self.steps[0]:
            keep().wait()
            for ds in range(self.place.sizes.ns):
                for line in range(self.own):
                    at = (ds * self.own + line) * self.width
                    lines[ds, line : line + 1] = self.main.bias_ref[:, at : at + self.width]
            for copy in self.rounds():
                copy.start()
        if moment == self.steps[1]:
            for copy in self.rounds():
                copy.wait()
            sums[...] = lines[0] + sum(first[at] for at in range(len(self.around)))
            for copy in self.spreads() + [mine()]:
                copy.start()
        if moment == "end":
            for copy in self.spreads() + [mine()]:
                copy.wait()


class Moved:
    def __init__(self, hbm, scratch, inward):
        count = len(hbm)
        self.vmem = scratch[:count]
        self.copies = []
        for ref, buffer, sem in zip(hbm, scratch[:count], scratch[count:]):
            ends = (ref, buffer) if inward else (buffer, ref)
            self.copies.append(pltpu.make_async_copy(*ends, sem))

    @staticmethod
    def scratch(arrays):
        return [pltpu.VMEM(a.shape, a.dtype) for a in arrays] + [DMA(()) for _ in arrays]

    def start(self):
        for copy in self.copies:
            copy.start()


class Main:
    kinds = ("mate", "line")
    big, small, results, kept, gathered, work = [], [], [], [], [], []

    def __init__(self, **arrays):
        self.grads = {}

    @property
    def ins(self):
        return list(self.big) + list(self.small)

    @property
    def in_specs(self):
        return [ANY_SPEC] * len(self.big) + [VMEM_SPEC] * len(self.small)

    @property
    def outs(self):
        return list(self.results) + list(self.kept) + list(self.gathered)

    @property
    def out_specs(self):
        return [VMEM_SPEC] * len(self.results) + [ANY_SPEC] * (len(self.kept) + len(self.gathered))

    def scratch(self, sizes):
        self.layout = [
            Moved.scratch(self.big),
            Moved.scratch(self.kept),
            [pltpu.VMEM(a.shape, a.dtype) for a in self.work],
            scatter_scratch(sizes, self.rows, self.width),
        ] + [Gather.scratch(sizes) for _ in self.gathered]
        return [one for group in self.layout for one in group]

    def run(self, place, ins, outs, scratch, moment):
        cuts, at = [], 0
        for group in self.layout:
            cuts.append(scratch[at : at + len(group)])
            at += len(group)
        count = len(self.big)
        self.loads = Moved(ins[:count], cuts[0], True)
        results, kept = outs[: len(self.results)], outs[len(self.results) : len(self.results) + len(self.kept)]
        gathered = outs[len(self.results) + len(self.kept) :]
        self.stores = Moved(kept, cuts[1], False)
        self.work_refs, self.bufs, self.gather_sems = cuts[2], cuts[3], cuts[4:]
        self.loads.start()
        moment("begin")
        self.compute(place, self.loads.vmem, ins[count:], results, self.stores.vmem, gathered, moment)
        self.sent()
        for copy in self.stores.copies:
            copy.wait()

    def fetch(self, *which):
        for at in which:
            self.loads.copies[at].wait()

    def store(self, *which):
        for at in which:
            self.stores.copies[at].start()

    def spread(self, place, gathers, moment):
        for gather in gathers:
            gather.begin()
        moment("summed")
        for step in range(1, place.sizes.nc):
            for gather in gathers:
                gather.forward(step)
            if step == 1:
                moment("spread")
        moment("late")
        for gather in gathers:
            gather.end()


def by_rows(count, block, step):
    def one(at, carry):
        step(pl.ds(pl.multiple_of(at * block, block), block))
        return carry

    lax.fori_loop(0, count // block, one, 0)


def unit_rows_of(values):
    row_mean = jnp.mean(values, -1, keepdims=True)
    centred = values - row_mean
    row_var = jnp.mean(centred * centred, -1, keepdims=True)
    inverse = lax.rsqrt(row_var + EPS)
    return centred * inverse, inverse


def norm_back(grad_rows, saved_rows, gain_row):
    unit_rows, inverse = unit_rows_of(saved_rows)
    scaled = grad_rows * gain_row
    inner = inverse * (
        scaled
        - jnp.mean(scaled, -1, keepdims=True)
        - unit_rows * jnp.mean(scaled * unit_rows, -1, keepdims=True)
    )
    return inner, jnp.sum(grad_rows * unit_rows, 0, keepdims=True), jnp.sum(grad_rows, 0, keepdims=True)


def norm_forward(new_rows, norm_ref, at):
    unit_rows, _ = unit_rows_of(new_rows)
    return (unit_rows * norm_ref[at : at + 1] + norm_ref[at + 1 : at + 2]).astype(BF)


def swap_lanes(values):
    lane = lax.broadcasted_iota(jnp.int32, values.shape, 1) % HD
    width = values.shape[1]
    up = pltpu.roll(values, width - ROT // 2, 1)
    down = pltpu.roll(values, ROT // 2, 1)
    return jnp.where(lane < ROT // 2, up, jnp.where(lane < ROT, down, 0.0))


def allowed_of(label_col, label_row):
    length = label_col.shape[0]
    row = lax.broadcasted_iota(jnp.int32, (length, length), 0)
    col = lax.broadcasted_iota(jnp.int32, (length, length), 1)
    return (label_col == label_row) & (row >= col)


def like(shape, dtype):
    return jax.ShapeDtypeStruct(shape, dtype)


ROW_BLOCK = 128
OUT_BLOCK = 256


class AttnForward(Main):
    def __init__(self, full, w_qkv, w_out, bias, tables, stream, norm):
        super().__init__()
        self.rows, self.width = stream.shape
        length = full.shape[0]
        self.big = [full, w_qkv, w_out]
        self.small, self.norm_at = [bias[0], *tables, stream, norm[0]], norm[1]
        self.bias_at = bias[1]
        heads = w_out.shape[1] // HD
        self.results = [like(stream.shape, F32), like((length, heads), F32)]
        mixed = like((length, w_out.shape[1]), BF)
        self.kept = [like((length, w_qkv.shape[1]), BF), mixed, mixed, mixed]
        self.gathered = [like(full.shape, BF)]
        self.work = [like(full.shape, BF), like(stream.shape, BF)]

    def compute(self, place, big, small, results, kept, gathered, moment):
        full, w_qkv, w_out = big
        bias_ref, col_ref, row_ref, cos_ref, sin_ref, stream_ref, norm_ref = small
        new_ref, lse_ref = results
        proj_ref, mix_ref, q_ref, k_ref = kept
        part_ref, low_ref = self.work_refs
        length = full.shape[0]
        ns = place.sizes.ns
        width = w_out.shape[1] // ns
        self.fetch(0, 1)

        def project(rows):
            proj_ref[rows] = (dot_nn(full[rows], w_qkv[...]) + bias_ref[self.bias_at : self.bias_at + 1]).astype(BF)

        by_rows(length, ROW_BLOCK, project)
        self.store(0)
        allowed = allowed_of(col_ref[...], row_ref[...])
        cosine, sine = cos_ref[...], sin_ref[...]
        scaling = HD ** (-0.5)
        for b in range(ns):
            base, own = 3 * width * b, slice(b * width, (b + 1) * width)
            for ref, at in ((q_ref, 0), (k_ref, 1)):
                values = proj_ref[:, base + at * width : base + (at + 1) * width].astype(F32)
                ref[:, own] = (values * cosine + swap_lanes(values) * sine).astype(BF)
            for h in range(width // HD):
                span = slice(b * width + h * HD, b * width + (h + 1) * HD)
                scores = scaling * dot_nt(q_ref[:, span], k_ref[:, span])
                scores = jnp.where(allowed, scores, NEGATIVE)
                peak = jnp.max(scores, -1, keepdims=True)
                exponent = jnp.exp(scores - peak)
                total = jnp.sum(exponent, -1, keepdims=True)
                probs = (exponent * (1.0 / total)).astype(BF)
                at = base + 2 * width + h * HD
                mix_ref[:, span] = dot_nn(probs, proj_ref[:, at : at + HD]).astype(BF)
                at = b * (width // HD) + h
                lse_ref[:, at : at + 1] = peak + jnp.log(total)
        self.store(1, 2, 3)
        self.fetch(2)
        for at in range(0, self.width, OUT_BLOCK):
            part_ref[:, at : at + OUT_BLOCK] = dot_nt(mix_ref[...], w_out[at : at + OUT_BLOCK]).astype(BF)
        moment("ready")
        total, self.sent = scatter_part(place, part_ref, self.bufs, self.rows, moment)
        new_rows = stream_ref[...] + total
        new_ref[...] = new_rows
        low_ref[...] = norm_forward(new_rows, norm_ref, self.norm_at)
        self.spread(place, [Gather(place, low_ref, gathered[0], self.gather_sems[0], self.rows)], moment)


class FfnForward(Main):
    def __init__(self, full, w_gate, w_up, w_down, stream, norm, cotangent=None):
        super().__init__()
        self.rows, self.width = stream.shape
        length = full.shape[0]
        self.last = cotangent is not None
        self.big = [full, w_gate, w_up, w_down]
        self.small = [stream, cotangent if self.last else norm[0]]
        self.norm_at = norm and norm[1]
        self.results = [like(stream.shape, F32)]
        hidden = (length, w_gate.shape[1])
        self.kept = [like(hidden, F32), like(hidden, F32), like(hidden, BF)]
        self.gathered = [like(full.shape, BF)]
        self.work = [like(full.shape, BF), like(stream.shape, BF)]

    def compute(self, place, big, small, results, kept, gathered, moment):
        full, w_gate, w_up, w_down = big
        stream_ref = small[0]
        gate_ref, up_ref, act_ref = kept
        part_ref, low_ref = self.work_refs
        gather = None
        if self.last:
            gather = Gather(place, small[1], gathered[0], self.gather_sems[0], self.rows)
            gather.begin()
        self.fetch(0, 1, 2)

        def gates(rows):
            gate = dot_nn(full[rows], w_gate[...])
            up = dot_nn(full[rows], w_up[...])
            gate_ref[rows] = gate
            up_ref[rows] = up
            act_ref[rows] = (gate * jax.nn.sigmoid(gate) * up).astype(BF)

        by_rows(full.shape[0], ROW_BLOCK, gates)
        self.store(0, 1, 2)
        self.fetch(3)
        for at in range(0, self.width, OUT_BLOCK):
            part_ref[:, at : at + OUT_BLOCK] = dot_nt(act_ref[...], w_down[at : at + OUT_BLOCK]).astype(BF)
        moment("ready")
        steps = list(range(1, place.sizes.nc)) if self.last else []

        def meanwhile(name):
            if steps and name in ("sent", "inside1", "inside2"):
                gather.forward(steps.pop(0))
            moment(name)

        total, self.sent = scatter_part(place, part_ref, self.bufs, self.rows, meanwhile)
        new_rows = stream_ref[...] + total
        results[0][...] = new_rows
        if self.last:
            moment("summed")
            for step in steps:
                gather.forward(step)
            moment("spread")
            moment("late")
            gather.end()
            return
        low_ref[...] = norm_forward(new_rows, small[1], self.norm_at)
        self.spread(place, [Gather(place, low_ref, gathered[0], self.gather_sems[0], self.rows)], moment)


class FfnBack(Main):
    names = ["down", "gate", "up"]

    def __init__(self, grad_full, w_gate, w_up, w_down, gates, ups, acts, full, grad, saved, norm):
        super().__init__()
        self.rows, self.width = grad.shape
        self.big = [grad_full, acts, w_down, gates, ups, w_gate, w_up, full]
        self.small, self.norm_at = [grad, saved, norm[0]], norm[1]
        self.results = [like(grad.shape, F32), like((2, self.width), F32)]
        self.kept = [like(w_down.shape, BF), like(w_gate.shape, BF), like(w_up.shape, BF)]
        self.gathered = [like(full.shape, BF)]
        hidden = like(acts.shape, BF)
        self.work = [hidden, hidden, like(full.shape, BF), like(grad.shape, BF)]

    def compute(self, place, big, small, results, kept, gathered, moment):
        grad_full, act_ref, w_down, gate_ref, up_ref, w_gate, w_up, full = big
        grad_ref, saved_ref, norms_ref = small
        new_ref, norm_ref = results
        down_grad, gate_grad, up_grad = kept
        low_gate, low_up, part_ref, grad_low_ref = self.work_refs
        self.grads = {"down": down_grad, "gate": gate_grad, "up": up_grad}

        def weights_of(which, target, left, right, name):
            for at in range(0, self.width, OUT_BLOCK):
                span = slice(at, at + OUT_BLOCK)
                target[span] = dot_tn(left[:, span], right[...]).astype(BF)
            self.store(which)
            moment(name)

        self.fetch(0, 1)
        weights_of(0, down_grad, grad_full, act_ref, "downs")
        self.fetch(2, 3, 4)

        def gates(rows):
            act_grad = dot_nn(grad_full[rows], w_down[...])
            gate, up = gate_ref[rows], up_ref[rows]
            sg = jax.nn.sigmoid(gate)
            low_gate[rows] = (act_grad * up * sg * (1.0 + gate * (1.0 - sg))).astype(BF)
            low_up[rows] = (act_grad * gate * sg).astype(BF)

        by_rows(full.shape[0], ROW_BLOCK, gates)
        self.fetch(5, 6)
        for at in range(0, self.width, OUT_BLOCK):
            span = slice(at, at + OUT_BLOCK)
            part_ref[:, span] = (dot_nt(low_gate[...], w_gate[span]) + dot_nt(low_up[...], w_up[span])).astype(BF)
        moment("ready")
        self.fetch(7)

        def weights(name):
            if name == "sent":
                weights_of(1, gate_grad, full, low_gate, "gates")
            if name == "inside0":
                weights_of(2, up_grad, full, low_up, "ups")
            moment(name)

        total, self.sent = scatter_part(place, part_ref, self.bufs, self.rows, weights)
        inner, gain_grad, shift_grad = norm_back(total, saved_ref[...], norms_ref[self.norm_at : self.norm_at + 1])
        new_rows = grad_ref[...] + inner
        new_ref[...] = new_rows
        grad_low_ref[...] = new_rows.astype(BF)
        norm_ref[0:1] = gain_grad
        norm_ref[1:2] = shift_grad
        self.spread(place, [Gather(place, grad_low_ref, gathered[0], self.gather_sems[0], self.rows)], moment)


class AttnBack(Main):
    names = ["qkv", "out"]

    def __init__(self, grad_full, w_qkv, w_out, kept, full, tables, lse, grad, saved, norm, last):
        super().__init__()
        proj, mixed, q_rot, k_rot = kept
        self.rows, self.width = grad.shape
        self.last = last
        self.big = [grad_full, w_out, q_rot, k_rot, proj, w_qkv, full, mixed]
        self.small, self.norm_at = [*tables, lse, grad, saved, norm[0]], norm[1]
        self.results = [like(grad.shape, F32), like((2, self.width), F32), like((1, w_qkv.shape[1]), F32)]
        self.kept = [like(w_qkv.shape, BF), like(w_out.shape, BF)]
        self.gathered = [] if last else [like(full.shape, BF)]
        self.work = [like(proj.shape, BF), like(full.shape, BF), like(grad.shape, BF), like(mixed.shape, BF)]

    def compute(self, place, big, small, results, kept, gathered, moment):
        grad_full, w_out, q_ref, k_ref, proj_ref, w_qkv, full, mix_ref = big
        col_ref, row_ref, cos_ref, sin_ref, lse_ref, grad_ref, saved_ref, norms_ref = small
        new_ref, norm_ref, bias_ref = results
        qkv_ref, out_ref = kept
        self.norm_ref, self.bias_ref, self.rows_ref = norm_ref, bias_ref, self.work_refs[2]
        low_ref, part_ref, grad_low_ref, mix_grad_ref = self.work_refs
        ns = place.sizes.ns
        width = w_out.shape[1] // ns
        self.grads = {"qkv": qkv_ref, "out": out_ref}
        self.fetch(0, 1)

        def mixed_grad(rows):
            mix_grad_ref[rows] = dot_nn(grad_full[rows], w_out[...]).astype(BF)

        by_rows(full.shape[0], ROW_BLOCK, mixed_grad)
        self.fetch(2, 3, 4)
        allowed = allowed_of(col_ref[...], row_ref[...])
        cosine, sine = cos_ref[...], sin_ref[...]
        scaling = HD ** (-0.5)
        for b in range(ns):
            parts = [[], [], []]
            base = 3 * width * b
            for h in range(width // HD):
                span = slice(b * width + h * HD, b * width + (h + 1) * HD)
                at = b * (width // HD) + h
                q_rows, k_rows, out_grad = q_ref[:, span], k_ref[:, span], mix_grad_ref[:, span]
                scores = jnp.where(allowed, scaling * dot_nt(q_rows, k_rows), NEGATIVE)
                probs = jnp.exp(scores - lse_ref[:, at : at + 1])
                first = base + 2 * width + h * HD
                prob_grad = dot_nt(out_grad, proj_ref[:, first : first + HD])
                inner = jnp.sum(probs * prob_grad, -1, keepdims=True)
                score_low = (probs * (prob_grad - inner)).astype(BF)
                parts[0].append(scaling * dot_nn(score_low, k_rows))
                parts[1].append(scaling * dot_tn(score_low, q_rows))
                parts[2].append(dot_tn(probs.astype(BF), out_grad))
            for at in range(3):
                values = jnp.concatenate(parts[at], axis=1)
                if at < 2:
                    values = values * cosine - swap_lanes(values) * sine
                low = values.astype(BF)
                lanes = slice(base + at * width, base + (at + 1) * width)
                low_ref[:, lanes] = low
                bias_ref[:, lanes] = jnp.sum(low.astype(F32), 0, keepdims=True)
        self.fetch(5)
        for at in range(0, self.width, OUT_BLOCK):
            part_ref[:, at : at + OUT_BLOCK] = dot_nt(low_ref[...], w_qkv[at : at + OUT_BLOCK]).astype(BF)
        moment("ready")
        self.fetch(6, 7)

        def weights(name):
            if name == "sent":
                for at in range(0, self.width, OUT_BLOCK):
                    span = slice(at, at + OUT_BLOCK)
                    qkv_ref[span] = dot_tn(full[:, span], low_ref[...]).astype(BF)
                    out_ref[span] = dot_tn(grad_full[:, span], mix_ref[...]).astype(BF)
                self.store(0, 1)
                moment("attns")
            moment(name)

        total, self.sent = scatter_part(place, part_ref, self.bufs, self.rows, weights)
        inner, gain_grad, shift_grad = norm_back(total, saved_ref[...], norms_ref[self.norm_at : self.norm_at + 1])
        new_rows = grad_ref[...] + inner
        new_ref[...] = new_rows
        norm_ref[0:1] = gain_grad
        norm_ref[1:2] = shift_grad
        grad_low_ref[...] = new_rows.astype(BF)
        if self.last:
            for name in ("summed", "spread", "late"):
                moment(name)
            return
        self.spread(place, [Gather(place, grad_low_ref, gathered[0], self.gather_sems[0], self.rows)], moment)


class Alone:
    kinds, ins, in_specs, outs, out_specs = (), [], [], [], []

    def scratch(self, sizes):
        return []

    def run(self, place, ins, outs, scratch, moment):
        moment("begin")


class Start:
    kinds = ("mate", "ctx", "fsdp", "twin")

    def __init__(self, sizes, small, hidden, cotangent, piece, q_sub, layers, chains, following):
        self.sizes, self.piece, self.chains, self.following = sizes, piece, chains, following
        self.q_sub, self.layers = q_sub, layers
        lines, lanes = small.shape
        count, self.width = hidden.shape
        self.rows = count // (sizes.ns * sizes.nk)
        group = sizes.nc * sizes.nk * self.rows
        self.ins, self.in_specs = [small, hidden, cotangent], [VMEM_SPEC] * 3
        self.outs = [
            like((sizes.nf, sizes.nc * lines, lanes), F32),
            like((lines, lanes), F32),
            like((lines, self.width), F32),
            like((self.rows, self.width), F32),
            like((self.rows, self.width), BF),
            like((group, 1), jnp.int32),
            like((1, group), jnp.int32),
            like((group, q_sub), F32),
            like((group, q_sub), F32),
            like((layers, sizes.ns * 3 * q_sub), F32),
            like((group, self.width), BF),
        ]
        self.out_specs = [VMEM_SPEC] * 10 + [ANY_SPEC]

    def scratch(self, sizes):
        others = max(sizes.nf - 1, 1)
        small = [DMA((sizes.nc,)), DMA((sizes.nc,)), DMA((others,)), DMA((others,)), DMA(()), DMA(())]
        return small + [pltpu.VMEM((self.rows, self.width), BF)] + Gather.scratch(sizes)

    def run(self, place, ins, outs, scratch, moment):
        sizes, rows, width = self.sizes, self.rows, self.width
        small_ref, hidden_ref, cotangent_ref = ins
        all_ref, twin_ref, norm_ref, stream_ref, grad_ref = outs[:5]
        full_ref = outs[10]
        cs, cr, fs, fr, ts, tr = scratch[:6]
        low_ref = scratch[6]
        lines = small_ref.shape[0]

        def line_of(c):
            return pl.ds(pl.multiple_of(c * lines, lines), lines)

        to_context = [
            push(small_ref, all_ref.at[0, line_of(place.c)], cs.at[step], cr.at[step], place.ahead(step))
            for step in range(1, sizes.nc)
        ]
        to_twin = push(small_ref, twin_ref, ts, tr, place.twin())
        moment("begin")
        for copy in to_context + [to_twin]:
            copy.start()
        for exchange, _ in self.chains:
            exchange.start()
        all_ref[0, line_of(place.c)] = small_ref[...]
        own_rows = pl.ds(pl.multiple_of((place.s * sizes.nk + place.k) * rows, rows), rows)
        part = width // sizes.nf
        for df in range(sizes.nf):
            lanes = pl.ds(pl.multiple_of(lax.rem(place.f + df, sizes.nf) * part, part), part)
            stream_ref[:, df * part : (df + 1) * part] = hidden_ref[own_rows, lanes].astype(F32)
            grad_ref[:, df * part : (df + 1) * part] = cotangent_ref[own_rows, lanes]
        unit_rows, _ = unit_rows_of(stream_ref[...])
        for copy in to_context:
            copy.wait()
        to_across = [
            push(all_ref.at[0], all_ref.at[sizes.nf - step], fs.at[step - 1], fr.at[step - 1], place.across(step))
            for step in range(1, sizes.nf)
        ]
        for copy in to_across:
            copy.start()
        for copy in to_across + [to_twin]:
            copy.wait()
        for df in range(sizes.nf):
            for c in range(sizes.nc):
                at = (df * sizes.nc + c) * self.piece
                norm_ref[:, at : at + self.piece] = all_ref[df, c * lines : (c + 1) * lines, : self.piece]
        low_ref[...] = (unit_rows * norm_ref[0:1] + norm_ref[1:2]).astype(BF)
        gather = Gather(place, low_ref, full_ref, scratch[7:12], rows)
        for exchange, spread in self.chains:
            exchange.wait_own()
            spread.first(place.c)
        self.tables(place, small_ref, all_ref, twin_ref, *outs[5:10])
        for step in range(1, sizes.nc):
            for exchange, spread in self.chains:
                exchange.wait_from(step)
                spread.first(lax.rem(place.c + sizes.nc - step, sizes.nc))
        gather.begin()
        for exchange in self.following:
            exchange.start()
        for step in range(sizes.nc):
            for _, chain in self.chains:
                chain.second(lax.rem(place.c + sizes.nc - step, sizes.nc))
            if step:
                gather.forward(step)
        gather.end()
        for exchange, spread in self.chains:
            exchange.wait_sent()
            for block in range(sizes.nc):
                spread.finish(block)
        for exchange in self.following:
            exchange.finish()


    def tables(self, place, small_ref, all_ref, twin_ref, col_ref, row_ref, cos_ref, sin_ref, bias_ref):
        sizes, q_sub = self.sizes, self.q_sub
        lines = small_ref.shape[0]
        shard = sizes.nk * self.rows
        for c in range(sizes.nc):
            mine = jnp.zeros((1, shard), F32)
            for at in range(sizes.ns):
                line = c * lines + at
                found = all_ref[0, line : line + 1, self.piece : self.piece + shard]
                mine = jnp.where(place.s == at, found, mine)
            row_ref[:, c * shard : (c + 1) * shard] = mine.astype(jnp.int32)
        length = row_ref.shape[1]
        row = row_ref[...].astype(F32)
        at_row = lax.broadcasted_iota(jnp.int32, (length, length), 0)
        at_col = lax.broadcasted_iota(jnp.int32, (length, length), 1)
        col = jnp.sum(jnp.where(at_row == at_col, row, 0.0), -1, keepdims=True)
        col_ref[...] = col.astype(jnp.int32)
        before = jnp.sum(jnp.where(row < col, 1.0, 0.0), -1, keepdims=True)
        places = lax.broadcasted_iota(jnp.int32, (length, 1), 0).astype(F32)
        lane = lax.broadcasted_iota(jnp.int32, (1, q_sub), 1) % HD
        turn = jnp.exp((lane % (ROT // 2)).astype(F32) * (-2.0 * math.log(ROPE_BASE) / ROT))
        angles = (places - before) * jnp.where(lane < ROT, turn, 0.0)
        sine = jnp.sin(angles)
        cos_ref[...] = jnp.cos(angles)
        sin_ref[...] = jnp.where(lane < ROT // 2, -sine, sine)
        for layer in range(self.layers):
            for ds, source in enumerate((small_ref, twin_ref)):
                for at in range(3):
                    line = 3 * layer + at
                    lanes = slice((ds * 3 + at) * q_sub, (ds * 3 + at + 1) * q_sub)
                    bias_ref[layer : layer + 1, lanes] = source[line : line + 1, self.piece + shard :]


class Guest(Rider):
    def __init__(self, rider):
        self.kinds, self.ins, self.outs, self.sems = rider.kinds, rider.ins, rider.outs, rider.sems
        self.rider = rider

    def bind(self, *refs):
        self.rider.bind(*refs)


def comm_kernel(sizes, main, riders, kinds, layout, *refs):
    cuts, at = [], 0
    for size in layout:
        cuts.append(refs[at : at + size])
        at += size
    count = len(riders)
    ins, outs, scratch = cuts[: count + 1], cuts[count + 1 : 2 * count + 2], cuts[2 * count + 2 :]
    place = Place(sizes)
    for i, rider in enumerate(riders):
        rider.bind(place, ins[i + 1], outs[i + 1], scratch[i + 1], main)
    count = greet(place, kinds)

    def moment(name):
        if name == "begin":
            pl.semaphore_wait(pltpu.get_barrier_semaphore(), count)
        for rider in riders:
            rider.at(name)

    main.run(place, ins[0], outs[0], scratch[0], moment)
    moment("end")


def comm_call(sizes, collective_id, main, riders=(), micros=50):
    kinds = set(main.kinds)
    for rider in riders:
        kinds |= set(rider.kinds)
    main_scratch = main.scratch(sizes)
    operands, in_specs = list(main.ins), list(main.in_specs)
    outs, out_specs = list(main.outs), list(main.out_specs)
    scratch = list(main_scratch)
    aliases = {}
    for rider in riders:
        if rider.aliased:
            aliases[len(operands)] = len(outs)
        operands += rider.ins
        in_specs += [ANY_SPEC] * len(rider.ins)
        outs += rider.outs
        out_specs += [ANY_SPEC] * len(rider.outs)
        scratch += rider.sems
    layout = [len(main.ins)] + [len(rider.ins) for rider in riders]
    layout += [len(main.outs)] + [len(rider.outs) for rider in riders]
    layout += [len(main_scratch)] + [len(rider.sems) for rider in riders]
    results = pl.pallas_call(
        functools.partial(comm_kernel, sizes, main, riders, kinds, layout),
        out_shape=outs,
        in_specs=in_specs,
        out_specs=out_specs,
        scratch_shapes=scratch,
        input_output_aliases=aliases,
        compiler_params=pltpu.CompilerParams(
            collective_id=collective_id, has_side_effects=True, vmem_limit_bytes=VMEM_BYTES
        ),
        cost_estimate=pl.CostEstimate(flops=0, bytes_accessed=micros * 3 * MIB, transcendentals=0),
    )(*operands)
    groups, at = [], 0
    for size in [len(main.outs)] + [len(rider.outs) for rider in riders]:
        groups.append(list(results[at : at + size]))
        at += size
    return groups[0], groups[1:]


def finish_kernel(count, hidden, *refs):
    ins, (qkv_out, out_out, gate_up_out, down_out) = refs[: 5 * count], refs[5 * count :]
    triple, rows, q_cols = qkv_out.shape[1:]
    for layer in range(count):

        @pl.when(pl.program_id(0) == layer)
        def _():
            qkv, out, gate, up, down = ins[5 * layer : 5 * layer + 5]

            def some(span):
                for at in range(triple):
                    qkv_out[0, at, span] = qkv[span, at * q_cols : (at + 1) * q_cols].astype(F32)
                out_out[0, span] = out[span].astype(F32)
                gate_up_out[0, span, 0] = gate[span, :hidden].astype(F32)
                gate_up_out[0, span, 1] = up[span, :hidden].astype(F32)
                down_out[0, span] = down[span, :hidden].astype(F32)

            by_rows(rows, 64, some)


def finish(grads, q_cols, hidden):
    count = len(grads)
    rows = grads[0][0].shape[0]
    shapes = [(3, rows, q_cols), (rows, q_cols), (rows, 2, hidden), (rows, hidden)]

    def block(shape):
        return pl.BlockSpec((1,) + shape, lambda layer: (layer,) + (0,) * len(shape))

    return pl.pallas_call(
        functools.partial(finish_kernel, count, hidden),
        grid=(count,),
        out_shape=[jax.ShapeDtypeStruct((count,) + shape, F32) for shape in shapes],
        in_specs=[VMEM_SPEC] * (5 * count),
        out_specs=[block(shape) for shape in shapes],
        compiler_params=pltpu.CompilerParams(vmem_limit_bytes=VMEM_BYTES),
    )(*[one for layer in grads for one in layer])


def body(
    mesh,
    hidden_in,
    segment_ids,
    norm_gains,
    norm_shifts,
    qkv_weight,
    qkv_bias,
    out_weight,
    gate_up_weight,
    down_weight,
    cotangent,
):
    ns, shard_rows, width = hidden_in.shape
    sizes = Sizes(mesh, ns)
    nf, nc, nk, nt = sizes.nf, sizes.nc, sizes.nk, sizes.nt
    f, c, t = lax.axis_index("fsdp"), lax.axis_index("context"), lax.axis_index("tensor")
    s = t // nk
    layers = qkv_weight.shape[0]
    rows = shard_rows // nk
    part = width // nf
    piece = part // nc
    q_cols = qkv_weight.shape[3]
    q_sub = q_cols // nc
    hidden = gate_up_weight.shape[3]
    f_sub = -(-hidden // (nc * TILE)) * TILE
    f_cols = nc * f_sub

    qkv_flat = qkv_weight.transpose(0, 2, 1, 3).reshape(layers * 3 * piece, q_cols)
    out_flat = out_weight.reshape(layers * piece, q_cols)
    fill = ((0, 0), (0, f_cols - hidden))
    down_flat = jnp.pad(down_weight.reshape(layers * piece, hidden), fill)
    gate_up_flat = jnp.pad(gate_up_weight, ((0, 0), (0, 0)) + fill).reshape(layers * piece, 2 * f_cols)

    def exchange(name, layer, when="begin", finish="end"):
        first = layer * piece
        array, corners, sub = {
            "qkv": (qkv_flat, [((3 * layer + at) * piece, 0) for at in range(3)], q_sub),
            "out": (out_flat, [(first, 0)], q_sub),
            "gate": (gate_up_flat, [(first, 0)], f_sub),
            "up": (gate_up_flat, [(first, f_cols)], f_sub),
            "down": (down_flat, [(first, 0)], f_sub),
        }[name]
        return WeightExchange(sizes, piece, array, corners, sub, when, finish)

    norms = jnp.stack([norm_gains, norm_shifts], axis=2).reshape(4 * layers, piece).astype(F32)
    own_bias = lax.dynamic_slice_in_dim(qkv_bias, c * q_sub, q_sub, 2).reshape(3 * layers, q_sub).astype(F32)
    lines = -(-max(4 * layers, 3 * layers, ns) // 8) * 8

    def lined(value):
        return jnp.pad(value, ((0, lines - value.shape[0]), (0, 0)))

    small = jnp.concatenate([lined(norms), lined(segment_ids.astype(F32)), lined(own_bias)], axis=1)
    chains = []
    for name in ("qkv", "out"):
        moved = exchange(name, 0, finish=None)
        chains.append((moved, Spread(sizes, moved, blocks=nc, steps=(None, None))))
    following = [exchange(name, 0, finish=None) for name in ("gate", "up")]
    start = Start(
        sizes,
        small,
        hidden_in.reshape(ns * shard_rows, width),
        cotangent.reshape(ns * shard_rows, width),
        piece,
        q_sub,
        layers,
        chains,
        following,
    )
    guests = [Guest(one) for chain in chains for one in chain] + [Guest(one) for one in following]
    results, extra = comm_call(sizes, 1, start, guests, 80)
    norm_rows, stream, grad_low = results[2:5]
    tables, bias_rows, full_one = results[5:9], results[9], results[10]
    w_qkv, w_out, gate_mine, up_mine = (extra[at][0] for at in (1, 3, 4, 5))

    def norm_of(layer, which):
        return (norm_rows, (layer * 2 + which) * 2)

    kept = []
    gate_own = None
    for layer in range(layers):
        more = layer + 1 < layers
        down_first = exchange("down", layer, finish=None)
        riders = [Spread(sizes, gate_mine) if gate_own is None else SpreadRelay(sizes, gate_own), Spread(sizes, up_mine)]
        riders += [down_first, Spread(sizes, down_first, steps=("inside0", "spread"))]
        if more:
            riders += [exchange("qkv", layer + 1, "spread"), exchange("out", layer + 1, "spread")]
        main = AttnForward(
            full_one, w_qkv, w_out, (bias_rows, layer), tables, stream, norm_of(layer, 1)
        )
        results, extra = comm_call(sizes, 2 + 2 * layer, main, riders, 85)
        middle, lse, proj, mixed, q_rot, k_rot, full_two = results
        w_gate, w_up, w_down = extra[0][0], extra[1][0], extra[3][0]
        attn_kept = (full_one, w_qkv, w_out, (proj, mixed, q_rot, k_rot), lse, stream)
        if more:
            gate_first = exchange("gate", layer + 1, finish=None)
            riders = [Spread(sizes, extra[4][0]), Spread(sizes, extra[5][0])]
            riders += [gate_first, SpreadOwn(sizes, gate_first, blocks=nc, steps=("summed",))]
            riders.append(exchange("up", layer + 1, "spread"))
            main = FfnForward(
                full_two, w_gate, w_up, w_down, middle, norm_of(layer + 1, 0)
            )
        else:
            riders = []
            main = FfnForward(full_two, w_gate, w_up, w_down, middle, None, grad_low)
        results, extra = comm_call(sizes, 3 + 2 * layer, main, riders, 55)
        stream, gates, ups, acts, full = results
        kept.append(attn_kept + (full_two, w_gate, w_up, w_down, gates, ups, acts, middle))
        if more:
            full_one = full
            w_qkv, w_out, _, gate_own, up_mine = (one[0] for one in extra)
        else:
            grad_full = full

    first_id = 2 + 2 * layers
    stream_out = stream
    grad = grad_low.astype(F32)
    firsts, totals = {}, {}
    done, norm_grads, bias_grads = {}, {}, {}
    calls = [0]

    def sub_of(name):
        return q_sub if name in ("qkv", "out") else f_sub

    def run(main, steps, others, micros):
        riders, after = [], []
        here = {}

        def ride(rider, what, name):
            here[(what, name)] = rider
            riders.append(rider)
            after.append((what, name))

        for what, name, layer, when in steps:
            at = (name, layer)
            if what == "first":
                ride(GradFirst(sizes, name, *main.kept[main.names.index(name)].shape, when), what, at)
            elif what == "middle":
                ride(GradMiddle(sizes, here.get(("first", at)) or firsts[at], when), what, at)
            else:
                ride(GradExchange(sizes, here.get(("middle", at)) or totals[at], sub_of(name), when), what, at)
        for name, rider in others:
            ride(rider, "other", name)
        results, extra = comm_call(sizes, first_id + calls[0], main, riders, micros)
        calls[0] += 1
        for (what, at), out in zip(after, extra):
            if what == "first":
                firsts[at] = (results[len(main.results) + main.names.index(at[0])], *out)
            elif what == "middle":
                totals[at] = out[0]
            else:
                done[at] = out[0]
        return results

    attn, ffn = ("qkv", "out"), ("gate", "up")
    for layer in range(layers - 1, -1, -1):
        full_one, w_qkv, w_out, attn_kept, lse, stream, full_two, w_gate, w_up, w_down, gates, ups, acts, middle = kept[
            layer
        ]
        main = FfnBack(grad_full, w_gate, w_up, w_down, gates, ups, acts, full_two, grad, middle, norm_of(layer, 1))
        top = layer + 1 == layers
        steps, others = [], []
        if not top:
            steps += [("exchange", "gate", layer + 1, "begin"), ("exchange", "up", layer + 1, "spread")]
            steps += [("exchange", name, layer + 1, "late") for name in attn]
        steps += [("first", "down", layer, "downs"), ("first", "gate", layer, "gates"), ("first", "up", layer, "ups")]
        steps += [("middle", "down", layer, ("inside1", "inside2", "late"))]
        if not top:
            steps += [("middle", name, layer, ("late", "late", "end")) for name in ffn]
        grad, norm_grads[(layer, 1)], _, _, _, middle_full = run(main, steps, others, 60)
        main = AttnBack(
            middle_full, w_qkv, w_out, attn_kept, full_one, tables, lse, grad, stream, norm_of(layer, 0), layer == 0
        )
        steps, others = [("exchange", "down", layer, "begin")], []
        if top:
            others.append(("block_out", share_rows(sizes, stream_out.astype(BF))))
        if not top:
            steps += [("exchange", "gate", layer, "begin"), ("exchange", "up", layer, "inside0")]
        if layer == 0:
            none = jnp.zeros((2, width), F32)
            pairs = [[norm_grads.get((at, which), none) for which in range(2)] for at in range(layers)]
            lines = jnp.stack([jnp.stack(pair, 1) for pair in pairs], 1).reshape(4 * layers, width)
            none = jnp.zeros((1, ns * 3 * q_sub), F32)
            bias = jnp.concatenate([bias_grads.get(at, none) for at in range(layers)]).reshape(layers, ns, 3, q_sub)
            bias = bias.transpose(1, 0, 2, 3).reshape(ns, 3 * layers, q_sub)
            bias = jnp.pad(bias, ((0, 0), (0, -3 * layers % 8), (0, 0)))
            others += [
                ("input_grad", MainRows(sizes, rows, width, "summed")),
                ("norm", NormSum(sizes, lines, (0, 2 * layers), piece, ("summed", "spread"))),
                ("bias", BiasSum(sizes, bias, 3, ("attns", "inside0"))),
            ]
            steps += [("first", name, 0, "attns") for name in attn]
            steps += [("middle", name, 0, ("inside0", "inside0", "inside2")) for name in attn]
            steps += [("exchange", name, 0, "inside2") for name in attn]
        else:
            steps += [("middle", name, layer, ("begin", "inside0", "late")) for name in (ffn if top else ())]
            steps += [("first", name, layer, "attns") for name in attn]
            steps += [("middle", name, layer, ("spread", "spread", "late")) for name in attn]
        results = run(main, steps, others, 60)
        grad, norm_grads[(layer, 0)], bias_grads[layer] = results[:3]
        if layer > 0:
            grad_full = results[5]
    block_out = done["block_out"].reshape(ns, shard_rows, width)
    input_grad = done["input_grad"].reshape(ns, shard_rows, width).astype(F32)
    norm_total = done["norm"].reshape(2, layers, 2, piece)
    bias_total = done["bias"][:, : 3 * layers].reshape(nc, layers, 3, q_sub)
    bias_total = bias_total.transpose(1, 2, 0, 3).reshape(layers, 3, q_cols)

    grads = [[done[(name, layer)] for name in ("qkv", "out", "gate", "up", "down")] for layer in range(layers)]
    qkv_grad, out_grad, gate_up_grad, down_grad = finish(grads, q_cols, hidden)
    return (
        block_out,
        input_grad,
        norm_total[0],
        norm_total[1],
        qkv_grad.transpose(0, 2, 1, 3),
        bias_total,
        out_grad,
        gate_up_grad,
        down_grad,
    )


def solution(mesh):
    return jax.shard_map(
        functools.partial(body, mesh),
        mesh=mesh,
        in_specs=(
            P("fsdp", "context", None),
            P("fsdp", "context"),
            P(None, None, ("fsdp", "context")),
            P(None, None, ("fsdp", "context")),
            P(None, ("fsdp", "context"), None, "tensor"),
            P(None, None, "tensor"),
            P(None, ("fsdp", "context"), "tensor"),
            P(None, ("fsdp", "context"), None, "tensor"),
            P(None, ("fsdp", "context"), "tensor"),
            P("fsdp", "context", None),
        ),
        out_specs=(
            P("fsdp", "context", None),
            P("fsdp", "context", None),
            P(None, None, ("fsdp", "context")),
            P(None, None, ("fsdp", "context")),
            P(None, ("fsdp", "context"), None, "tensor"),
            P(None, None, "tensor"),
            P(None, ("fsdp", "context"), "tensor"),
            P(None, ("fsdp", "context"), None, "tensor"),
            P(None, ("fsdp", "context"), "tensor"),
        ),
        check_vma=False,
    )
```
